128 devices in a mesh: dp: 2 (over core), ctx: 8 (over x, y_hi), heads: 8 (over y_lo, z).
Axes of the slice: x: 4, y: 4 (y_hi: 2, y_lo: 2; y = y_hi * 2 + y_lo), z: 4, core: 2. Of those that a mesh axis runs over, the one named last changes fastest.
Arguments:
- tokens: bfloat16 [16, 1024, 1536], P(('dp', 'heads'), 'ctx'), may hold values from -6 to 6
- span_order: int32 [16], replicated, may hold values from 0 to 15, each once
- attn_gain: bfloat16 [2, 1536], P(None, ('dp', 'ctx')), may hold values from 0.099609375 to 1.8984375
- w_query: bfloat16 [2, 1536, 1536], P(None, ('dp', 'ctx')), may hold values from -0.15625 to 0.15625
- key_matrix: bfloat16 [2, 1536, 768], P(None, ('dp', 'ctx')), may hold values from -0.15625 to 0.15625
- value_matrix: bfloat16 [2, 1536, 768], P(None, ('dp', 'ctx')), may hold values from -0.15625 to 0.15625
- w_out: bfloat16 [2, 1536, 1536], P(None, ('dp', 'ctx')), may hold values from -0.875 to 0.875
- mlp_gain: bfloat16 [2, 1536], P(None, ('dp', 'ctx')), may hold values from 0.099609375 to 1.8984375
- w_gate: bfloat16 [2, 1536, 4096], P(None, ('dp', 'ctx')), may hold values from -0.15625 to 0.15625
- w_up: bfloat16 [2, 1536, 4096], P(None, ('dp', 'ctx')), may hold values from -0.15625 to 0.15625
- w_down: bfloat16 [2, 4096, 1536], P(None, ('dp', 'ctx')), may hold values from -0.09375 to 0.09375
- cotangent: bfloat16 [16, 1024, 1536], P(('dp', 'heads'), 'ctx'), may hold values from -6 to 6
Outputs:
- block_out: bfloat16 [16, 1024, 1536], P(('dp', 'heads'), 'ctx')
- input_grad: float32 [16, 1024, 1536], P(('dp', 'heads'), 'ctx')
- attn_gain_grad: float32 [2, 1536], P(None, ('dp', 'ctx', 'heads'))
- w_query_grad: float32 [2, 1536, 1536], P(None, ('dp', 'ctx', 'heads'))
- w_key_grad: float32 [2, 1536, 768], P(None, ('dp', 'ctx', 'heads'))
- w_value_grad: float32 [2, 1536, 768], P(None, ('dp', 'ctx', 'heads'))
- w_out_grad: float32 [2, 1536, 1536], P(None, ('dp', 'ctx', 'heads'))
- mlp_gain_grad: float32 [2, 1536], P(None, ('dp', 'ctx', 'heads'))
- w_gate_grad: float32 [2, 1536, 4096], P(None, ('dp', 'ctx', 'heads'))
- w_up_grad: float32 [2, 1536, 4096], P(None, ('dp', 'ctx', 'heads'))
- w_down_grad: float32 [2, 4096, 1536], P(None, ('dp', 'ctx', 'heads'))
The draws below stay inside these ranges and needn't reach their ends.
Inputs may be any that keep to these rules, and one draw needn't show every extreme that they name: span_order[j] is the place in its sequence of the j-th stored block of 64 positions; every value appears once.
All inputs are finite; a program needn't handle non-finite values.
Results may differ from the reference program's by a relative error of at most 0.039.
Values may be sent and summed in bfloat16 or wider, within the bound.
A program may use at most 320 MiB of HBM per device.

```python
import math
import jax
import jax.numpy as jnp
from jax import lax

MODEL_WIDTH = 1536
FF = 4096
QUERY_HEADS = 16
KEY_VALUE_HEADS = 8
HEAD_SIZE = 96
LAYER_COUNT = 2
SEQS = 16
SEQ_LEN = 1024
SPAN = 64
N_CTX = 8


def steps_of(rng, shape, cuts, smallest, high):
    level, own = 1.0, jax.random.fold_in(rng, 6)
    for dim, shards_of in cuts:
        draws = jnp.exp(jax.random.uniform(jax.random.fold_in(own, dim), (shards_of,), jnp.float32, smallest / len(cuts), high / len(cuts)))
        level = level * jnp.repeat(draws, shape[dim] // shards_of).reshape([-1 if axis == dim else 1 for axis in range(len(shape))])
    return level


def scatter_about(stream_key, dims, width, most, split=(), kind=jnp.bfloat16):
    array = width * jax.random.normal(stream_key, dims, jnp.float32)
    if split:
        array = array * steps_of(stream_key, dims, split, -0.22, 0.18)
    return jnp.clip(array, -most, most).astype(kind)


def setup_inputs(seed: int = 0) -> dict:
    key_list = jax.random.split(jax.random.key(seed), 13)
    tokens = scatter_about(key_list[0], (SEQS, SEQ_LEN, MODEL_WIDTH), 1.0, 6.0, ((0, 16), (1, 8)))
    span_order = jax.random.permutation(key_list[1], 2 * N_CTX).astype(jnp.int32)
    attn_gain = jnp.clip(1.0 + 0.18 * jax.random.normal(key_list[2], (LAYER_COUNT, MODEL_WIDTH), jnp.float32), 0.099609375, 1.8984375).astype(jnp.bfloat16)
    w_query = scatter_about(key_list[3], (LAYER_COUNT, MODEL_WIDTH, QUERY_HEADS * HEAD_SIZE), MODEL_WIDTH ** -0.5, 0.15625, ((1, 16),))
    key_matrix = scatter_about(key_list[4], (LAYER_COUNT, MODEL_WIDTH, KEY_VALUE_HEADS * HEAD_SIZE), MODEL_WIDTH ** -0.5, 0.15625, ((1, 16),))
    value_matrix = scatter_about(key_list[5], (LAYER_COUNT, MODEL_WIDTH, KEY_VALUE_HEADS * HEAD_SIZE), MODEL_WIDTH ** -0.5, 0.15625, ((1, 16),))
    w_out = scatter_about(key_list[6], (LAYER_COUNT, QUERY_HEADS * HEAD_SIZE, MODEL_WIDTH), (QUERY_HEADS * HEAD_SIZE // 32) ** -0.5, 0.875, ((1, 16),))
    mlp_gain = jnp.clip(1.0 + 0.18 * jax.random.normal(key_list[7], (LAYER_COUNT, MODEL_WIDTH), jnp.float32), 0.099609375, 1.8984375).astype(jnp.bfloat16)
    w_gate = scatter_about(key_list[8], (LAYER_COUNT, MODEL_WIDTH, FF), MODEL_WIDTH ** -0.5, 0.15625, ((1, 16),))
    w_up = scatter_about(key_list[9], (LAYER_COUNT, MODEL_WIDTH, FF), MODEL_WIDTH ** -0.5, 0.15625, ((1, 16),))
    w_down = scatter_about(key_list[10], (LAYER_COUNT, FF, MODEL_WIDTH), FF ** -0.5, 0.09375, ((1, 16),))
    cotangent = scatter_about(key_list[11], (SEQS, SEQ_LEN, MODEL_WIDTH), 1.0, 6.0, ((0, 16), (1, 8)))
    return {"tokens": tokens, "span_order": span_order, "attn_gain": attn_gain, "w_query": w_query, "key_matrix": key_matrix, "value_matrix": value_matrix, "w_out": w_out, "mlp_gain": mlp_gain, "w_gate": w_gate, "w_up": w_up, "w_down": w_down, "cotangent": cotangent}


@jax.custom_vjp
def low(v):
    return lax.optimization_barrier(v.astype(jnp.bfloat16)).astype(jnp.float32)

@jax.custom_vjp
def low_back(v):
    return v

def low_keep(v):
    return (low(v), None)

def low_pass(kept, grad):
    return (grad,)

def back_keep(v):
    return (v, None)

def back_low(kept, grad):
    return (low(grad),)
low.defvjp(low_keep, low_pass)
low_back.defvjp(back_keep, back_low)
rope_base = 100000.0
norm_eps = 1e-05

def matmul(left_side, right_side):
    return jnp.dot(left_side, right_side, precision=lax.Precision.HIGHEST)

def rms_norm(values, gain):
    return values * lax.rsqrt(lax.optimization_barrier(jnp.mean(values * values, axis=-1, keepdims=True)) + norm_eps) * gain

def angle_table(places):
    frequency = rope_base ** (-2.0 * jnp.arange(HEAD_SIZE // 2, dtype=jnp.float32) / HEAD_SIZE)
    return places.astype(jnp.float32)[:, None] * frequency[None, :]

def rotate(values, angles):
    count_of_rows = values.shape[0]
    shaped = values.reshape(count_of_rows, -1, HEAD_SIZE)
    half_dim = HEAD_SIZE // 2
    first_half = shaped[:, :, :half_dim]
    second_half = shaped[:, :, half_dim:]
    cosine = jnp.cos(angles)[:, None, :]
    sine_table = jnp.sin(angles)[:, None, :]
    turned = jnp.concatenate([first_half * cosine - second_half * sine_table, second_half * cosine + first_half * sine_table], axis=2)
    return turned.reshape(count_of_rows, -1)

def attend(queries, key_row_block, value_row_block, allowed):
    count_of_rows = queries.shape[0]
    head_cluster = QUERY_HEADS // KEY_VALUE_HEADS
    score_scale = 1.0 / math.sqrt(HEAD_SIZE)
    query_heads = queries.reshape(count_of_rows, QUERY_HEADS, HEAD_SIZE).transpose(1, 0, 2)
    key_head_split = jnp.repeat(key_row_block.reshape(count_of_rows, KEY_VALUE_HEADS, HEAD_SIZE).transpose(1, 0, 2), head_cluster, axis=0)
    value_head_split = jnp.repeat(value_row_block.reshape(count_of_rows, KEY_VALUE_HEADS, HEAD_SIZE).transpose(1, 0, 2), head_cluster, axis=0)

    def one_head(inputs):
        query_head, key_head, value_head = inputs
        scores = low_back(matmul(query_head, key_head.T) * score_scale)
        scores = jnp.where(allowed, scores, -1e+30)
        row_max = lax.optimization_barrier(jnp.max(scores, axis=1, keepdims=True))
        weights = jnp.where(allowed, jnp.exp(scores - row_max), 0.0)
        probabilities = weights / lax.optimization_barrier(jnp.sum(weights, axis=1, keepdims=True))
        return matmul(low(probabilities), value_head)
    heads_out = lax.map(jax.checkpoint(one_head), (query_heads, key_head_split, value_head_split))
    return heads_out.transpose(1, 0, 2).reshape(count_of_rows, QUERY_HEADS * HEAD_SIZE)

def layer(stream, weights, angles, allowed):
    attn_gain, w_query, key_matrix, value_matrix, w_out, mlp_gain, w_gate, w_up, w_down = weights
    normed = low(rms_norm(stream, attn_gain))
    queries = low(low_back(rotate(low_back(matmul(normed, w_query)), angles)))
    key_row_block = low(low_back(rotate(low_back(matmul(normed, key_matrix)), angles)))
    value_row_block = low(low_back(matmul(normed, value_matrix)))
    mixed_tok = low(low_back(attend(queries, key_row_block, value_row_block, allowed)))
    middle = stream + low_back(matmul(mixed_tok, w_out))
    normed_mlp = low(rms_norm(middle, mlp_gain))
    gate_pre = low_back(matmul(normed_mlp, w_gate))
    up_proj = low_back(matmul(normed_mlp, w_up))
    hidden = low(jax.nn.silu(gate_pre) * up_proj)
    return middle + low_back(matmul(hidden, w_down))

def reference(tokens, span_order, attn_gain, w_query, key_matrix, value_matrix, w_out, mlp_gain, w_gate, w_up, w_down, cotangent):
    row_ids = jnp.arange(SEQ_LEN, dtype=jnp.int32)
    places = span_order[row_ids // SPAN].astype(jnp.int32) * SPAN + row_ids % SPAN
    angles = angle_table(places)
    allowed = places[None, :] <= places[:, None]
    params = tuple((item.astype(jnp.float32) for item in (attn_gain, w_query, key_matrix, value_matrix, w_out, mlp_gain, w_gate, w_up, w_down)))

    def forward(sequence, weights):
        stream = sequence
        for layer_index in range(LAYER_COUNT):
            stream = layer(stream, tuple((item[layer_index] for item in weights)), angles, allowed)
        return stream

    def one_sequence(totals, inputs):
        sequence, seq_cot = inputs
        result, pullback = jax.vjp(forward, sequence, params)
        seq_grad, weight_grads = pullback(seq_cot)
        return (tuple((left_side + right_side for left_side, right_side in zip(totals, weight_grads))), (result.astype(jnp.bfloat16), seq_grad))
    zero_grads = tuple((jnp.zeros_like(item) for item in params))
    totals, outputs = lax.scan(one_sequence, zero_grads, (tokens.astype(jnp.float32), cotangent.astype(jnp.float32)))
    block_out, input_grad = outputs
    return (block_out, input_grad, totals[0], totals[1], totals[2], totals[3], totals[4], totals[5], totals[6], totals[7], totals[8])
```

```python
import functools
import math

import jax
import jax.numpy as jnp
import numpy as np
from jax import lax
from jax.experimental import pallas as pl
from jax.experimental.pallas import tpu as pltpu
from jax.sharding import Mesh, PartitionSpec as P

HEAD = 96
LAYERS = 2
ROPE_BASE = 100000.0
EPS = 1e-05
CTX = ("x", "yh")
TP = ("z", "core")
OWN = ("core", "x", "yh")
ALL = ("core", "x", "yh", "yl", "z")
BF = jnp.bfloat16
F32 = jnp.float32
MESH = pl.DeviceIdType.MESH
SCALE = 1.0 / math.sqrt(HEAD)
WIDE = 1536


def mm(a, b):
    return jnp.dot(a, b, preferred_element_type=F32)


def mm_tn(a, b):
    return lax.dot_general(a, b, (((0,), (0,)), ((), ())), preferred_element_type=F32)


def mm_nt(a, b):
    return lax.dot_general(a, b, (((1,), (1,)), ((), ())), preferred_element_type=F32)


def place_rows(span_order, first, count, span):
    ids = first + jnp.arange(count, dtype=jnp.int32)
    slots = jnp.arange(span_order.shape[0], dtype=jnp.int32)
    picked = jnp.sum(
        jnp.where((ids // span)[:, None] == slots[None, :], span_order[None, :], 0), axis=1
    )
    return picked * span + ids % span


def rope_tables(places):
    freq = ROPE_BASE ** (-2.0 * jnp.arange(HEAD // 2, dtype=F32) / HEAD)
    angles = places.astype(F32)[:, None] * freq[None, :]
    cos, sin = jnp.cos(angles), jnp.sin(angles)
    one, zero = jnp.ones((places.shape[0], 16), F32), jnp.zeros((places.shape[0], 16), F32)
    return (
        jnp.concatenate([cos, one, cos, one], axis=1),
        jnp.concatenate([-sin, zero, sin, zero], axis=1),
    )


def pack_heads(wq, wk, wv):
    lead = wq.shape[:-1]
    q = wq.reshape(*lead, 8, 2, HEAD)
    k = wk.reshape(*lead, 8, 1, HEAD)
    v = wv.reshape(*lead, 8, 3, 32)
    qk = jnp.concatenate([q, k], axis=-2)
    tiles = jnp.concatenate([qk[..., :48], v[..., :16], qk[..., 48:], v[..., 16:]], axis=-1)
    return tiles.reshape(*lead, 8, 384)


def unpack_grads(packed):
    lead = packed.shape[:-2]
    tiles = packed.reshape(*lead, 8, 3, 128)
    qk = jnp.concatenate([tiles[..., :48], tiles[..., 64:112]], axis=-1)
    v = jnp.concatenate([tiles[..., 48:64], tiles[..., 112:]], axis=-1)
    return (
        qk[..., :2, :].reshape(*lead, 1536),
        qk[..., 2, :].reshape(*lead, 768),
        v.reshape(*lead, 768),
    )


def spread_rows(rows):
    r = rows.reshape(3, 2, 16, -1)
    z = jnp.zeros_like(r[0, 0])
    return jnp.concatenate(
        [r[1, 1], r[2, 1], z, r[0, 0], r[1, 0], r[2, 0], z, r[0, 1]], axis=0
    )


def gather_rows(padded):
    c = padded.reshape(8, 16, -1)
    return jnp.concatenate([c[3], c[7], c[4], c[0], c[5], c[1]], axis=0)


class Place:
    def __init__(self):
        self.z, self.core = lax.axis_index("z"), lax.axis_index("core")
        self.c = lax.axis_index("x") * 2 + lax.axis_index("yh")
        self.zp, self.zm, self.zo = (lax.rem(self.z + k, 4) for k in (1, 3, 2))
        self.oc = 1 - self.core

    def greet(self):
        barrier = pltpu.get_barrier_semaphore()
        for dev in ({"z": self.zp}, {"z": self.zm}, {"core": self.oc}):
            pl.semaphore_signal(barrier, inc=1, device_id=dev, device_id_type=MESH)
        for k in range(1, 8):
            there = lax.rem(self.c + k, 8)
            pl.semaphore_signal(barrier, inc=1, device_id=at_ctx(there), device_id_type=MESH)
        pl.semaphore_wait(barrier, 10)


def at_ctx(c):
    return {"x": c // 2, "yh": lax.rem(c, 2)}


def span_of(start, size):
    return pl.ds(pl.multiple_of(start, 64), size)


def slot_rows(zz, cc, half=None):
    base = (zz * 2 + cc) * 128
    return span_of(base, 128) if half is None else span_of(base + 64 * half, 64)


def all_gather(me, buf, ssem, rsem, on_pair):
    z, zp, zm, zo, core, oc = me.z, me.zp, me.zm, me.zo, me.core, me.oc
    up, down, across = {"z": zp}, {"z": zm}, {"core": oc}
    sent = [
        (z, core, 0, up), (z, core, 1, up), (z, core, 1, down), (z, core, 0, down),
        (zm, core, 0, up), (zp, core, 1, down), (z, core, None, across),
        (zm, core, 0, across), (zm, core, 1, across), (zp, core, 1, across), (zp, core, 0, across),
        (zo, core, 0, across), (zo, core, 1, across),
    ]
    come = [
        (zm, core, 0), (zm, core, 1), (zp, core, 1), (zp, core, 0), (zo, core, 0), (zo, core, 1),
        (z, oc, None), (zm, oc, 0), (zm, oc, 1), (zp, oc, 1), (zp, oc, 0), (zo, oc, 0), (zo, oc, 1),
    ]

    def copy(i, rows, dev):
        return pltpu.make_async_remote_copy(
            src_ref=buf.at[rows], dst_ref=buf.at[rows], send_sem=ssem.at[i], recv_sem=rsem.at[i],
            device_id=dev, device_id_type=MESH,
        )

    def send(*which):
        for i in which:
            copy(i, slot_rows(*sent[i][:3]), sent[i][3]).start()

    def arrive(*which):
        for i in which:
            copy(i, slot_rows(*come[i]), sent[i][3]).wait_recv()

    send(0, 2, 1, 3, 6)
    arrive(6)
    on_pair(z)
    arrive(0)
    send(4, 7)
    arrive(2)
    send(5, 9)
    arrive(1)
    send(8)
    arrive(3)
    send(10)
    arrive(7, 8)
    on_pair(zm)
    arrive(9, 10)
    on_pair(zp)
    arrive(4)
    send(11)
    arrive(5)
    send(12)
    arrive(11, 12)
    on_pair(zo)

    def finish():
        for i in range(13):
            copy(i, slot_rows(*sent[i][:3]), sent[i][3]).wait_send()

    return finish


def reduce_scatter(me, part, parts, give, take, ring_out, ring_in, ssem, rsem):
    z, zp, zm, zo, core, oc = me.z, me.zp, me.zm, me.zo, me.core, me.oc
    up, down, across = {"z": zp}, {"z": zm}, {"core": oc}
    mine = span_of(core * 128, 128)
    theirs = span_of(oc * 128, 128)

    def swap(k):
        return pltpu.make_async_remote_copy(
            src_ref=give.at[k], dst_ref=take.at[k], send_sem=ssem.at[k], recv_sem=rsem.at[k],
            device_id=across, device_id_type=MESH,
        )

    def ring(i):
        return pltpu.make_async_remote_copy(
            src_ref=ring_out.at[i], dst_ref=ring_in.at[i], send_sem=ssem.at[4 + i], recv_sem=rsem.at[4 + i],
            device_id=up if i < 3 else down, device_id_type=MESH,
        )

    def make(k, zz):
        parts[k] = part(zz)
        give[k] = parts[k, theirs].astype(BF)
        swap(k).start()

    def merged(k, half):
        rows = span_of(core * 128 + 64 * half, 64)
        return parts[k, rows] + take[k, 64 * half : 64 * half + 64].astype(F32)

    def push(i, value):
        ring_out[i] = value.astype(BF)
        ring(i).start()

    make(0, zo)
    make(1, zp)
    swap(0).wait_recv()
    push(0, merged(0, 0))
    push(3, merged(0, 1))
    make(2, zm)
    swap(1).wait_recv()
    push(1, merged(1, 1))
    swap(2).wait_recv()
    push(4, merged(2, 0))
    make(3, z)
    ring(0).wait_recv()
    push(2, merged(1, 0) + ring_in[0].astype(F32))
    ring(3).wait_recv()
    push(5, merged(2, 1) + ring_in[3].astype(F32))
    swap(3).wait_recv()
    own = [merged(3, 0), merged(3, 1)]
    ring(1).wait_recv()
    own[1] = own[1] + ring_in[1].astype(F32)
    ring(4).wait_recv()
    own[0] = own[0] + ring_in[4].astype(F32)
    ring(2).wait_recv()
    own[0] = own[0] + ring_in[2].astype(F32)
    ring(5).wait_recv()
    own[1] = own[1] + ring_in[5].astype(F32)

    def finish():
        for k in range(4):
            swap(k).wait_send()
        for i in range(6):
            ring(i).wait_send()

    return jnp.concatenate(own, axis=0), finish


class Exchange:
    def __init__(self, me, src, dst, ssem, rsem):
        self.me, self.src, self.dst, self.ssem, self.rsem = me, src, dst, ssem, rsem

    def copy(self, s, come):
        return pltpu.make_async_remote_copy(
            src_ref=self.src.at[span_of(s * 128, 128)], dst_ref=self.dst.at[span_of(come * 128, 128)],
            send_sem=self.ssem.at[s], recv_sem=self.rsem.at[come],
            device_id=at_ctx(s), device_id_type=MESH,
        )

    def send(self, s):
        c = self.me.c

        @pl.when(s != c)
        def _():
            self.copy(s, c).start()

        @pl.when(s == c)
        def _():
            rows = span_of(s * 128, 128)
            self.dst[rows] = self.src[rows]

    def arrive(self):
        @pl.loop(1, 8)
        def _(k):
            there = lax.rem(self.me.c + k, 8)
            self.copy(there, there).wait_recv()

    def finish(self):
        @pl.loop(1, 8)
        def _(k):
            there = lax.rem(self.me.c + k, 8)
            self.copy(there, self.me.c).wait_send()


def lane_masks(rows):
    lane = lax.broadcasted_iota(jnp.int32, (rows, 128), 1)
    v0 = ((lane >= 48) & (lane < 64)) | (lane >= 112)
    v1 = ((lane >= 64) & (lane < 80)) | (lane < 16)
    v2 = ((lane >= 80) & (lane < 96)) | ((lane >= 16) & (lane < 32))
    return v0, v1, v2


def split_packed(packed, key_ref, value_ref):
    v0, v1, v2 = lane_masks(128)

    @pl.loop(0, 8)
    def _(p):
        rows = span_of(p * 128, 128)
        t0, t1, t2 = (packed[rows, 128 * t : 128 * t + 128].astype(F32) for t in range(3))
        key_ref[rows] = jnp.where(v0, 0.0, t2).astype(BF)
        value = jnp.where(v0, t0, 0.0)
        value = value + jnp.where(v1, pltpu.roll(t1, 16, 1), 0.0)
        value = value + jnp.where(v2, pltpu.roll(t2, 32, 1), 0.0)
        value_ref[rows] = value.astype(BF)


def flip(ref):
    return jnp.transpose(ref[...].astype(F32)).astype(BF)


def stacked(ref, rows):
    return jnp.concatenate([ref[rows, 0:128], ref[rows, 128:256]], axis=0)


def rms_of(values):
    return lax.rsqrt(jnp.mean(values * values, axis=-1, keepdims=True) + EPS)


def fwd_kernel(
    stream, gains, cos, sin, pcol, prow, h_in, h_o, h_g, h_u, h_d,
    o_stream, o_middle, o_lse, o_normed, o_qkv, o_mixed, o_nmlp, o_gate, o_up, o_hidden,
    w_in, w_o, w_g, w_u, w_d, buf1, buf2, qs, qr, ms, mr, gate_v, up_v, hid, keys, vals, vals_t, middle,
    parts, give, take, ring_out, ring_in, give2, take2, ring_out2, ring_in2,
    ag_s, ag_r, ag2_s, ag2_r, rs_s, rs_r, rs2_s, rs2_r, ax_s, ax_r, bx_s, bx_r, loc, loc2,
):
    me = Place()
    loads = [
        pltpu.make_async_copy(h, v, loc.at[i])
        for i, (h, v) in enumerate(((h_in, w_in), (h_o, w_o), (h_g, w_g), (h_u, w_u), (h_d, w_d)))
    ]
    for load in loads:
        load.start()
    stores = []

    def store(src, dst):
        stores.append(pltpu.make_async_copy(src, dst, loc2.at[len(stores)]))
        stores[-1].start()

    s = stream[...]
    buf1[slot_rows(me.z, me.core)] = (s * rms_of(s) * gains[0:1, :]).astype(BF)
    me.greet()
    ax = Exchange(me, qs, qr, ax_s, ax_r)
    loads[0].wait()

    def project(zz):
        rows = span_of(zz * 256, 256)
        y = mm(buf1[rows], w_in[...])
        for t in range(3):
            tile = y[:, 128 * t : 128 * t + 128]
            tile = tile * cos[...] + pltpu.roll(tile, 64, 1) * sin[...]
            qs[rows, 128 * t : 128 * t + 128] = tile.astype(BF)
        ax.send(zz * 2)
        ax.send(zz * 2 + 1)

    done_ag = all_gather(me, buf1, ag_s, ag_r, project)
    ax.arrive()
    store(buf1, o_normed)
    store(qr, o_qkv)
    split_packed(qr, keys, vals)
    vals_t[...] = flip(vals)
    bx = Exchange(me, ms, mr, bx_s, bx_r)

    @pl.loop(0, 8)
    def _(k):
        p = lax.rem(me.c + 1 + k, 8)
        rows = span_of(p * 128, 128)
        q = stacked(qr, rows)
        scores = mm_nt(keys[...], q) * SCALE
        scores = jnp.where(pcol[...] <= prow[pl.ds(p, 1), :], scores, -1e30)
        top = jnp.max(scores, axis=0, keepdims=True)
        weights = jnp.exp(scores - top)
        total = jnp.sum(weights, axis=0, keepdims=True)
        o_lse[pl.ds(p, 1), :] = top + jnp.log(total)
        probs = (weights / total).astype(BF)
        out = jnp.transpose(mm(vals_t[...], probs)).astype(BF)
        ms[rows, 0:128] = out[0:128]
        ms[rows, 128:256] = out[128:256]
        bx.send(p)

    bx.arrive()
    store(mr, o_mixed)
    loads[1].wait()

    def out_part(zz):
        return mm(mr[span_of(zz * 256, 256)], w_o[...])

    total, done_rs = reduce_scatter(me, out_part, parts, give, take, ring_out, ring_in, rs_s, rs_r)
    mid = stream[...] + total
    middle[...] = mid
    o_middle[...] = mid
    buf2[slot_rows(me.z, me.core)] = (mid * rms_of(mid) * gains[1:2, :]).astype(BF)
    for load in loads[2:]:
        load.wait()

    def gated(zz):
        rows = span_of(zz * 256, 256)
        gate = mm(buf2[rows], w_g[...])
        gate_v[rows] = gate
        up = mm(buf2[rows], w_u[...])
        up_v[rows] = up
        hid[rows] = (gate / (1.0 + jnp.exp(-gate)) * up).astype(BF)

    done_ag2 = all_gather(me, buf2, ag2_s, ag2_r, gated)
    store(buf2, o_nmlp)
    store(gate_v, o_gate)
    store(up_v, o_up)
    store(hid, o_hidden)

    def down_part(zz):
        return mm(hid[span_of(zz * 256, 256)], w_d[...])

    total, done_rs2 = reduce_scatter(me, down_part, parts, give2, take2, ring_out2, ring_in2, rs2_s, rs2_r)
    o_stream[...] = middle[...] + total
    for done in (done_ag, ax.finish, bx.finish, done_rs, done_ag2, done_rs2):
        done()
    for item in stores:
        item.wait()


def norm_back_of(e, values, gain):
    q = rms_of(values)
    n = values * q
    dn = e * gain
    part = q * (dn - n * jnp.mean(dn * n, axis=-1, keepdims=True))
    return part, jnp.sum(e * n, axis=0, keepdims=True)


def bwd_kernel(
    grad, stream, middle, gains, cos, sin, pcol, prow, lse, h_in, h_o, h_g, h_u, h_d, h_qkv, h_gate, h_up,
    o_grad, o_gains, o_down, o_out, o_gg, o_ug, o_pre,
    w_in, w_o, w_g, w_u, w_d, buf1, buf2, qr, gate_v, up_v, gg, ug, mgs, mgr, keys, vals, keys_t, dk, dv,
    dqs, ps, pr, mid_grad, parts, give, take, ring_out, ring_in, give2, take2, ring_out2, ring_in2,
    ag_s, ag_r, ag2_s, ag2_r, rs_s, rs_r, rs2_s, rs2_r, ax_s, ax_r, bx_s, bx_r, loc, loc2,
):
    me = Place()
    pairs = ((h_d, w_d), (h_gate, gate_v), (h_up, up_v), (h_g, w_g), (h_u, w_u), (h_o, w_o), (h_qkv, qr), (h_in, w_in))
    loads = [pltpu.make_async_copy(h, v, loc.at[i]) for i, (h, v) in enumerate(pairs)]
    for load in loads:
        load.start()
    stores = []

    def store(src, dst):
        stores.append(pltpu.make_async_copy(src, dst, loc2.at[len(stores)]))
        stores[-1].start()

    buf1[slot_rows(me.z, me.core)] = grad[...].astype(BF)
    me.greet()
    for load in loads[:3]:
        load.wait()

    def unit(zz):
        rows = span_of(zz * 256, 256)
        hg = mm_nt(buf1[rows], w_d[...])
        gate, up = gate_v[rows], up_v[rows]
        sig = 1.0 / (1.0 + jnp.exp(-gate))
        gg[rows] = (hg * up * (sig * (1.0 + gate * (1.0 - sig)))).astype(BF)
        ug[rows] = (hg * (gate * sig)).astype(BF)

    done_ag = all_gather(me, buf1, ag_s, ag_r, unit)
    store(buf1, o_down)
    store(gg, o_gg)
    store(ug, o_ug)
    for load in loads[3:5]:
        load.wait()

    def mlp_part(zz):
        rows = span_of(zz * 256, 256)
        return mm_nt(gg[rows], w_g[...]) + mm_nt(ug[rows], w_u[...])

    e, done_rs = reduce_scatter(me, mlp_part, parts, give, take, ring_out, ring_in, rs_s, rs_r)
    part, gain_part = norm_back_of(e, middle[...], gains[1:2, :])
    o_gains[1:2, :] = gain_part
    gm = grad[...] + part
    mid_grad[...] = gm
    buf2[slot_rows(me.z, me.core)] = gm.astype(BF)
    for load in loads[5:7]:
        load.wait()
    ax = Exchange(me, mgs, mgr, ax_s, ax_r)

    def mixed_back(zz):
        rows = span_of(zz * 256, 256)
        mgs[rows] = mm_nt(buf2[rows], w_o[...]).astype(BF)
        ax.send(zz * 2)
        ax.send(zz * 2 + 1)

    done_ag2 = all_gather(me, buf2, ag2_s, ag2_r, mixed_back)
    store(buf2, o_out)
    split_packed(qr, keys, vals)
    keys_t[...] = flip(keys)
    dk[...] = jnp.zeros_like(dk)
    dv[...] = jnp.zeros_like(dv)
    ax.arrive()

    @pl.loop(0, 8)
    def _(p):
        rows = span_of(p * 128, 128)
        q = stacked(qr, rows)
        mg = stacked(mgr, rows)
        scores = mm_nt(keys[...], q) * SCALE
        allowed = pcol[...] <= prow[pl.ds(p, 1), :]
        probs = jnp.where(allowed, jnp.exp(scores - lse[pl.ds(p, 1), :]), 0.0)
        pg = mm_nt(vals[...], mg)
        inner = jnp.sum(probs * pg, axis=0, keepdims=True)
        sg = (probs * (pg - inner)).astype(BF)
        dk[...] += mm(sg, q)
        dv[...] += mm(probs.astype(BF), mg)
        dq = jnp.transpose(mm(keys_t[...], sg)) * SCALE
        dqs[rows, 0:128] = dq[0:128]
        dqs[rows, 128:256] = dq[128:256]

    bx = Exchange(me, ps, pr, bx_s, bx_r)
    v0, _, _ = lane_masks(128)

    @pl.loop(0, 8)
    def _(k):
        p = lax.rem(me.c + 1 + k, 8)
        rows = span_of(p * 128, 128)
        value = dv[rows]
        ps[rows, 0:128] = jnp.where(v0, value, dqs[rows, 0:128]).astype(BF)
        ps[rows, 128:256] = jnp.where(v0, pltpu.roll(value, 112, 1), dqs[rows, 128:256]).astype(BF)
        ps[rows, 256:384] = jnp.where(v0, pltpu.roll(value, 96, 1), dk[rows] * SCALE).astype(BF)
        bx.send(p)

    loads[7].wait()
    bx.arrive()

    def in_part(zz):
        rows = span_of(zz * 256, 256)
        for t in range(3):
            cols = slice(128 * t, 128 * t + 128)
            tile = pr[rows, cols].astype(F32)
            mgs_tile = tile * cos[...] - pltpu.roll(tile, 64, 1) * sin[...]
            ps2[rows, cols] = mgs_tile.astype(BF)
        return mm_nt(ps2[rows], w_in[...])

    ps2 = qr
    e, done_rs2 = reduce_scatter(me, in_part, parts, give2, take2, ring_out2, ring_in2, rs2_s, rs2_r)
    store(ps2, o_pre)
    part, gain_part = norm_back_of(e, stream[...], gains[0:1, :])
    o_gains[0:1, :] = gain_part
    o_grad[...] = mid_grad[...] + part
    for done in (done_ag, done_rs, done_ag2, ax.finish, bx.finish, done_rs2):
        done()
    for item in stores:
        item.wait()


def vm(shape, dtype=BF):
    return pltpu.VMEM(shape, dtype)


def rs_scratch():
    return [vm((4, 128, WIDE)), vm((4, 128, WIDE)), vm((6, 64, WIDE)), vm((6, 64, WIDE))]


def sems():
    dma = pltpu.SemaphoreType.DMA
    return [dma((n,)) for n in (13, 13, 13, 13, 10, 10, 10, 10, 8, 8, 8, 8, 8, 8)]


WEIGHTS = [(WIDE, 384), (256, WIDE), (WIDE, 512), (WIDE, 512), (512, WIDE)]


def run_kernel(kernel, name, cid, ins, in_vmem, outs, out_vmem, scratch, flops):
    place = {True: pltpu.VMEM, False: pl.ANY}
    return pl.pallas_call(
        kernel,
        name=name,
        out_shape=[jax.ShapeDtypeStruct(s, d) for s, d in outs],
        in_specs=[pl.BlockSpec(memory_space=place[i < in_vmem]) for i in range(len(ins))],
        out_specs=[pl.BlockSpec(memory_space=place[i < out_vmem]) for i in range(len(outs))],
        scratch_shapes=scratch,
        cost_estimate=pl.CostEstimate(flops=flops, bytes_accessed=60 * 2**20, transcendentals=0),
        compiler_params=pltpu.CompilerParams(
            collective_id=cid, has_side_effects=True, vmem_limit_bytes=60 * 2**20
        ),
    )(*ins)


def layer_fwd(l, stream, gains, cos, sin, pcol, prow, weights):
    outs = [
        ((128, WIDE), F32), ((128, WIDE), F32), ((8, 256), F32),
        ((1024, WIDE), BF), ((1024, 384), BF), ((1024, 256), BF), ((1024, WIDE), BF),
        ((1024, 512), F32), ((1024, 512), F32), ((1024, 512), BF),
    ]
    scratch = [vm(s) for s in WEIGHTS] + [
        vm((1024, WIDE)), vm((1024, WIDE)), vm((1024, 384)), vm((1024, 384)), vm((1024, 256)), vm((1024, 256)),
        vm((1024, 512), F32), vm((1024, 512), F32), vm((1024, 512)),
        vm((1024, 128)), vm((1024, 128)), vm((128, 1024)), vm((128, WIDE), F32), vm((4, 256, WIDE), F32),
    ] + rs_scratch() + rs_scratch() + sems()
    ins = [stream, gains, cos, sin, pcol, prow, *weights]
    return run_kernel(fwd_kernel, f"layer_forward_{l}", 1 + l, ins, 6, outs, 3, scratch, 40 * 10**9)


def layer_bwd(l, grad, stream, middle, gains, cos, sin, pcol, prow, lse, weights, qkv, gate, up):
    outs = [
        ((128, WIDE), F32), ((2, WIDE), F32),
        ((1024, WIDE), BF), ((1024, WIDE), BF), ((1024, 512), BF), ((1024, 512), BF), ((1024, 384), BF),
    ]
    scratch = [vm(s) for s in WEIGHTS] + [
        vm((1024, WIDE)), vm((1024, WIDE)), vm((1024, 384)), vm((1024, 512), F32), vm((1024, 512), F32),
        vm((1024, 512)), vm((1024, 512)), vm((1024, 256)), vm((1024, 256)),
        vm((1024, 128)), vm((1024, 128)), vm((128, 1024)), vm((1024, 128), F32), vm((1024, 128), F32),
        vm((1024, 256), F32), vm((1024, 384)), vm((1024, 384)), vm((128, WIDE), F32), vm((4, 256, WIDE), F32),
    ] + rs_scratch() + rs_scratch() + sems()
    ins = [grad, stream, middle, gains, cos, sin, pcol, prow, lse, *weights, qkv, gate, up]
    return run_kernel(bwd_kernel, f"layer_backward_{l}", 3 + l, ins, 9, outs, 2, scratch, 60 * 10**9)


def collect(rows):
    l, r, _, n = rows.shape
    got = lax.all_gather(rows, OWN, axis=0, tiled=False)
    got = lax.dynamic_index_in_dim(got, lax.axis_index("core"), axis=3, keepdims=False)
    return got.transpose(1, 0, 2, 3).reshape(l, 16 * r, n)


def body(
    tokens, span_order, attn_gain, w_query, key_matrix, value_matrix, w_out, mlp_gain, w_gate, w_up,
    w_down, cotangent,
):
    rows = tokens.shape[1]
    ctx = lax.axis_index("x") * 2 + lax.axis_index("yh")
    core, z = lax.axis_index("core"), lax.axis_index("z")
    member = core * 4 + z
    seq_len = 8 * rows
    span = seq_len // span_order.shape[0]
    cos, sin = rope_tables(place_rows(span_order, ctx * rows, rows, span))
    cos, sin = jnp.tile(cos, (2, 1)), jnp.tile(sin, (2, 1))
    places = place_rows(span_order, 0, seq_len, span)
    pcol = places[:, None]
    prow = jnp.tile(places.reshape(8, rows), (1, 2))

    def mine(packed):
        l, r, _, n = packed.shape
        return lax.dynamic_index_in_dim(packed.reshape(l, r, 2, 4, n), z, axis=3, keepdims=False)

    gains = lax.all_gather(
        jnp.concatenate([attn_gain, mlp_gain], axis=0), OWN, axis=1, tiled=True
    ).astype(F32)
    w_in = collect(mine(pack_heads(w_query, key_matrix, value_matrix)))

    def hidden_split(w):
        return w.reshape(LAYERS, -1, 16, 8, 32).transpose(0, 1, 3, 2, 4).reshape(LAYERS, -1, 8, 512)

    w_g = collect(mine(hidden_split(w_gate)))
    w_u = collect(mine(hidden_split(w_up)))
    w_d = collect(mine(w_down.reshape(LAYERS, 8, 32, 1536).transpose(0, 2, 1, 3)))
    w_o_all = lax.all_gather(w_out, OWN, axis=1, tiled=True)
    w_o_two = lax.dynamic_slice_in_dim(w_o_all, member * 192, 192, axis=1)
    w_o = [
        jnp.concatenate([spread_rows(w_o_two[l, :96]), spread_rows(w_o_two[l, 96:])], axis=0)
        for l in range(LAYERS)
    ]

    stream = tokens[0].astype(F32)
    kept = []
    for l in range(LAYERS):
        weights = (w_in[l], w_o[l], w_g[l], w_u[l], w_d[l])
        two = jnp.stack([gains[l], gains[2 + l]])
        outs = layer_fwd(l, stream, two, cos, sin, pcol, prow, weights)
        kept.append((stream, two, weights, outs))
        stream = outs[0]
    block_out = stream.astype(BF)[None]

    g = cotangent[0].astype(F32)
    gain_parts = [None] * 4
    grads = [None] * LAYERS
    for l in reversed(range(LAYERS)):
        stream, two, weights, outs = kept[l]
        _, middle, lse, normed, qkv, mixed, nmlp, gate, up, hidden = outs
        g, gp, down_grad, out_grad, gate_grad, up_grad, pre = layer_bwd(
            l, g, stream, middle, two, cos, sin, pcol, prow, lse, weights, qkv, gate, up
        )
        gain_parts[l], gain_parts[2 + l] = gp[0], gp[1]
        d_wo = mm_tn(mixed, out_grad)
        d_wo = jnp.concatenate([gather_rows(d_wo[:128]), gather_rows(d_wo[128:])], axis=0)
        d_wgu = jnp.concatenate([mm_tn(nmlp, gate_grad), mm_tn(nmlp, up_grad)], axis=1)
        grads[l] = (mm_tn(normed, pre), d_wgu, mm_tn(hidden, down_grad), d_wo)

    def by_columns(both):
        l, _, n = both.shape
        t = both.astype(BF).reshape(l, 2, 8, 2, 4, 12, n).transpose(2, 3, 1, 4, 0, 5, 6)
        t = t.reshape(16, 8, l, 12, n)
        t = lax.psum_scatter(t, ("x", "yh", "yl"), scatter_dimension=0, tiled=True)[0]
        t = lax.all_to_all(t, ("core", "z"), split_axis=0, concat_axis=0, tiled=True)
        return t.astype(F32).transpose(1, 2, 0, 3)

    d_in = by_columns(jnp.stack([grads[l][0] for l in range(LAYERS)]))
    d_q, d_k, d_v = unpack_grads(d_in)
    d_gu = by_columns(jnp.stack([grads[l][1] for l in range(LAYERS)]))

    def hidden_join(d):
        return d.reshape(LAYERS, 12, 8, 16, 32).transpose(0, 1, 3, 2, 4).reshape(LAYERS, 12, 4096)

    d_g, d_u = hidden_join(d_gu[..., :512]), hidden_join(d_gu[..., 512:])

    d_d = jnp.stack([grads[l][2] for l in range(LAYERS)]).astype(BF)
    d_d = d_d.reshape(LAYERS, 2, 8, 32, 1536).transpose(2, 1, 0, 3, 4).reshape(16, LAYERS, 32, 1536)
    d_d = lax.psum_scatter(d_d, ("x", "yh", "yl"), scatter_dimension=0, tiled=True)[0]
    d_d = lax.ppermute(d_d, ("core", "yl"), [(0, 0), (1, 2), (2, 1), (3, 3)]).astype(F32)

    d_o = jnp.stack([grads[l][3] for l in range(LAYERS)]).astype(BF)
    d_o = d_o.reshape(LAYERS, 2, 2, 4, 12, 1536).transpose(3, 1, 2, 0, 4, 5).reshape(16, LAYERS, 12, 1536)
    d_o = lax.psum_scatter(d_o, ("x", "yh", "yl"), scatter_dimension=0, tiled=True)[0]
    d_o = lax.ppermute(
        d_o, ("x", "z"), [(a * 4 + b, b * 4 + a) for a in range(4) for b in range(4)]
    ).astype(F32)

    gp = jnp.stack(gain_parts).reshape(4, 128, 12).transpose(1, 0, 2)
    gp = lax.psum_scatter(gp, ALL, scatter_dimension=0, tiled=True)[0]
    return (block_out, g[None], gp[:2], d_q, d_k, d_v, d_o, gp[2:], d_g, d_u, d_d)


def solution(mesh):
    fine = Mesh(mesh.devices.reshape(2, 4, 2, 2, 4), ALL)
    seq, ctx, own, every = ("core", "yl", "z"), CTX, OWN, ALL
    act = P(seq, ctx, None)
    in_specs = (act, P(), P(None, own)) + (P(None, own, None),) * 4 + (P(None, own),) + (P(None, own, None),) * 3 + (act,)
    grad = P(None, every, None)
    out_specs = (act, act, P(None, every)) + (grad,) * 4 + (P(None, every),) + (grad,) * 3
    return jax.shard_map(body, mesh=fine, in_specs=in_specs, out_specs=out_specs, check_vma=False)
```

```python
import functools
import math

import jax
import jax.numpy as jnp
import numpy as np
from jax import lax
from jax.experimental import pallas as pl
from jax.experimental.pallas import tpu as pltpu
from jax.sharding import Mesh, PartitionSpec as P

HEAD = 96
LAYERS = 2
ROPE_BASE = 100000.0
EPS = 1e-05
CTX = ("x", "yh")
TP = ("z", "core")
OWN = ("core", "x", "yh")
ALL = ("core", "x", "yh", "yl", "z")
BF = jnp.bfloat16
F32 = jnp.float32
MESH = pl.DeviceIdType.MESH
SCALE = 1.0 / math.sqrt(HEAD)
WIDE = 1536


def mm(a, b):
    return jnp.dot(a, b, preferred_element_type=F32)


def mm_tn(a, b):
    return lax.dot_general(a, b, (((0,), (0,)), ((), ())), preferred_element_type=F32)


def mm_nt(a, b):
    return lax.dot_general(a, b, (((1,), (1,)), ((), ())), preferred_element_type=F32)


def place_rows(span_order, first, count, span):
    ids = first + jnp.arange(count, dtype=jnp.int32)
    slots = jnp.arange(span_order.shape[0], dtype=jnp.int32)
    picked = jnp.sum(
        jnp.where((ids // span)[:, None] == slots[None, :], span_order[None, :], 0), axis=1
    )
    return picked * span + ids % span


def rope_tables(places):
    freq = ROPE_BASE ** (-2.0 * jnp.arange(HEAD // 2, dtype=F32) / HEAD)
    angles = places.astype(F32)[:, None] * freq[None, :]
    cos, sin = jnp.cos(angles), jnp.sin(angles)
    one, zero = jnp.ones((places.shape[0], 16), F32), jnp.zeros((places.shape[0], 16), F32)
    return (
        jnp.concatenate([cos, one, cos, one], axis=1),
        jnp.concatenate([-sin, zero, sin, zero], axis=1),
    )


def pack_heads(q, k, v):
    lead = q.shape[:-1]
    qk = jnp.concatenate([q.reshape(*lead, 2, HEAD), k.reshape(*lead, 1, HEAD)], axis=-2)
    v = v.reshape(*lead, 3, 32)
    tiles = jnp.concatenate([qk[..., :48], v[..., :16], qk[..., 48:], v[..., 16:]], axis=-1)
    return tiles.reshape(*lead, 384)


def unpack_grads(packed):
    lead = packed.shape[:-2]
    tiles = packed.reshape(*lead, 8, 3, 128)
    qk = jnp.concatenate([tiles[..., :48], tiles[..., 64:112]], axis=-1)
    v = jnp.concatenate([tiles[..., 48:64], tiles[..., 112:]], axis=-1)
    return (
        qk[..., :2, :].reshape(*lead, 1536),
        qk[..., 2, :].reshape(*lead, 768),
        v.reshape(*lead, 768),
    )


def spread_rows(rows):
    r = rows.reshape(3, 2, 16, -1)
    z = jnp.zeros_like(r[0, 0])
    return jnp.concatenate(
        [r[1, 1], r[2, 1], z, r[0, 0], r[1, 0], r[2, 0], z, r[0, 1]], axis=0
    )


class Place:
    def __init__(self):
        self.z, self.core = lax.axis_index("z"), lax.axis_index("core")
        self.x, self.yh, self.yl = lax.axis_index("x"), lax.axis_index("yh"), lax.axis_index("yl")
        self.y = self.yh * 2 + self.yl
        self.c = self.x * 2 + self.yh
        self.zp, self.zm, self.zo = (lax.rem(self.z + k, 4) for k in (1, 3, 2))
        self.oc = 1 - self.core

    def near(self, axis, k):
        if axis == "x":
            return {"x": lax.rem(self.x + k, 4)}
        return at_y(lax.rem(self.y + k, 4))

    def greet(self, others, mirror=False):
        barrier = pltpu.get_barrier_semaphore()
        for dev in others:
            pl.semaphore_signal(barrier, inc=1, device_id=dev, device_id_type=MESH)
        if not mirror:
            pl.semaphore_wait(barrier, len(others))
            return

        @pl.when(self.x != self.z)
        def _():
            there = {"x": self.z, "z": self.x}
            pl.semaphore_signal(barrier, inc=1, device_id=there, device_id_type=MESH)
            pl.semaphore_wait(barrier, len(others) + 1)

        @pl.when(self.x == self.z)
        def _():
            pl.semaphore_wait(barrier, len(others))

    def layer_partners(self):
        return (
            [{"z": self.zp}, {"z": self.zm}, {"core": self.oc}]
            + [at_ctx(lax.rem(self.c + k, 8)) for k in range(1, 8)]
            + [{"yl": 1 - self.yl}, {"yh": 1 - self.yh, "yl": 1 - self.yl}]
        )


def at_y(y):
    return {"yh": y // 2, "yl": lax.rem(y, 2)}


def at_ctx(c):
    return {"x": c // 2, "yh": lax.rem(c, 2)}


def span_of(start, size):
    return pl.ds(pl.multiple_of(start, 64), size)


def slot_rows(zz, cc, half=None):
    base = (zz * 2 + cc) * 128
    return span_of(base, 128) if half is None else span_of(base + 64 * half, 64)


def all_gather(me, buf, ssem, rsem, on_pair, hooks=()):
    z, zp, zm, zo, core, oc = me.z, me.zp, me.zm, me.zo, me.core, me.oc
    up, down, across = {"z": zp}, {"z": zm}, {"core": oc}
    sent = [
        (z, core, 0, up), (z, core, 1, up), (z, core, 1, down), (z, core, 0, down),
        (zm, core, 0, up), (zp, core, 1, down), (z, core, None, across),
        (zm, core, 0, across), (zm, core, 1, across), (zp, core, 1, across), (zp, core, 0, across),
        (zo, core, 0, across), (zo, core, 1, across),
    ]
    come = [
        (zm, core, 0), (zm, core, 1), (zp, core, 1), (zp, core, 0), (zo, core, 0), (zo, core, 1),
        (z, oc, None), (zm, oc, 0), (zm, oc, 1), (zp, oc, 1), (zp, oc, 0), (zo, oc, 0), (zo, oc, 1),
    ]

    def copy(i, rows, dev):
        return pltpu.make_async_remote_copy(
            src_ref=buf.at[rows], dst_ref=buf.at[rows], send_sem=ssem.at[i], recv_sem=rsem.at[i],
            device_id=dev, device_id_type=MESH,
        )

    def send(*which):
        for i in which:
            copy(i, slot_rows(*sent[i][:3]), sent[i][3]).start()

    def arrive(*which):
        for i in which:
            copy(i, slot_rows(*come[i]), sent[i][3]).wait_recv()

    def hook(i):
        if i < len(hooks):
            hooks[i]()

    send(0, 2, 1, 3, 6)
    hook(0)
    arrive(6)
    on_pair(z)
    arrive(0)
    send(4, 7)
    arrive(2)
    send(5, 9)
    hook(1)
    arrive(1)
    send(8)
    arrive(3)
    send(10)
    hook(2)
    arrive(7, 8)
    on_pair(zm)
    arrive(9, 10)
    on_pair(zp)
    hook(3)
    arrive(4)
    send(11)
    arrive(5)
    send(12)
    arrive(11, 12)
    on_pair(zo)

    def finish():
        for i in range(13):
            copy(i, slot_rows(*sent[i][:3]), sent[i][3]).wait_send()

    return finish


def reduce_scatter(me, part, parts, give, take, ring_out, ring_in, ssem, rsem, fill=lambda n: None):
    z, zp, zm, zo, core, oc = me.z, me.zp, me.zm, me.zo, me.core, me.oc
    up, down, across = {"z": zp}, {"z": zm}, {"core": oc}
    mine = span_of(core * 128, 128)
    theirs = span_of(oc * 128, 128)

    def swap(k):
        return pltpu.make_async_remote_copy(
            src_ref=give.at[k], dst_ref=take.at[k], send_sem=ssem.at[k], recv_sem=rsem.at[k],
            device_id=across, device_id_type=MESH,
        )

    def ring(i):
        return pltpu.make_async_remote_copy(
            src_ref=ring_out.at[i], dst_ref=ring_in.at[i], send_sem=ssem.at[4 + i], recv_sem=rsem.at[4 + i],
            device_id=up if i < 3 else down, device_id_type=MESH,
        )

    def make(k, zz):
        parts[k] = part(zz)
        give[k] = parts[k, theirs].astype(BF)
        swap(k).start()

    def merged(k, half):
        rows = span_of(core * 128 + 64 * half, 64)
        return parts[k, rows] + take[k, 64 * half : 64 * half + 64].astype(F32)

    def push(i, value):
        ring_out[i] = value.astype(BF)
        ring(i).start()

    make(0, zo)
    make(1, zp)
    swap(0).wait_recv()
    push(0, merged(0, 0))
    push(3, merged(0, 1))
    make(2, zm)
    swap(1).wait_recv()
    push(1, merged(1, 1))
    swap(2).wait_recv()
    push(4, merged(2, 0))
    make(3, z)
    fill(0)
    ring(0).wait_recv()
    push(2, merged(1, 0) + ring_in[0].astype(F32))
    ring(3).wait_recv()
    push(5, merged(2, 1) + ring_in[3].astype(F32))
    swap(3).wait_recv()
    fill(1)
    own = [merged(3, 0), merged(3, 1)]
    ring(1).wait_recv()
    own[1] = own[1] + ring_in[1].astype(F32)
    ring(4).wait_recv()
    own[0] = own[0] + ring_in[4].astype(F32)
    fill(2)
    ring(2).wait_recv()
    own[0] = own[0] + ring_in[2].astype(F32)
    ring(5).wait_recv()
    own[1] = own[1] + ring_in[5].astype(F32)

    def finish():
        for k in range(4):
            swap(k).wait_send()
        for i in range(6):
            ring(i).wait_send()

    return jnp.concatenate(own, axis=0), finish


class Exchange:
    def __init__(self, me, src, dst, ssem, rsem):
        self.me, self.src, self.dst, self.ssem, self.rsem = me, src, dst, ssem, rsem

    def copy(self, s, come):
        return pltpu.make_async_remote_copy(
            src_ref=self.src.at[span_of(s * 128, 128)], dst_ref=self.dst.at[span_of(come * 128, 128)],
            send_sem=self.ssem.at[s], recv_sem=self.rsem.at[come],
            device_id=at_ctx(s), device_id_type=MESH,
        )

    def send(self, s):
        c = self.me.c

        @pl.when(s != c)
        def _():
            self.copy(s, c).start()

        @pl.when(s == c)
        def _():
            rows = span_of(s * 128, 128)
            self.dst[rows] = self.src[rows]

    def arrive(self):
        @pl.loop(1, 8)
        def _(k):
            there = lax.rem(self.me.c + k, 8)
            self.copy(there, there).wait_recv()

    def finish(self):
        @pl.loop(1, 8)
        def _(k):
            there = lax.rem(self.me.c + k, 8)
            self.copy(there, self.me.c).wait_send()


def push(src, dst, ssem, rsem, dev):
    return pltpu.make_async_remote_copy(
        src_ref=src, dst_ref=dst, send_sem=ssem, recv_sem=rsem, device_id=dev, device_id_type=MESH
    )


class Gather:
    def __init__(self, me, src, dst, ssem, rsem, loc, order):
        self.me, self.src, self.dst, self.ssem, self.rsem, self.order = me, src, dst, ssem, rsem, order
        x, yh, yl = me.x, me.yh, me.yl
        self.own = lambda: pltpu.make_async_copy(src.at[me.core], dst.at[me.core, x, yh, yl], loc)
        self.cross = lambda: push(
            src.at[me.oc], dst.at[me.core, x, yh, yl], ssem.at[0], rsem.at[0], {"core": me.oc}
        )

    def region(self, stage, k):
        me = self.me
        if stage == 0:
            back = 4 - k
            x = lax.rem(me.x + back, 4) if self.order[0] == "x" else me.x
            y = lax.rem(me.y + back, 4) if self.order[0] == "y" else me.y
            return self.dst.at[:, x, y // 2, lax.rem(y, 2)]
        if self.order[1] == "y":
            y = lax.rem(me.y + 4 - k, 4)
            return self.dst.at[:, :, y // 2, lax.rem(y, 2)]
        return self.dst.at[:, lax.rem(me.x + 4 - k, 4)]

    def copy(self, stage, k, come):
        ref = self.region(stage, k if come else 0)
        i = 1 + 3 * stage + k - 1
        return push(ref, ref, self.ssem.at[i], self.rsem.at[i], self.me.near(self.order[stage], k))

    def zero(self):
        self.own().start()
        self.cross().start()

    def one(self):
        me = self.me
        self.own().wait()
        here = self.dst.at[me.oc, me.x, me.yh, me.yl]
        push(here, here, self.ssem.at[0], self.rsem.at[0], {"core": me.oc}).wait_recv()
        for k in (2, 1, 3):
            self.copy(0, k, False).start()

    def two(self):
        for k in (1, 3, 2):
            self.copy(0, k, True).wait_recv()
        for k in (2, 1, 3):
            self.copy(1, k, False).start()

    def three(self):
        for k in (1, 3, 2):
            self.copy(1, k, True).wait_recv()

    def finish(self):
        self.cross().wait_send()
        for stage in (0, 1):
            for k in (1, 2, 3):
                self.copy(stage, k, False).wait_send()


class OutGather:
    def __init__(self, me, src, dst, ssem, rsem, loc):
        self.me, self.dst, self.ssem, self.rsem = me, dst, ssem, rsem
        self.own = pltpu.make_async_copy(src, dst.at[me.y], loc)
        self.far = lax.rem(me.x + 4 - me.z, 4)

    def copy(self, stage, k, come):
        me = self.me
        y = lax.rem(me.y + 4 - k, 4) if stage and come else me.y
        ref, i = self.dst.at[y], 3 * stage + k - 1
        return push(ref, ref, self.ssem.at[i], self.rsem.at[i], me.near("xy"[stage], k))

    def zero(self):
        @pl.when(self.far == 0)
        def _():
            self.own.start()

    def one(self):
        @pl.when(self.far == 0)
        def _():
            self.own.wait()
            for k in (2, 1, 3):
                self.copy(0, k, False).start()

    def two(self):
        for k in (1, 2, 3):

            @pl.when(self.far == k)
            def _(k=k):
                self.copy(0, k, True).wait_recv()

        for k in (2, 1, 3):
            self.copy(1, k, False).start()

    def three(self):
        for k in (1, 3, 2):
            self.copy(1, k, True).wait_recv()

    def finish(self):
        @pl.when(self.far == 0)
        def _():
            for k in (1, 2, 3):
                self.copy(0, k, False).wait_send()

        for k in (1, 2, 3):
            self.copy(1, k, False).wait_send()


class Reduce:
    def __init__(self, me, quarter, inner, mine, got1, sum1, got2, ssem, rsem, loc, order):
        self.me, self.quarter, self.inner, self.order = me, quarter, inner, order
        self.mine, self.got1, self.sum1, self.got2, self.ssem, self.rsem = mine, got1, sum1, got2, ssem, rsem
        self.load = pltpu.make_async_copy(quarter(order[0], self.at(order[0], 0)), mine, loc)

    def at(self, axis, k):
        return lax.rem((self.me.x if axis == "x" else self.me.y) + k, 4)

    def copy(self, stage, k):
        axis = self.order[stage]
        to = self.at(axis, k)
        src = self.inner(self.sum1, to) if stage else self.quarter(axis, to)
        dst = (self.got2 if stage else self.got1).at[k - 1]
        i = 3 * stage + k - 1
        return push(src, dst, self.ssem.at[i], self.rsem.at[i], self.me.near(axis, k))

    def one(self):
        self.load.start()
        for k in (2, 1, 3):
            self.copy(0, k).start()

    def two(self):
        self.load.wait()
        for k in (1, 2, 3):
            self.copy(0, k).wait_recv()
        lead = math.prod(self.sum1.shape[:-2])
        dims = self.sum1.shape[:-2]

        @pl.loop(0, lead)
        def _(n):
            at = []
            for d in reversed(dims):
                at.insert(0, lax.rem(n, d))
                n = n // d
            at = tuple(at)
            total = self.mine[at].astype(F32)
            for k in range(3):
                total = total + self.got1[(k, *at)].astype(F32)
            self.sum1[at] = total.astype(self.sum1.dtype)

        for k in (2, 1, 3):
            self.copy(1, k).start()

    def three(self):
        for k in (1, 2, 3):
            self.copy(1, k).wait_recv()
        total = self.inner(self.sum1, self.at(self.order[1], 0))[...].astype(F32)
        for k in range(3):
            total = total + self.got2[k].astype(F32)
        return total

    def finish(self):
        for stage in (0, 1):
            for k in (1, 2, 3):
                self.copy(stage, k).wait_send()


def lane_masks(rows):
    lane = lax.broadcasted_iota(jnp.int32, (rows, 128), 1)
    v0 = ((lane >= 48) & (lane < 64)) | (lane >= 112)
    v1 = ((lane >= 64) & (lane < 80)) | (lane < 16)
    v2 = ((lane >= 80) & (lane < 96)) | ((lane >= 16) & (lane < 32))
    return v0, v1, v2


def split_packed(packed, key_ref, value_ref):
    v0, v1, v2 = lane_masks(128)

    @pl.loop(0, 8)
    def _(p):
        rows = span_of(p * 128, 128)
        t0, t1, t2 = (packed[rows, 128 * t : 128 * t + 128].astype(F32) for t in range(3))
        key_ref[rows] = jnp.where(v0, 0.0, t2).astype(BF)
        value = jnp.where(v0, t0, 0.0)
        value = value + jnp.where(v1, pltpu.roll(t1, 16, 1), 0.0)
        value = value + jnp.where(v2, pltpu.roll(t2, 32, 1), 0.0)
        value_ref[rows] = value.astype(BF)


def flip(ref):
    return jnp.transpose(ref[...].astype(F32)).astype(BF)


def stacked(ref, rows):
    return jnp.concatenate([ref[rows, 0:128], ref[rows, 128:256]], axis=0)


def rms_of(values):
    return lax.rsqrt(jnp.mean(values * values, axis=-1, keepdims=True) + EPS)


def fwd_kernel(
    first, stream, gains_in, cos, sin, pcol, prow, s_gain, s_in, s_o, s_g, s_u, s_d,
    o_stream, o_middle, o_lse, o_gains, o_normed, o_qkv, o_mixed, o_nmlp, o_gate, o_up, o_hidden,
    o_win, o_wo, o_wg, o_wu, o_wd,
    w_in, w_o, w_g, w_u, w_d, w_gain, buf1, buf2, qs, qr, ms, mr, gate_v, up_v, hid, keys, vals, vals_t, middle,
    parts, give, take, ring_out, ring_in,
    ag_s, ag_r, ag2_s, ag2_r, rs_s, rs_r, rs2_s, rs2_r, ax_s, ax_r, bx_s, bx_r, loc, loc2, ga_s, ga_r,
):
    me = Place()
    stores = []

    def store(src, dst):
        stores.append(pltpu.make_async_copy(src, dst, loc2.at[len(stores)]))
        stores[-1].start()

    items = ((s_in, w_in, "xy"), (s_g, w_g, "xy"), (s_u, w_u, "yx"), (s_d, w_d, "xy"), (s_gain, w_gain, "yx"))
    g_in, g_g, g_u, g_d, g_gain = (
        Gather(me, s, d, ga_s.at[i], ga_r.at[i], loc.at[i], order) for i, (s, d, order) in enumerate(items)
    )
    g_o = OutGather(me, s_o, w_o, ga_s.at[5], ga_r.at[5], loc.at[5])
    own_rows = slot_rows(me.z, me.core)
    if first:
        buf2[own_rows] = stream[...]
    else:
        o_gains[...] = gains_in[...]
        s = stream[...]
        buf1[own_rows] = (s * rms_of(s) * gains_in[0:1, :]).astype(BF)
    me.greet(me.layer_partners())
    if first:
        g_gain.zero()
    g_in.zero()
    g_o.zero()
    g_g.zero()
    g_u.zero()
    g_d.zero()

    def hook0():
        if first:
            g_gain.one()
        g_in.one()

    def hook1():
        if first:
            g_gain.two()
        g_in.two()

    def hook2():
        g_o.one()

    def skip(zz):
        pass

    done_ag = all_gather(me, buf2 if first else buf1, ag_s, ag_r, skip, (hook0, hook1, hook2))
    if first:
        g_gain.three()
        o_gains[...] = jnp.zeros_like(o_gains)
        for owner in range(16):
            base = 96 * owner // 128 * 128
            width = min(256, WIDE - base)
            row = w_gain[owner // 8, owner % 8 // 2, owner % 2, 0]
            o_gains[:, base : base + width] += row[:, :width]

        @pl.loop(0, 8)
        def _(p):
            rows = span_of(p * 128, 128)
            s = buf2[rows].astype(F32)
            buf1[rows] = (s * rms_of(s) * o_gains[0:1, :]).astype(BF)

    done_ag()

    ax = Exchange(me, qs, qr, ax_s, ax_r)
    g_in.three()

    @pl.loop(0, 4)
    def _(k):
        zz = lax.rem(me.z + k, 4)
        rows = span_of(zz * 256, 256)
        y = mm(buf1[rows], w_in[...].reshape(WIDE, 384))
        for t in range(3):
            tile = y[:, 128 * t : 128 * t + 128]
            tile = tile * cos[...] + pltpu.roll(tile, 64, 1) * sin[...]
            qs[rows, 128 * t : 128 * t + 128] = tile.astype(BF)
        ax.send(zz * 2)
        ax.send(zz * 2 + 1)

    g_o.two()
    g_g.one()
    g_u.one()
    ax.arrive()
    store(buf1, o_normed)
    store(qr, o_qkv)
    split_packed(qr, keys, vals)
    vals_t[...] = flip(vals)
    bx = Exchange(me, ms, mr, bx_s, bx_r)

    @pl.loop(0, 8)
    def _(k):
        p = lax.rem(me.c + 1 + k, 8)
        rows = span_of(p * 128, 128)
        q = stacked(qr, rows)
        scores = mm_nt(keys[...], q) * SCALE
        scores = jnp.where(pcol[...] <= prow[pl.ds(p, 1), :], scores, -1e30)
        top = jnp.max(scores, axis=0, keepdims=True)
        weights = jnp.exp(scores - top)
        total = jnp.sum(weights, axis=0, keepdims=True)
        o_lse[pl.ds(p, 1), :] = top + jnp.log(total)
        probs = (weights / total).astype(BF)
        out = jnp.transpose(mm(vals_t[...], probs)).astype(BF)
        ms[rows, 0:128] = out[0:128]
        ms[rows, 128:256] = out[128:256]
        bx.send(p)

    g_g.two()
    g_u.two()
    g_d.one()
    g_o.three()
    bx.arrive()
    store(mr, o_mixed)

    def out_part(zz):
        return mm(mr[span_of(zz * 256, 256)], w_o[...].reshape(256, WIDE))

    rs = (parts, give, take, ring_out, ring_in)
    total, done_rs = reduce_scatter(me, out_part, *rs, rs_s, rs_r)
    mid = total + (stream[...].astype(F32) if first else stream[...])
    middle[...] = mid
    o_middle[...] = mid
    buf2[own_rows] = (mid * rms_of(mid) * o_gains[1:2, :]).astype(BF)
    waited = []

    def gated(zz):
        if not waited:
            g_g.three()
            g_u.three()
            waited.append(1)
        rows = span_of(zz * 256, 256)
        gate = mm(buf2[rows], w_g[...].reshape(WIDE, 512))
        gate_v[rows] = gate
        up = mm(buf2[rows], w_u[...].reshape(WIDE, 512))
        up_v[rows] = up
        hid[rows] = (gate / (1.0 + jnp.exp(-gate)) * up).astype(BF)

    done_ag2 = all_gather(me, buf2, ag2_s, ag2_r, gated, (g_d.two,))
    store(buf2, o_nmlp)
    store(gate_v, o_gate)
    store(up_v, o_up)
    store(hid, o_hidden)
    g_d.three()
    done_rs()
    for w, o in ((w_in, o_win), (w_o, o_wo), (w_g, o_wg), (w_u, o_wu), (w_d, o_wd)):
        store(w, o)

    def down_part(zz):
        return mm(hid[span_of(zz * 256, 256)], w_d[...].reshape(512, WIDE))

    total, done_rs2 = reduce_scatter(me, down_part, *rs, rs2_s, rs2_r)
    o_stream[...] = middle[...] + total
    for done in (ax.finish, bx.finish, done_ag2, done_rs2):
        done()
    for item in (g_in, g_g, g_u, g_d, g_o) + ((g_gain,) if first else ()):
        item.finish()
    for item in stores:
        item.wait()


def norm_back_of(e, values, gain):
    q = rms_of(values)
    n = values * q
    dn = e * gain
    part = q * (dn - n * jnp.mean(dn * n, axis=-1, keepdims=True))
    return part, jnp.sum(e * n, axis=0, keepdims=True)


def bwd_kernel(
    grad, stream, middle, gains, cos, sin, pcol, prow, lse,
    h_in, h_o, h_g, h_u, h_d, h_qkv, h_gate, h_up, h_normed, h_mixed, h_nmlp, h_hidden,
    o_grad, o_gains, o_din, o_dgu, o_dd, o_do,
    w_in, w_o, w_g, w_u, w_d, buf1, buf2, qr, gate_v, up_v, gu, mgs, mgr, keys, vals, keys_t, dk, dv,
    dqs, ps, pr, mid_grad, normed, mixed, nmlp, hid, d_in, d_gu, d_d, d_o,
    parts, give, take, ring_out, ring_in,
    ag_s, ag_r, ag2_s, ag2_r, rs_s, rs_r, rs2_s, rs2_r, ax_s, ax_r, bx_s, bx_r, loc, loc2,
):
    me = Place()
    pairs = (
        (h_d, w_d), (h_gate, gate_v), (h_up, up_v), (h_g, w_g), (h_u, w_u), (h_o, w_o), (h_qkv, qr), (h_in, w_in),
        (h_hidden, hid), (h_nmlp, nmlp), (h_mixed, mixed), (h_normed, normed),
    )
    loads = [pltpu.make_async_copy(h, v, loc.at[i]) for i, (h, v) in enumerate(pairs)]
    for load in loads:
        load.start()
    stores = []

    def store(src, dst):
        stores.append(pltpu.make_async_copy(src, dst, loc2.at[len(stores)]))
        stores[-1].start()

    own_rows = slot_rows(me.z, me.core)
    buf1[own_rows] = grad[...].astype(BF)
    me.greet(me.layer_partners())
    for load in loads[:3]:
        load.wait()

    def unit(zz):
        rows = span_of(zz * 256, 256)
        hg = mm_nt(buf1[rows], w_d[...])
        gate, up = gate_v[rows], up_v[rows]
        sig = 1.0 / (1.0 + jnp.exp(-gate))
        gu[rows, 0:512] = (hg * up * (sig * (1.0 + gate * (1.0 - sig)))).astype(BF)
        gu[rows, 512:1024] = (hg * (gate * sig)).astype(BF)

    done_ag = all_gather(me, buf1, ag_s, ag_r, unit)
    for load in loads[3:]:
        load.wait()

    def mlp_part(zz):
        rows = span_of(zz * 256, 256)
        return mm_nt(gu[rows, 0:512], w_g[...]) + mm_nt(gu[rows, 512:1024], w_u[...])

    def grad_down(b):
        cols = slice(256 * b, 256 * b + 256)
        d_d[cols] = mm_tn(hid[:, cols], buf1[...]).astype(BF)

    def grad_gu(b):
        cols = slice(256 * b, 256 * b + 256)
        d_gu[cols] = mm_tn(nmlp[:, cols], gu[...]).astype(BF)

    def fill1(n):
        if n == 0:
            grad_down(0)
            grad_down(1)
        elif n == 1:
            grad_gu(0)
            grad_gu(1)
        else:
            grad_gu(2)
            grad_gu(3)

    rs = (parts, give, take, ring_out, ring_in)
    e, done_rs = reduce_scatter(me, mlp_part, *rs, rs_s, rs_r, fill1)
    part, gain_part = norm_back_of(e, middle[...], gains[1:2, :])
    o_gains[1:2, :] = gain_part
    gm = grad[...] + part
    mid_grad[...] = gm
    buf2[own_rows] = gm.astype(BF)
    ax = Exchange(me, mgs, mgr, ax_s, ax_r)

    def mixed_back(zz):
        rows = span_of(zz * 256, 256)
        mgs[rows] = mm_nt(buf2[rows], w_o[...]).astype(BF)
        ax.send(zz * 2)
        ax.send(zz * 2 + 1)

    def hook0():
        split_packed(qr, keys, vals)
        keys_t[...] = flip(keys)
        dk[...] = jnp.zeros_like(dk)
        dv[...] = jnp.zeros_like(dv)

    def hook2():
        grad_gu(4)
        grad_gu(5)

    done_ag2 = all_gather(me, buf2, ag2_s, ag2_r, mixed_back, (hook0, lambda: None, hook2))
    store(d_d, o_dd)
    store(d_gu, o_dgu)
    lanes = mm_tn(mixed[...], buf2[...])
    for head in range(2):
        chunk = [lanes[128 * head + 16 * c : 128 * head + 16 * c + 16] for c in (3, 7, 4, 0, 5, 1)]
        for b in range(8):
            first, shift = 12 * b // 16, 12 * b % 16
            piece = chunk[first][shift:]
            if shift > 4:
                piece = jnp.concatenate([piece, chunk[first + 1][: shift - 4]], axis=0)
            d_o[head, b // 4, b % 4] = padded(piece[0:12])
    store(d_o, o_do)
    ax.arrive()

    @pl.loop(0, 8)
    def _(p):
        rows = span_of(p * 128, 128)
        q = stacked(qr, rows)
        mg = stacked(mgr, rows)
        scores = mm_nt(keys[...], q) * SCALE
        allowed = pcol[...] <= prow[pl.ds(p, 1), :]
        probs = jnp.where(allowed, jnp.exp(scores - lse[pl.ds(p, 1), :]), 0.0)
        pg = mm_nt(vals[...], mg)
        inner = jnp.sum(probs * pg, axis=0, keepdims=True)
        sg = (probs * (pg - inner)).astype(BF)
        dk[...] += mm(sg, q)
        dv[...] += mm(probs.astype(BF), mg)
        dq = jnp.transpose(mm(keys_t[...], sg)) * SCALE
        dqs[rows, 0:128] = dq[0:128]
        dqs[rows, 128:256] = dq[128:256]

    bx = Exchange(me, ps, pr, bx_s, bx_r)
    v0, _, _ = lane_masks(128)

    @pl.loop(0, 8)
    def _(k):
        p = lax.rem(me.c + 1 + k, 8)
        rows = span_of(p * 128, 128)
        value = dv[rows]
        ps[rows, 0:128] = jnp.where(v0, value, dqs[rows, 0:128]).astype(BF)
        ps[rows, 128:256] = jnp.where(v0, pltpu.roll(value, 112, 1), dqs[rows, 128:256]).astype(BF)
        ps[rows, 256:384] = jnp.where(v0, pltpu.roll(value, 96, 1), dk[rows] * SCALE).astype(BF)
        bx.send(p)

    done_rs()
    bx.arrive()
    pre = qr

    def in_part(zz):
        rows = span_of(zz * 256, 256)
        for t in range(3):
            cols = slice(128 * t, 128 * t + 128)
            tile = pr[rows, cols].astype(F32)
            pre[rows, cols] = (tile * cos[...] - pltpu.roll(tile, 64, 1) * sin[...]).astype(BF)
        return mm_nt(pre[rows], w_in[...])

    def fill2(n):
        for b in (2 * n, 2 * n + 1):
            cols = slice(256 * b, 256 * b + 256)
            d_in[cols] = mm_tn(normed[:, cols], pre[...]).astype(BF)

    e, done_rs2 = reduce_scatter(me, in_part, *rs, rs2_s, rs2_r, fill2)
    store(d_in, o_din)
    part, gain_part = norm_back_of(e, stream[...].astype(F32), gains[0:1, :])
    o_gains[0:1, :] = gain_part
    o_grad[...] = mid_grad[...] + part
    for done in (done_ag, done_ag2, ax.finish, bx.finish, done_rs2):
        done()
    for item in stores:
        item.wait()


def padded(rows):
    return jnp.concatenate([rows, jnp.zeros((4, rows.shape[1]), F32)], axis=0).astype(BF)


def reduce_specs(d_in, d_gu, d_d, d_o):
    def split(ref, lo, hi, r, order):
        cols = slice(lo, hi)

        def quarter(axis, i):
            if axis == "x":
                return ref.at[:, i, :, :, :, cols]
            return ref.at[:, :, i // 2, lax.rem(i, 2), :, cols]

        def inner(s, i):
            return s.at[:, i] if order == "yx" else s.at[:, i // 2, lax.rem(i, 2)]

        lead = (2, 4) if order == "yx" else (2, 2, 2)
        return quarter, inner, order, lead + (r, hi - lo), (2, r, hi - lo)

    def out_quarter(axis, i):
        return d_o.at[i // 2, lax.rem(i, 2)]

    return [
        split(d_gu, 0, 512, 48, "yx"),
        split(d_gu, 512, 1024, 48, "xy"),
        split(d_d, 0, 768, 16, "yx"),
        split(d_d, 768, 1536, 16, "xy"),
        split(d_in, 0, 384, 48, "yx"),
        (out_quarter, lambda s, i: s.at[i], "yx", (4, 16, WIDE), (16, WIDE)),
    ]


def reduce_scratch():
    out = []
    for _, _, _, big, small in reduce_specs(None, None, None, None):
        out += [vm(big), vm((3,) + big), vm(big), vm((3,) + small)]
    return out


def grads_kernel(layers, *refs):
    parts, gains = refs[: 4 * layers], refs[4 * layers]
    o_rows, o_down, o_out, o_gains = refs[4 * layers + 1 : 4 * layers + 5]
    scratch = list(refs[4 * layers + 5 :])
    n_red = 6 * layers
    red_scratch, scratch = scratch[: 4 * n_red], scratch[4 * n_red :]
    fin_s, fin_r, down_s, down_r, out_s, out_r, sum_a, sum_b, got_a, got_b, got_c = scratch[:11]
    red_s, red_r, loc, fin_ss, fin_rs, gain_s, gain_r, down_ss, down_rs, out_ss = scratch[11:]
    me = Place()
    reds = []
    for l in range(layers):
        for quarter, inner, order, _, _ in reduce_specs(*parts[4 * l : 4 * l + 4]):
            n = len(reds)
            reds.append(
                Reduce(me, quarter, inner, *red_scratch[4 * n : 4 * n + 4], red_s.at[n], red_r.at[n], loc.at[n], order)
            )
    group = [(k, c) for k in range(4) for c in range(2) if k or c]

    def mate(k, c):
        return {"z": lax.rem(me.z + k, 4), "core": lax.rem(me.core + c, 2)}

    mirror = {"x": me.z, "z": me.x}
    apart = me.x != me.z
    me.greet(
        [me.near("x", k) for k in (1, 2, 3)] + [me.near("y", k) for k in (1, 2, 3)]
        + [mate(*m) for m in group] + [{"yl": 1 - me.yl, "core": me.oc}],
        mirror=True,
    )

    def gain_copy(stage, axis, src, got, k):
        i = 3 * stage + k - 1
        return push(src, got.at[k - 1], gain_s.at[i], gain_r.at[i], me.near(axis, k))

    def gain_sum(stage, axis, src, got, dst):
        total = src[...]
        for k in (1, 2, 3):
            gain_copy(stage, axis, src, got, k).wait_recv()
            total = total + got[k - 1]
        dst[...] = total

    for k in (1, 2, 3):
        gain_copy(0, "y", gains, got_a, k).start()
    for red in reds:
        red.one()
    gain_sum(0, "y", gains, got_a, sum_a)
    for k in (1, 2, 3):
        gain_copy(1, "x", sum_a, got_b, k).start()
    for red in reds:
        red.two()
    gain_sum(1, "x", sum_a, got_b, sum_b)

    def gain_mate(i):
        return push(sum_b, got_c.at[i], gain_s.at[6 + i], gain_r.at[6 + i], mate(*group[i]))

    for i in range(7):
        gain_mate(i).start()
    for l in range(layers):
        gate, up, down_a, down_b, first, out = reds[6 * l : 6 * l + 6]
        for lo, hi, red in ((384, 896, gate), (896, 1408, up), (0, 384, first)):
            total = red.three()
            for dp in range(2):
                for z in range(4):
                    fin_s[dp, z, l, :, lo:hi] = padded(total[dp, 12 * z : 12 * z + 12])
        down_s[:, l, :, 0:768] = down_a.three().astype(BF)
        down_s[:, l, :, 768:1536] = down_b.three().astype(BF)
        out_s[l] = out.three().astype(BF)

    slot = me.z * 2 + me.core

    def fin(i, come):
        k, c = group[i]
        to_z, to_core = lax.rem(me.z + k, 4), lax.rem(me.core + c, 2)
        from_z = lax.rem(me.z + 4 - k, 4)
        dst = fin_r.at[from_z * 2 + to_core] if come else fin_r.at[slot]
        return push(fin_s.at[to_core, to_z], dst, fin_ss.at[i], fin_rs.at[i], mate(k, c))

    def down(dp, half):
        dev = {"core": jnp.int32(dp), "yl": me.core}
        return push(down_s.at[dp], down_r.at[half], down_ss.at[dp], down_rs.at[half], dev)

    mine = me.yl == me.core

    def out_copy():
        return push(out_s, out_r, out_ss.at[0], out_ss.at[1], mirror)

    for i in range(7):
        fin(i, False).start()
    for dp in range(2):
        keep = mine & (me.core == dp)

        @pl.when(jnp.logical_not(keep))
        def _(dp=dp):
            down(dp, me.yl).start()

        @pl.when(keep)
        def _(dp=dp):
            down_r[me.yl] = down_s[dp]

    @pl.when(apart)
    def _():
        out_copy().start()

    @pl.when(jnp.logical_not(apart))
    def _():
        out_r[...] = out_s[...]

    fin_r[slot] = fin_s[me.core, me.z]
    total = sum_b[...]
    for i in range(7):
        gain_mate(i).wait_recv()
        total = total + got_c[i]
    o_gains[...] = total
    for i in range(7):
        fin(i, True).wait_recv()
    o_rows[...] = fin_r[...]
    for half in range(2):

        @pl.when(jnp.logical_not(mine & (me.yl == half)))
        def _(half=half):
            down(0, half).wait_recv()

    o_down[...] = down_r[...]

    @pl.when(apart)
    def _():
        out_copy().wait_recv()

    o_out[...] = out_r[...]
    for red in reds:
        red.finish()
    for k in (1, 2, 3):
        gain_copy(0, "y", gains, got_a, k).wait_send()
        gain_copy(1, "x", sum_a, got_b, k).wait_send()
    for i in range(7):
        gain_mate(i).wait_send()
        fin(i, False).wait_send()
    for dp in range(2):

        @pl.when(jnp.logical_not(mine & (me.core == dp)))
        def _(dp=dp):
            down(dp, me.yl).wait_send()

    @pl.when(apart)
    def _():
        out_copy().wait_send()


def vm(shape, dtype=BF):
    return pltpu.VMEM(shape, dtype)


def rs_scratch():
    return [vm((4, 128, WIDE)), vm((4, 128, WIDE)), vm((6, 64, WIDE)), vm((6, 64, WIDE))]


def dma(*shape):
    return pltpu.SemaphoreType.DMA(shape)


def sems():
    return [dma(n) for n in (13, 13, 13, 13, 10, 10, 10, 10, 8, 8, 8, 8, 12, 16)]


WEIGHTS = [(WIDE, 384), (256, WIDE), (WIDE, 512), (WIDE, 512), (512, WIDE)]
SPLIT = [(2, 4, 2, 2, 48, 384), (4, 64, WIDE), (2, 4, 2, 2, 48, 512), (2, 4, 2, 2, 48, 512), (2, 4, 2, 2, 16, WIDE)]


def run_kernel(kernel, name, cid, ins, in_vmem, outs, out_vmem, scratch, flops):
    place = {True: pltpu.VMEM, False: pl.ANY}
    return pl.pallas_call(
        kernel,
        name=name,
        out_shape=[jax.ShapeDtypeStruct(s, d) for s, d in outs],
        in_specs=[pl.BlockSpec(memory_space=place[i < in_vmem]) for i in range(len(ins))],
        out_specs=[pl.BlockSpec(memory_space=place[i < out_vmem]) for i in range(len(outs))],
        scratch_shapes=scratch,
        cost_estimate=pl.CostEstimate(flops=flops, bytes_accessed=60 * 2**20, transcendentals=0),
        compiler_params=pltpu.CompilerParams(
            collective_id=cid, has_side_effects=True, vmem_limit_bytes=60 * 2**20
        ),
    )(*ins)


def layer_fwd(l, stream, gains, cos, sin, pcol, prow, sources):
    outs = [
        ((128, WIDE), F32), ((128, WIDE), F32), ((8, 256), F32), ((8, WIDE), F32),
        ((1024, WIDE), BF), ((1024, 384), BF), ((1024, 256), BF), ((1024, WIDE), BF),
        ((1024, 512), F32), ((1024, 512), F32), ((1024, 512), BF),
    ] + [(s, BF) for s in SPLIT]
    scratch = [vm(s) for s in SPLIT] + [vm((2, 4, 2, 2, 8, 256), F32)] + [
        vm((1024, WIDE)), vm((1024, WIDE)), vm((1024, 384)), vm((1024, 384)), vm((1024, 256)), vm((1024, 256)),
        vm((1024, 512), F32), vm((1024, 512), F32), vm((1024, 512)),
        vm((1024, 128)), vm((1024, 128)), vm((128, 1024)), vm((128, WIDE), F32), vm((4, 256, WIDE), F32),
    ] + rs_scratch() + sems() + [dma(6, 7), dma(6, 7)]
    ins = [stream, gains, cos, sin, pcol, prow, *sources]
    kernel = functools.partial(fwd_kernel, l == 0)
    return run_kernel(kernel, f"layer_forward_{l}", 1 + l, ins, 6, outs, 4, scratch, 40 * 10**9)


def layer_bwd(l, grad, stream, middle, gains, cos, sin, pcol, prow, lse, weights, saved):
    outs = [((128, WIDE), F32), ((8, WIDE), F32), ((WIDE, 384), BF), ((WIDE, 1024), BF), ((512, WIDE), BF), ((2, 2, 4, 16, WIDE), BF)]
    scratch = [vm(s) for s in WEIGHTS] + [
        vm((1024, WIDE)), vm((1024, WIDE)), vm((1024, 384)), vm((1024, 512), F32), vm((1024, 512), F32),
        vm((1024, 1024)), vm((1024, 256)), vm((1024, 256)),
        vm((1024, 128)), vm((1024, 128)), vm((128, 1024)), vm((1024, 128), F32), vm((1024, 128), F32),
        vm((1024, 256), F32), vm((1024, 384)), vm((1024, 384)), vm((128, WIDE), F32),
        vm((1024, WIDE)), vm((1024, 256)), vm((1024, WIDE)), vm((1024, 512)),
        vm((WIDE, 384)), vm((WIDE, 1024)), vm((512, WIDE)), vm((2, 2, 4, 16, WIDE)), vm((4, 256, WIDE), F32),
    ] + rs_scratch() + sems()
    weights = [w.reshape(s) for w, s in zip(weights, WEIGHTS)]
    ins = [grad, stream, middle, gains, cos, sin, pcol, prow, lse, *weights, *saved]
    return run_kernel(bwd_kernel, f"layer_backward_{l}", 3 + l, ins, 9, outs, 2, scratch, 60 * 10**9)


def reduce_grads(parts, gains):
    layers = len(parts) // 4
    outs = [((8, layers, 16, 1408), BF), ((2, layers, 16, WIDE), BF), ((layers, 16, WIDE), BF), ((8, WIDE), F32)]
    scratch = reduce_scratch() * layers + [
        vm((2, 4, layers, 16, 1408)), vm((8, layers, 16, 1408)), vm((2, layers, 16, WIDE)), vm((2, layers, 16, WIDE)),
        vm((layers, 16, WIDE)), vm((layers, 16, WIDE)), vm((8, WIDE), F32), vm((8, WIDE), F32),
        vm((3, 8, WIDE), F32), vm((3, 8, WIDE), F32), vm((7, 8, WIDE), F32),
        dma(6 * layers, 6), dma(6 * layers, 6), dma(6 * layers), dma(7), dma(7), dma(13), dma(13), dma(2), dma(2), dma(2),
    ]
    kernel = functools.partial(grads_kernel, layers)
    place = {True: pltpu.VMEM, False: pl.ANY}
    ins = [*parts, gains]
    return pl.pallas_call(
        kernel,
        name="reduce_gradients",
        out_shape=[jax.ShapeDtypeStruct(s, d) for s, d in outs],
        in_specs=[pl.BlockSpec(memory_space=place[i == 4 * layers]) for i in range(len(ins))],
        out_specs=[pl.BlockSpec(memory_space=pltpu.VMEM) for _ in outs],
        scratch_shapes=scratch,
        compiler_params=pltpu.CompilerParams(collective_id=5, has_side_effects=True, vmem_limit_bytes=60 * 2**20),
    )(*ins)


def body(
    tokens, span_order, attn_gain, w_query, key_matrix, value_matrix, w_out, mlp_gain, w_gate, w_up,
    w_down, cotangent,
):
    rows = tokens.shape[1]
    core, z, yl = lax.axis_index("core"), lax.axis_index("z"), lax.axis_index("yl")
    ctx = lax.axis_index("x") * 2 + lax.axis_index("yh")
    seq_len = 8 * rows
    span = seq_len // span_order.shape[0]
    cos, sin = rope_tables(place_rows(span_order, ctx * rows, rows, span))
    cos, sin = jnp.tile(cos, (2, 1)), jnp.tile(sin, (2, 1))
    places = place_rows(span_order, 0, seq_len, span)
    pcol = places[:, None]
    prow = jnp.tile(places.reshape(8, rows), (1, 2))

    def pick(values, index, axis):
        return lax.dynamic_index_in_dim(values, index, axis=axis, keepdims=False)

    def half(w):
        return lax.dynamic_slice_in_dim(w, yl * 48, 48, axis=1)

    def heads(w, n):
        return pick(half(w).reshape(LAYERS, 48, 2, 4, n), z, 3)

    s_in = pack_heads(heads(w_query, 192), heads(key_matrix, 96), heads(value_matrix, 96)).transpose(0, 2, 1, 3)

    def hidden(w):
        own = pick(half(w).reshape(LAYERS, 48, 16, 2, 4, 32), z, 4)
        return own.transpose(0, 3, 1, 2, 4).reshape(LAYERS, 2, 48, 512)

    s_g, s_u = hidden(w_gate), hidden(w_up)
    s_d = pick(pick(w_down.reshape(LAYERS, 2, 4, 2, 16, WIDE), z, 2), yl, 2)
    s_o = jnp.stack([spread_rows(w_out[l]) for l in range(LAYERS)])
    s_o = lax.dynamic_slice_in_dim(s_o, yl * 64, 64, axis=1)
    own_gains = jnp.concatenate([attn_gain[:1], mlp_gain[:1], attn_gain[1:], mlp_gain[1:]], axis=0).astype(F32)
    s_gain = lax.dynamic_update_slice(jnp.zeros((8, 256), F32), own_gains, (0, lax.rem(96 * (core * 8 + ctx), 128)))
    s_gain = jnp.stack([s_gain, s_gain])

    stream = tokens[0]
    kept = []
    gains = jnp.zeros((8, WIDE), F32)
    for l in range(LAYERS):
        sources = (s_gain, s_in[l], s_o[l], s_g[l], s_u[l], s_d[l])
        outs = layer_fwd(l, stream, gains, cos, sin, pcol, prow, sources)
        kept.append((stream, gains if l else outs[3], outs))
        stream = outs[0]
        gains = outs[3][2:]
        gains = jnp.concatenate([gains, jnp.zeros((2, WIDE), F32)], axis=0)
    block_out = stream.astype(BF)[None]

    g = cotangent[0].astype(F32)
    gain_parts = [None] * LAYERS
    grads = [None] * LAYERS
    for l in reversed(range(LAYERS)):
        stream, gains, outs = kept[l]
        _, middle, lse, _, normed, qkv, mixed, nmlp, gate, up, hid = outs[:11]
        g, gain_parts[l], d_in, d_gu, d_d, d_o = layer_bwd(
            l, g, stream, middle, gains, cos, sin, pcol, prow, lse, outs[11:], (qkv, gate, up, normed, mixed, nmlp, hid)
        )
        grads[l] = (
            d_in.reshape(2, 4, 2, 2, 48, 384), d_gu.reshape(2, 4, 2, 2, 48, 1024), d_d.reshape(2, 4, 2, 2, 16, WIDE), d_o,
        )
    gp = jnp.concatenate([gain_parts[0][:2], gain_parts[1][:2], jnp.zeros((4, WIDE), F32)], axis=0)
    cols, d_d, d_o, gp = reduce_grads(grads[0] + grads[1], gp)
    cols = cols.reshape(4, 2, LAYERS, 16, 1408)[:, :, :, :12].transpose(2, 3, 1, 0, 4).reshape(LAYERS, 12, 8, 1408)
    cols = cols.astype(F32)
    d_q, d_k, d_v = unpack_grads(cols[..., :384])

    def hidden_join(d):
        return d.reshape(LAYERS, 12, 8, 16, 32).transpose(0, 1, 3, 2, 4).reshape(LAYERS, 12, 4096)

    d_g, d_u = hidden_join(cols[..., 384:896]), hidden_join(cols[..., 896:])
    d_d = d_d.transpose(1, 0, 2, 3).reshape(LAYERS, 32, WIDE).astype(F32)
    d_o = d_o[:, :12].astype(F32)
    owner = (core * 8 + ctx) * 8 + yl * 4 + z
    gp = lax.dynamic_slice(gp, (0, owner * 12), (4, 12)).reshape(2, 2, 12)
    return (block_out, g[None], gp[:, 0], d_q, d_k, d_v, d_o, gp[:, 1], d_g, d_u, d_d)


def solution(mesh):
    fine = Mesh(mesh.devices.reshape(2, 4, 2, 2, 4), ALL)
    seq, ctx, own, every = ("core", "yl", "z"), CTX, OWN, ALL
    act = P(seq, ctx, None)
    in_specs = (act, P(), P(None, own)) + (P(None, own, None),) * 4 + (P(None, own),) + (P(None, own, None),) * 3 + (act,)
    grad = P(None, every, None)
    out_specs = (act, act, P(None, every)) + (grad,) * 4 + (P(None, every),) + (grad,) * 3
    return jax.shard_map(body, mesh=fine, in_specs=in_specs, out_specs=out_specs, check_vma=False)
```

```python
import functools
import math

import jax
import jax.numpy as jnp
import numpy as np
from jax import lax
from jax.experimental import pallas as pl
from jax.experimental.pallas import tpu as pltpu
from jax.sharding import Mesh, PartitionSpec as P

HEAD = 96
LAYERS = 2
ROPE_BASE = 100000.0
EPS = 1e-05
CTX = ("x", "yh")
TP = ("z", "core")
OWN = ("core", "x", "yh")
ALL = ("core", "x", "yh", "yl", "z")
BF = jnp.bfloat16
F32 = jnp.float32
MESH = pl.DeviceIdType.MESH
SCALE = 1.0 / math.sqrt(HEAD)
SCALE2 = SCALE * math.log2(math.e)
WIDE = 1536


def mm(a, b):
    return jnp.dot(a, b, preferred_element_type=F32)


def mm_tn(a, b):
    return lax.dot_general(a, b, (((0,), (0,)), ((), ())), preferred_element_type=F32)


def mm_nt(a, b):
    return lax.dot_general(a, b, (((1,), (1,)), ((), ())), preferred_element_type=F32)


def place_rows(span_order, first, count, span):
    ids = first + jnp.arange(count, dtype=jnp.int32)
    slots = jnp.arange(span_order.shape[0], dtype=jnp.int32)
    picked = jnp.sum(
        jnp.where((ids // span)[:, None] == slots[None, :], span_order[None, :], 0), axis=1
    )
    return picked * span + ids % span


def rope_tables(places):
    freq = ROPE_BASE ** (-2.0 * jnp.arange(HEAD // 2, dtype=F32) / HEAD)
    angles = places.astype(F32)[:, None] * freq[None, :]
    cos, sin = jnp.cos(angles), jnp.sin(angles)
    one, zero = jnp.ones((places.shape[0], 16), F32), jnp.zeros((places.shape[0], 16), F32)
    return (
        jnp.concatenate([cos, one, cos, one], axis=1),
        jnp.concatenate([-sin, zero, sin, zero], axis=1),
    )


def pack_heads(q, k, v):
    lead = q.shape[:-1]
    qk = jnp.concatenate([q.reshape(*lead, 2, HEAD), k.reshape(*lead, 1, HEAD)], axis=-2)
    v = v.reshape(*lead, 3, 32)
    tiles = jnp.concatenate([qk[..., :48], v[..., :16], qk[..., 48:], v[..., 16:]], axis=-1)
    return tiles.reshape(*lead, 384)


def unpack_grads(packed):
    lead = packed.shape[:-2]
    tiles = packed.reshape(*lead, 8, 3, 128)
    qk = jnp.concatenate([tiles[..., :48], tiles[..., 64:112]], axis=-1)
    v = jnp.concatenate([tiles[..., 48:64], tiles[..., 112:]], axis=-1)
    return (
        qk[..., :2, :].reshape(*lead, 1536),
        qk[..., 2, :].reshape(*lead, 768),
        v.reshape(*lead, 768),
    )


def spread_rows(rows):
    r = rows.reshape(3, 2, 16, -1)
    z = jnp.zeros_like(r[0, 0])
    return jnp.concatenate(
        [r[1, 1], r[2, 1], z, r[0, 0], r[1, 0], r[2, 0], z, r[0, 1]], axis=0
    )


class Place:
    def __init__(self):
        self.z, self.core = lax.axis_index("z"), lax.axis_index("core")
        self.x, self.yh, self.yl = lax.axis_index("x"), lax.axis_index("yh"), lax.axis_index("yl")
        self.y = self.yh * 2 + self.yl
        self.c = self.x * 2 + self.yh
        self.zp, self.zm, self.zo = (lax.rem(self.z + k, 4) for k in (1, 3, 2))
        self.oc = 1 - self.core

    def near(self, axis, k):
        if axis == "x":
            return {"x": lax.rem(self.x + k, 4)}
        return at_y(lax.rem(self.y + k, 4))

    def greet(self, others, mirror=False):
        barrier = pltpu.get_barrier_semaphore()
        for dev in others:
            pl.semaphore_signal(barrier, inc=1, device_id=dev, device_id_type=MESH)
        if not mirror:
            pl.semaphore_wait(barrier, len(others))
            return

        @pl.when(self.x != self.z)
        def _():
            there = {"x": self.z, "z": self.x}
            pl.semaphore_signal(barrier, inc=1, device_id=there, device_id_type=MESH)
            pl.semaphore_wait(barrier, len(others) + 1)

        @pl.when(self.x == self.z)
        def _():
            pl.semaphore_wait(barrier, len(others))

    def layer_partners(self):
        return (
            [{"z": self.zp}, {"z": self.zm}, {"core": self.oc}]
            + [at_ctx(lax.rem(self.c + k, 8)) for k in range(1, 8)]
            + [{"yl": 1 - self.yl}, {"yh": 1 - self.yh, "yl": 1 - self.yl}]
        )


def at_y(y):
    return {"yh": y // 2, "yl": lax.rem(y, 2)}


def at_ctx(c):
    return {"x": c // 2, "yh": lax.rem(c, 2)}


def span_of(start, size):
    return pl.ds(pl.multiple_of(start, 64), size)


def slot_rows(zz, cc, half=None):
    base = (zz * 2 + cc) * 128
    return span_of(base, 128) if half is None else span_of(base + 64 * half, 64)


def all_gather(me, buf, ssem, rsem, on_pair, hooks=()):
    z, zp, zm, zo, core, oc = me.z, me.zp, me.zm, me.zo, me.core, me.oc
    up, down, across = {"z": zp}, {"z": zm}, {"core": oc}
    sent = [
        (z, core, 0, up), (z, core, 1, up), (z, core, 1, down), (z, core, 0, down),
        (zm, core, 0, up), (zp, core, 1, down), (z, core, None, across),
        (zm, core, 0, across), (zm, core, 1, across), (zp, core, 1, across), (zp, core, 0, across),
        (zo, core, 0, across), (zo, core, 1, across),
    ]
    come = [
        (zm, core, 0), (zm, core, 1), (zp, core, 1), (zp, core, 0), (zo, core, 0), (zo, core, 1),
        (z, oc, None), (zm, oc, 0), (zm, oc, 1), (zp, oc, 1), (zp, oc, 0), (zo, oc, 0), (zo, oc, 1),
    ]

    def copy(i, rows, dev):
        return pltpu.make_async_remote_copy(
            src_ref=buf.at[rows], dst_ref=buf.at[rows], send_sem=ssem.at[i], recv_sem=rsem.at[i],
            device_id=dev, device_id_type=MESH,
        )

    def send(*which):
        for i in which:
            copy(i, slot_rows(*sent[i][:3]), sent[i][3]).start()

    def arrive(*which):
        for i in which:
            copy(i, slot_rows(*come[i]), sent[i][3]).wait_recv()

    def hook(i):
        if i < len(hooks):
            hooks[i]()

    send(0, 2, 1, 3, 6)
    hook(0)
    arrive(6)
    on_pair(z)
    arrive(0)
    send(4, 7)
    arrive(2)
    send(5, 9)
    hook(1)
    arrive(1)
    send(8)
    arrive(3)
    send(10)
    hook(2)
    arrive(7, 8)
    on_pair(zm)
    arrive(9, 10)
    on_pair(zp)
    hook(3)
    arrive(4)
    send(11)
    arrive(5)
    send(12)
    arrive(11, 12)
    on_pair(zo)

    def finish():
        for i in range(13):
            copy(i, slot_rows(*sent[i][:3]), sent[i][3]).wait_send()

    return finish


def reduce_scatter(me, part, whole, keep, give, take, ring_out, ring_in, ssem, rsem, fill=lambda n: None):
    z, zp, zm, zo, core, oc = me.z, me.zp, me.zm, me.zo, me.core, me.oc
    up, down, across = {"z": zp}, {"z": zm}, {"core": oc}
    mine = span_of(core * 128, 128)
    theirs = span_of(oc * 128, 128)

    def swap(k):
        return pltpu.make_async_remote_copy(
            src_ref=give.at[k], dst_ref=take.at[k], send_sem=ssem.at[k], recv_sem=rsem.at[k],
            device_id=across, device_id_type=MESH,
        )

    def ring(i):
        return pltpu.make_async_remote_copy(
            src_ref=ring_out.at[i], dst_ref=ring_in.at[i], send_sem=ssem.at[4 + i], recv_sem=rsem.at[4 + i],
            device_id=up if i < 3 else down, device_id_type=MESH,
        )

    def make(k, zz):
        whole[...] = part(zz)
        give[k] = whole[theirs].astype(BF)
        keep[k] = whole[mine]
        swap(k).start()

    def merged(k, half):
        rows = slice(64 * half, 64 * half + 64)
        return keep[k, rows] + take[k, rows].astype(F32)

    def push(i, value):
        ring_out[i] = value.astype(BF)
        ring(i).start()

    make(0, zo)
    make(1, zp)
    swap(0).wait_recv()
    push(0, merged(0, 0))
    push(3, merged(0, 1))
    make(2, zm)
    swap(1).wait_recv()
    push(1, merged(1, 1))
    swap(2).wait_recv()
    push(4, merged(2, 0))
    make(3, z)
    fill(0)
    ring(0).wait_recv()
    push(2, merged(1, 0) + ring_in[0].astype(F32))
    ring(3).wait_recv()
    push(5, merged(2, 1) + ring_in[3].astype(F32))
    swap(3).wait_recv()
    fill(1)
    own = [merged(3, 0), merged(3, 1)]
    ring(1).wait_recv()
    own[1] = own[1] + ring_in[1].astype(F32)
    ring(4).wait_recv()
    own[0] = own[0] + ring_in[4].astype(F32)
    fill(2)
    ring(2).wait_recv()
    own[0] = own[0] + ring_in[2].astype(F32)
    ring(5).wait_recv()
    own[1] = own[1] + ring_in[5].astype(F32)

    def finish():
        for k in range(4):
            swap(k).wait_send()
        for i in range(6):
            ring(i).wait_send()

    return jnp.concatenate(own, axis=0), finish


class Exchange:
    def __init__(self, me, src, dst, ssem, rsem):
        self.me, self.src, self.dst, self.ssem, self.rsem = me, src, dst, ssem, rsem

    def copy(self, s, come):
        return pltpu.make_async_remote_copy(
            src_ref=self.src.at[span_of(s * 128, 128)], dst_ref=self.dst.at[span_of(come * 128, 128)],
            send_sem=self.ssem.at[s], recv_sem=self.rsem.at[come],
            device_id=at_ctx(s), device_id_type=MESH,
        )

    def send(self, s):
        c = self.me.c

        @pl.when(s != c)
        def _():
            self.copy(s, c).start()

        @pl.when(s == c)
        def _():
            rows = span_of(s * 128, 128)
            self.dst[rows] = self.src[rows]

    def arrive(self):
        @pl.loop(1, 8)
        def _(k):
            there = lax.rem(self.me.c + k, 8)
            self.copy(there, there).wait_recv()

    def finish(self):
        @pl.loop(1, 8)
        def _(k):
            there = lax.rem(self.me.c + k, 8)
            self.copy(there, self.me.c).wait_send()


def push(src, dst, ssem, rsem, dev):
    return pltpu.make_async_remote_copy(
        src_ref=src, dst_ref=dst, send_sem=ssem, recv_sem=rsem, device_id=dev, device_id_type=MESH
    )


class Gather:
    def __init__(self, me, src, dst, ssem, rsem, loc, order, cols):
        self.me, self.src, self.dst, self.ssem, self.rsem, self.order = me, src, dst, ssem, rsem, order
        self.loc, self.cols = loc, slice(*cols)

    def own(self):
        me = self.me
        return pltpu.make_async_copy(
            self.src.at[me.core, :, self.cols], self.dst.at[me.core, me.x, me.y, :, self.cols], self.loc
        )

    def cross(self, come=False):
        me = self.me
        row = me.oc if come else me.core
        return push(
            self.src.at[me.oc, :, self.cols], self.dst.at[row, me.x, me.y, :, self.cols],
            self.ssem.at[0], self.rsem.at[0], {"core": me.oc},
        )

    def region(self, stage, k):
        me = self.me
        x, y = (lax.rem(v + 4 - k, 4) for v in (me.x, me.y))
        if stage == 0:
            return self.dst.at[:, x if self.order[0] == "x" else me.x, y if self.order[0] == "y" else me.y, :, self.cols]
        if self.order[1] == "y":
            return self.dst.at[:, :, y, :, self.cols]
        return self.dst.at[:, x, :, :, self.cols]

    def copy(self, stage, k, come):
        ref = self.region(stage, k if come else 0)
        i = 1 + 3 * stage + k - 1
        return push(ref, ref, self.ssem.at[i], self.rsem.at[i], self.me.near(self.order[stage], k))

    def zero(self):
        self.own().start()
        self.cross().start()

    def one(self):
        self.own().wait()
        self.cross(True).wait_recv()
        for k in (2, 1, 3):
            self.copy(0, k, False).start()

    def two(self):
        for k in (1, 3, 2):
            self.copy(0, k, True).wait_recv()
        for k in (2, 1, 3):
            self.copy(1, k, False).start()

    def three(self):
        for k in (1, 3, 2):
            self.copy(1, k, True).wait_recv()

    def finish(self):
        self.cross().wait_send()
        for stage in (0, 1):
            for k in (1, 2, 3):
                self.copy(stage, k, False).wait_send()


class OutGather:
    def __init__(self, me, src, dst, ssem, rsem, loc):
        self.me, self.dst, self.ssem, self.rsem = me, dst, ssem, rsem
        self.own = pltpu.make_async_copy(src, dst.at[me.y], loc)
        self.far = lax.rem(me.x + 4 - me.z, 4)

    def copy(self, stage, k, come):
        me = self.me
        y = lax.rem(me.y + 4 - k, 4) if stage and come else me.y
        ref, i = self.dst.at[y], 3 * stage + k - 1
        return push(ref, ref, self.ssem.at[i], self.rsem.at[i], me.near("xy"[stage], k))

    def zero(self):
        @pl.when(self.far == 0)
        def _():
            self.own.start()

    def one(self):
        @pl.when(self.far == 0)
        def _():
            self.own.wait()
            for k in (2, 1, 3):
                self.copy(0, k, False).start()

    def two(self):
        for k in (1, 2, 3):

            @pl.when(self.far == k)
            def _(k=k):
                self.copy(0, k, True).wait_recv()

        for k in (2, 1, 3):
            self.copy(1, k, False).start()

    def three(self):
        for k in (1, 3, 2):
            self.copy(1, k, True).wait_recv()

    def finish(self):
        @pl.when(self.far == 0)
        def _():
            for k in (1, 2, 3):
                self.copy(0, k, False).wait_send()

        for k in (1, 2, 3):
            self.copy(1, k, False).wait_send()


class Reduce:
    def __init__(self, me, spec, mine, got1, sum1, got2, ssem, rsem, loc, land=None, landed=False):
        self.me = me
        self.quarter, self.inner, self.order = spec[:3]
        self.mine, self.got1, self.sum1, self.got2, self.ssem, self.rsem, self.loc = mine, got1, sum1, got2, ssem, rsem, loc
        self.land, self.landed = land, landed

    def at(self, axis, k):
        return lax.rem((self.me.x if axis == "x" else self.me.y) + k, 4)

    def copy(self, stage, k):
        axis = self.order[stage]
        to = self.at(axis, k)
        src = self.inner(self.sum1, to) if stage else self.quarter(axis, to)
        dst = (self.got2 if stage else self.got1 if self.land is None else self.land).at[k - 1]
        i = 3 * stage + k - 1
        return push(src, dst, self.ssem.at[i], self.rsem.at[i], self.me.near(axis, k))

    def loads(self):
        axis = self.order[0]
        out = [pltpu.make_async_copy(self.quarter(axis, self.at(axis, 0)), self.mine, self.loc.at[0])]
        if self.land is not None:
            out.append(pltpu.make_async_copy(self.land, self.got1, self.loc.at[1]))
        return out

    def load(self):
        for load in self.loads():
            load.start()

    def one(self):
        for k in (2, 1, 3):
            self.copy(0, k).start()

    def arrive(self):
        if not self.landed:
            for k in (1, 2, 3):
                self.copy(0, k).wait_recv()

    def two(self):
        for load in self.loads():
            load.wait()
        dims = self.sum1.shape[:-2]

        @pl.loop(0, math.prod(dims))
        def _(n):
            at = (n,) if len(dims) == 1 else (n // dims[1], lax.rem(n, dims[1]))
            total = self.mine[at].astype(F32)
            for k in range(3):
                total = total + self.got1[(k, *at)].astype(F32)
            self.sum1[at] = total.astype(BF)

        for k in (2, 1, 3):
            self.copy(1, k).start()

    def three(self):
        for k in (1, 2, 3):
            self.copy(1, k).wait_recv()
        total = self.inner(self.sum1, self.at(self.order[1], 0))[...].astype(F32)
        for k in range(3):
            total = total + self.got2[k].astype(F32)
        return total

    def finish(self, stages=(0, 1)):
        for stage in stages:
            for k in (1, 2, 3):
                self.copy(stage, k).wait_send()


def reduce_specs(d_in, d_gu, d_d, d_o):
    def split(ref, lo, hi, r, order):
        def quarter(axis, i):
            return ref.at[:, i, :, :, lo:hi] if axis == "x" else ref.at[:, :, i, :, lo:hi]

        return quarter, lambda q, i: q.at[:, i], order, (2, 4, r, hi - lo), (2, r, hi - lo)

    return {
        "g": split(d_gu, 0, 512, 48, "yx"),
        "u": split(d_gu, 512, 1024, 48, "xy"),
        "da": split(d_d, 0, 768, 16, "yx"),
        "db": split(d_d, 768, 1536, 16, "xy"),
        "ia": split(d_in, 0, 256, 48, "yx"),
        "ib": split(d_in, 256, 384, 48, "xy"),
        "o": (lambda axis, i: d_o.at[:, i], lambda q, i: q.at[i], "xy", (4, 16, WIDE), (16, WIDE)),
    }


REDUCE = reduce_specs(None, None, None, None)
MLP = ("g", "u", "da", "db")


def reduce_scratch(staged=REDUCE):
    out = []
    for name, (_, _, _, big, small) in REDUCE.items():
        out += [vm(big), vm((3,) + big)] if name in staged else []
        out += [vm(big), vm((3,) + small)]
    return out + [dma(7, 6), dma(7, 6), dma(7, 2)]


def make_reduces(me, parts, refs, land=None, landed=False, stage=None):
    out, n = {}, 0
    for name, spec in reduce_specs(*parts).items():
        own, got = stage[name] if stage and name in stage else (refs.pop(0), refs.pop(0))
        sum1, got2 = refs.pop(0), refs.pop(0)
        out[name] = (spec, own, got, sum1, got2)
    ssem, rsem, loc = refs.pop(0), refs.pop(0), refs.pop(0)
    for n, (name, (spec, own, got, sum1, got2)) in enumerate(out.items()):
        there = land.get(name) if land else None
        out[name] = Reduce(
            me, spec, own, got, sum1, got2, ssem.at[n], rsem.at[n], loc.at[n], there, landed and there is not None
        )
    return out


def finish_reduces(reds, fin, down, out):
    for lo, hi, name in ((0, 256, "ia"), (256, 384, "ib"), (384, 896, "g"), (896, 1408, "u")):
        total = reds[name].three()
        for dp in range(2):
            for z in range(4):
                fin[dp, z, :, lo:hi] = padded(total[dp, 12 * z : 12 * z + 12])
    down[:, :, 0:768] = reds["da"].three().astype(BF)
    down[:, :, 768:1536] = reds["db"].three().astype(BF)
    out[...] = reds["o"].three().astype(BF)


def lane_masks(rows):
    lane = lax.broadcasted_iota(jnp.int32, (rows, 128), 1)
    v0 = ((lane >= 48) & (lane < 64)) | (lane >= 112)
    v1 = ((lane >= 64) & (lane < 80)) | (lane < 16)
    v2 = ((lane >= 80) & (lane < 96)) | ((lane >= 16) & (lane < 32))
    return v0, v1, v2


def split_packed(packed, key_ref, value_ref):
    v0, v1, v2 = lane_masks(128)

    @pl.loop(0, 8)
    def _(p):
        rows = span_of(p * 128, 128)
        t0, t1, t2 = (packed[rows, 128 * t : 128 * t + 128].astype(F32) for t in range(3))
        key_ref[rows] = jnp.where(v0, 0.0, t2).astype(BF)
        value = jnp.where(v0, t0, 0.0)
        value = value + jnp.where(v1, pltpu.roll(t1, 16, 1), 0.0)
        value = value + jnp.where(v2, pltpu.roll(t2, 32, 1), 0.0)
        value_ref[rows] = value.astype(BF)


def flip(ref):
    return jnp.transpose(ref[...].astype(F32)).astype(BF)


def stacked(ref, rows):
    return jnp.concatenate([ref[rows, 0:128], ref[rows, 128:256]], axis=0)


def rms_of(values):
    return lax.rsqrt(jnp.mean(values * values, axis=-1, keepdims=True) + EPS)


def fwd_kernel(l, *refs):
    first = l == 0
    g_attn, g_mlp = (slice(2 * l + i, 2 * l + i + 1) for i in (0, 1))
    refs = list(refs)
    take = lambda n: [refs.pop(0) for _ in range(n)]
    stream, gains_in, cos, sin, pcol, prow = take(6)
    (h_in,) = take(1)
    s_o, s_g, s_u, s_d = take(4)
    s_gain, s_next = take(2) if first else (None, None)
    o_stream, o_middle, o_lse = take(3)
    (o_gains,) = take(1) if first else (gains_in,)
    o_normed, o_qkv, o_mixed, o_nmlp, o_gate, o_up, o_hidden, o_wo, o_wg, o_wu, o_wd = take(11)
    o_win, o_next = take(2) if first else (None, None)
    w_in, w_o, w_g, w_u, w_d = take(5)
    buf1, buf2, qs, qr, ms, mr, gate_v, up_v, hid, keys, vals, vals_t, middle = take(13)
    whole, keep, give, got, ring_out, ring_in = take(6)
    ag_s, ag_r, ag2_s, ag2_r, rs_s, rs_r, rs2_s, rs2_r, ax_s, ax_r, bx_s, bx_r, loc, loc2, ga_s, ga_r = take(16)
    w_gain, w_next = take(2) if first else (None, None)
    me = Place()
    stores = []

    def store(src, dst):
        stores.append(pltpu.make_async_copy(src, dst, loc2.at[len(stores)]))
        stores[-1].start()

    n_item = [0]

    def item(src, dst, order, *cols):
        i = n_item[0]
        n_item[0] += 1
        return Gather(me, src, dst, ga_s.at[i], ga_r.at[i], loc.at[i], order, cols)

    g_g, g_u = item(s_g, w_g, "xy", 0, 512), item(s_u, w_u, "yx", 0, 512)
    g_d = [item(s_d, w_d, "xy", 0, 768), item(s_d, w_d, "yx", 768, WIDE)]
    g_o = OutGather(me, s_o, w_o, ga_s.at[4], ga_r.at[4], loc.at[4])
    n_item[0] = 5
    g_in, g_next, g_gain = [], [], []
    if first:
        g_gain = [item(s_gain, w_gain, "yx", 0, 256)]
        g_in = [item(h_in, w_in, "yx", 0, 256), item(h_in, w_in, "xy", 256, 384)]
        g_next = [item(s_next, w_next, "yx", 0, 256), item(s_next, w_next, "xy", 256, 384)]
    everything = g_gain + g_in + [g_o, g_g, g_u] + g_d + g_next

    def each(items, step):
        for one in items:
            getattr(one, step)()

    own_rows = slot_rows(me.z, me.core)
    raw = buf2 if first else buf1
    if first:
        raw[own_rows] = stream[...]
    else:
        load_in = pltpu.make_async_copy(h_in, w_in, loc.at[5])
        load_in.start()
        s = stream[...]
        raw[own_rows] = (s * rms_of(s) * gains_in[g_attn, :]).astype(BF)
    me.greet(me.layer_partners())
    each(everything, "zero")
    ax = Exchange(me, qs, qr, ax_s, ax_r)

    def project(zz):
        rows = span_of(zz * 256, 256)
        y = mm(buf1[rows], w_in[...].reshape(WIDE, 384))
        for t in range(3):
            tile = y[:, 128 * t : 128 * t + 128]
            tile = tile * cos[...] + pltpu.roll(tile, 64, 1) * sin[...]
            qs[rows, 128 * t : 128 * t + 128] = tile.astype(BF)
        ax.send(zz * 2)
        ax.send(zz * 2 + 1)

    def normalise(zz):
        rows = span_of(zz * 256, 256)
        s = raw[rows].astype(F32)
        buf1[rows] = (s * rms_of(s) * o_gains[g_attn, :]).astype(BF)

    if first:

        def own_pair():
            each(g_gain + g_in, "two")

        def gains_here():
            each(g_gain, "three")
            o_gains[...] = jnp.zeros_like(o_gains)
            for owner in range(16):
                base = 96 * owner // 128 * 128
                width = min(256, WIDE - base)
                row = w_gain[owner // 8, owner % 8 // 2, owner % 2 * 2]
                o_gains[:, base : base + width] += row[:, :width]
            normalise(me.z)
            g_o.one()

        hooks = (lambda: each(g_gain + g_in, "one"), own_pair, gains_here)

        def others(zz):
            if zz is not me.z:
                normalise(zz)

        done_ag = all_gather(me, raw, ag_s, ag_r, others, hooks)
        done_ag()
        each(g_in, "three")

        @pl.loop(0, 4)
        def _(k):
            project(lax.rem(me.z + k, 4))

    else:
        load_in.wait()
        done_ag = all_gather(me, raw, ag_s, ag_r, project, (g_o.one,))
    g_o.two()
    each((g_g, g_u), "one")
    ax.arrive()
    store(buf1, o_normed)
    store(qr, o_qkv)
    split_packed(qr, keys, vals)
    vals_t[...] = flip(vals)
    bx = Exchange(me, ms, mr, bx_s, bx_r)

    @pl.loop(0, 8)
    def _(k):
        p = lax.rem(me.c + 1 + k, 8)
        rows = span_of(p * 128, 128)
        q = stacked(qr, rows)
        scores = mm_nt(keys[...], q)
        scores = jnp.where(pcol[...] <= prow[pl.ds(p, 1), :], scores, -1e30)
        top = jnp.max(scores, axis=0, keepdims=True)
        weights = jnp.exp2((scores - top) * SCALE2)
        total = jnp.sum(weights, axis=0, keepdims=True)
        o_lse[pl.ds(p, 1), :] = top * SCALE2 + jnp.log2(total)
        probs = (weights * (1.0 / total)).astype(BF)
        out = jnp.transpose(mm(vals_t[...], probs)).astype(BF)
        ms[rows, 0:128] = out[0:128]
        ms[rows, 128:256] = out[128:256]
        bx.send(p)

    each((g_g, g_u), "two")
    each(g_d, "one")
    g_o.three()
    bx.arrive()
    store(mr, o_mixed)

    def out_part(zz):
        return mm(mr[span_of(zz * 256, 256)], w_o[...].reshape(256, WIDE))

    rs = (whole, keep, give, got, ring_out, ring_in)
    total, done_rs = reduce_scatter(me, out_part, *rs, rs_s, rs_r)
    mid = total + (stream[...].astype(F32) if first else stream[...])
    middle[...] = mid
    o_middle[...] = mid
    buf2[own_rows] = (mid * rms_of(mid) * o_gains[g_mlp, :]).astype(BF)
    waited = []

    def gated(zz):
        if not waited:
            waited.append(1)
            each((g_g, g_u), "three")
        rows = span_of(zz * 256, 256)
        gate = mm(buf2[rows], w_g[...].reshape(WIDE, 512))
        gate_v[rows] = gate.astype(BF)
        up = mm(buf2[rows], w_u[...].reshape(WIDE, 512))
        up_v[rows] = up.astype(BF)
        hid[rows] = (gate / (1.0 + jnp.exp(-gate)) * up).astype(BF)

    hooks = (lambda: each(g_d, "two"), lambda: None, lambda: each(g_next, "one"))
    done_ag2 = all_gather(me, buf2, ag2_s, ag2_r, gated, hooks)
    store(buf2, o_nmlp)
    store(gate_v, o_gate)
    store(up_v, o_up)
    store(hid, o_hidden)
    each(g_next, "two")
    each(g_d, "three")
    done_rs()
    pairs = [(w_o, o_wo), (w_g, o_wg), (w_u, o_wu), (w_d, o_wd)] + ([(w_in, o_win)] if first else [])
    for w, o in pairs:
        store(w, o)

    def down_part(zz):
        return mm(hid[span_of(zz * 256, 256)], w_d[...].reshape(512, WIDE))

    total, done_rs2 = reduce_scatter(me, down_part, *rs, rs2_s, rs2_r)
    o_stream[...] = middle[...] + total
    each(g_next, "three")
    if first:
        store(w_next, o_next)
    for done in ((() if first else (done_ag,)) + (ax.finish, bx.finish, done_ag2, done_rs2)):
        done()
    each(everything, "finish")
    for copy in stores:
        copy.wait()


def norm_back_of(e, values, gain):
    q = rms_of(values)
    n = values * q
    dn = e * gain
    part = q * (dn - n * jnp.mean(dn * n, axis=-1, keepdims=True))
    return part, jnp.sum(e * n, axis=0, keepdims=True)


def bwd_kernel(l, *refs):
    last = l == 0
    g_attn, g_mlp = (slice(2 * l + i, 2 * l + i + 1) for i in (0, 1))
    refs = list(refs)
    take = lambda n: [refs.pop(0) for _ in range(n)]
    grad, stream, middle, gains, cos, sin, pcol, prow, lse = take(9)
    h_in, h_o, h_g, h_u, h_d, h_qkv, h_gate, h_up, h_normed, h_mixed, h_nmlp, h_hidden = take(12)
    above = take(4) if last else None
    o_grad, o_gains = take(2)
    o_fin, o_down, o_out = take(3) if last else (None,) * 3
    parts = take(4)
    o_din, o_dgu, o_dd, o_do = parts
    landing, landing1 = (dict(zip(MLP, take(4))) if last else {} for _ in range(2))
    w_in, w_o, w_g, w_u, w_d, buf1, buf2, qr, gate_v, up_v, gu, mgs, mgr = take(13)
    keys, vals, keys_t, dk, dv, dqs, ps, pr, mid_grad, mixed, nmlp, hid = take(12)
    d_in, d_gu, d_d, d_o = take(4)
    whole, keep, give, got, ring_out, ring_in = take(6)
    ag_s, ag_r, ag2_s, ag2_r, rs_s, rs_r, rs2_s, rs2_r, ax_s, ax_r, bx_s, bx_r, loc, loc2 = take(14)
    me = Place()
    pairs = (
        (h_d, w_d), (h_gate, gate_v), (h_up, up_v), (h_g, w_g), (h_u, w_u), (h_o, w_o), (h_qkv, qr), (h_in, w_in),
        (h_hidden, hid), (h_nmlp, nmlp), (h_mixed, mixed),
    )
    loads = [pltpu.make_async_copy(h, v, loc.at[i]) for i, (h, v) in enumerate(pairs)]
    for load in loads:
        load.start()
    stores = []

    def store(src, dst):
        stores.append(pltpu.make_async_copy(src, dst, loc2.at[len(stores)]))
        stores[-1].start()

    reds, early = {}, {}
    if last:
        stage = {
            "g": (w_g.at[3], w_g.at[0:3]), "u": (w_u.at[3], w_u.at[0:3]),
            "da": (w_d.at[3, :, :, :, 0:768], w_d.at[0:3, :, :, :, 0:768]),
            "db": (w_d.at[3, :, :, :, 768:WIDE], w_d.at[0:3, :, :, :, 768:WIDE]),
        }
        reds = make_reduces(me, above, refs, landing1, False, stage)
        specs, (es, er) = reduce_specs(*parts), refs
        early = {
            name: Reduce(me, specs[name], None, landing[name], None, None, es.at[n], er.at[n], None)
            for n, name in enumerate(MLP)
        }

    own_rows = slot_rows(me.z, me.core)
    buf1[own_rows] = grad[...].astype(BF)
    me.greet(me.layer_partners())
    for red in reds.values():
        red.one()
    for load in loads[:3]:
        load.wait()

    def unit(zz):
        rows = span_of(zz * 256, 256)
        hg = mm_nt(buf1[rows], w_d[...].reshape(512, WIDE))
        gate, up = gate_v[rows].astype(F32), up_v[rows].astype(F32)
        sig = 1.0 / (1.0 + jnp.exp(-gate))
        gu[rows, 0:512] = (hg * up * (sig * (1.0 + gate * (1.0 - sig)))).astype(BF)
        gu[rows, 512:1024] = (hg * (gate * sig)).astype(BF)

    done_ag = all_gather(me, buf1, ag_s, ag_r, unit)
    for load in loads[3:]:
        load.wait()

    def mlp_part(zz):
        rows = span_of(zz * 256, 256)
        return mm_nt(gu[rows, 0:512], w_g[...].reshape(WIDE, 512)) + mm_nt(gu[rows, 512:1024], w_u[...].reshape(WIDE, 512))

    def grad_down(b):
        cols = slice(256 * b, 256 * b + 256)
        d_d[b] = mm_tn(hid[:, cols], buf1[...]).astype(BF).reshape(4, 4, 16, WIDE)

    def grad_gu(b):
        cols = slice(384 * b, 384 * b + 384)
        pair = slice(b % 2 * 2, b % 2 * 2 + 2)
        d_gu[b // 2, pair] = mm_tn(nmlp[:, cols], gu[...]).astype(BF).reshape(2, 4, 48, 1024)

    def fill1(n):
        if n == 0:
            grad_down(0)
            grad_down(1)
        elif n == 1:
            grad_gu(0)
            grad_gu(1)
        else:
            grad_gu(2)
            grad_gu(3)

    rs = (whole, keep, give, got, ring_out, ring_in)
    e, done_rs = reduce_scatter(me, mlp_part, *rs, rs_s, rs_r, fill1)
    part, gain_part = norm_back_of(e, middle[...], gains[g_mlp, :])
    o_gains[1:2, :] = gain_part
    gm = grad[...] + part
    mid_grad[...] = gm
    buf2[own_rows] = gm.astype(BF)
    ax = Exchange(me, mgs, mgr, ax_s, ax_r)

    def mixed_back(zz):
        rows = span_of(zz * 256, 256)
        mgs[rows] = mm_nt(buf2[rows], w_o[...]).astype(BF)
        ax.send(zz * 2)
        ax.send(zz * 2 + 1)

    def hook0():
        split_packed(qr, keys, vals)
        keys_t[...] = flip(keys)
        dk[...] = jnp.zeros_like(dk)
        dv[...] = jnp.zeros_like(dv)

    def hook1():
        for red in reds.values():
            red.arrive()
            red.load()

    def hook2():
        for red in reds.values():
            red.two()

    done_ag2 = all_gather(me, buf2, ag2_s, ag2_r, mixed_back, (hook0, hook1, hook2))
    done_ag()
    normed = buf1
    load_normed = pltpu.make_async_copy(h_normed, normed, loc.at[11])
    load_normed.start()
    store(d_d, o_dd)
    store(d_gu, o_dgu)
    lanes = mm_tn(mixed[...], buf2[...])
    for head in range(2):
        chunk = [lanes[128 * head + 16 * c : 128 * head + 16 * c + 16] for c in (3, 7, 4, 0, 5, 1)]
        for b in range(8):
            first, shift = 12 * b // 16, 12 * b % 16
            piece = chunk[first][shift:]
            if shift > 4:
                piece = jnp.concatenate([piece, chunk[first + 1][: shift - 4]], axis=0)
            d_o[head * 2 + b // 4, b % 4] = padded(piece[0:12])
    store(d_o, o_do)
    if last:
        stores[0].wait()
        early["da"].one()
        early["db"].one()
    ax.arrive()

    @pl.loop(0, 8)
    def _(p):
        rows = span_of(p * 128, 128)
        q = stacked(qr, rows)
        mg = stacked(mgr, rows)
        scores = mm_nt(keys[...], q)
        allowed = pcol[...] <= prow[pl.ds(p, 1), :]
        probs = jnp.where(allowed, jnp.exp2(scores * SCALE2 - lse[pl.ds(p, 1), :]), 0.0)
        pg = mm_nt(vals[...], mg)
        inner = jnp.sum(probs * pg, axis=0, keepdims=True)
        sg = (probs * (pg - inner)).astype(BF)
        dk[...] += mm(sg, q)
        dv[...] += mm(probs.astype(BF), mg)
        dq = jnp.transpose(mm(keys_t[...], sg)) * SCALE
        dqs[rows, 0:128] = dq[0:128]
        dqs[rows, 128:256] = dq[128:256]

    bx = Exchange(me, ps, pr, bx_s, bx_r)
    v0, _, _ = lane_masks(128)

    @pl.loop(0, 8)
    def _(k):
        p = lax.rem(me.c + 1 + k, 8)
        rows = span_of(p * 128, 128)
        value = dv[rows]
        ps[rows, 0:128] = jnp.where(v0, value, dqs[rows, 0:128]).astype(BF)
        ps[rows, 128:256] = jnp.where(v0, pltpu.roll(value, 112, 1), dqs[rows, 128:256]).astype(BF)
        ps[rows, 256:384] = jnp.where(v0, pltpu.roll(value, 96, 1), dk[rows] * SCALE).astype(BF)
        bx.send(p)

    if last:
        stores[1].wait()
        early["g"].one()
        early["u"].one()
    done_rs()
    load_normed.wait()
    bx.arrive()
    pre = qr

    def in_part(zz):
        rows = span_of(zz * 256, 256)
        for t in range(3):
            cols = slice(128 * t, 128 * t + 128)
            tile = pr[rows, cols].astype(F32)
            pre[rows, cols] = (tile * cos[...] - pltpu.roll(tile, 64, 1) * sin[...]).astype(BF)
        return mm_nt(pre[rows], w_in[...])

    def fill2(n):
        for b in ((0, 1), (2,), (3,))[n]:
            cols = slice(384 * b, 384 * b + 384)
            pair = slice(b % 2 * 2, b % 2 * 2 + 2)
            d_in[b // 2, pair] = mm_tn(normed[:, cols], pre[...]).astype(BF).reshape(2, 4, 48, 384)
        if n == 1 and last:
            finish_reduces(reds, o_fin, o_down, o_out)

    e, done_rs2 = reduce_scatter(me, in_part, *rs, rs2_s, rs2_r, fill2)
    store(d_in, o_din)
    part, gain_part = norm_back_of(e, stream[...].astype(F32), gains[g_attn, :])
    o_gains[0:1, :] = gain_part
    o_grad[...] = mid_grad[...] + part
    for done in (done_ag2, ax.finish, bx.finish, done_rs2):
        done()
    for red in reds.values():
        red.finish()
    for red in early.values():
        red.arrive()
        red.finish((0,))
    for copy in stores[2 if last else 0 :]:
        copy.wait()


def padded(rows):
    return jnp.concatenate([rows, jnp.zeros((4, rows.shape[1]), F32)], axis=0).astype(BF)


def grads_kernel(*refs):
    refs = list(refs)
    take = lambda n: [refs.pop(0) for _ in range(n)]
    gains, fin1, down1, out1 = take(4)
    parts = take(4)
    landed = dict(zip(MLP, take(4)))
    o_rows, o_down, o_out, o_gains = take(4)
    reds = make_reduces(Place(), parts, refs, landed, True)
    fin_s, fin_r, down_s, down_r, out_s, out_r, sum_a, sum_b, got_a, got_b, got_c = take(11)
    fin_ss, fin_rs, gain_s, gain_r, down_ss, down_rs, out_ss = take(7)
    me = Place()
    mlp, rest = [reds[n] for n in MLP], [reds[n] for n in ("ia", "ib", "o")]
    group = [(k, c) for k in range(4) for c in range(2) if k or c]

    def mate(k, c):
        return {"z": lax.rem(me.z + k, 4), "core": lax.rem(me.core + c, 2)}

    mirror = {"x": me.z, "z": me.x}
    apart = me.x != me.z
    for red in reds.values():
        red.load()
    me.greet(
        [me.near("x", k) for k in (1, 2, 3)] + [me.near("y", k) for k in (1, 2, 3)]
        + [mate(*m) for m in group] + [{"yl": 1 - me.yl, "core": me.oc}],
        mirror=True,
    )

    def gain_copy(stage, axis, src, got, k):
        i = 3 * stage + k - 1
        return push(src, got.at[k - 1], gain_s.at[i], gain_r.at[i], me.near(axis, k))

    def gain_sum(stage, axis, src, got, dst):
        total = src[...]
        for k in (1, 2, 3):
            gain_copy(stage, axis, src, got, k).wait_recv()
            total = total + got[k - 1]
        dst[...] = total

    for k in (1, 2, 3):
        gain_copy(0, "y", gains, got_a, k).start()
    for red in rest:
        red.one()
    for red in mlp:
        red.two()
    for red in rest:
        red.arrive()
    gain_sum(0, "y", gains, got_a, sum_a)
    for k in (1, 2, 3):
        gain_copy(1, "x", sum_a, got_b, k).start()
    for red in rest:
        red.two()
    gain_sum(1, "x", sum_a, got_b, sum_b)

    def gain_mate(i):
        return push(sum_b, got_c.at[i], gain_s.at[6 + i], gain_r.at[6 + i], mate(*group[i]))

    for i in range(7):
        gain_mate(i).start()
    fin_s[:, :, 1] = fin1[...]
    down_s[:, 1] = down1[...]
    out_s[1] = out1[...]
    finish_reduces(reds, fin_s.at[:, :, 0], down_s.at[:, 0], out_s.at[0])
    slot = me.z * 2 + me.core

    def fin(i, come):
        k, c = group[i]
        to_z, to_core = lax.rem(me.z + k, 4), lax.rem(me.core + c, 2)
        from_z = lax.rem(me.z + 4 - k, 4)
        dst = fin_r.at[from_z * 2 + to_core] if come else fin_r.at[slot]
        return push(fin_s.at[to_core, to_z], dst, fin_ss.at[i], fin_rs.at[i], mate(k, c))

    def down(dp, half):
        dev = {"core": jnp.int32(dp), "yl": me.core}
        return push(down_s.at[dp], down_r.at[half], down_ss.at[dp], down_rs.at[half], dev)

    mine = me.yl == me.core

    def out_copy():
        return push(out_s, out_r, out_ss.at[0], out_ss.at[1], mirror)

    for i in range(7):
        fin(i, False).start()
    for dp in range(2):
        keep = mine & (me.core == dp)

        @pl.when(jnp.logical_not(keep))
        def _(dp=dp):
            down(dp, me.yl).start()

        @pl.when(keep)
        def _(dp=dp):
            down_r[me.yl] = down_s[dp]

    @pl.when(apart)
    def _():
        out_copy().start()

    @pl.when(jnp.logical_not(apart))
    def _():
        out_r[...] = out_s[...]

    fin_r[slot] = fin_s[me.core, me.z]
    total = sum_b[...]
    for i in range(7):
        gain_mate(i).wait_recv()
        total = total + got_c[i]
    o_gains[...] = total
    for i in range(7):
        fin(i, True).wait_recv()
    o_rows[...] = fin_r[...]
    for half in range(2):

        @pl.when(jnp.logical_not(mine & (me.yl == half)))
        def _(half=half):
            down(0, half).wait_recv()

    o_down[...] = down_r[...]

    @pl.when(apart)
    def _():
        out_copy().wait_recv()

    o_out[...] = out_r[...]
    for red in mlp:
        red.finish((1,))
    for red in rest:
        red.finish()
    for k in (1, 2, 3):
        gain_copy(0, "y", gains, got_a, k).wait_send()
        gain_copy(1, "x", sum_a, got_b, k).wait_send()
    for i in range(7):
        gain_mate(i).wait_send()
        fin(i, False).wait_send()
    for dp in range(2):

        @pl.when(jnp.logical_not(mine & (me.core == dp)))
        def _(dp=dp):
            down(dp, me.yl).wait_send()

    @pl.when(apart)
    def _():
        out_copy().wait_send()


def vm(shape, dtype=BF):
    return pltpu.VMEM(shape, dtype)


def rs_scratch():
    return [vm((4, 128, WIDE)), vm((4, 128, WIDE)), vm((6, 64, WIDE)), vm((6, 64, WIDE))]


def dma(*shape):
    return pltpu.SemaphoreType.DMA(shape)


def sems():
    return [dma(n) for n in (13, 13, 13, 13, 10, 10, 10, 10, 8, 8, 8, 8, 12, 16)]


WEIGHTS = [(WIDE, 384), (256, WIDE), (WIDE, 512), (WIDE, 512), (512, WIDE)]
SPLIT = [(2, 4, 4, 48, 384), (4, 64, WIDE), (2, 4, 4, 48, 512), (2, 4, 4, 48, 512), (2, 4, 4, 16, WIDE)]
PARTS = [(2, 4, 4, 48, 384), (2, 4, 4, 48, 1024), (2, 4, 4, 16, WIDE), (4, 4, 16, WIDE)]
RING = [(256, WIDE), (4, 128, WIDE)]


def run_kernel(kernel, name, cid, ins, in_vmem, outs, out_vmem, scratch):
    place = {True: pltpu.VMEM, False: pl.ANY}
    return pl.pallas_call(
        kernel,
        name=name,
        out_shape=[jax.ShapeDtypeStruct(s, d) for s, d in outs],
        in_specs=[pl.BlockSpec(memory_space=place[i < in_vmem]) for i in range(len(ins))],
        out_specs=[pl.BlockSpec(memory_space=place[i < out_vmem]) for i in range(len(outs))],
        scratch_shapes=scratch,
        compiler_params=pltpu.CompilerParams(
            collective_id=cid, has_side_effects=True, vmem_limit_bytes=58 * 2**20
        ),
    )(*ins)


def layer_fwd(l, stream, gains, tables, h_in, sources, extra):
    first = l == 0
    outs = [((128, WIDE), F32), ((128, WIDE), F32), ((8, 256), F32)] + ([((8, WIDE), F32)] if first else [])
    n_vmem = len(outs)
    outs += [
        ((1024, WIDE), BF), ((1024, 384), BF), ((1024, 256), BF), ((1024, WIDE), BF),
        ((1024, 512), BF), ((1024, 512), BF), ((1024, 512), BF),
    ] + [(s, BF) for s in SPLIT[1:]] + ([(SPLIT[0], BF)] * 2 if first else [])
    scratch = [vm(s) for s in SPLIT] + [
        vm((1024, WIDE)), vm((1024, WIDE)), vm((1024, 384)), vm((1024, 384)), vm((1024, 256)), vm((1024, 256)),
        vm((1024, 512)), vm((1024, 512)), vm((1024, 512)),
        vm((1024, 128)), vm((1024, 128)), vm((128, 1024)), vm((128, WIDE), F32),
    ] + [vm(s, F32) for s in RING] + rs_scratch() + sems() + [dma(10, 7), dma(10, 7)]
    if first:
        scratch += [vm((2, 4, 4, 8, 256), F32), vm(SPLIT[0])]
    ins = [stream, gains, *tables, h_in, *sources, *extra]
    kernel = functools.partial(fwd_kernel, l)
    return run_kernel(kernel, f"layer_forward_{l}", 1 + l, ins, 6, outs, n_vmem, scratch)


def layer_bwd(l, grad, stream, middle, gains, tables, lse, weights, saved, above):
    last = l == 0
    outs = [((128, WIDE), F32), ((8, WIDE), F32)]
    outs += [((2, 4, 16, 1408), BF), ((2, 16, WIDE), BF), ((16, WIDE), BF)] if last else []
    n_vmem = len(outs)
    outs += [((WIDE, 384), BF), ((WIDE, 1024), BF), ((512, WIDE), BF), ((4, 4, 16, WIDE), BF)]
    outs = outs[:n_vmem] + [(s, BF) for s in PARTS]
    outs += [((3,) + REDUCE[n][3], BF) for n in MLP] * 2 if last else []
    shapes = WEIGHTS[:2] + [(4, 2, 4, 48, 512), (4, 2, 4, 48, 512), (4, 2, 4, 16, WIDE)]
    scratch = [vm(s) for s in shapes] + [
        vm((1024, WIDE)), vm((1024, WIDE)), vm((1024, 384)), vm((1024, 512)), vm((1024, 512)),
        vm((1024, 1024)), vm((1024, 256)), vm((1024, 256)),
        vm((1024, 128)), vm((1024, 128)), vm((128, 1024)), vm((1024, 128), F32), vm((1024, 128), F32),
        vm((1024, 256), F32), vm((1024, 384)), vm((1024, 384)), vm((128, WIDE), F32),
        vm((1024, 256)), vm((1024, WIDE)), vm((1024, 512)),
    ] + [vm(s) for s in PARTS] + [vm(s, F32) for s in RING] + rs_scratch() + sems()
    if last:
        scratch += reduce_scratch(("ia", "ib", "o")) + [dma(4, 6), dma(4, 6)]
    weights = [w.reshape(s) for w, s in zip(weights, shapes)]
    ins = [grad, stream, middle, gains, *tables, lse, *weights, *saved, *(above or ())]
    kernel = functools.partial(bwd_kernel, l)
    return run_kernel(kernel, f"layer_backward_{l}", 3 + l, ins, 9, outs, n_vmem, scratch)


def reduce_grads(gains, done, parts, landed):
    outs = [((8, 2, 16, 1408), BF), ((2, 2, 16, WIDE), BF), ((2, 16, WIDE), BF), ((8, WIDE), F32)]
    scratch = reduce_scratch() + [
        vm((2, 4, 2, 16, 1408)), vm((8, 2, 16, 1408)), vm((2, 2, 16, WIDE)), vm((2, 2, 16, WIDE)),
        vm((2, 16, WIDE)), vm((2, 16, WIDE)), vm((8, WIDE), F32), vm((8, WIDE), F32),
        vm((3, 8, WIDE), F32), vm((3, 8, WIDE), F32), vm((7, 8, WIDE), F32),
        dma(7), dma(7), dma(13), dma(13), dma(2), dma(2), dma(2),
    ]
    return run_kernel(grads_kernel, "reduce_gradients", 5, [gains, *done, *parts, *landed], 4, outs, 4, scratch)


def body(
    tokens, span_order, attn_gain, w_query, key_matrix, value_matrix, w_out, mlp_gain, w_gate, w_up,
    w_down, cotangent,
):
    rows = tokens.shape[1]
    core, z, yl = lax.axis_index("core"), lax.axis_index("z"), lax.axis_index("yl")
    ctx = lax.axis_index("x") * 2 + lax.axis_index("yh")
    seq_len = 8 * rows
    span = seq_len // span_order.shape[0]
    cos, sin = rope_tables(place_rows(span_order, ctx * rows, rows, span))
    cos, sin = jnp.tile(cos, (2, 1)), jnp.tile(sin, (2, 1))
    places = place_rows(span_order, 0, seq_len, span)
    pcol = places[:, None]
    prow = jnp.tile(places.reshape(8, rows), (1, 2))

    def pick(values, index, axis):
        return lax.dynamic_index_in_dim(values, index, axis=axis, keepdims=False)

    def half(w):
        return lax.dynamic_slice_in_dim(w, yl * 48, 48, axis=1)

    def heads(w, n):
        return pick(half(w).reshape(LAYERS, 48, 2, 4, n), z, 3)

    s_in = pack_heads(heads(w_query, 192), heads(key_matrix, 96), heads(value_matrix, 96)).transpose(0, 2, 1, 3)

    def hidden(w):
        own = pick(half(w).reshape(LAYERS, 48, 16, 2, 4, 32), z, 4)
        return own.transpose(0, 3, 1, 2, 4).reshape(LAYERS, 2, 48, 512)

    s_g, s_u = hidden(w_gate), hidden(w_up)
    s_d = pick(pick(w_down.reshape(LAYERS, 2, 4, 2, 16, WIDE), z, 2), yl, 2)
    s_o = jnp.stack([spread_rows(w_out[l]) for l in range(LAYERS)])
    s_o = lax.dynamic_slice_in_dim(s_o, yl * 64, 64, axis=1)
    own_gains = jnp.concatenate([attn_gain[:1], mlp_gain[:1], attn_gain[1:], mlp_gain[1:]], axis=0).astype(F32)
    s_gain = lax.dynamic_update_slice(jnp.zeros((8, 256), F32), own_gains, (0, lax.rem(96 * (core * 8 + ctx), 128)))
    s_gain = jnp.stack([s_gain, s_gain])

    tables = (cos, sin, pcol, prow)
    stream, gains = tokens[0], jnp.zeros((8, WIDE), F32)
    kept = []
    for l in range(LAYERS):
        sources = (s_o[l], s_g[l], s_u[l], s_d[l])
        if l == 0:
            outs = layer_fwd(l, stream, gains, tables, s_in[0], sources, (s_gain, s_in[1]))
            gains, w_in, w_next = outs[3], outs[-2], outs[-1]
            outs = outs[:3] + outs[4:-2]
        else:
            w_in = w_next
            outs = layer_fwd(l, stream, gains, tables, w_in, sources, ())
        kept.append((stream, w_in, outs))
        stream = outs[0]
    block_out = stream.astype(BF)[None]

    g = cotangent[0].astype(F32)
    gain_parts, above = [None] * LAYERS, None
    for l in reversed(range(LAYERS)):
        stream, w_in, outs = kept[l]
        _, middle, lse, normed, qkv, mixed, nmlp, gate, up, hid = outs[:10]
        saved = (qkv, gate, up, normed, mixed, nmlp, hid)
        res = layer_bwd(l, g, stream, middle, gains, tables, lse, (w_in, *outs[10:]), saved, above)
        g, gain_parts[l] = res[:2]
        above = tuple(res[2:6])
    gp = jnp.concatenate([gain_parts[0][:2], gain_parts[1][:2], jnp.zeros((4, WIDE), F32)], axis=0)
    cols, d_d, d_o, gp = reduce_grads(gp, res[2:5], res[5:9], res[9:13])
    cols = cols.reshape(4, 2, LAYERS, 16, 1408)[:, :, :, :12].transpose(2, 3, 1, 0, 4).reshape(LAYERS, 12, 8, 1408)
    cols = cols.astype(F32)
    d_q, d_k, d_v = unpack_grads(cols[..., :384])

    def hidden_join(d):
        return d.reshape(LAYERS, 12, 8, 16, 32).transpose(0, 1, 3, 2, 4).reshape(LAYERS, 12, 4096)

    d_g, d_u = hidden_join(cols[..., 384:896]), hidden_join(cols[..., 896:])
    d_d = d_d.transpose(1, 0, 2, 3).reshape(LAYERS, 32, WIDE).astype(F32)
    d_o = d_o[:, :12].astype(F32)
    owner = (core * 8 + ctx) * 8 + yl * 4 + z
    gp = lax.dynamic_slice(gp, (0, owner * 12), (4, 12)).reshape(2, 2, 12)
    return (block_out, g[None], gp[:, 0], d_q, d_k, d_v, d_o, gp[:, 1], d_g, d_u, d_d)


def solution(mesh):
    fine = Mesh(mesh.devices.reshape(2, 4, 2, 2, 4), ALL)
    seq, ctx, own, every = ("core", "yl", "z"), CTX, OWN, ALL
    act = P(seq, ctx, None)
    in_specs = (act, P(), P(None, own)) + (P(None, own, None),) * 4 + (P(None, own),) + (P(None, own, None),) * 3 + (act,)
    grad = P(None, every, None)
    out_specs = (act, act, P(None, every)) + (grad,) * 4 + (P(None, every),) + (grad,) * 3
    return jax.shard_map(body, mesh=fine, in_specs=in_specs, out_specs=out_specs, check_vma=False)
```

```python
import functools
import math

import jax
import jax.numpy as jnp
import numpy as np
from jax import lax
from jax.experimental import pallas as pl
from jax.experimental.pallas import tpu as pltpu
from jax.sharding import Mesh, PartitionSpec as P

HEAD = 96
LAYERS = 2
ROPE_BASE = 100000.0
EPS = 1e-05
CTX = ("x", "yh")
TP = ("z", "core")
OWN = ("core", "x", "yh")
ALL = ("core", "x", "yh", "yl", "z")
BF = jnp.bfloat16
F32 = jnp.float32
MESH = pl.DeviceIdType.MESH
SCALE = 1.0 / math.sqrt(HEAD)
SCALE2 = SCALE * math.log2(math.e)
WIDE = 1536


def mm(a, b):
    return jnp.dot(a, b, preferred_element_type=F32)


def mm_tn(a, b):
    return lax.dot_general(a, b, (((0,), (0,)), ((), ())), preferred_element_type=F32)


def mm_nt(a, b):
    return lax.dot_general(a, b, (((1,), (1,)), ((), ())), preferred_element_type=F32)


class Place:
    def __init__(self):
        self.z, self.core = lax.axis_index("z"), lax.axis_index("core")
        self.x, self.yh, self.yl = lax.axis_index("x"), lax.axis_index("yh"), lax.axis_index("yl")
        self.y = self.yh * 2 + self.yl
        self.c = self.x * 2 + self.yh
        self.zp, self.zm, self.zo = (lax.rem(self.z + k, 4) for k in (1, 3, 2))
        self.oc = 1 - self.core

    def near(self, axis, k):
        if axis == "x":
            return {"x": lax.rem(self.x + k, 4)}
        return at_y(lax.rem(self.y + k, 4))

    def greet(self, others, mirror=False):
        barrier = pltpu.get_barrier_semaphore()
        for dev in others:
            pl.semaphore_signal(barrier, inc=1, device_id=dev, device_id_type=MESH)
        if not mirror:
            pl.semaphore_wait(barrier, len(others))
            return

        @pl.when(self.x != self.z)
        def _():
            there = {"x": self.z, "z": self.x}
            pl.semaphore_signal(barrier, inc=1, device_id=there, device_id_type=MESH)
            pl.semaphore_wait(barrier, len(others) + 1)

        @pl.when(self.x == self.z)
        def _():
            pl.semaphore_wait(barrier, len(others))

    def layer_partners(self):
        return (
            [{"z": self.zp}, {"z": self.zm}, {"core": self.oc}]
            + [at_ctx(lax.rem(self.c + k, 8)) for k in range(1, 8)]
            + [{"yl": 1 - self.yl}, {"yh": 1 - self.yh, "yl": 1 - self.yl}]
        )


def at_y(y):
    return {"yh": y // 2, "yl": lax.rem(y, 2)}


def at_ctx(c):
    return {"x": c // 2, "yh": lax.rem(c, 2)}


def span_of(start, size):
    return pl.ds(pl.multiple_of(start, 64), size)


def slot_rows(zz, cc, half=None):
    base = (zz * 2 + cc) * 128
    return span_of(base, 128) if half is None else span_of(base + 64 * half, 64)


def all_gather(*args):
    return run(gather_steps(*args))


def run(steps):
    while True:
        try:
            next(steps)
        except StopIteration as stop:
            return stop.value


def gather_steps(me, buf, ssem, rsem, on_pair, hooks=()):
    z, zp, zm, zo, core, oc = me.z, me.zp, me.zm, me.zo, me.core, me.oc
    up, down, across = {"z": zp}, {"z": zm}, {"core": oc}
    sent = [
        (z, core, 0, up), (z, core, 1, up), (z, core, 1, down), (z, core, 0, down),
        (zm, core, 0, up), (zp, core, 1, down), (z, core, None, across),
        (zm, core, 0, across), (zm, core, 1, across), (zp, core, 1, across), (zp, core, 0, across),
        (zo, core, 0, across), (zo, core, 1, across),
    ]
    come = [
        (zm, core, 0), (zm, core, 1), (zp, core, 1), (zp, core, 0), (zo, core, 0), (zo, core, 1),
        (z, oc, None), (zm, oc, 0), (zm, oc, 1), (zp, oc, 1), (zp, oc, 0), (zo, oc, 0), (zo, oc, 1),
    ]

    def copy(i, rows, dev):
        return pltpu.make_async_remote_copy(
            src_ref=buf.at[rows], dst_ref=buf.at[rows], send_sem=ssem.at[i], recv_sem=rsem.at[i],
            device_id=dev, device_id_type=MESH,
        )

    def send(*which):
        for i in which:
            copy(i, slot_rows(*sent[i][:3]), sent[i][3]).start()

    def arrive(*which):
        for i in which:
            copy(i, slot_rows(*come[i]), sent[i][3]).wait_recv()

    def hook(i):
        if i < len(hooks):
            hooks[i]()

    send(0, 2, 1, 3, 6)
    hook(0)
    yield
    arrive(6)
    on_pair(z)
    arrive(0)
    send(4, 7)
    arrive(2)
    send(5, 9)
    hook(1)
    arrive(1)
    send(8)
    arrive(3)
    send(10)
    hook(2)
    yield
    arrive(7, 8)
    on_pair(zm)
    arrive(9, 10)
    on_pair(zp)
    hook(3)
    arrive(4)
    send(11)
    arrive(5)
    send(12)
    yield
    arrive(11, 12)
    on_pair(zo)

    def finish():
        for i in range(13):
            copy(i, slot_rows(*sent[i][:3]), sent[i][3]).wait_send()

    return finish


def reduce_scatter(*args):
    return run(reduce_steps(*args))


def reduce_steps(me, part, whole, keep, give, take, ring_out, ring_in, ssem, rsem, fill=lambda n: None):
    z, zp, zm, zo, core, oc = me.z, me.zp, me.zm, me.zo, me.core, me.oc
    up, down, across = {"z": zp}, {"z": zm}, {"core": oc}
    mine = span_of(core * 128, 128)
    theirs = span_of(oc * 128, 128)

    def swap(k):
        return pltpu.make_async_remote_copy(
            src_ref=give.at[k], dst_ref=take.at[k], send_sem=ssem.at[k], recv_sem=rsem.at[k],
            device_id=across, device_id_type=MESH,
        )

    def ring(i):
        return pltpu.make_async_remote_copy(
            src_ref=ring_out.at[i], dst_ref=ring_in.at[i], send_sem=ssem.at[4 + i], recv_sem=rsem.at[4 + i],
            device_id=up if i < 3 else down, device_id_type=MESH,
        )

    def make(k, zz):
        whole[...] = part(zz)
        give[k] = whole[theirs].astype(BF)
        keep[k] = whole[mine]
        swap(k).start()

    def merged(k, half):
        rows = slice(64 * half, 64 * half + 64)
        return keep[k, rows] + take[k, rows].astype(F32)

    def push(i, value):
        ring_out[i] = value.astype(BF)
        ring(i).start()

    make(0, zo)
    make(1, zp)
    swap(0).wait_recv()
    push(0, merged(0, 0))
    push(3, merged(0, 1))
    make(2, zm)
    swap(1).wait_recv()
    push(1, merged(1, 1))
    swap(2).wait_recv()
    push(4, merged(2, 0))
    make(3, z)
    fill(0)
    yield
    ring(0).wait_recv()
    push(2, merged(1, 0) + ring_in[0].astype(F32))
    ring(3).wait_recv()
    push(5, merged(2, 1) + ring_in[3].astype(F32))
    swap(3).wait_recv()
    fill(1)
    own = [merged(3, 0), merged(3, 1)]
    ring(1).wait_recv()
    own[1] = own[1] + ring_in[1].astype(F32)
    ring(4).wait_recv()
    own[0] = own[0] + ring_in[4].astype(F32)
    fill(2)
    yield
    ring(2).wait_recv()
    own[0] = own[0] + ring_in[2].astype(F32)
    ring(5).wait_recv()
    own[1] = own[1] + ring_in[5].astype(F32)

    def finish():
        for k in range(4):
            swap(k).wait_send()
        for i in range(6):
            ring(i).wait_send()

    return jnp.concatenate(own, axis=0), finish


def ctx_of(slot):
    zz, cc = slot // 2, lax.rem(slot, 2)
    return lax.rem(zz + 2 * cc, 4) * 2 + cc


def slot_of(ctx):
    x, yh = ctx // 2, lax.rem(ctx, 2)
    return lax.rem(x + 2 * yh, 4) * 2 + yh


class Exchange:
    def __init__(self, me, src, dst, ssem, rsem, out):
        self.me, self.src, self.dst, self.ssem, self.rsem = me, src, dst, ssem, rsem
        same = lambda v: v
        self.to, self.block, self.lands = (ctx_of, slot_of, same) if out else (same, same, slot_of)

    def copy(self, b, come):
        return pltpu.make_async_remote_copy(
            src_ref=self.src.at[span_of(b * 128, 128)], dst_ref=self.dst.at[span_of(come * 128, 128)],
            send_sem=self.ssem.at[b], recv_sem=self.rsem.at[come],
            device_id=at_ctx(self.to(b)), device_id_type=MESH,
        )

    def send(self, b):
        there, come = self.to(b), self.lands(self.me.c)

        @pl.when(there != self.me.c)
        def _():
            self.copy(b, come).start()

        @pl.when(there == self.me.c)
        def _():
            self.dst[span_of(come * 128, 128)] = self.src[span_of(b * 128, 128)]

    def arrive(self):
        @pl.loop(1, 8)
        def _(k):
            there = lax.rem(self.me.c + k, 8)
            self.copy(self.block(there), self.lands(there)).wait_recv()

    def finish(self):
        @pl.loop(1, 8)
        def _(k):
            there = lax.rem(self.me.c + k, 8)
            self.copy(self.block(there), self.lands(self.me.c)).wait_send()


def push(src, dst, ssem, rsem, dev):
    return pltpu.make_async_remote_copy(
        src_ref=src, dst_ref=dst, send_sem=ssem, recv_sem=rsem, device_id=dev, device_id_type=MESH
    )


class Gather:
    def __init__(self, me, src, dst, ssem, rsem, loc, order, cols):
        self.me, self.src, self.dst, self.ssem, self.rsem, self.order = me, src, dst, ssem, rsem, order
        self.loc, self.cols = loc, slice(*cols)

    def own(self):
        me = self.me
        return pltpu.make_async_copy(
            self.src(me.core, self.cols), self.dst.at[me.core, me.x, me.y, :, self.cols], self.loc
        )

    def cross(self, come=False):
        me = self.me
        row = me.oc if come else me.core
        return push(
            self.src(me.oc, self.cols), self.dst.at[row, me.x, me.y, :, self.cols],
            self.ssem.at[0], self.rsem.at[0], {"core": me.oc},
        )

    def region(self, stage, k):
        me = self.me
        x, y = (lax.rem(v + 4 - k, 4) for v in (me.x, me.y))
        if stage == 0:
            return self.dst.at[:, x if self.order[0] == "x" else me.x, y if self.order[0] == "y" else me.y, :, self.cols]
        if self.order[1] == "y":
            return self.dst.at[:, :, y, :, self.cols]
        return self.dst.at[:, x, :, :, self.cols]

    def copy(self, stage, k, come):
        ref = self.region(stage, k if come else 0)
        i = 1 + 3 * stage + k - 1
        return push(ref, ref, self.ssem.at[i], self.rsem.at[i], self.me.near(self.order[stage], k))

    def zero(self):
        self.own().start()
        self.cross().start()

    def one(self):
        self.own().wait()
        self.cross(True).wait_recv()
        for k in (2, 1, 3):
            self.copy(0, k, False).start()

    def two(self):
        for k in (1, 3, 2):
            self.copy(0, k, True).wait_recv()
        for k in (2, 1, 3):
            self.copy(1, k, False).start()

    def three(self):
        for k in (1, 3, 2):
            self.copy(1, k, True).wait_recv()

    def finish(self):
        self.cross().wait_send()
        for stage in (0, 1):
            for k in (1, 2, 3):
                self.copy(stage, k, False).wait_send()


class OutGather:
    def __init__(self, me, src, dst, ssem, rsem, loc):
        self.me, self.dst, self.ssem, self.rsem = me, dst, ssem, rsem
        self.src, self.loc = src, loc
        self.far = lax.rem(me.x + 4 - me.z, 4)

    def copy(self, stage, k, come):
        me = self.me
        y = lax.rem(me.y + 4 - k, 4) if stage and come else me.y
        ref, i = self.dst.at[y], 3 * stage + k - 1
        return push(ref, ref, self.ssem.at[i], self.rsem.at[i], me.near("xy"[stage], k))

    def own(self):
        y, yl = self.me.y, self.me.yl
        return [
            pltpu.make_async_copy(
                self.src.at[pl.ds(pl.multiple_of(row, 16), 16)], self.dst.at[y, to : to + 16], self.loc.at[i]
            )
            for i, (row, to) in enumerate(((48 - 16 * yl, 0), (80 - 16 * yl, 16), (16 * yl, 48)))
        ]

    def zero(self):
        @pl.when(self.far == 0)
        def _():
            for copy in self.own():
                copy.start()
            self.dst[self.me.y, 32:48] = jnp.zeros((16, WIDE), BF)

    def one(self):
        @pl.when(self.far == 0)
        def _():
            for copy in self.own():
                copy.wait()
            for k in (2, 1, 3):
                self.copy(0, k, False).start()

    def two(self):
        for k in (1, 2, 3):

            @pl.when(self.far == k)
            def _(k=k):
                self.copy(0, k, True).wait_recv()

        for k in (2, 1, 3):
            self.copy(1, k, False).start()

    def three(self):
        for k in (1, 3, 2):
            self.copy(1, k, True).wait_recv()

    def finish(self):
        @pl.when(self.far == 0)
        def _():
            for k in (1, 2, 3):
                self.copy(0, k, False).wait_send()

        for k in (1, 2, 3):
            self.copy(1, k, False).wait_send()


class Reduce:
    def __init__(self, me, spec, mine, got1, sum1, got2, ssem, rsem, loc, land=None, landed=False):
        self.me = me
        self.quarter, self.inner, self.order = spec[:3]
        self.mine, self.got1, self.sum1, self.got2, self.ssem, self.rsem, self.loc = mine, got1, sum1, got2, ssem, rsem, loc
        self.land, self.landed = land, landed

    def at(self, axis, k):
        return lax.rem((self.me.x if axis == "x" else self.me.y) + k, 4)

    def copy(self, stage, k):
        axis = self.order[stage]
        to = self.at(axis, k)
        src = self.inner(self.sum1, to) if stage else self.quarter(axis, to)
        dst = (self.got2 if stage else self.got1 if self.land is None else self.land).at[k - 1]
        i = 3 * stage + k - 1
        return push(src, dst, self.ssem.at[i], self.rsem.at[i], self.me.near(axis, k))

    def loads(self):
        axis = self.order[0]
        out = [pltpu.make_async_copy(self.quarter(axis, self.at(axis, 0)), self.mine, self.loc.at[0])]
        if self.land is not None:
            out.append(pltpu.make_async_copy(self.land, self.got1, self.loc.at[1]))
        return out

    def load(self):
        for load in self.loads():
            load.start()

    def one(self):
        for k in (2, 1, 3):
            self.copy(0, k).start()

    def arrive(self):
        if not self.landed:
            for k in (1, 2, 3):
                self.copy(0, k).wait_recv()

    def two(self):
        for load in self.loads():
            load.wait()
        dims = self.sum1.shape[:-2]

        @pl.loop(0, math.prod(dims))
        def _(n):
            at = (n,) if len(dims) == 1 else (n // dims[1], lax.rem(n, dims[1]))
            total = self.mine[at].astype(F32)
            for k in range(3):
                total = total + self.got1[(k, *at)].astype(F32)
            self.sum1[at] = total.astype(BF)

        for k in (2, 1, 3):
            self.copy(1, k).start()

    def three(self):
        for k in (1, 2, 3):
            self.copy(1, k).wait_recv()
        total = self.inner(self.sum1, self.at(self.order[1], 0))[...].astype(F32)
        for k in range(3):
            total = total + self.got2[k].astype(F32)
        return total

    def finish(self, stages=(0, 1)):
        for stage in stages:
            for k in (1, 2, 3):
                self.copy(stage, k).wait_send()


def reduce_specs(d_in, d_gu, d_d, d_o):
    def split(ref, lo, hi, r, order):
        def quarter(axis, i):
            return ref.at[:, i, :, :, lo:hi] if axis == "x" else ref.at[:, :, i, :, lo:hi]

        return quarter, lambda q, i: q.at[:, i], order, (2, 4, r, hi - lo), (2, r, hi - lo)

    return {
        "g": split(d_gu, 0, 512, 48, "yx"),
        "u": split(d_gu, 512, 1024, 48, "xy"),
        "da": split(d_d, 0, 768, 16, "yx"),
        "db": split(d_d, 768, 1536, 16, "xy"),
        "ia": split(d_in, 0, 256, 48, "yx"),
        "ib": split(d_in, 256, 384, 48, "xy"),
        "o": (lambda axis, i: d_o.at[:, i], lambda q, i: q.at[i], "xy", (4, 16, WIDE), (16, WIDE)),
    }


REDUCE = reduce_specs(None, None, None, None)
MLP = ("g", "u", "da", "db")


def reduce_scratch(staged=REDUCE):
    out = []
    for name, (_, _, _, big, small) in REDUCE.items():
        out += [vm(big), vm((3,) + big)] if name in staged else []
        out += [vm(big), vm((3,) + small)]
    return out + [dma(7, 6), dma(7, 6), dma(7, 2)]


def make_reduces(me, parts, refs, land=None, landed=False, stage=None):
    out, n = {}, 0
    for name, spec in reduce_specs(*parts).items():
        own, got = stage[name] if stage and name in stage else (refs.pop(0), refs.pop(0))
        sum1, got2 = refs.pop(0), refs.pop(0)
        out[name] = (spec, own, got, sum1, got2)
    ssem, rsem, loc = refs.pop(0), refs.pop(0), refs.pop(0)
    for n, (name, (spec, own, got, sum1, got2)) in enumerate(out.items()):
        there = land.get(name) if land else None
        out[name] = Reduce(
            me, spec, own, got, sum1, got2, ssem.at[n], rsem.at[n], loc.at[n], there, landed and there is not None
        )
    return out


def finish_reduces(reds, fin, down, out):
    for lo, hi, name in ((0, 256, "ia"), (256, 384, "ib"), (384, 896, "g"), (896, 1408, "u")):
        total = reds[name].three()
        for dp in range(2):
            for z in range(4):
                fin[dp, z, :, lo:hi] = padded(total[dp, 12 * z : 12 * z + 12])
    down[:, :, 0:768] = reds["da"].three().astype(BF)
    down[:, :, 768:1536] = reds["db"].three().astype(BF)
    out[...] = reds["o"].three().astype(BF)


def lane_masks(rows):
    lane = lax.broadcasted_iota(jnp.int32, (rows, 128), 1)
    v0 = ((lane >= 48) & (lane < 64)) | (lane >= 112)
    v1 = ((lane >= 64) & (lane < 80)) | (lane < 16)
    v2 = ((lane >= 80) & (lane < 96)) | ((lane >= 16) & (lane < 32))
    return v0, v1, v2


def split_packed(packed, key_ref, value_ref):
    v0, v1, v2 = lane_masks(128)

    @pl.loop(0, 8)
    def _(p):
        rows = span_of(p * 128, 128)
        t0, t1, t2 = (packed[rows, 128 * t : 128 * t + 128].astype(F32) for t in range(3))
        key_ref[rows] = jnp.where(v0, 0.0, t2).astype(BF)
        value = jnp.where(v0, t0, 0.0)
        value = value + jnp.where(v1, pltpu.roll(t1, 16, 1), 0.0)
        value = value + jnp.where(v2, pltpu.roll(t2, 32, 1), 0.0)
        value_ref[rows] = value.astype(BF)


def flip(ref):
    return jnp.transpose(ref[...].astype(F32)).astype(BF)


def stacked(ref, rows):
    return jnp.concatenate([ref[rows, 0:128], ref[rows, 128:256]], axis=0)


def rms_of(values):
    return lax.rsqrt(jnp.mean(values * values, axis=-1, keepdims=True) + EPS)


def fwd_kernel(l, *refs):
    first = l == 0
    g_attn, g_mlp = (slice(2 * l + i, 2 * l + i + 1) for i in (0, 1))
    refs = list(refs)
    take = lambda n: [refs.pop(0) for _ in range(n)]
    (stream,) = take(1)
    (gains_in,) = (None,) if first else take(1)
    cos, sin, pcol, prow = take(4)
    (h_in,) = take(1)
    w_out, w_down, s_g, s_u = take(4)
    s_gain, s_next = take(2) if first else (None, None)
    (cot,) = (None,) if first else take(1)
    (o_stream,) = take(1) if first else (None,)
    o_middle, o_lse = take(2)
    (o_gains,) = take(1) if first else (gains_in,)
    o_normed, o_qkv, o_mixed, o_nmlp, o_gate, o_up, o_hidden, o_wo, o_wg, o_wu, o_wd = take(11)
    o_win, o_next = take(2) if first else (None, None)
    (o_down,) = (None,) if first else take(1)
    w_in, w_o, w_g, w_u, w_d = take(5)
    buf1, buf2, qs, qr, ms, mr, gate_v, up_v, hid, keys, vals, vals_t, middle = take(13)
    whole, keep, give, got, ring_out, ring_in = take(6)
    ag_s, ag_r, ag2_s, ag2_r, rs_s, rs_r, rs2_s, rs2_r, ax_s, ax_r, bx_s, bx_r, loc, loc2, ga_s, ga_r = take(16)
    w_gain, w_next = take(2) if first else (None, None)
    cot_all, cot_s, cot_r = (None,) * 3 if first else take(3)
    me = Place()
    stores = []

    def store(src, dst):
        stores.append(pltpu.make_async_copy(src, dst, loc2.at[len(stores)]))
        stores[-1].start()

    n_item = [0]

    def down_rows(core, cols):
        row = pl.multiple_of((core * 4 + me.z) * 32 + me.yl * 16, 16)
        return w_down.at[l, pl.ds(row, 16), cols]

    def item(src, dst, order, *cols):
        i = n_item[0]
        n_item[0] += 1
        if not callable(src):
            src = lambda core, cols, ref=src: ref.at[core, :, cols]
        return Gather(me, src, dst, ga_s.at[i], ga_r.at[i], loc.at[i], order, cols)

    g_g, g_u = item(s_g.at[l], w_g, "xy", 0, 512), item(s_u.at[l], w_u, "yx", 0, 512)
    g_d = [item(down_rows, w_d, "xy", 0, 768), item(down_rows, w_d, "yx", 768, WIDE)]
    g_o = OutGather(me, w_out.at[l], w_o, ga_s.at[4], ga_r.at[4], loc.at[pl.ds(10, 3)])
    n_item[0] = 5
    g_in, g_next, g_gain = [], [], []
    if first:
        g_gain = [item(s_gain, w_gain, "yx", 0, 256)]
        g_in = [item(h_in.at[0], w_in, "yx", 0, 256), item(h_in.at[0], w_in, "xy", 256, 384)]
        g_next = [item(s_next.at[1], w_next, "yx", 0, 256), item(s_next.at[1], w_next, "xy", 256, 384)]
    everything = g_gain + g_in + [g_o, g_g, g_u] + g_d + g_next

    def each(items, step):
        for one in items:
            getattr(one, step)()

    own_rows = slot_rows(me.z, me.core)
    raw = buf2 if first else buf1
    if first:
        raw[own_rows] = stream[...]
    else:
        load_in = pltpu.make_async_copy(h_in, w_in, loc.at[5])
        load_in.start()
        load_cot = pltpu.make_async_copy(cot, cot_all.at[own_rows], loc.at[6])
        load_cot.start()
        s = stream[...]
        raw[own_rows] = (s * rms_of(s) * gains_in[g_attn, :]).astype(BF)
    me.greet(me.layer_partners())
    each(everything, "zero")
    ax = Exchange(me, qs, qr, ax_s, ax_r, True)

    def project(zz):
        rows = span_of(zz * 256, 256)
        y = mm(buf1[rows], w_in[...].reshape(WIDE, 384))
        for t in range(3):
            tile = y[:, 128 * t : 128 * t + 128]
            tile = tile * cos[...] + pltpu.roll(tile, 64, 1) * sin[...]
            qs[rows, 128 * t : 128 * t + 128] = tile.astype(BF)
        ax.send(zz * 2)
        ax.send(zz * 2 + 1)

    def normalise(zz):
        rows = span_of(zz * 256, 256)
        s = raw[rows].astype(F32)
        buf1[rows] = (s * rms_of(s) * o_gains[g_attn, :]).astype(BF)

    if first:

        def own_pair():
            each(g_gain + g_in, "two")

        def gains_here():
            each(g_gain, "three")
            o_gains[...] = jnp.zeros_like(o_gains)
            for owner in range(16):
                base = 96 * owner // 128 * 128
                width = min(256, WIDE - base)
                row = w_gain[owner // 8, owner % 8 // 2, owner % 2 * 2]
                o_gains[:, base : base + width] += row[:, :width]
            normalise(me.z)
            g_o.one()

        hooks = (lambda: each(g_gain + g_in, "one"), own_pair, gains_here)

        def others(zz):
            if zz is not me.z:
                normalise(zz)

        done_ag = all_gather(me, raw, ag_s, ag_r, others, hooks)
        done_ag()
        each(g_in, "three")

        @pl.loop(0, 4)
        def _(k):
            project(lax.rem(me.z + k, 4))

    else:
        load_in.wait()
        done_ag = all_gather(me, raw, ag_s, ag_r, project, (g_o.one,))
        load_cot.wait()
        ring = gather_steps(me, cot_all, cot_s, cot_r, lambda zz: None)
        next(ring)
    g_o.two()
    each((g_g, g_u), "one")
    ax.arrive()
    if not first:
        next(ring)
    store(buf1, o_normed)
    store(qr, o_qkv)
    split_packed(qr, keys, vals)
    vals_t[...] = flip(vals)
    bx = Exchange(me, ms, mr, bx_s, bx_r, False)

    @pl.loop(0, 8)
    def _(k):
        p = lax.rem(me.c + 1 + k, 8)
        rows = span_of(p * 128, 128)
        q = stacked(qr, rows)
        scores = mm_nt(keys[...], q)
        scores = jnp.where(pcol[...] <= prow[pl.ds(p, 1), :], scores, -1e30)
        top = jnp.max(scores, axis=0, keepdims=True)
        weights = jnp.exp2((scores - top) * SCALE2)
        total = jnp.sum(weights, axis=0, keepdims=True)
        o_lse[pl.ds(p, 1), :] = top * SCALE2 + jnp.log2(total)
        probs = (weights * (1.0 / total)).astype(BF)
        out = jnp.transpose(mm(vals_t[...], probs)).astype(BF)
        ms[rows, 0:128] = out[0:128]
        ms[rows, 128:256] = out[128:256]
        bx.send(p)

    each((g_g, g_u), "two")
    if not first:
        next(ring)
    each(g_d, "one")
    g_o.three()
    bx.arrive()
    store(mr, o_mixed)

    def out_part(zz):
        return mm(mr[span_of(zz * 256, 256)], w_o[...].reshape(256, WIDE))

    rs = (whole, keep, give, got, ring_out, ring_in)
    total, done_rs = reduce_scatter(me, out_part, *rs, rs_s, rs_r)
    mid = total + (stream[...].astype(F32) if first else stream[...])
    middle[...] = mid
    o_middle[...] = mid
    buf2[own_rows] = (mid * rms_of(mid) * o_gains[g_mlp, :]).astype(BF)
    waited = []

    def gated(zz):
        if not waited:
            waited.append(1)
            each((g_g, g_u), "three")
        rows = span_of(zz * 256, 256)
        gate = mm(buf2[rows], w_g[...].reshape(WIDE, 512))
        gate_v[rows] = gate.astype(BF)
        up = mm(buf2[rows], w_u[...].reshape(WIDE, 512))
        up_v[rows] = up.astype(BF)
        hid[rows] = (gate / (1.0 + jnp.exp(-gate)) * up).astype(BF)

    hooks = (lambda: each(g_d, "two"), lambda: None, lambda: each(g_next, "one"))
    done_ag2 = all_gather(me, buf2, ag2_s, ag2_r, gated, hooks)
    store(buf2, o_nmlp)
    store(gate_v, o_gate)
    store(up_v, o_up)
    store(hid, o_hidden)
    each(g_next, "two")
    each(g_d, "three")
    done_rs()
    pairs = [(w_o, o_wo), (w_g, o_wg), (w_u, o_wu), (w_d, o_wd)] + ([(w_in, o_win)] if first else [])
    for w, o in pairs:
        store(w, o)

    if not first:
        done_cot = run(ring)
        store(cot_all, o_down)
        for done in (done_ag, ax.finish, bx.finish, done_ag2, done_cot):
            done()
        each(everything, "finish")
        for copy in stores:
            copy.wait()
        return

    def down_part(zz):
        return mm(hid[span_of(zz * 256, 256)], w_d[...].reshape(512, WIDE))

    total, done_rs2 = reduce_scatter(me, down_part, *rs, rs2_s, rs2_r)
    o_stream[...] = middle[...] + total
    each(g_next, "three")
    store(w_next, o_next)
    for done in (ax.finish, bx.finish, done_ag2, done_rs2):
        done()
    each(everything, "finish")
    for copy in stores:
        copy.wait()


def norm_back_of(e, values, gain):
    q = rms_of(values)
    n = values * q
    dn = e * gain
    part = q * (dn - n * jnp.mean(dn * n, axis=-1, keepdims=True))
    return part, jnp.sum(e * n, axis=0, keepdims=True)


def bwd_kernel(l, *refs):
    last = l == 0
    g_attn, g_mlp = (slice(2 * l + i, 2 * l + i + 1) for i in (0, 1))
    refs = list(refs)
    take = lambda n: [refs.pop(0) for _ in range(n)]
    grad, stream, middle, gains, cos, sin, pcol, prow, lse = take(9)
    h_in, h_o, h_g, h_u, h_d, h_qkv, h_gate, h_up, h_normed, h_mixed, h_nmlp, h_hidden = take(12)
    above = take(4) if last else None
    (h_down,) = (None,) if last else take(1)
    o_grad, o_gains = take(2)
    (o_block,) = (None,) if last else take(1)
    o_fin, o_down, o_out = take(3) if last else (None,) * 3
    parts = take(4)
    o_din, o_dgu, o_dd, o_do = parts
    landing, landing1 = (dict(zip(MLP, take(4))) if last else {} for _ in range(2))
    w_in, w_o, w_g, w_u, w_d, buf1, buf2, qr, gate_v, up_v, gu, mgs, mgr = take(13)
    keys, vals, keys_t, dk, dv, dqs, ps, pr, mid_grad, mixed, nmlp, hid = take(12)
    d_in, d_gu, d_d, d_o = take(4)
    whole, keep, give, got, ring_out, ring_in = take(6)
    ag_s, ag_r, ag2_s, ag2_r, rs_s, rs_r, rs2_s, rs2_r, ax_s, ax_r, bx_s, bx_r, loc, loc2 = take(14)
    me = Place()
    pairs = (
        (h_d, w_d), (h_gate, gate_v), (h_up, up_v), (h_g, w_g), (h_u, w_u), (h_o, w_o), (h_qkv, qr), (h_in, w_in),
        (h_hidden, hid), (h_nmlp, nmlp), (h_mixed, mixed),
    )
    loads = [pltpu.make_async_copy(h, v, loc.at[i]) for i, (h, v) in enumerate(pairs)]
    for load in loads:
        load.start()
    stores = []

    def store(src, dst):
        stores.append(pltpu.make_async_copy(src, dst, loc2.at[len(stores)]))
        stores[-1].start()

    reds, early = {}, {}
    rs3 = refs
    if last:
        stage = {
            "g": (w_g.at[3], w_g.at[0:3]), "u": (w_u.at[3], w_u.at[0:3]),
            "da": (w_d.at[3, :, :, :, 0:768], w_d.at[0:3, :, :, :, 0:768]),
            "db": (w_d.at[3, :, :, :, 768:WIDE], w_d.at[0:3, :, :, :, 768:WIDE]),
        }
        reds = make_reduces(me, above, refs, landing1, False, stage)
        specs, (es, er) = reduce_specs(*parts), refs
        early = {
            name: Reduce(me, specs[name], None, landing[name], None, None, es.at[n], er.at[n], None)
            for n, name in enumerate(MLP)
        }

    own_rows = slot_rows(me.z, me.core)
    if last:
        buf1[own_rows] = grad[...].astype(BF)
    else:
        load_down = pltpu.make_async_copy(h_down, buf1, loc.at[11])
        load_down.start()
    me.greet(me.layer_partners())
    for red in reds.values():
        red.one()
    for load in loads[:3]:
        load.wait()

    def unit(zz):
        rows = span_of(zz * 256, 256)
        hg = mm_nt(buf1[rows], w_d[...].reshape(512, WIDE))
        gate, up = gate_v[rows].astype(F32), up_v[rows].astype(F32)
        sig = 1.0 / (1.0 + jnp.exp(-gate))
        gu[rows, 0:512] = (hg * up * (sig * (1.0 + gate * (1.0 - sig)))).astype(BF)
        gu[rows, 512:1024] = (hg * (gate * sig)).astype(BF)

    if last:
        done_ag = all_gather(me, buf1, ag_s, ag_r, unit)
    else:
        load_down.wait()
        for zz in range(4):
            unit(zz)
    for load in loads[3:]:
        load.wait()

    def mlp_part(zz):
        rows = span_of(zz * 256, 256)
        return mm_nt(gu[rows, 0:512], w_g[...].reshape(WIDE, 512)) + mm_nt(gu[rows, 512:1024], w_u[...].reshape(WIDE, 512))

    def grad_down(b):
        cols = slice(256 * b, 256 * b + 256)
        d_d[b] = mm_tn(hid[:, cols], buf1[...]).astype(BF).reshape(4, 4, 16, WIDE)

    def grad_gu(b):
        cols = slice(384 * b, 384 * b + 384)
        pair = slice(b % 2 * 2, b % 2 * 2 + 2)
        d_gu[b // 2, pair] = mm_tn(nmlp[:, cols], gu[...]).astype(BF).reshape(2, 4, 48, 1024)

    def fill1(n):
        if n == 0:
            grad_down(0)
            grad_down(1)
        elif n == 1:
            grad_gu(0)
            grad_gu(1)
        else:
            grad_gu(2)
            grad_gu(3)

    rs = (whole, keep, give, got, ring_out, ring_in)
    e, done_rs = reduce_scatter(me, mlp_part, *rs, rs_s, rs_r, fill1)
    part, gain_part = norm_back_of(e, middle[...], gains[g_mlp, :])
    o_gains[1:2, :] = gain_part
    gm = grad[...].astype(F32) + part
    mid_grad[...] = gm
    buf2[own_rows] = gm.astype(BF)
    ax = Exchange(me, mgs, mgr, ax_s, ax_r, True)

    def mixed_back(zz):
        rows = span_of(zz * 256, 256)
        mgs[rows] = mm_nt(buf2[rows], w_o[...]).astype(BF)
        ax.send(zz * 2)
        ax.send(zz * 2 + 1)

    def hook0():
        split_packed(qr, keys, vals)
        keys_t[...] = flip(keys)
        dk[...] = jnp.zeros_like(dk)
        dv[...] = jnp.zeros_like(dv)

    def hook1():
        for red in reds.values():
            red.arrive()
            red.load()

    def hook2():
        for red in reds.values():
            red.two()

    done_ag2 = all_gather(me, buf2, ag2_s, ag2_r, mixed_back, (hook0, hook1, hook2))
    if last:
        done_ag()
    normed = buf1
    load_normed = pltpu.make_async_copy(h_normed, normed, loc.at[11])
    load_normed.start()
    store(d_d, o_dd)
    store(d_gu, o_dgu)
    lanes = mm_tn(mixed[...], buf2[...])
    for head in range(2):
        chunk = [lanes[128 * head + 16 * c : 128 * head + 16 * c + 16] for c in (3, 7, 4, 0, 5, 1)]
        for b in range(8):
            first, shift = 12 * b // 16, 12 * b % 16
            piece = chunk[first][shift:]
            if shift > 4:
                piece = jnp.concatenate([piece, chunk[first + 1][: shift - 4]], axis=0)
            d_o[head * 2 + b // 4, b % 4] = padded(piece[0:12])
    store(d_o, o_do)
    if not last:

        def down_part(zz):
            return mm(hid[span_of(zz * 256, 256)], w_d[...].reshape(512, WIDE))

        done_rs()
        final = reduce_steps(me, down_part, whole, keep, *rs3)
        next(final)
    if last:
        stores[0].wait()
        early["da"].one()
        early["db"].one()
    ax.arrive()

    @pl.loop(0, 8)
    def _(p):
        rows = span_of(p * 128, 128)
        q = stacked(qr, rows)
        mg = stacked(mgr, rows)
        scores = mm_nt(keys[...], q)
        allowed = pcol[...] <= prow[pl.ds(p, 1), :]
        probs = jnp.where(allowed, jnp.exp2(scores * SCALE2 - lse[pl.ds(p, 1), :]), 0.0)
        pg = mm_nt(vals[...], mg)
        inner = jnp.sum(probs * pg, axis=0, keepdims=True)
        sg = (probs * (pg - inner)).astype(BF)
        dk[...] += mm(sg, q)
        dv[...] += mm(probs.astype(BF), mg)
        dq = jnp.transpose(mm(keys_t[...], sg)) * SCALE
        dqs[rows, 0:128] = dq[0:128]
        dqs[rows, 128:256] = dq[128:256]

    if not last:
        next(final)
    bx = Exchange(me, ps, pr, bx_s, bx_r, False)
    v0, _, _ = lane_masks(128)

    @pl.loop(0, 8)
    def _(k):
        p = lax.rem(me.c + 1 + k, 8)
        rows = span_of(p * 128, 128)
        value = dv[rows]
        ps[rows, 0:128] = jnp.where(v0, value, dqs[rows, 0:128]).astype(BF)
        ps[rows, 128:256] = jnp.where(v0, pltpu.roll(value, 112, 1), dqs[rows, 128:256]).astype(BF)
        ps[rows, 256:384] = jnp.where(v0, pltpu.roll(value, 96, 1), dk[rows] * SCALE).astype(BF)
        bx.send(p)

    if last:
        stores[1].wait()
        early["g"].one()
        early["u"].one()
        done_rs()
    else:
        total, done_rs3 = run(final)
        o_block[...] = (middle[...] + total).astype(BF)
    load_normed.wait()
    bx.arrive()
    pre = qr

    def in_part(zz):
        rows = span_of(zz * 256, 256)
        for t in range(3):
            cols = slice(128 * t, 128 * t + 128)
            tile = pr[rows, cols].astype(F32)
            pre[rows, cols] = (tile * cos[...] - pltpu.roll(tile, 64, 1) * sin[...]).astype(BF)
        return mm_nt(pre[rows], w_in[...])

    def fill2(n):
        for b in ((0, 1), (2,), (3,))[n]:
            cols = slice(384 * b, 384 * b + 384)
            pair = slice(b % 2 * 2, b % 2 * 2 + 2)
            d_in[b // 2, pair] = mm_tn(normed[:, cols], pre[...]).astype(BF).reshape(2, 4, 48, 384)
        if n == 1 and last:
            finish_reduces(reds, o_fin, o_down, o_out)

    e, done_rs2 = reduce_scatter(me, in_part, *rs, rs2_s, rs2_r, fill2)
    store(d_in, o_din)
    part, gain_part = norm_back_of(e, stream[...].astype(F32), gains[g_attn, :])
    o_gains[0:1, :] = gain_part
    o_grad[...] = mid_grad[...] + part
    for done in (done_ag2, ax.finish, bx.finish, done_rs2):
        done()
    for red in reds.values():
        red.finish()
    if not last:
        done_rs3()
    for red in early.values():
        red.arrive()
        red.finish((0,))
    for copy in stores[2 if last else 0 :]:
        copy.wait()


def padded(rows):
    return jnp.concatenate([rows, jnp.zeros((4, rows.shape[1]), F32)], axis=0).astype(BF)


def grads_kernel(*refs):
    refs = list(refs)
    take = lambda n: [refs.pop(0) for _ in range(n)]
    gp0, gp1, fin1, down1, out1 = take(5)
    parts = take(4)
    landed = dict(zip(MLP, take(4)))
    o_rows, o_down, o_out, o_gains = take(4)
    reds = make_reduces(Place(), parts, refs, landed, True)
    gains, fin_s, fin_r, down_s, down_r, out_s, out_r, sum_a, sum_b, got_a, got_b, got_c = take(12)
    fin_ss, fin_rs, gain_s, gain_r, down_ss, down_rs, out_ss = take(7)
    me = Place()
    mlp, rest = [reds[n] for n in MLP], [reds[n] for n in ("ia", "ib", "o")]
    group = [(k, c) for k in range(4) for c in range(2) if k or c]

    def mate(k, c):
        return {"z": lax.rem(me.z + k, 4), "core": lax.rem(me.core + c, 2)}

    mirror = {"x": me.z, "z": me.x}
    apart = me.x != me.z
    for red in reds.values():
        red.load()
    gains[...] = jnp.zeros_like(gains)
    gains[0:2] = gp0[0:2]
    gains[2:4] = gp1[0:2]
    me.greet(
        [me.near("x", k) for k in (1, 2, 3)] + [me.near("y", k) for k in (1, 2, 3)]
        + [mate(*m) for m in group] + [{"yl": 1 - me.yl, "core": me.oc}],
        mirror=True,
    )

    def gain_copy(stage, axis, src, got, k):
        i = 3 * stage + k - 1
        return push(src, got.at[k - 1], gain_s.at[i], gain_r.at[i], me.near(axis, k))

    def gain_sum(stage, axis, src, got, dst):
        total = src[...]
        for k in (1, 2, 3):
            gain_copy(stage, axis, src, got, k).wait_recv()
            total = total + got[k - 1]
        dst[...] = total

    slot = me.z * 2 + me.core

    def fin(l, i, come):
        k, c = group[i]
        to_z, to_core = lax.rem(me.z + k, 4), lax.rem(me.core + c, 2)
        from_z = lax.rem(me.z + 4 - k, 4)
        dst = fin_r.at[from_z * 2 + to_core, l] if come else fin_r.at[slot, l]
        return push(fin_s.at[to_core, to_z, l], dst, fin_ss.at[l, i], fin_rs.at[l, i], mate(k, c))

    for k in (1, 2, 3):
        gain_copy(0, "y", gains, got_a, k).start()
    for red in rest:
        red.one()
    fin_s[:, :, 1] = fin1[...]
    for i in range(7):
        fin(1, i, False).start()
    for red in mlp:
        red.two()
    for red in rest:
        red.arrive()
    gain_sum(0, "y", gains, got_a, sum_a)
    for k in (1, 2, 3):
        gain_copy(1, "x", sum_a, got_b, k).start()
    for red in rest:
        red.two()
    gain_sum(1, "x", sum_a, got_b, sum_b)

    def gain_mate(i):
        return push(sum_b, got_c.at[i], gain_s.at[6 + i], gain_r.at[6 + i], mate(*group[i]))

    for i in range(7):
        gain_mate(i).start()
    down_s[:, 1] = down1[...]
    out_s[1] = out1[...]
    finish_reduces(reds, fin_s.at[:, :, 0], down_s.at[:, 0], out_s.at[0])
    def down(dp, half):
        dev = {"core": jnp.int32(dp), "yl": me.core}
        return push(down_s.at[dp], down_r.at[half], down_ss.at[dp], down_rs.at[half], dev)

    mine = me.yl == me.core

    def out_copy():
        return push(out_s, out_r, out_ss.at[0], out_ss.at[1], mirror)

    for i in range(7):
        fin(0, i, False).start()
    for dp in range(2):
        keep = mine & (me.core == dp)

        @pl.when(jnp.logical_not(keep))
        def _(dp=dp):
            down(dp, me.yl).start()

        @pl.when(keep)
        def _(dp=dp):
            down_r[me.yl] = down_s[dp]

    @pl.when(apart)
    def _():
        out_copy().start()

    @pl.when(jnp.logical_not(apart))
    def _():
        out_r[...] = out_s[...]

    fin_r[slot] = fin_s[me.core, me.z]
    total = sum_b[...]
    for i in range(7):
        gain_mate(i).wait_recv()
        total = total + got_c[i]
    o_gains[...] = total
    for i in range(7):
        fin(0, i, True).wait_recv()
        fin(1, i, True).wait_recv()
    o_rows[...] = fin_r[...]
    for half in range(2):

        @pl.when(jnp.logical_not(mine & (me.yl == half)))
        def _(half=half):
            down(0, half).wait_recv()

    o_down[...] = down_r[...]

    @pl.when(apart)
    def _():
        out_copy().wait_recv()

    o_out[...] = out_r[...]
    for red in mlp:
        red.finish((1,))
    for red in rest:
        red.finish()
    for k in (1, 2, 3):
        gain_copy(0, "y", gains, got_a, k).wait_send()
        gain_copy(1, "x", sum_a, got_b, k).wait_send()
    for i in range(7):
        gain_mate(i).wait_send()
        fin(0, i, False).wait_send()
        fin(1, i, False).wait_send()
    for dp in range(2):

        @pl.when(jnp.logical_not(mine & (me.core == dp)))
        def _(dp=dp):
            down(dp, me.yl).wait_send()

    @pl.when(apart)
    def _():
        out_copy().wait_send()


def vm(shape, dtype=BF):
    return pltpu.VMEM(shape, dtype)


def rs_scratch():
    return [vm((4, 128, WIDE)), vm((4, 128, WIDE)), vm((6, 64, WIDE)), vm((6, 64, WIDE))]


def dma(*shape):
    return pltpu.SemaphoreType.DMA(shape)


def sems():
    return [dma(n) for n in (13, 13, 13, 13, 10, 10, 10, 10, 8, 8, 8, 8, 16, 16)]


WEIGHTS = [(WIDE, 384), (256, WIDE), (WIDE, 512), (WIDE, 512), (512, WIDE)]
SPLIT = [(2, 4, 4, 48, 384), (4, 64, WIDE), (2, 4, 4, 48, 512), (2, 4, 4, 48, 512), (2, 4, 4, 16, WIDE)]
PARTS = [(2, 4, 4, 48, 384), (2, 4, 4, 48, 1024), (2, 4, 4, 16, WIDE), (4, 4, 16, WIDE)]
RING = [(256, WIDE), (4, 128, WIDE)]


def run_kernel(kernel, name, cid, ins, in_vmem, outs, out_vmem, scratch):
    place = {True: pltpu.VMEM, False: pl.ANY}
    return pl.pallas_call(
        kernel,
        name=name,
        out_shape=[jax.ShapeDtypeStruct(s, d) for s, d in outs],
        in_specs=[pl.BlockSpec(memory_space=place[i < in_vmem]) for i in range(len(ins))],
        out_specs=[pl.BlockSpec(memory_space=place[i < out_vmem]) for i in range(len(outs))],
        scratch_shapes=scratch,
        compiler_params=pltpu.CompilerParams(
            collective_id=cid, has_side_effects=True, vmem_limit_bytes=58 * 2**20
        ),
    )(*ins)


def layer_fwd(l, stream, gains, tables, h_in, sources, extra):
    first = l == 0
    outs = [((128, WIDE), F32)] * (2 if first else 1) + [((8, 256), F32)] + ([((8, WIDE), F32)] if first else [])
    n_vmem = len(outs)
    outs += [
        ((1024, WIDE), BF), ((1024, 384), BF), ((1024, 256), BF), ((1024, WIDE), BF),
        ((1024, 512), BF), ((1024, 512), BF), ((1024, 512), BF),
    ] + [(s, BF) for s in SPLIT[1:]] + ([(SPLIT[0], BF)] * 2 if first else [((1024, WIDE), BF)])
    scratch = [vm(s) for s in SPLIT] + [
        vm((1024, WIDE)), vm((1024, WIDE)), vm((1024, 384)), vm((1024, 384)), vm((1024, 256)), vm((1024, 256)),
        vm((1024, 512)), vm((1024, 512)), vm((1024, 512)),
        vm((1024, 128)), vm((1024, 128)), vm((128, 1024)), vm((128, WIDE), F32),
    ] + [vm(s, F32) for s in RING] + rs_scratch() + sems() + [dma(10, 7), dma(10, 7)]
    if first:
        scratch += [vm((2, 4, 4, 8, 256), F32), vm(SPLIT[0])]
    else:
        scratch += [vm((1024, WIDE)), dma(13), dma(13)]
    ins = [stream] + ([] if first else [gains]) + [*tables, h_in, *sources, *extra]
    kernel = functools.partial(fwd_kernel, l)
    return run_kernel(kernel, f"layer_forward_{l}", 1 + l, ins, 5 if first else 6, outs, n_vmem, scratch)


def layer_bwd(l, grad, stream, middle, gains, tables, lse, weights, saved, above):
    last = l == 0
    outs = [((128, WIDE), F32), ((8, WIDE), F32)]
    outs += [((2, 4, 16, 1408), BF), ((2, 16, WIDE), BF), ((16, WIDE), BF)] if last else [((128, WIDE), BF)]
    n_vmem = len(outs)
    outs += [(s, BF) for s in PARTS]
    outs += [((3,) + REDUCE[n][3], BF) for n in MLP] * 2 if last else []
    shapes = WEIGHTS[:2] + [(4, 2, 4, 48, 512), (4, 2, 4, 48, 512), (4, 2, 4, 16, WIDE)]
    scratch = [vm(s) for s in shapes] + [
        vm((1024, WIDE)), vm((1024, WIDE)), vm((1024, 384)), vm((1024, 512)), vm((1024, 512)),
        vm((1024, 1024)), vm((1024, 256)), vm((1024, 256)),
        vm((1024, 128)), vm((1024, 128)), vm((128, 1024)), vm((1024, 128), F32), vm((1024, 128), F32),
        vm((1024, 256), F32), vm((1024, 384)), vm((1024, 384)), vm((128, WIDE), F32),
        vm((1024, 256)), vm((1024, WIDE)), vm((1024, 512)),
    ] + [vm(s) for s in PARTS] + [vm(s, F32) for s in RING] + rs_scratch() + sems()
    if last:
        scratch += reduce_scratch(("ia", "ib", "o")) + [dma(4, 6), dma(4, 6)]
    else:
        scratch += rs_scratch() + [dma(10), dma(10)]
    weights = [w.reshape(s) for w, s in zip(weights, shapes)]
    ins = [grad, stream, middle, gains, *tables, lse, *weights, *saved, *(above or ())]
    kernel = functools.partial(bwd_kernel, l)
    return run_kernel(kernel, f"layer_backward_{l}", 3 + l, ins, 9, outs, n_vmem, scratch)


def picks(rows, cols, test):
    r = lax.broadcasted_iota(jnp.int32, (rows, cols), 0)
    c = lax.broadcasted_iota(jnp.int32, (rows, cols), 1)
    return jnp.where(test(r, c), 1.0, 0.0).astype(BF)


def packed_place(n):
    t, i = n // 128, n % 128
    value = ((i >= 48) & (i < 64)) | (i >= 112)
    feature = jnp.where(value, 32 * t + jnp.where(i < 64, i - 48, i - 96), jnp.where(i < 48, i, i - 16))
    return t, feature, value


def prepare_kernel(
    order, wq, wk, wv, wg, wu, ga, gm, o_in, o_g, o_u, o_gain, o_cos, o_sin, o_pcol, o_prow, vq, vk, vv, vg, vu, loc
):
    core, z, yl = lax.axis_index("core"), lax.axis_index("z"), lax.axis_index("yl")
    own = pl.ds(pl.multiple_of(yl * 48, 16), 48)
    loads = [
        pltpu.make_async_copy(h.at[:, own], v, loc.at[i])
        for i, (h, v) in enumerate(((wq, vq), (wk, vk), (wv, vv), (wg, vg), (wu, vu)))
    ]
    for load in loads:
        load.start()
    ctx = lax.axis_index("x") * 2 + lax.axis_index("yh")
    for span in range(16):
        o_pcol[64 * span : 64 * span + 64] = order[span] * 64 + lax.broadcasted_iota(jnp.int32, (64, 1), 0)
    lane = lax.broadcasted_iota(jnp.int32, (1, 256), 1)
    for p in range(8):
        start = jnp.where(lane % 128 < 64, order[2 * p], order[2 * p + 1]) * 64
        o_prow[p : p + 1, :] = start + lane % 64
    row = lax.broadcasted_iota(jnp.int32, (128, 128), 0)
    col = lax.broadcasted_iota(jnp.int32, (128, 128), 1)
    place = jnp.where(row < 64, order[2 * ctx], order[2 * ctx + 1]) * 64 + row % 64
    turning = (col % 64) < 48
    freq = jnp.exp((col % 64).astype(F32) * (-2.0 * math.log(ROPE_BASE) / HEAD))
    angles = place.astype(F32) * freq
    cos = jnp.where(turning, jnp.cos(angles), 1.0)
    sin = jnp.where(turning, jnp.sin(angles), 0.0)
    sin = jnp.where(col < 64, -sin, sin)
    for half in range(2):
        o_cos[128 * half : 128 * half + 128] = cos
        o_sin[128 * half : 128 * half + 128] = sin
    owner = core * 8 + ctx
    shift = lax.rem(96 * owner, 128)
    move = picks(96, 256, lambda r, c: c == r + shift)
    zero = jnp.zeros((4, 96), F32)
    both = jnp.concatenate([ga[0:1], gm[0:1], ga[1:2], gm[1:2]], axis=0).astype(F32)
    placed = mm(jnp.concatenate([both, zero], axis=0).astype(BF), move)
    o_gain[0] = placed
    o_gain[1] = placed
    spread = [
        picks(1024, 128, lambda r, c, j=cc * 4 + z: (r // 256 == c // 32) & (r % 256 == 32 * j + c % 32)) for cc in range(2)
    ]
    spread = jnp.concatenate(spread, axis=1)

    def query(r, n, j):
        t, f, value = packed_place(n)
        return jnp.logical_not(value) & (t < 2) & (r == j * 192 + t * 96 + f)

    def key(r, n, j):
        t, f, value = packed_place(n)
        return jnp.logical_not(value) & (t == 2) & (r == j * 96 + f)

    def val(r, n, j):
        t, f, value = packed_place(n)
        return value & (r == j * 96 + f)

    for load in loads[:3]:
        load.wait()
    for cc in range(2):
        j = cc * 4 + z
        out = mm(vq[...].reshape(96, WIDE), picks(WIDE, 384, lambda r, n: query(r, n, j)))
        out = out + mm(vk[...].reshape(96, 768), picks(768, 384, lambda r, n: key(r, n, j)))
        out = out + mm(vv[...].reshape(96, 768), picks(768, 384, lambda r, n: val(r, n, j)))
        o_in[:, cc] = out.astype(BF).reshape(LAYERS, 48, 384)
    for load in loads[3:]:
        load.wait()
    for v, o in ((vg, o_g), (vu, o_u)):
        for b in range(4):
            out = mm(v[:, :, 1024 * b : 1024 * b + 1024].reshape(96, 1024), spread).astype(BF)
            for cc in range(2):
                o[:, cc, :, 128 * b : 128 * b + 128] = out[:, 128 * cc : 128 * cc + 128].reshape(LAYERS, 48, 128)


def prepare(order, wq, wk, wv, wg, wu, ga, gm):
    shapes = [((LAYERS, 2, 48, 384), BF), ((LAYERS, 2, 48, 512), BF), ((LAYERS, 2, 48, 512), BF), ((2, 8, 256), F32)]
    shapes += [((256, 128), F32), ((256, 128), F32), ((1024, 1), jnp.int32), ((8, 256), jnp.int32)]
    in_vmem = pl.BlockSpec(memory_space=pltpu.VMEM)
    return pl.pallas_call(
        prepare_kernel,
        name="prepare_sources",
        out_shape=[jax.ShapeDtypeStruct(s, d) for s, d in shapes],
        in_specs=[pl.BlockSpec(memory_space=pltpu.SMEM)] + [pl.BlockSpec(memory_space=pl.ANY)] * 5 + [in_vmem] * 2,
        out_specs=[in_vmem] * 8,
        scratch_shapes=[vm((LAYERS, 48, n)) for n in (WIDE, 768, 768, 4096, 4096)] + [dma(5)],
        compiler_params=pltpu.CompilerParams(vmem_limit_bytes=60 * 2**20),
    )(order, wq, wk, wv, wg, wu, ga, gm)


def assemble_kernel(cols, downs, outs, o_q, o_k, o_v, o_o, o_g, o_u, o_d):
    def member(j, lo, hi):
        return cols[j % 4 * 2 + j // 4, :, :, lo:hi].reshape(32, hi - lo)

    def put(dst, lo, hi, value):
        for l in range(LAYERS):
            dst[:, l, lo:hi] = value[16 * l : 16 * l + 12]

    def query(n, c, i):
        t, f, value = packed_place(n)
        return jnp.logical_not(value) & (t < 2) & (c == i * 192 + t * 96 + f)

    def key(n, c, i):
        t, f, value = packed_place(n)
        return jnp.logical_not(value) & (t == 2) & (c == i * 96 + f)

    def val(n, c, i):
        t, f, value = packed_place(n)
        return value & (c == i * 96 + f)

    for dst, test, per in ((o_q, query, 2), (o_k, key, 4), (o_v, val, 4)):
        moves = [picks(384, 384, lambda n, c, i=i: test(n, c, i)) for i in range(per)]
        for m in range(8 // per):
            total = sum(mm(member(per * m + i, 0, 384), moves[i]) for i in range(per))
            put(dst, 384 * m, 384 * m + 384, total)
    back = [picks(128, 1024, lambda r, c, j=j: (c // 256 == r // 32) & (c % 256 == 32 * j + r % 32)) for j in range(8)]
    for dst, start in ((o_g, 384), (o_u, 896)):
        for b in range(4):
            total = sum(mm(member(j, start + 128 * b, start + 128 * b + 128), back[j]) for j in range(8))
            put(dst, 1024 * b, 1024 * b + 1024, total)
    for l in range(LAYERS):
        o_o[:, l, :] = outs[l, 0:12].astype(F32)
        for h in range(2):
            o_d[l, 16 * h : 16 * h + 16] = downs[h, l].astype(F32)


def assemble(cols, downs, outs):
    shapes = [(12, LAYERS, n) for n in (WIDE, 768, 768, WIDE, 4096, 4096)] + [(LAYERS, 32, WIDE)]
    in_vmem = pl.BlockSpec(memory_space=pltpu.VMEM)
    *grads, d_d = pl.pallas_call(
        assemble_kernel,
        name="assemble_gradients",
        out_shape=[jax.ShapeDtypeStruct(s, F32) for s in shapes],
        in_specs=[in_vmem] * 3,
        out_specs=[in_vmem] * 7,
        compiler_params=pltpu.CompilerParams(vmem_limit_bytes=60 * 2**20),
    )(cols, downs, outs)
    return [grad.transpose(1, 0, 2) for grad in grads] + [d_d]


def reduce_grads(gain_parts, done, parts, landed):
    outs = [((8, 2, 16, 1408), BF), ((2, 2, 16, WIDE), BF), ((2, 16, WIDE), BF), ((8, WIDE), F32)]
    scratch = reduce_scratch() + [
        vm((8, WIDE), F32), vm((2, 4, 2, 16, 1408)), vm((8, 2, 16, 1408)), vm((2, 2, 16, WIDE)), vm((2, 2, 16, WIDE)),
        vm((2, 16, WIDE)), vm((2, 16, WIDE)), vm((8, WIDE), F32), vm((8, WIDE), F32),
        vm((3, 8, WIDE), F32), vm((3, 8, WIDE), F32), vm((7, 8, WIDE), F32),
        dma(2, 7), dma(2, 7), dma(13), dma(13), dma(2), dma(2), dma(2),
    ]
    return run_kernel(grads_kernel, "reduce_gradients", 5, [*gain_parts, *done, *parts, *landed], 5, outs, 4, scratch)


def body(
    tokens, span_order, attn_gain, w_query, key_matrix, value_matrix, w_out, mlp_gain, w_gate, w_up,
    w_down, cotangent,
):
    core, z, yl = lax.axis_index("core"), lax.axis_index("z"), lax.axis_index("yl")
    ctx = lax.axis_index("x") * 2 + lax.axis_index("yh")
    s_in, s_g, s_u, s_gain, *tables = prepare(
        span_order, w_query, key_matrix, value_matrix, w_gate, w_up, attn_gain, mlp_gain
    )
    stream, gains = tokens[0], None
    kept = []
    sources = (w_out, w_down, s_g, s_u)
    outs = layer_fwd(0, stream, gains, tables, s_in, sources, (s_gain, s_in))
    gains, w_next = outs[3], outs[-1]
    kept.append((stream, outs[1:3], outs[-2], outs[4:-2]))
    stream = outs[0]
    outs = layer_fwd(1, stream, gains, tables, w_next, sources, (cotangent[0],))
    kept.append((stream, outs[:2], w_next, outs[2:-1]))
    down_grad = outs[-1]

    g, gain_parts, above = cotangent[0], [None] * LAYERS, (down_grad,)
    for l in reversed(range(LAYERS)):
        stream, (middle, lse), w_in, outs = kept[l]
        normed, qkv, mixed, nmlp, gate, up, hid = outs[:7]
        saved = (qkv, gate, up, normed, mixed, nmlp, hid)
        res = layer_bwd(l, g, stream, middle, gains, tables, lse, (w_in, *outs[7:]), saved, above)
        g, gain_parts[l] = res[:2]
        if l:
            block_out, above = res[2][None], tuple(res[3:])
    cols, d_d, d_o, gp = reduce_grads(gain_parts, res[2:5], res[5:9], res[9:13])
    d_q, d_k, d_v, d_o, d_g, d_u, d_d = assemble(cols, d_d, d_o)
    owner = (core * 8 + ctx) * 8 + yl * 4 + z
    gp = lax.dynamic_slice(gp, (0, owner * 12), (4, 12)).reshape(2, 2, 12)
    return (block_out, g[None], gp[:, 0], d_q, d_k, d_v, d_o, gp[:, 1], d_g, d_u, d_d)


def solution(mesh):
    fine = Mesh(mesh.devices.reshape(2, 4, 2, 2, 4), ALL)
    seq, ctx, own, every = ("core", "yl", "z"), CTX, OWN, ALL
    act = P(seq, ctx, None)
    in_specs = (act, P(), P(None, own)) + (P(None, own, None),) * 4 + (P(None, own),) + (P(None, own, None),) * 3 + (act,)
    grad = P(None, every, None)
    out_specs = (act, act, P(None, every)) + (grad,) * 4 + (P(None, every),) + (grad,) * 3
    return jax.shard_map(body, mesh=fine, in_specs=in_specs, out_specs=out_specs, check_vma=False)
```

```python
import functools
import math

import jax
import jax.numpy as jnp
import numpy as np
from jax import lax
from jax.experimental import pallas as pl
from jax.experimental.pallas import tpu as pltpu
from jax.sharding import Mesh, PartitionSpec as P

HEAD = 96
LAYERS = 2
ROPE_BASE = 100000.0
EPS = 1e-05
CTX = ("x", "yh")
TP = ("z", "core")
OWN = ("core", "x", "yh")
ALL = ("core", "x", "yh", "yl", "z")
BF = jnp.bfloat16
F32 = jnp.float32
MESH = pl.DeviceIdType.MESH
SCALE = 1.0 / math.sqrt(HEAD)
SCALE2 = SCALE * math.log2(math.e)
WIDE = 1536


def mm(a, b):
    return jnp.dot(a, b, preferred_element_type=F32)


def mm_tn(a, b):
    return lax.dot_general(a, b, (((0,), (0,)), ((), ())), preferred_element_type=F32)


def mm_nt(a, b):
    return lax.dot_general(a, b, (((1,), (1,)), ((), ())), preferred_element_type=F32)


class Place:
    def __init__(self):
        self.z, self.core = lax.axis_index("z"), lax.axis_index("core")
        self.x, self.yh, self.yl = lax.axis_index("x"), lax.axis_index("yh"), lax.axis_index("yl")
        self.y = self.yh * 2 + self.yl
        self.c = self.x * 2 + self.yh
        self.zp, self.zm, self.zo = (lax.rem(self.z + k, 4) for k in (1, 3, 2))
        self.oc = 1 - self.core

    def near(self, axis, k):
        if axis == "x":
            return {"x": lax.rem(self.x + k, 4)}
        return at_y(lax.rem(self.y + k, 4))

    def greet(self, others, mirror=False):
        barrier = pltpu.get_barrier_semaphore()
        for dev in others:
            pl.semaphore_signal(barrier, inc=1, device_id=dev, device_id_type=MESH)
        if not mirror:
            pl.semaphore_wait(barrier, len(others))
            return

        @pl.when(self.x != self.z)
        def _():
            there = {"x": self.z, "z": self.x}
            pl.semaphore_signal(barrier, inc=1, device_id=there, device_id_type=MESH)
            pl.semaphore_wait(barrier, len(others) + 1)

        @pl.when(self.x == self.z)
        def _():
            pl.semaphore_wait(barrier, len(others))

    def layer_partners(self):
        return (
            [{"z": self.zp}, {"z": self.zm}, {"core": self.oc}]
            + [at_ctx(lax.rem(self.c + k, 8)) for k in range(1, 8)]
            + [{"yl": 1 - self.yl}, {"yh": 1 - self.yh, "yl": 1 - self.yl}]
        )


def at_y(y):
    return {"yh": y // 2, "yl": lax.rem(y, 2)}


def at_ctx(c):
    return {"x": c // 2, "yh": lax.rem(c, 2)}


def span_of(start, size):
    return pl.ds(pl.multiple_of(start, 64), size)


def slot_rows(zz, cc, half=None):
    base = (zz * 2 + cc) * 128
    return span_of(base, 128) if half is None else span_of(base + 64 * half, 64)


def all_gather(*args):
    return run(gather_steps(*args))


def run(steps):
    while True:
        try:
            next(steps)
        except StopIteration as stop:
            return stop.value


def gather_steps(me, buf, ssem, rsem, on_pair, hooks=()):
    z, zp, zm, zo, core, oc = me.z, me.zp, me.zm, me.zo, me.core, me.oc
    up, down, across = {"z": zp}, {"z": zm}, {"core": oc}
    sent = [
        (z, core, 0, up), (z, core, 1, up), (z, core, 1, down), (z, core, 0, down),
        (zm, core, 0, up), (zp, core, 1, down), (z, core, None, across),
        (zm, core, 0, across), (zm, core, 1, across), (zp, core, 1, across), (zp, core, 0, across),
        (zo, core, 0, across), (zo, core, 1, across),
    ]
    come = [
        (zm, core, 0), (zm, core, 1), (zp, core, 1), (zp, core, 0), (zo, core, 0), (zo, core, 1),
        (z, oc, None), (zm, oc, 0), (zm, oc, 1), (zp, oc, 1), (zp, oc, 0), (zo, oc, 0), (zo, oc, 1),
    ]

    def copy(i, rows, dev):
        return pltpu.make_async_remote_copy(
            src_ref=buf.at[rows], dst_ref=buf.at[rows], send_sem=ssem.at[i], recv_sem=rsem.at[i],
            device_id=dev, device_id_type=MESH,
        )

    def send(*which):
        for i in which:
            copy(i, slot_rows(*sent[i][:3]), sent[i][3]).start()

    def arrive(*which):
        for i in which:
            copy(i, slot_rows(*come[i]), sent[i][3]).wait_recv()

    def hook(i):
        if i < len(hooks):
            hooks[i]()

    send(0, 2, 1, 3, 6)
    hook(0)
    yield
    arrive(6)
    on_pair(z)
    arrive(0)
    send(4, 7)
    arrive(2)
    send(5, 9)
    hook(1)
    arrive(1)
    send(8)
    arrive(3)
    send(10)
    hook(2)
    yield
    arrive(7, 8)
    on_pair(zm)
    arrive(9, 10)
    on_pair(zp)
    hook(3)
    arrive(4)
    send(11)
    arrive(5)
    send(12)
    yield
    arrive(11, 12)
    on_pair(zo)

    def finish():
        for i in range(13):
            copy(i, slot_rows(*sent[i][:3]), sent[i][3]).wait_send()

    return finish


def reduce_scatter(*args):
    return run(reduce_steps(*args))


def reduce_steps(me, part, whole, keep, give, take, ring_out, ring_in, ssem, rsem, fill=lambda n: None):
    z, zp, zm, zo, core, oc = me.z, me.zp, me.zm, me.zo, me.core, me.oc
    up, down, across = {"z": zp}, {"z": zm}, {"core": oc}
    mine = span_of(core * 128, 128)
    theirs = span_of(oc * 128, 128)

    def swap(k):
        return pltpu.make_async_remote_copy(
            src_ref=give.at[k], dst_ref=take.at[k], send_sem=ssem.at[k], recv_sem=rsem.at[k],
            device_id=across, device_id_type=MESH,
        )

    def ring(i):
        return pltpu.make_async_remote_copy(
            src_ref=ring_out.at[i], dst_ref=ring_in.at[i], send_sem=ssem.at[4 + i], recv_sem=rsem.at[4 + i],
            device_id=up if i < 3 else down, device_id_type=MESH,
        )

    def make(k, zz):
        whole[...] = part(zz)
        give[k] = whole[theirs].astype(BF)
        keep[k] = whole[mine].astype(BF)
        swap(k).start()

    def merged(k, half):
        rows = slice(64 * half, 64 * half + 64)
        return keep[k, rows].astype(F32) + take[k, rows].astype(F32)

    def push(i, value):
        ring_out[i] = value.astype(BF)
        ring(i).start()

    make(0, zo)
    make(1, zp)
    swap(0).wait_recv()
    push(0, merged(0, 0))
    push(3, merged(0, 1))
    make(2, zm)
    swap(1).wait_recv()
    push(1, merged(1, 1))
    swap(2).wait_recv()
    push(4, merged(2, 0))
    make(3, z)
    fill(0)
    yield
    ring(0).wait_recv()
    push(2, merged(1, 0) + ring_in[0].astype(F32))
    ring(3).wait_recv()
    push(5, merged(2, 1) + ring_in[3].astype(F32))
    swap(3).wait_recv()
    fill(1)
    own = [merged(3, 0), merged(3, 1)]
    ring(1).wait_recv()
    own[1] = own[1] + ring_in[1].astype(F32)
    ring(4).wait_recv()
    own[0] = own[0] + ring_in[4].astype(F32)
    fill(2)
    yield
    ring(2).wait_recv()
    own[0] = own[0] + ring_in[2].astype(F32)
    ring(5).wait_recv()
    own[1] = own[1] + ring_in[5].astype(F32)

    def finish():
        for k in range(4):
            swap(k).wait_send()
        for i in range(6):
            ring(i).wait_send()

    return jnp.concatenate(own, axis=0), finish


def ctx_of(slot, core):
    zz, cc = slot // 2, lax.rem(slot, 2)
    return lax.rem(zz + 2 * cc + core, 4) * 2 + cc


def slot_of(ctx, core):
    x, yh = ctx // 2, lax.rem(ctx, 2)
    return lax.rem(x + 2 * yh + 3 * core, 4) * 2 + yh


class Exchange:
    def __init__(self, me, src, dst, ssem, rsem, out):
        self.me, self.src, self.dst, self.ssem, self.rsem = me, src, dst, ssem, rsem
        same = lambda v: v
        ctx, slot = (lambda v, f=f: f(v, me.core) for f in (ctx_of, slot_of))
        self.to, self.block, self.lands = (ctx, slot, same) if out else (same, same, slot)

    def copy(self, b, come):
        return pltpu.make_async_remote_copy(
            src_ref=self.src.at[span_of(b * 128, 128)], dst_ref=self.dst.at[span_of(come * 128, 128)],
            send_sem=self.ssem.at[b], recv_sem=self.rsem.at[come],
            device_id=at_ctx(self.to(b)), device_id_type=MESH,
        )

    def send(self, b):
        there, come = self.to(b), self.lands(self.me.c)

        @pl.when(there != self.me.c)
        def _():
            self.copy(b, come).start()

        @pl.when(there == self.me.c)
        def _():
            self.dst[span_of(come * 128, 128)] = self.src[span_of(b * 128, 128)]

    def arrive(self):
        @pl.loop(1, 8)
        def _(k):
            there = lax.rem(self.me.c + k, 8)
            self.copy(self.block(there), self.lands(there)).wait_recv()

    def finish(self):
        @pl.loop(1, 8)
        def _(k):
            there = lax.rem(self.me.c + k, 8)
            self.copy(self.block(there), self.lands(self.me.c)).wait_send()


def push(src, dst, ssem, rsem, dev):
    return pltpu.make_async_remote_copy(
        src_ref=src, dst_ref=dst, send_sem=ssem, recv_sem=rsem, device_id=dev, device_id_type=MESH
    )


class Gather:
    def __init__(self, me, src, dst, ssem, rsem, loc, order, cols):
        self.me, self.src, self.dst, self.ssem, self.rsem, self.order = me, src, dst, ssem, rsem, order
        self.loc, self.cols = loc, slice(*cols)

    def own(self):
        me = self.me
        return pltpu.make_async_copy(
            self.src(me.core, self.cols), self.dst.at[me.core, me.x, me.y, :, self.cols], self.loc
        )

    def cross(self, come=False):
        me = self.me
        row = me.oc if come else me.core
        return push(
            self.src(me.oc, self.cols), self.dst.at[row, me.x, me.y, :, self.cols],
            self.ssem.at[0], self.rsem.at[0], {"core": me.oc},
        )

    def region(self, stage, k):
        me = self.me
        x, y = (lax.rem(v + 4 - k, 4) for v in (me.x, me.y))
        if stage == 0:
            return self.dst.at[:, x if self.order[0] == "x" else me.x, y if self.order[0] == "y" else me.y, :, self.cols]
        if self.order[1] == "y":
            return self.dst.at[:, :, y, :, self.cols]
        return self.dst.at[:, x, :, :, self.cols]

    def copy(self, stage, k, come):
        ref = self.region(stage, k if come else 0)
        i = 1 + 3 * stage + k - 1
        return push(ref, ref, self.ssem.at[i], self.rsem.at[i], self.me.near(self.order[stage], k))

    def zero(self):
        self.own().start()
        self.cross().start()

    def one(self):
        self.own().wait()
        self.cross(True).wait_recv()
        for k in (2, 1, 3):
            self.copy(0, k, False).start()

    def two(self):
        for k in (1, 3, 2):
            self.copy(0, k, True).wait_recv()
        for k in (2, 1, 3):
            self.copy(1, k, False).start()

    def three(self):
        for k in (1, 3, 2):
            self.copy(1, k, True).wait_recv()

    def finish(self):
        self.cross().wait_send()
        for stage in (0, 1):
            for k in (1, 2, 3):
                self.copy(stage, k, False).wait_send()


class OutGather:
    def __init__(self, me, src, dst, ssem, rsem, loc):
        self.me, self.dst, self.ssem, self.rsem = me, dst, ssem, rsem
        self.src, self.loc = src, loc
        self.far = lax.rem(me.x + 4 - me.z, 4)

    def copy(self, stage, k, come):
        me = self.me
        y = lax.rem(me.y + 4 - k, 4) if stage and come else me.y
        ref, i = self.dst.at[y], 3 * stage + k - 1
        return push(ref, ref, self.ssem.at[i], self.rsem.at[i], me.near("xy"[stage], k))

    def own(self):
        y, yl = self.me.y, self.me.yl
        return [
            pltpu.make_async_copy(
                self.src.at[pl.ds(pl.multiple_of(row, 16), 16)], self.dst.at[y, to : to + 16], self.loc.at[i]
            )
            for i, (row, to) in enumerate(((48 - 16 * yl, 0), (80 - 16 * yl, 16), (16 * yl, 48)))
        ]

    def zero(self):
        @pl.when(self.far == 0)
        def _():
            for copy in self.own():
                copy.start()
            self.dst[self.me.y, 32:48] = jnp.zeros((16, WIDE), BF)

    def one(self):
        @pl.when(self.far == 0)
        def _():
            for copy in self.own():
                copy.wait()
            for k in (2, 1, 3):
                self.copy(0, k, False).start()

    def two(self):
        for k in (1, 2, 3):

            @pl.when(self.far == k)
            def _(k=k):
                self.copy(0, k, True).wait_recv()

        for k in (2, 1, 3):
            self.copy(1, k, False).start()

    def three(self):
        for k in (1, 3, 2):
            self.copy(1, k, True).wait_recv()

    def finish(self):
        @pl.when(self.far == 0)
        def _():
            for k in (1, 2, 3):
                self.copy(0, k, False).wait_send()

        for k in (1, 2, 3):
            self.copy(1, k, False).wait_send()


class Reduce:
    def __init__(self, me, spec, mine, got1, sum1, got2, ssem, rsem, loc, land=None, landed=False):
        self.me = me
        self.quarter, self.inner, self.order = spec[:3]
        self.mine, self.got1, self.sum1, self.got2, self.ssem, self.rsem, self.loc = mine, got1, sum1, got2, ssem, rsem, loc
        self.land, self.landed = land, landed

    def at(self, axis, k):
        return lax.rem((self.me.x if axis == "x" else self.me.y) + k, 4)

    def copy(self, stage, k):
        axis = self.order[stage]
        to = self.at(axis, k)
        src = self.inner(self.sum1, to) if stage else self.quarter(axis, to)
        dst = self.got2.at[k - 1] if stage else self.got1[k - 1] if self.land is None else self.land.at[k - 1]
        i = 3 * stage + k - 1
        return push(src, dst, self.ssem.at[i], self.rsem.at[i], self.me.near(axis, k))

    def loads(self):
        axis = self.order[0]
        out = [pltpu.make_async_copy(self.quarter(axis, self.at(axis, 0)), self.mine, self.loc.at[0])]
        if self.land is not None:
            for k in range(3):
                out.append(pltpu.make_async_copy(self.land.at[k], self.got1[k], self.loc.at[1 + k]))
        return out

    def load(self):
        for load in self.loads():
            load.start()

    def one(self):
        for k in (2, 1, 3):
            self.copy(0, k).start()

    def arrive(self):
        if not self.landed:
            for k in (1, 2, 3):
                self.copy(0, k).wait_recv()

    def two(self):
        for load in self.loads():
            load.wait()
        dims = self.sum1.shape[:-2]

        @pl.loop(0, math.prod(dims))
        def _(n):
            at = (n,) if len(dims) == 1 else (n // dims[1], lax.rem(n, dims[1]))
            total = self.mine[at].astype(F32)
            for k in range(3):
                total = total + self.got1[k][at].astype(F32)
            self.sum1[at] = total.astype(BF)

        for k in (2, 1, 3):
            self.copy(1, k).start()

    def three(self):
        for k in (1, 2, 3):
            self.copy(1, k).wait_recv()
        total = self.inner(self.sum1, self.at(self.order[1], 0))[...].astype(F32)
        for k in range(3):
            total = total + self.got2[k].astype(F32)
        return total

    def finish(self, stages=(0, 1)):
        for stage in stages:
            for k in (1, 2, 3):
                self.copy(stage, k).wait_send()


def reduce_specs(d_in, d_gu, d_d, d_o):
    def split(ref, lo, hi, r, order):
        def quarter(axis, i):
            return ref.at[:, i, :, :, lo:hi] if axis == "x" else ref.at[:, :, i, :, lo:hi]

        return quarter, lambda q, i: q.at[:, i], order, (2, 4, r, hi - lo), (2, r, hi - lo)

    return {
        "g": split(d_gu, 0, 512, 48, "yx"),
        "u": split(d_gu, 512, 1024, 48, "xy"),
        "da": split(d_d, 0, 768, 16, "yx"),
        "db": split(d_d, 768, 1536, 16, "xy"),
        "ia": split(d_in, 0, 256, 48, "yx"),
        "ib": split(d_in, 256, 384, 48, "xy"),
        "o": (lambda axis, i: d_o.at[:, i], lambda q, i: q.at[i], "xy", (4, 16, WIDE), (16, WIDE)),
    }


REDUCE = reduce_specs(None, None, None, None)
def reduce_scratch(names, staged):
    out = []
    for name in names:
        big, small = REDUCE[name][3:]
        out += [vm(big), vm((3,) + big)] if name in staged else []
        out += [vm(big), vm((3,) + small)]
    n = len(names)
    return out + [dma(n, 6), dma(n, 6), dma(n, 4)]


def make_reduces(me, names, parts, refs, land=None, landed=(), stage=None):
    specs, out = reduce_specs(*parts), {}
    for name in names:
        if stage and name in stage:
            own, got = stage[name]
        else:
            own, got = refs.pop(0), refs.pop(0)
            got = [got.at[k] for k in range(3)]
        out[name] = (own, got, refs.pop(0), refs.pop(0))
    ssem, rsem, loc = refs.pop(0), refs.pop(0), refs.pop(0)
    for n, (name, bufs) in enumerate(out.items()):
        there = land.get(name) if land else None
        out[name] = Reduce(me, specs[name], *bufs, ssem.at[n], rsem.at[n], loc.at[n], there, name in landed)
    return out


COLUMNS = {"ia": (0, 256), "ib": (256, 384), "g": (384, 896), "u": (896, 1408)}
MLP = ("g", "u", "da", "db")
REST = ("ia", "ib", "o")


def finish_columns(reds, names, fin):
    for name in names:
        lo, hi = COLUMNS[name]
        total = reds[name].three()
        for dp in range(2):
            for z in range(4):
                fin[dp, z, :, lo:hi] = padded(total[dp, 12 * z : 12 * z + 12])


def finish_down(reds, down):
    down[:, :, 0:768] = reds["da"].three().astype(BF)
    down[:, :, 768:1536] = reds["db"].three().astype(BF)


def lane_masks(rows):
    lane = lax.broadcasted_iota(jnp.int32, (rows, 128), 1)
    v0 = ((lane >= 48) & (lane < 64)) | (lane >= 112)
    v1 = ((lane >= 64) & (lane < 80)) | (lane < 16)
    v2 = ((lane >= 80) & (lane < 96)) | ((lane >= 16) & (lane < 32))
    return v0, v1, v2


def split_packed(packed, key_ref, value_ref):
    v0, v1, v2 = lane_masks(128)

    @pl.loop(0, 8)
    def _(p):
        rows = span_of(p * 128, 128)
        t0, t1, t2 = (packed[rows, 128 * t : 128 * t + 128].astype(F32) for t in range(3))
        key_ref[rows] = jnp.where(v0, 0.0, t2).astype(BF)
        value = jnp.where(v0, t0, 0.0)
        value = value + jnp.where(v1, pltpu.roll(t1, 16, 1), 0.0)
        value = value + jnp.where(v2, pltpu.roll(t2, 32, 1), 0.0)
        value_ref[rows] = value.astype(BF)


def flip(ref):
    return jnp.transpose(ref[...].astype(F32)).astype(BF)


def stacked(ref, rows):
    return jnp.concatenate([ref[rows, 0:128], ref[rows, 128:256]], axis=0)


def rms_of(values):
    return lax.rsqrt(jnp.mean(values * values, axis=-1, keepdims=True) + EPS)


def fwd_kernel(l, *refs):
    first = l == 0
    g_attn, g_mlp = (slice(2 * l + i, 2 * l + i + 1) for i in (0, 1))
    refs = list(refs)
    take = lambda n: [refs.pop(0) for _ in range(n)]
    (stream,) = take(1)
    (gains_in,) = (None,) if first else take(1)
    cos, sin, pcol, prow = take(4)
    (h_in,) = take(1)
    w_out, w_down, s_g, s_u = take(4)
    s_gain, s_next = take(2) if first else (None, None)
    (cot,) = (None,) if first else take(1)
    (o_stream,) = take(1) if first else (None,)
    o_middle, o_lse = take(2)
    (o_gains,) = take(1) if first else (gains_in,)
    o_normed, o_qkv, o_mixed, o_nmlp, o_gate, o_up, o_hidden, o_wo, o_wg, o_wu, o_wd = take(11)
    o_win, o_next = take(2) if first else (None, None)
    (o_down,) = (None,) if first else take(1)
    w_in, w_o, w_g, w_u, w_d = take(5)
    buf1, buf2, qs, qr, ms, mr, gate_v, up_v, hid, keys, vals, vals_t, middle = take(13)
    whole, keep, give, got, ring_out, ring_in = take(6)
    ag_s, ag_r, ag2_s, ag2_r, rs_s, rs_r, rs2_s, rs2_r, ax_s, ax_r, bx_s, bx_r, loc, loc2, ga_s, ga_r = take(16)
    w_gain, w_next = take(2) if first else (None, None)
    cot_all, cot_s, cot_r = (None,) * 3 if first else take(3)
    me = Place()
    stores = []

    def store(src, dst):
        stores.append(pltpu.make_async_copy(src, dst, loc2.at[len(stores)]))
        stores[-1].start()

    n_item = [0]

    def down_rows(core, cols):
        row = pl.multiple_of((core * 4 + me.z) * 32 + me.yl * 16, 16)
        return w_down.at[l, pl.ds(row, 16), cols]

    def item(src, dst, order, *cols):
        i = n_item[0]
        n_item[0] += 1
        if not callable(src):
            src = lambda core, cols, ref=src: ref.at[core, :, cols]
        return Gather(me, src, dst, ga_s.at[i], ga_r.at[i], loc.at[i], order, cols)

    g_g, g_u = item(s_g.at[l], w_g, "xy", 0, 512), item(s_u.at[l], w_u, "yx", 0, 512)
    g_d = [item(down_rows, w_d, "xy", 0, 768), item(down_rows, w_d, "yx", 768, WIDE)]
    g_o = OutGather(me, w_out.at[l], w_o, ga_s.at[4], ga_r.at[4], loc.at[pl.ds(10, 3)])
    n_item[0] = 5
    g_in, g_next, g_gain = [], [], []
    if first:
        g_gain = [item(s_gain, w_gain, "yx", 0, 256)]
        g_in = [item(h_in.at[0], w_in, "yx", 0, 256), item(h_in.at[0], w_in, "xy", 256, 384)]
        g_next = [item(s_next.at[1], w_next, "yx", 0, 256), item(s_next.at[1], w_next, "xy", 256, 384)]
    everything = g_gain + g_in + [g_o, g_g, g_u] + g_d + g_next

    def each(items, step):
        for one in items:
            getattr(one, step)()

    own_rows = slot_rows(me.z, me.core)
    raw = buf2 if first else buf1
    if first:
        raw[own_rows] = stream[...]
    else:
        load_in = pltpu.make_async_copy(h_in, w_in, loc.at[5])
        load_in.start()
        load_cot = pltpu.make_async_copy(cot, cot_all.at[own_rows], loc.at[6])
        load_cot.start()
        s = stream[...]
        raw[own_rows] = (s * rms_of(s) * gains_in[g_attn, :]).astype(BF)
    me.greet(me.layer_partners())
    each(everything, "zero")
    ax = Exchange(me, qs, qr, ax_s, ax_r, True)

    def project(zz):
        rows = span_of(zz * 256, 256)
        y = mm(buf1[rows], w_in[...].reshape(WIDE, 384))
        for t in range(3):
            tile = y[:, 128 * t : 128 * t + 128]
            tile = tile * cos[...] + pltpu.roll(tile, 64, 1) * sin[...]
            qs[rows, 128 * t : 128 * t + 128] = tile.astype(BF)
        ax.send(zz * 2)
        ax.send(zz * 2 + 1)

    def normalise(zz):
        rows = span_of(zz * 256, 256)
        s = raw[rows].astype(F32)
        buf1[rows] = (s * rms_of(s) * o_gains[g_attn, :]).astype(BF)

    if first:

        def own_pair():
            each(g_gain + g_in, "two")

        def gains_here():
            each(g_gain, "three")
            o_gains[...] = jnp.zeros_like(o_gains)
            for owner in range(16):
                base = 96 * owner // 128 * 128
                width = min(256, WIDE - base)
                row = w_gain[owner // 8, owner % 8 // 2, owner % 2 * 2]
                o_gains[:, base : base + width] += row[:, :width]
            normalise(me.z)
            g_o.one()

        hooks = (lambda: each(g_gain + g_in, "one"), own_pair, gains_here)

        def others(zz):
            if zz is not me.z:
                normalise(zz)

        done_ag = all_gather(me, raw, ag_s, ag_r, others, hooks)
        done_ag()
        each(g_in, "three")

        @pl.loop(0, 4)
        def _(k):
            project(lax.rem(me.z + k, 4))

    else:
        load_in.wait()
        done_ag = all_gather(me, raw, ag_s, ag_r, project, (g_o.one,))
        load_cot.wait()
        ring = gather_steps(me, cot_all, cot_s, cot_r, lambda zz: None)
        next(ring)
    g_o.two()
    each((g_g, g_u), "one")
    ax.arrive()
    if not first:
        next(ring)
    store(buf1, o_normed)
    store(qr, o_qkv)
    split_packed(qr, keys, vals)
    vals_t[...] = flip(vals)
    bx = Exchange(me, ms, mr, bx_s, bx_r, False)

    @pl.loop(0, 8)
    def _(k):
        p = lax.rem(me.c + 1 + k, 8)
        rows = span_of(p * 128, 128)
        q = stacked(qr, rows)
        scores = mm_nt(keys[...], q)
        scores = jnp.where(pcol[...] <= prow[pl.ds(p, 1), :], scores, -1e30)
        top = jnp.max(scores, axis=0, keepdims=True)
        weights = jnp.exp2((scores - top) * SCALE2)
        total = jnp.sum(weights, axis=0, keepdims=True)
        o_lse[pl.ds(p, 1), :] = top * SCALE2 + jnp.log2(total)
        probs = (weights * (1.0 / total)).astype(BF)
        out = jnp.transpose(mm(vals_t[...], probs)).astype(BF)
        ms[rows, 0:128] = out[0:128]
        ms[rows, 128:256] = out[128:256]
        bx.send(p)

    each((g_g, g_u), "two")
    if not first:
        next(ring)
    each(g_d, "one")
    g_o.three()
    bx.arrive()
    store(mr, o_mixed)

    def out_part(zz):
        return mm(mr[span_of(zz * 256, 256)], w_o[...].reshape(256, WIDE))

    rs = (whole, keep, give, got, ring_out, ring_in)
    total, done_rs = reduce_scatter(me, out_part, *rs, rs_s, rs_r)
    mid = total + (stream[...].astype(F32) if first else stream[...])
    middle[...] = mid
    o_middle[...] = mid
    buf2[own_rows] = (mid * rms_of(mid) * o_gains[g_mlp, :]).astype(BF)
    waited = []

    def gated(zz):
        if not waited:
            waited.append(1)
            each((g_g, g_u), "three")
        rows = span_of(zz * 256, 256)
        gate = mm(buf2[rows], w_g[...].reshape(WIDE, 512))
        gate_v[rows] = gate.astype(BF)
        up = mm(buf2[rows], w_u[...].reshape(WIDE, 512))
        up_v[rows] = up.astype(BF)
        hid[rows] = (gate / (1.0 + jnp.exp(-gate)) * up).astype(BF)
        for src, dst in ((buf2, o_nmlp), (gate_v, o_gate), (up_v, o_up), (hid, o_hidden)):
            store(src.at[rows], dst.at[rows])

    def weights_out():
        each(g_next, "one")
        for w, o in [(w_o, o_wo), (w_g, o_wg), (w_u, o_wu)] + ([(w_in, o_win)] if first else []):
            store(w, o)

    hooks = (lambda: each(g_d, "two"), lambda: None, weights_out)
    done_ag2 = all_gather(me, buf2, ag2_s, ag2_r, gated, hooks)
    each(g_next, "two")
    each(g_d, "three")
    store(w_d, o_wd)
    done_rs()

    if not first:
        done_cot = run(ring)
        store(cot_all, o_down)
        for done in (done_ag, ax.finish, bx.finish, done_ag2, done_cot):
            done()
        each(everything, "finish")
        for copy in stores:
            copy.wait()
        return

    def down_part(zz):
        return mm(hid[span_of(zz * 256, 256)], w_d[...].reshape(512, WIDE))

    total, done_rs2 = reduce_scatter(me, down_part, *rs, rs2_s, rs2_r)
    o_stream[...] = middle[...] + total
    each(g_next, "three")
    store(w_next, o_next)
    for done in (ax.finish, bx.finish, done_ag2, done_rs2):
        done()
    each(everything, "finish")
    for copy in stores:
        copy.wait()


def norm_back_of(e, values, gain):
    q = rms_of(values)
    n = values * q
    dn = e * gain
    part = q * (dn - n * jnp.mean(dn * n, axis=-1, keepdims=True))
    return part, jnp.sum(e * n, axis=0, keepdims=True)


def bwd_kernel(l, *refs):
    last = l == 0
    g_attn, g_mlp = (slice(2 * l + i, 2 * l + i + 1) for i in (0, 1))
    refs = list(refs)
    take = lambda n: [refs.pop(0) for _ in range(n)]
    grad, stream, middle, gains, cos, sin, pcol, prow, lse = take(9)
    h_in, h_o, h_g, h_u, h_d, h_qkv, h_gate, h_up, h_normed, h_mixed, h_nmlp, h_hidden = take(12)
    above, landed = (take(4), dict(zip(MLP, take(4)))) if last else (None, None)
    (h_down,) = (None,) if last else take(1)
    o_grad, o_gains = take(2)
    (o_block,) = (None,) if last else take(1)
    o_fin, o_down, o_out = take(3) if last else (None,) * 3
    parts = take(4)
    o_din, o_dgu, o_dd, o_do = parts
    landing = dict(zip(MLP, take(4)))
    if last:
        landing["o"] = take(1)[0]
    w_in, w_o, w_g, w_u, w_d, buf1, buf2, qr, gate_v, up_v, gu, mgs, mgr = take(13)
    keys, vals, keys_t, dk, dv, dqs, ps, pr, mid_grad, mixed, nmlp, hid = take(12)
    d_in, d_gu, d_d, d_o = take(4)
    whole, keep, give, got, ring_out, ring_in = take(6)
    ag_s, ag_r, ag2_s, ag2_r, rs_s, rs_r, rs2_s, rs2_r, ax_s, ax_r, bx_s, bx_r, loc, loc2 = take(14)
    me = Place()
    pairs = (
        (h_d, w_d), (h_gate, gate_v), (h_up, up_v), (h_g, w_g), (h_u, w_u), (h_o, w_o), (h_qkv, qr), (h_in, w_in),
        (h_hidden, hid), (h_nmlp, nmlp), (h_mixed, mixed),
    )
    loads = [pltpu.make_async_copy(h, v, loc.at[i]) for i, (h, v) in enumerate(pairs)]
    for load in loads:
        load.start()
    stores = []

    def store(src, dst):
        stores.append(pltpu.make_async_copy(src, dst, loc2.at[len(stores)]))
        stores[-1].start()

    rs3 = refs
    local = (d_in, d_gu, d_d, d_o)
    upper = {}
    if last:
        stage = {
            "g": [d_gu.at[:, :, k, :, 0:512] for k in range(4)], "u": [d_gu.at[:, :, k, :, 512:1024] for k in range(4)],
            "da": [d_d.at[:, :, k, :, 0:768] for k in range(4)], "db": [d_d.at[:, :, k, :, 768:WIDE] for k in range(4)],
        }
        stage["ia"] = [d_in.at[:, :, k, :, 0:256] for k in range(4)]
        stage["ib"] = [d_in.at[:, :, k, :, 256:384] for k in range(4)]
        stage["o"] = [d_o.at[:, k] for k in range(4)]
        stage = {name: (views[3], views[:3]) for name, views in stage.items()}
        upper = make_reduces(me, MLP + REST, above, refs, landed, MLP, stage)
        stage = {
            "g": [w_g.at[k] for k in range(4)], "u": [w_u.at[k] for k in range(4)],
            "da": [w_d.at[k, :, :, :, 0:768] for k in range(4)], "db": [w_d.at[k, :, :, :, 768:WIDE] for k in range(4)],
        }
        stage = {name: (views[3], views[:3]) for name, views in stage.items()}
        own = make_reduces(me, MLP, local, refs, landing, (), stage)
        es, er = refs
        own["o"] = Reduce(me, reduce_specs(*local)["o"], None, None, None, None, es, er, None, landing["o"])
    else:
        es, er = rs3[6:]
        specs = reduce_specs(*local)
        own = {
            name: Reduce(me, specs[name], None, None, None, None, es.at[n], er.at[n], None, landing[name])
            for n, name in enumerate(MLP)
        }

    def each(reds, names, step):
        for name in names:
            if name in reds:
                getattr(reds[name], step)()

    own_rows = slot_rows(me.z, me.core)
    if last:
        buf1[own_rows] = grad[...].astype(BF)
    else:
        load_down = pltpu.make_async_copy(h_down, buf1, loc.at[11])
        load_down.start()
    me.greet(me.layer_partners())
    each(upper, MLP, "load")
    each(upper, REST, "one")
    for load in loads[:3]:
        load.wait()

    def unit(zz):
        rows = span_of(zz * 256, 256)
        hg = mm_nt(buf1[rows], w_d[...].reshape(512, WIDE))
        gate, up = gate_v[rows].astype(F32), up_v[rows].astype(F32)
        sig = 1.0 / (1.0 + jnp.exp(-gate))
        gu[rows, 0:512] = (hg * up * (sig * (1.0 + gate * (1.0 - sig)))).astype(BF)
        gu[rows, 512:1024] = (hg * (gate * sig)).astype(BF)

    if last:
        hooks = (lambda: each(upper, REST, "load"), lambda: None, lambda: each(upper, MLP, "two"))
        done_ag = all_gather(me, buf1, ag_s, ag_r, unit, hooks)
    else:
        load_down.wait()
        for zz in range(4):
            unit(zz)
    for load in loads[3:]:
        load.wait()

    def mlp_part(zz):
        rows = span_of(zz * 256, 256)
        return mm_nt(gu[rows, 0:512], w_g[...].reshape(WIDE, 512)) + mm_nt(gu[rows, 512:1024], w_u[...].reshape(WIDE, 512))

    def grad_down(b):
        cols = slice(256 * b, 256 * b + 256)
        d_d[b] = mm_tn(hid[:, cols], buf1[...]).astype(BF).reshape(4, 4, 16, WIDE)

    def grad_gu(b):
        cols = slice(384 * b, 384 * b + 384)
        pair = slice(b % 2 * 2, b % 2 * 2 + 2)
        d_gu[b // 2, pair] = mm_tn(nmlp[:, cols], gu[...]).astype(BF).reshape(2, 4, 48, 1024)

    def fill1(n):
        if n == 0:
            grad_down(0)
            grad_down(1)
        elif n == 1:
            grad_gu(0)
            grad_gu(1)
        else:
            grad_gu(2)
            grad_gu(3)
            each(own, ("g", "u"), "one")

    rs = (whole, keep, give, got, ring_out, ring_in)
    e, done_rs = reduce_scatter(me, mlp_part, *rs, rs_s, rs_r, fill1)
    part, gain_part = norm_back_of(e, middle[...], gains[g_mlp, :])
    o_gains[1:2, :] = gain_part
    gm = grad[...].astype(F32) + part
    mid_grad[...] = gm
    buf2[own_rows] = gm.astype(BF)
    ax = Exchange(me, mgs, mgr, ax_s, ax_r, True)

    def mixed_back(zz):
        rows = span_of(zz * 256, 256)
        mgs[rows] = mm_nt(buf2[rows], w_o[...]).astype(BF)
        ax.send(zz * 2)
        ax.send(zz * 2 + 1)

    def hook0():
        split_packed(qr, keys, vals)
        keys_t[...] = flip(keys)
        dk[...] = jnp.zeros_like(dk)
        dv[...] = jnp.zeros_like(dv)

    def hook2():
        each(upper, REST, "arrive")
        each(upper, REST, "two")

    done_ag2 = all_gather(me, buf2, ag2_s, ag2_r, mixed_back, (hook0, lambda: None, hook2))
    if last:
        done_ag()
    normed = buf1
    load_normed = pltpu.make_async_copy(h_normed, normed, loc.at[11])
    load_normed.start()
    store(d_d, o_dd)
    store(d_gu, o_dgu)
    lanes = mm_tn(mixed[...], buf2[...])
    for head in range(2):
        chunk = [lanes[128 * head + 16 * c : 128 * head + 16 * c + 16] for c in (3, 7, 4, 0, 5, 1)]
        for b in range(8):
            first, shift = 12 * b // 16, 12 * b % 16
            piece = chunk[first][shift:]
            if shift > 4:
                piece = jnp.concatenate([piece, chunk[first + 1][: shift - 4]], axis=0)
            d_o[head * 2 + b // 4, b % 4] = padded(piece[0:12])
    store(d_o, o_do)
    if not last:

        def down_part(zz):
            return mm(hid[span_of(zz * 256, 256)], w_d[...].reshape(512, WIDE))

        done_rs()
        final = reduce_steps(me, down_part, whole, keep, *rs3[:6])
        next(final)
    ax.arrive()
    each(own, ("da", "db"), "one")

    @pl.loop(0, 8)
    def _(p):
        rows = span_of(p * 128, 128)
        q = stacked(qr, rows)
        mg = stacked(mgr, rows)
        scores = mm_nt(keys[...], q)
        allowed = pcol[...] <= prow[pl.ds(p, 1), :]
        probs = jnp.where(allowed, jnp.exp2(scores * SCALE2 - lse[pl.ds(p, 1), :]), 0.0)
        pg = mm_nt(vals[...], mg)
        inner = jnp.sum(probs * pg, axis=0, keepdims=True)
        sg = (probs * (pg - inner)).astype(BF)
        dk[...] += mm(sg, q)
        dv[...] += mm(probs.astype(BF), mg)
        dq = jnp.transpose(mm(keys_t[...], sg)) * SCALE
        dqs[rows, 0:128] = dq[0:128].astype(BF)
        dqs[rows, 128:256] = dq[128:256].astype(BF)

    if not last:
        next(final)
    bx = Exchange(me, ps, pr, bx_s, bx_r, False)
    v0, _, _ = lane_masks(128)

    @pl.loop(0, 8)
    def _(k):
        p = lax.rem(me.c + 1 + k, 8)
        rows = span_of(p * 128, 128)
        value = dv[rows]
        ps[rows, 0:128] = jnp.where(v0, value, dqs[rows, 0:128].astype(F32)).astype(BF)
        ps[rows, 128:256] = jnp.where(v0, pltpu.roll(value, 112, 1), dqs[rows, 128:256].astype(F32)).astype(BF)
        ps[rows, 256:384] = jnp.where(v0, pltpu.roll(value, 96, 1), dk[rows] * SCALE).astype(BF)
        bx.send(p)

    if last:
        each(own, MLP, "arrive")
        each(own, MLP, "load")
        done_rs()
    else:
        total, done_rs3 = run(final)
        o_block[...] = (middle[...] + total).astype(BF)
    load_normed.wait()
    bx.arrive()
    pre = qr

    def in_part(zz):
        rows = span_of(zz * 256, 256)
        for t in range(3):
            cols = slice(128 * t, 128 * t + 128)
            tile = pr[rows, cols].astype(F32)
            pre[rows, cols] = (tile * cos[...] - pltpu.roll(tile, 64, 1) * sin[...]).astype(BF)
        return mm_nt(pre[rows], w_in[...])

    def fill2(n):
        for b in ((0, 1), (2,), (3,))[n]:
            cols = slice(384 * b, 384 * b + 384)
            pair = slice(b % 2 * 2, b % 2 * 2 + 2)
            d_in[b // 2, pair] = mm_tn(normed[:, cols], pre[...]).astype(BF).reshape(2, 4, 48, 384)
        if n == 0 and last:
            each(own, MLP, "two")
            each(own, ("o",), "one")
        if n == 1 and last:
            finish_columns(upper, COLUMNS, o_fin.at[:, :, 1])
            finish_down(upper, o_down.at[:, 1])
            o_out[...] = upper["o"].three().astype(BF)

    e, done_rs2 = reduce_scatter(me, in_part, *rs, rs2_s, rs2_r, fill2)
    store(d_in, o_din)
    part, gain_part = norm_back_of(e, stream[...].astype(F32), gains[g_attn, :])
    o_gains[0:1, :] = gain_part
    o_grad[...] = mid_grad[...] + part
    for done in (done_ag2, ax.finish, bx.finish, done_rs2):
        done()
    for name, red in upper.items():
        red.finish((1,) if name in MLP else (0, 1))
    if last:
        finish_columns(own, ("g", "u"), o_fin.at[:, :, 0])
        finish_down(own, o_down.at[:, 0])
        own["o"].arrive()
    else:
        done_rs3()
        each(own, MLP, "arrive")
    for name, red in own.items():
        red.finish((0, 1) if last and name in MLP else (0,))
    for copy in stores:
        copy.wait()


def padded(rows):
    return jnp.concatenate([rows, jnp.zeros((4, rows.shape[1]), F32)], axis=0).astype(BF)


def grads_kernel(*refs):
    refs = list(refs)
    take = lambda n: [refs.pop(0) for _ in range(n)]
    gp0, gp1, fin_in, down_s, out1 = take(5)
    d_in, d_o, land_o = take(3)
    o_rows, o_down, o_out, o_gains = take(4)
    me = Place()
    reds = make_reduces(me, REST, (d_in, None, None, d_o), refs, {"o": land_o}, ("o",))
    gains, fin_s, fin_r, down_r, out_s, out_r, sum_a, sum_b, got_a, got_b, got_c = take(11)
    fin_ss, fin_rs, gain_s, gain_r, down_ss, down_rs, out_ss = take(7)
    rest = [reds["ia"], reds["ib"]]
    group = [(k, c) for k in range(4) for c in range(2) if k or c]

    def mate(k, c):
        return {"z": lax.rem(me.z + k, 4), "core": lax.rem(me.core + c, 2)}

    mirror = {"x": me.z, "z": me.x}
    apart = me.x != me.z
    for red in reds.values():
        red.load()
    gains[...] = jnp.zeros_like(gains)
    gains[0:2] = gp0[0:2]
    gains[2:4] = gp1[0:2]
    me.greet(
        [me.near("x", k) for k in (1, 2, 3)] + [me.near("y", k) for k in (1, 2, 3)]
        + [mate(*m) for m in group] + [{"yl": 1 - me.yl, "core": me.oc}],
        mirror=True,
    )

    def gain_copy(stage, axis, src, got, k):
        i = 3 * stage + k - 1
        return push(src, got.at[k - 1], gain_s.at[i], gain_r.at[i], me.near(axis, k))

    def gain_sum(stage, axis, src, got, dst):
        total = src[...]
        for k in (1, 2, 3):
            gain_copy(stage, axis, src, got, k).wait_recv()
            total = total + got[k - 1]
        dst[...] = total

    slot = me.z * 2 + me.core

    def fin(l, i, come):
        k, c = group[i]
        to_z, to_core = lax.rem(me.z + k, 4), lax.rem(me.core + c, 2)
        from_z = lax.rem(me.z + 4 - k, 4)
        dst = fin_r.at[from_z * 2 + to_core, l] if come else fin_r.at[slot, l]
        src = fin_in.at[to_core, to_z, l] if l else fin_s.at[to_core, to_z]
        return push(src, dst, fin_ss.at[l, i], fin_rs.at[l, i], mate(k, c))

    def down(dp, half):
        dev = {"core": jnp.int32(dp), "yl": me.core}
        return push(down_s.at[dp], down_r.at[half], down_ss.at[dp], down_rs.at[half], dev)

    mine = me.yl == me.core

    for k in (1, 2, 3):
        gain_copy(0, "y", gains, got_a, k).start()
    for red in rest:
        red.one()
    for i in range(7):
        fin(1, i, False).start()
    for dp in range(2):
        keep = mine & (me.core == dp)

        @pl.when(jnp.logical_not(keep))
        def _(dp=dp):
            down(dp, me.yl).start()

        @pl.when(keep)
        def _(dp=dp):
            down_r[me.yl] = down_s[dp]

    reds["o"].two()
    fin_s[...] = fin_in[:, :, 0]
    for red in rest:
        red.arrive()
    gain_sum(0, "y", gains, got_a, sum_a)
    for k in (1, 2, 3):
        gain_copy(1, "x", sum_a, got_b, k).start()
    for red in rest:
        red.two()
    gain_sum(1, "x", sum_a, got_b, sum_b)

    def gain_mate(i):
        return push(sum_b, got_c.at[i], gain_s.at[6 + i], gain_r.at[6 + i], mate(*group[i]))

    for i in range(7):
        gain_mate(i).start()
    out_s[1] = out1[...]
    finish_columns(reds, ("ia", "ib"), fin_s)
    out_s[0] = reds["o"].three().astype(BF)

    def out_copy():
        return push(out_s, out_r, out_ss.at[0], out_ss.at[1], mirror)

    for i in range(7):
        fin(0, i, False).start()
    @pl.when(apart)
    def _():
        out_copy().start()

    @pl.when(jnp.logical_not(apart))
    def _():
        out_r[...] = out_s[...]

    fin_r[slot, 0] = fin_s[me.core, me.z]
    fin_r[slot, 1] = fin_in[me.core, me.z, 1]
    total = sum_b[...]
    for i in range(7):
        gain_mate(i).wait_recv()
        total = total + got_c[i]
    o_gains[...] = total
    for i in range(7):
        fin(0, i, True).wait_recv()
        fin(1, i, True).wait_recv()
    o_rows[...] = fin_r[...]
    for half in range(2):

        @pl.when(jnp.logical_not(mine & (me.yl == half)))
        def _(half=half):
            down(0, half).wait_recv()

    o_down[...] = down_r[...]

    @pl.when(apart)
    def _():
        out_copy().wait_recv()

    o_out[...] = out_r[...]
    reds["o"].finish((1,))
    for red in rest:
        red.finish()
    for k in (1, 2, 3):
        gain_copy(0, "y", gains, got_a, k).wait_send()
        gain_copy(1, "x", sum_a, got_b, k).wait_send()
    for i in range(7):
        gain_mate(i).wait_send()
        fin(0, i, False).wait_send()
        fin(1, i, False).wait_send()
    for dp in range(2):

        @pl.when(jnp.logical_not(mine & (me.core == dp)))
        def _(dp=dp):
            down(dp, me.yl).wait_send()

    @pl.when(apart)
    def _():
        out_copy().wait_send()


def vm(shape, dtype=BF):
    return pltpu.VMEM(shape, dtype)


def rs_scratch():
    return [vm((4, 128, WIDE)), vm((4, 128, WIDE)), vm((6, 64, WIDE)), vm((6, 64, WIDE))]


def dma(*shape):
    return pltpu.SemaphoreType.DMA(shape)


def sems():
    return [dma(n) for n in (13, 13, 13, 13, 10, 10, 10, 10, 8, 8, 8, 8, 16, 32)]


WEIGHTS = [(WIDE, 384), (256, WIDE), (WIDE, 512), (WIDE, 512), (512, WIDE)]
SPLIT = [(2, 4, 4, 48, 384), (4, 64, WIDE), (2, 4, 4, 48, 512), (2, 4, 4, 48, 512), (2, 4, 4, 16, WIDE)]
PARTS = [(2, 4, 4, 48, 384), (2, 4, 4, 48, 1024), (2, 4, 4, 16, WIDE), (4, 4, 16, WIDE)]
RING = [((256, WIDE), F32), ((4, 128, WIDE), BF)]


def run_kernel(kernel, name, cid, ins, in_vmem, outs, out_vmem, scratch):
    place = {True: pltpu.VMEM, False: pl.ANY}
    return pl.pallas_call(
        kernel,
        name=name,
        out_shape=[jax.ShapeDtypeStruct(s, d) for s, d in outs],
        in_specs=[pl.BlockSpec(memory_space=place[i < in_vmem]) for i in range(len(ins))],
        out_specs=[pl.BlockSpec(memory_space=place[i < out_vmem]) for i in range(len(outs))],
        scratch_shapes=scratch,
        compiler_params=pltpu.CompilerParams(
            collective_id=cid, has_side_effects=True, vmem_limit_bytes=58 * 2**20
        ),
    )(*ins)


def layer_fwd(l, stream, gains, tables, h_in, sources, extra):
    first = l == 0
    outs = [((128, WIDE), F32)] * (2 if first else 1) + [((8, 256), F32)] + ([((8, WIDE), F32)] if first else [])
    n_vmem = len(outs)
    outs += [
        ((1024, WIDE), BF), ((1024, 384), BF), ((1024, 256), BF), ((1024, WIDE), BF),
        ((1024, 512), BF), ((1024, 512), BF), ((1024, 512), BF),
    ] + [(s, BF) for s in SPLIT[1:]] + ([(SPLIT[0], BF)] * 2 if first else [((1024, WIDE), BF)])
    scratch = [vm(s) for s in SPLIT] + [
        vm((1024, WIDE)), vm((1024, WIDE)), vm((1024, 384)), vm((1024, 384)), vm((1024, 256)), vm((1024, 256)),
        vm((1024, 512)), vm((1024, 512)), vm((1024, 512)),
        vm((1024, 128)), vm((1024, 128)), vm((128, 1024)), vm((128, WIDE), F32),
    ] + [vm(*s) for s in RING] + rs_scratch() + sems() + [dma(10, 7), dma(10, 7)]
    if first:
        scratch += [vm((2, 4, 4, 8, 256), F32), vm(SPLIT[0])]
    else:
        scratch += [vm((1024, WIDE)), dma(13), dma(13)]
    ins = [stream] + ([] if first else [gains]) + [*tables, h_in, *sources, *extra]
    kernel = functools.partial(fwd_kernel, l)
    return run_kernel(kernel, f"layer_forward_{l}", 1 + l, ins, 5 if first else 6, outs, n_vmem, scratch)


def layer_bwd(l, grad, stream, middle, gains, tables, lse, weights, saved, above):
    last = l == 0
    outs = [((128, WIDE), F32), ((8, WIDE), F32)]
    outs += [((2, 4, 2, 16, 1408), BF), ((2, 2, 16, WIDE), BF), ((16, WIDE), BF)] if last else [((128, WIDE), BF)]
    n_vmem = len(outs)
    outs += [(s, BF) for s in PARTS]
    outs += [((3,) + REDUCE[n][3], BF) for n in (MLP + ("o",) if last else MLP)]
    shapes = WEIGHTS[:2] + [(4, 2, 4, 48, 512), (4, 2, 4, 48, 512), (4, 2, 4, 16, WIDE)]
    scratch = [vm(s) for s in shapes] + [
        vm((1024, WIDE)), vm((1024, WIDE)), vm((1024, 384)), vm((1024, 512)), vm((1024, 512)),
        vm((1024, 1024)), vm((1024, 256)), vm((1024, 256)),
        vm((1024, 128)), vm((1024, 128)), vm((128, 1024)), vm((1024, 128), F32), vm((1024, 128), F32),
        vm((1024, 256)), vm((1024, 384)), vm((1024, 384)), vm((128, WIDE), F32),
        vm((1024, 256)), vm((1024, WIDE)), vm((1024, 512)),
    ] + [vm(s) for s in PARTS] + [vm(*s) for s in RING] + rs_scratch() + sems()
    if last:
        scratch += reduce_scratch(MLP + REST, ()) + reduce_scratch(MLP, ()) + [dma(6), dma(6)]
    else:
        scratch += rs_scratch() + [dma(10), dma(10), dma(4, 6), dma(4, 6)]
    weights = [w.reshape(s) for w, s in zip(weights, shapes)]
    ins = [grad, stream, middle, gains, *tables, lse, *weights, *saved, *(above or ())]
    kernel = functools.partial(bwd_kernel, l)
    return run_kernel(kernel, f"layer_backward_{l}", 3 + l, ins, 9, outs, n_vmem, scratch)


def picks(rows, cols, test):
    r = lax.broadcasted_iota(jnp.int32, (rows, cols), 0)
    c = lax.broadcasted_iota(jnp.int32, (rows, cols), 1)
    return jnp.where(test(r, c), 1.0, 0.0).astype(BF)


def packed_place(n):
    t, i = n // 128, n % 128
    value = ((i >= 48) & (i < 64)) | (i >= 112)
    feature = jnp.where(value, 32 * t + jnp.where(i < 64, i - 48, i - 96), jnp.where(i < 48, i, i - 16))
    return t, feature, value


def prepare_kernel(
    order, wq, wk, wv, wg, wu, ga, gm, o_in, o_g, o_u, o_gain, o_cos, o_sin, o_pcol, o_prow, vq, vk, vv, vg, vu, loc
):
    core, z, yl = lax.axis_index("core"), lax.axis_index("z"), lax.axis_index("yl")
    own = pl.ds(pl.multiple_of(yl * 48, 16), 48)
    loads = [
        pltpu.make_async_copy(h.at[:, own], v, loc.at[i])
        for i, (h, v) in enumerate(((wq, vq), (wk, vk), (wv, vv), (wg, vg), (wu, vu)))
    ]
    for load in loads:
        load.start()
    ctx = lax.axis_index("x") * 2 + lax.axis_index("yh")
    for span in range(16):
        o_pcol[64 * span : 64 * span + 64] = order[span] * 64 + lax.broadcasted_iota(jnp.int32, (64, 1), 0)
    lane = lax.broadcasted_iota(jnp.int32, (1, 256), 1)
    for p in range(8):
        start = jnp.where(lane % 128 < 64, order[2 * p], order[2 * p + 1]) * 64
        o_prow[p : p + 1, :] = start + lane % 64
    row = lax.broadcasted_iota(jnp.int32, (128, 128), 0)
    col = lax.broadcasted_iota(jnp.int32, (128, 128), 1)
    place = jnp.where(row < 64, order[2 * ctx], order[2 * ctx + 1]) * 64 + row % 64
    turning = (col % 64) < 48
    freq = jnp.exp((col % 64).astype(F32) * (-2.0 * math.log(ROPE_BASE) / HEAD))
    angles = place.astype(F32) * freq
    cos = jnp.where(turning, jnp.cos(angles), 1.0)
    sin = jnp.where(turning, jnp.sin(angles), 0.0)
    sin = jnp.where(col < 64, -sin, sin)
    for half in range(2):
        o_cos[128 * half : 128 * half + 128] = cos
        o_sin[128 * half : 128 * half + 128] = sin
    owner = core * 8 + ctx
    shift = lax.rem(96 * owner, 128)
    move = picks(96, 256, lambda r, c: c == r + shift)
    zero = jnp.zeros((4, 96), F32)
    both = jnp.concatenate([ga[0:1], gm[0:1], ga[1:2], gm[1:2]], axis=0).astype(F32)
    placed = mm(jnp.concatenate([both, zero], axis=0).astype(BF), move)
    o_gain[0] = placed
    o_gain[1] = placed
    spread = [
        picks(1024, 128, lambda r, c, j=cc * 4 + z: (r // 256 == c // 32) & (r % 256 == 32 * j + c % 32)) for cc in range(2)
    ]
    spread = jnp.concatenate(spread, axis=1)

    def query(r, n, j):
        t, f, value = packed_place(n)
        return jnp.logical_not(value) & (t < 2) & (r == j * 192 + t * 96 + f)

    def key(r, n, j):
        t, f, value = packed_place(n)
        return jnp.logical_not(value) & (t == 2) & (r == j * 96 + f)

    def val(r, n, j):
        t, f, value = packed_place(n)
        return value & (r == j * 96 + f)

    for load in loads[:3]:
        load.wait()
    for cc in range(2):
        j = cc * 4 + z
        out = mm(vq[...].reshape(96, WIDE), picks(WIDE, 384, lambda r, n: query(r, n, j)))
        out = out + mm(vk[...].reshape(96, 768), picks(768, 384, lambda r, n: key(r, n, j)))
        out = out + mm(vv[...].reshape(96, 768), picks(768, 384, lambda r, n: val(r, n, j)))
        o_in[:, cc] = out.astype(BF).reshape(LAYERS, 48, 384)
    for load in loads[3:]:
        load.wait()
    for v, o in ((vg, o_g), (vu, o_u)):
        for b in range(4):
            out = mm(v[:, :, 1024 * b : 1024 * b + 1024].reshape(96, 1024), spread).astype(BF)
            for cc in range(2):
                o[:, cc, :, 128 * b : 128 * b + 128] = out[:, 128 * cc : 128 * cc + 128].reshape(LAYERS, 48, 128)


def prepare(order, wq, wk, wv, wg, wu, ga, gm):
    shapes = [((LAYERS, 2, 48, 384), BF), ((LAYERS, 2, 48, 512), BF), ((LAYERS, 2, 48, 512), BF), ((2, 8, 256), F32)]
    shapes += [((256, 128), F32), ((256, 128), F32), ((1024, 1), jnp.int32), ((8, 256), jnp.int32)]
    in_vmem = pl.BlockSpec(memory_space=pltpu.VMEM)
    return pl.pallas_call(
        prepare_kernel,
        name="prepare_sources",
        out_shape=[jax.ShapeDtypeStruct(s, d) for s, d in shapes],
        in_specs=[pl.BlockSpec(memory_space=pltpu.SMEM)] + [pl.BlockSpec(memory_space=pl.ANY)] * 5 + [in_vmem] * 2,
        out_specs=[in_vmem] * 8,
        scratch_shapes=[vm((LAYERS, 48, n)) for n in (WIDE, 768, 768, 4096, 4096)] + [dma(5)],
        compiler_params=pltpu.CompilerParams(vmem_limit_bytes=60 * 2**20),
    )(order, wq, wk, wv, wg, wu, ga, gm)


def assemble_kernel(cols, downs, outs, o_q, o_k, o_v, o_o, o_g, o_u, o_d):
    def member(j, lo, hi):
        return cols[j % 4 * 2 + j // 4, :, :, lo:hi].reshape(32, hi - lo)

    def put(dst, lo, hi, value):
        for l in range(LAYERS):
            dst[:, l, lo:hi] = value[16 * l : 16 * l + 12]

    def query(n, c, i):
        t, f, value = packed_place(n)
        return jnp.logical_not(value) & (t < 2) & (c == i * 192 + t * 96 + f)

    def key(n, c, i):
        t, f, value = packed_place(n)
        return jnp.logical_not(value) & (t == 2) & (c == i * 96 + f)

    def val(n, c, i):
        t, f, value = packed_place(n)
        return value & (c == i * 96 + f)

    for dst, test, per in ((o_q, query, 2), (o_k, key, 4), (o_v, val, 4)):
        moves = [picks(384, 384, lambda n, c, i=i: test(n, c, i)) for i in range(per)]
        for m in range(8 // per):
            total = sum(mm(member(per * m + i, 0, 384), moves[i]) for i in range(per))
            put(dst, 384 * m, 384 * m + 384, total)
    back = [picks(128, 1024, lambda r, c, j=j: (c // 256 == r // 32) & (c % 256 == 32 * j + r % 32)) for j in range(8)]
    for dst, start in ((o_g, 384), (o_u, 896)):
        for b in range(4):
            total = sum(mm(member(j, start + 128 * b, start + 128 * b + 128), back[j]) for j in range(8))
            put(dst, 1024 * b, 1024 * b + 1024, total)
    for l in range(LAYERS):
        o_o[:, l, :] = outs[l, 0:12].astype(F32)
        for h in range(2):
            o_d[l, 16 * h : 16 * h + 16] = downs[h, l].astype(F32)


def assemble(cols, downs, outs):
    shapes = [(12, LAYERS, n) for n in (WIDE, 768, 768, WIDE, 4096, 4096)] + [(LAYERS, 32, WIDE)]
    in_vmem = pl.BlockSpec(memory_space=pltpu.VMEM)
    *grads, d_d = pl.pallas_call(
        assemble_kernel,
        name="assemble_gradients",
        out_shape=[jax.ShapeDtypeStruct(s, F32) for s in shapes],
        in_specs=[in_vmem] * 3,
        out_specs=[in_vmem] * 7,
        compiler_params=pltpu.CompilerParams(vmem_limit_bytes=60 * 2**20),
    )(cols, downs, outs)
    return [grad.transpose(1, 0, 2) for grad in grads] + [d_d]


def reduce_grads(gain_parts, done, parts):
    outs = [((8, 2, 16, 1408), BF), ((2, 2, 16, WIDE), BF), ((2, 16, WIDE), BF), ((8, WIDE), F32)]
    scratch = reduce_scratch(REST, REST) + [
        vm((8, WIDE), F32), vm((2, 4, 16, 1408)), vm((8, 2, 16, 1408)), vm((2, 2, 16, WIDE)),
        vm((2, 16, WIDE)), vm((2, 16, WIDE)), vm((8, WIDE), F32), vm((8, WIDE), F32),
        vm((3, 8, WIDE), F32), vm((3, 8, WIDE), F32), vm((7, 8, WIDE), F32),
        dma(2, 7), dma(2, 7), dma(13), dma(13), dma(2), dma(2), dma(2),
    ]
    return run_kernel(grads_kernel, "reduce_gradients", 5, [*gain_parts, *done, *parts], 5, outs, 4, scratch)


def body(
    tokens, span_order, attn_gain, w_query, key_matrix, value_matrix, w_out, mlp_gain, w_gate, w_up,
    w_down, cotangent,
):
    core, z, yl = lax.axis_index("core"), lax.axis_index("z"), lax.axis_index("yl")
    ctx = lax.axis_index("x") * 2 + lax.axis_index("yh")
    s_in, s_g, s_u, s_gain, *tables = prepare(
        span_order, w_query, key_matrix, value_matrix, w_gate, w_up, attn_gain, mlp_gain
    )
    stream, gains = tokens[0], None
    kept = []
    sources = (w_out, w_down, s_g, s_u)
    outs = layer_fwd(0, stream, gains, tables, s_in, sources, (s_gain, s_in))
    gains, w_next = outs[3], outs[-1]
    kept.append((stream, outs[1:3], outs[-2], outs[4:-2]))
    stream = outs[0]
    outs = layer_fwd(1, stream, gains, tables, w_next, sources, (cotangent[0],))
    kept.append((stream, outs[:2], w_next, outs[2:-1]))
    down_grad = outs[-1]

    g, gain_parts, above = cotangent[0], [None] * LAYERS, (down_grad,)
    for l in reversed(range(LAYERS)):
        stream, (middle, lse), w_in, outs = kept[l]
        normed, qkv, mixed, nmlp, gate, up, hid = outs[:7]
        saved = (qkv, gate, up, normed, mixed, nmlp, hid)
        res = layer_bwd(l, g, stream, middle, gains, tables, lse, (w_in, *outs[7:]), saved, above)
        g, gain_parts[l] = res[:2]
        if l:
            block_out, above = res[2][None], tuple(res[3:])
    cols, d_d, d_o, gp = reduce_grads(gain_parts, res[2:5], (res[5], res[8], res[13]))
    d_q, d_k, d_v, d_o, d_g, d_u, d_d = assemble(cols, d_d, d_o)
    owner = (core * 8 + ctx) * 8 + yl * 4 + z
    gp = lax.dynamic_slice(gp, (0, owner * 12), (4, 12)).reshape(2, 2, 12)
    return (block_out, g[None], gp[:, 0], d_q, d_k, d_v, d_o, gp[:, 1], d_g, d_u, d_d)


def solution(mesh):
    fine = Mesh(mesh.devices.reshape(2, 4, 2, 2, 4), ALL)
    seq, ctx, own, every = ("core", "yl", "z"), CTX, OWN, ALL
    act = P(seq, ctx, None)
    in_specs = (act, P(), P(None, own)) + (P(None, own, None),) * 4 + (P(None, own),) + (P(None, own, None),) * 3 + (act,)
    grad = P(None, every, None)
    out_specs = (act, act, P(None, every)) + (grad,) * 4 + (P(None, every),) + (grad,) * 3
    return jax.shard_map(body, mesh=fine, in_specs=in_specs, out_specs=out_specs, check_vma=False)
```

```python
import functools
import math

import jax
import jax.numpy as jnp
import numpy as np
from jax import lax
from jax.experimental import pallas as pl
from jax.experimental.pallas import tpu as pltpu
from jax.sharding import Mesh, PartitionSpec as P

HEAD = 96
LAYERS = 2
ROPE_BASE = 100000.0
EPS = 1e-05
CTX = ("x", "yh")
TP = ("z", "core")
OWN = ("core", "x", "yh")
ALL = ("core", "x", "yh", "yl", "z")
BF = jnp.bfloat16
F32 = jnp.float32
MESH = pl.DeviceIdType.MESH
SCALE = 1.0 / math.sqrt(HEAD)
SCALE2 = SCALE * math.log2(math.e)
WIDE = 1536


def mm(a, b):
    return jnp.dot(a, b, preferred_element_type=F32)


def mm_tn(a, b):
    return lax.dot_general(a, b, (((0,), (0,)), ((), ())), preferred_element_type=F32)


def mm_nt(a, b):
    return lax.dot_general(a, b, (((1,), (1,)), ((), ())), preferred_element_type=F32)


class Place:
    def __init__(self):
        self.z, self.core = lax.axis_index("z"), lax.axis_index("core")
        self.x, self.yh, self.yl = lax.axis_index("x"), lax.axis_index("yh"), lax.axis_index("yl")
        self.y = self.yh * 2 + self.yl
        self.c = self.x * 2 + self.yh
        self.zp, self.zm, self.zo = (lax.rem(self.z + k, 4) for k in (1, 3, 2))
        self.oc = 1 - self.core

    def near(self, axis, k):
        if axis == "x":
            return {"x": lax.rem(self.x + k, 4)}
        return at_y(lax.rem(self.y + k, 4))

    def greet(self, others, mirror=False):
        barrier = pltpu.get_barrier_semaphore()
        for dev in others:
            pl.semaphore_signal(barrier, inc=1, device_id=dev, device_id_type=MESH)
        if not mirror:
            pl.semaphore_wait(barrier, len(others))
            return

        @pl.when(self.x != self.z)
        def _():
            there = {"x": self.z, "z": self.x}
            pl.semaphore_signal(barrier, inc=1, device_id=there, device_id_type=MESH)
            pl.semaphore_wait(barrier, len(others) + 1)

        @pl.when(self.x == self.z)
        def _():
            pl.semaphore_wait(barrier, len(others))

    def layer_partners(self):
        return (
            [{"z": self.zp}, {"z": self.zm}, {"core": self.oc}]
            + [at_ctx(lax.rem(self.c + k, 8)) for k in range(1, 8)]
            + [{"yl": 1 - self.yl}, {"yh": 1 - self.yh, "yl": 1 - self.yl}]
        )


def at_y(y):
    return {"yh": y // 2, "yl": lax.rem(y, 2)}


def at_ctx(c):
    return {"x": c // 2, "yh": lax.rem(c, 2)}


def span_of(start, size):
    return pl.ds(pl.multiple_of(start, 64), size)


def slot_rows(zz, cc, half=None):
    base = (zz * 2 + cc) * 128
    return span_of(base, 128) if half is None else span_of(base + 64 * half, 64)


def all_gather(*args):
    return run(gather_steps(*args))


def run(steps):
    while True:
        try:
            next(steps)
        except StopIteration as stop:
            return stop.value


def gather_steps(me, buf, ssem, rsem, on_pair, hooks=()):
    z, zp, zm, zo, core, oc = me.z, me.zp, me.zm, me.zo, me.core, me.oc
    up, down, across = {"z": zp}, {"z": zm}, {"core": oc}
    sent = [
        (z, core, 0, up), (z, core, 1, up), (z, core, 1, down), (z, core, 0, down),
        (zm, core, 0, up), (zp, core, 1, down), (z, core, None, across),
        (zm, core, 0, across), (zm, core, 1, across), (zp, core, 1, across), (zp, core, 0, across),
        (zo, core, 0, across), (zo, core, 1, across),
    ]
    come = [
        (zm, core, 0), (zm, core, 1), (zp, core, 1), (zp, core, 0), (zo, core, 0), (zo, core, 1),
        (z, oc, None), (zm, oc, 0), (zm, oc, 1), (zp, oc, 1), (zp, oc, 0), (zo, oc, 0), (zo, oc, 1),
    ]

    def copy(i, rows, dev):
        return pltpu.make_async_remote_copy(
            src_ref=buf.at[rows], dst_ref=buf.at[rows], send_sem=ssem.at[i], recv_sem=rsem.at[i],
            device_id=dev, device_id_type=MESH,
        )

    def send(*which):
        for i in which:
            copy(i, slot_rows(*sent[i][:3]), sent[i][3]).start()

    def arrive(*which):
        for i in which:
            copy(i, slot_rows(*come[i]), sent[i][3]).wait_recv()

    def hook(i):
        if i < len(hooks):
            hooks[i]()

    send(0, 2, 1, 3, 6)
    hook(0)
    yield
    arrive(6)
    on_pair(z)
    arrive(0)
    send(4, 7)
    arrive(2)
    send(5, 9)
    hook(1)
    arrive(1)
    send(8)
    arrive(3)
    send(10)
    hook(2)
    yield
    arrive(7, 8)
    on_pair(zm)
    arrive(9, 10)
    on_pair(zp)
    hook(3)
    arrive(4)
    send(11)
    arrive(5)
    send(12)
    yield
    arrive(11, 12)
    on_pair(zo)

    def finish():
        for i in range(13):
            copy(i, slot_rows(*sent[i][:3]), sent[i][3]).wait_send()

    return finish


def reduce_scatter(*args):
    return run(reduce_steps(*args))


def reduce_steps(me, part, whole, keep, give, take, ring_out, ring_in, ssem, rsem, fill=lambda n: None):
    z, zp, zm, zo, core, oc = me.z, me.zp, me.zm, me.zo, me.core, me.oc
    up, down, across = {"z": zp}, {"z": zm}, {"core": oc}
    mine = span_of(core * 128, 128)
    theirs = span_of(oc * 128, 128)

    def swap(k):
        return pltpu.make_async_remote_copy(
            src_ref=give.at[k], dst_ref=take.at[k], send_sem=ssem.at[k], recv_sem=rsem.at[k],
            device_id=across, device_id_type=MESH,
        )

    def ring(i):
        return pltpu.make_async_remote_copy(
            src_ref=ring_out.at[i], dst_ref=ring_in.at[i], send_sem=ssem.at[4 + i], recv_sem=rsem.at[4 + i],
            device_id=up if i < 3 else down, device_id_type=MESH,
        )

    def make(k, zz):
        whole[...] = part(zz)
        give[k] = whole[theirs].astype(BF)
        keep[k] = whole[mine].astype(BF)
        swap(k).start()

    def merged(k, half):
        rows = slice(64 * half, 64 * half + 64)
        return keep[k, rows].astype(F32) + take[k, rows].astype(F32)

    def push(i, value):
        ring_out[i] = value.astype(BF)
        ring(i).start()

    make(0, zo)
    make(1, zp)
    swap(0).wait_recv()
    push(0, merged(0, 0))
    push(3, merged(0, 1))
    make(2, zm)
    swap(1).wait_recv()
    push(1, merged(1, 1))
    swap(2).wait_recv()
    push(4, merged(2, 0))
    make(3, z)
    fill(0)
    yield
    ring(0).wait_recv()
    push(2, merged(1, 0) + ring_in[0].astype(F32))
    ring(3).wait_recv()
    push(5, merged(2, 1) + ring_in[3].astype(F32))
    swap(3).wait_recv()
    fill(1)
    own = [merged(3, 0), merged(3, 1)]
    ring(1).wait_recv()
    own[1] = own[1] + ring_in[1].astype(F32)
    ring(4).wait_recv()
    own[0] = own[0] + ring_in[4].astype(F32)
    fill(2)
    yield
    ring(2).wait_recv()
    own[0] = own[0] + ring_in[2].astype(F32)
    ring(5).wait_recv()
    own[1] = own[1] + ring_in[5].astype(F32)

    def finish():
        for k in range(4):
            swap(k).wait_send()
        for i in range(6):
            ring(i).wait_send()

    return jnp.concatenate(own, axis=0), finish


def ctx_of(slot, core):
    zz, cc = slot // 2, lax.rem(slot, 2)
    return lax.rem(zz + 2 * cc + core, 4) * 2 + cc


def slot_of(ctx, core):
    x, yh = ctx // 2, lax.rem(ctx, 2)
    return lax.rem(x + 2 * yh + 3 * core, 4) * 2 + yh


class Exchange:
    def __init__(self, me, src, dst, ssem, rsem, out):
        self.me, self.src, self.dst, self.ssem, self.rsem = me, src, dst, ssem, rsem
        same = lambda v: v
        ctx, slot = (lambda v, f=f: f(v, me.core) for f in (ctx_of, slot_of))
        self.to, self.block, self.lands = (ctx, slot, same) if out else (same, same, slot)

    def copy(self, b, come):
        return pltpu.make_async_remote_copy(
            src_ref=self.src.at[span_of(b * 128, 128)], dst_ref=self.dst.at[span_of(come * 128, 128)],
            send_sem=self.ssem.at[b], recv_sem=self.rsem.at[come],
            device_id=at_ctx(self.to(b)), device_id_type=MESH,
        )

    def send(self, b):
        there, come = self.to(b), self.lands(self.me.c)

        @pl.when(there != self.me.c)
        def _():
            self.copy(b, come).start()

        @pl.when(there == self.me.c)
        def _():
            self.dst[span_of(come * 128, 128)] = self.src[span_of(b * 128, 128)]

    def arrive(self):
        @pl.loop(1, 8)
        def _(k):
            there = lax.rem(self.me.c + k, 8)
            self.copy(self.block(there), self.lands(there)).wait_recv()

    def finish(self):
        @pl.loop(1, 8)
        def _(k):
            there = lax.rem(self.me.c + k, 8)
            self.copy(self.block(there), self.lands(self.me.c)).wait_send()


def push(src, dst, ssem, rsem, dev):
    return pltpu.make_async_remote_copy(
        src_ref=src, dst_ref=dst, send_sem=ssem, recv_sem=rsem, device_id=dev, device_id_type=MESH
    )


class Gather:
    def __init__(self, me, src, dst, ssem, rsem, loc, order, cols):
        self.me, self.src, self.dst, self.ssem, self.rsem, self.order = me, src, dst, ssem, rsem, order
        self.loc, self.cols = loc, slice(*cols)

    def own(self):
        me = self.me
        return pltpu.make_async_copy(
            self.src(me.core, self.cols), self.dst.at[me.core, me.x, me.y, :, self.cols], self.loc
        )

    def cross(self, come=False):
        me = self.me
        row = me.oc if come else me.core
        return push(
            self.src(me.oc, self.cols), self.dst.at[row, me.x, me.y, :, self.cols],
            self.ssem.at[0], self.rsem.at[0], {"core": me.oc},
        )

    def region(self, stage, k):
        me = self.me
        x, y = (lax.rem(v + 4 - k, 4) for v in (me.x, me.y))
        if stage == 0:
            return self.dst.at[:, x if self.order[0] == "x" else me.x, y if self.order[0] == "y" else me.y, :, self.cols]
        if self.order[1] == "y":
            return self.dst.at[:, :, y, :, self.cols]
        return self.dst.at[:, x, :, :, self.cols]

    def copy(self, stage, k, come):
        ref = self.region(stage, k if come else 0)
        i = 1 + 3 * stage + k - 1
        return push(ref, ref, self.ssem.at[i], self.rsem.at[i], self.me.near(self.order[stage], k))

    def zero(self):
        self.own().start()
        self.cross().start()

    def one(self):
        self.own().wait()
        self.cross(True).wait_recv()
        for k in (2, 1, 3):
            self.copy(0, k, False).start()

    def two(self):
        for k in (1, 3, 2):
            self.copy(0, k, True).wait_recv()
        for k in (2, 1, 3):
            self.copy(1, k, False).start()

    def three(self):
        for k in (1, 3, 2):
            self.copy(1, k, True).wait_recv()

    def finish(self):
        self.cross().wait_send()
        for stage in (0, 1):
            for k in (1, 2, 3):
                self.copy(stage, k, False).wait_send()


class OutGather:
    def __init__(self, me, src, dst, ssem, rsem, loc):
        self.me, self.dst, self.ssem, self.rsem = me, dst, ssem, rsem
        self.src, self.loc = src, loc
        self.far = lax.rem(me.x + 4 - me.z, 4)

    def copy(self, stage, k, come):
        me = self.me
        y = lax.rem(me.y + 4 - k, 4) if stage and come else me.y
        ref, i = self.dst.at[y], 3 * stage + k - 1
        return push(ref, ref, self.ssem.at[i], self.rsem.at[i], me.near("xy"[stage], k))

    def own(self):
        y, yl = self.me.y, self.me.yl
        return [
            pltpu.make_async_copy(
                self.src.at[pl.ds(pl.multiple_of(row, 16), 16)], self.dst.at[y, to : to + 16], self.loc.at[i]
            )
            for i, (row, to) in enumerate(((48 - 16 * yl, 0), (80 - 16 * yl, 16), (16 * yl, 48)))
        ]

    def zero(self):
        @pl.when(self.far == 0)
        def _():
            for copy in self.own():
                copy.start()
            self.dst[self.me.y, 32:48] = jnp.zeros((16, WIDE), BF)

    def one(self):
        @pl.when(self.far == 0)
        def _():
            for copy in self.own():
                copy.wait()
            for k in (2, 1, 3):
                self.copy(0, k, False).start()

    def two(self):
        for k in (1, 2, 3):

            @pl.when(self.far == k)
            def _(k=k):
                self.copy(0, k, True).wait_recv()

        for k in (2, 1, 3):
            self.copy(1, k, False).start()

    def three(self):
        for k in (1, 3, 2):
            self.copy(1, k, True).wait_recv()

    def finish(self):
        @pl.when(self.far == 0)
        def _():
            for k in (1, 2, 3):
                self.copy(0, k, False).wait_send()

        for k in (1, 2, 3):
            self.copy(1, k, False).wait_send()


class Reduce:
    def __init__(self, me, spec, mine, got1, sum1, got2, ssem, rsem, loc, land=None, landed=False):
        self.me = me
        self.quarter, self.inner, self.order = spec[:3]
        self.mine, self.got1, self.sum1, self.got2, self.ssem, self.rsem, self.loc = mine, got1, sum1, got2, ssem, rsem, loc
        self.land, self.landed = land, landed

    def at(self, axis, k):
        return lax.rem((self.me.x if axis == "x" else self.me.y) + k, 4)

    def copy(self, stage, k):
        axis = self.order[stage]
        to = self.at(axis, k)
        src = self.inner(self.sum1, to) if stage else self.quarter(axis, to)
        dst = self.got2.at[k - 1] if stage else self.got1[k - 1] if self.land is None else self.land.at[k - 1]
        i = 3 * stage + k - 1
        return push(src, dst, self.ssem.at[i], self.rsem.at[i], self.me.near(axis, k))

    def loads(self):
        axis = self.order[0]
        out = [pltpu.make_async_copy(self.quarter(axis, self.at(axis, 0)), self.mine, self.loc.at[0])]
        if self.land is not None:
            for k in range(3):
                out.append(pltpu.make_async_copy(self.land.at[k], self.got1[k], self.loc.at[1 + k]))
        return out

    def load(self):
        for load in self.loads():
            load.start()

    def one(self):
        for k in (2, 1, 3):
            self.copy(0, k).start()

    def arrive(self):
        if not self.landed:
            for k in (1, 2, 3):
                self.copy(0, k).wait_recv()

    def two(self):
        for load in self.loads():
            load.wait()
        dims = self.sum1.shape[:-2]

        @pl.loop(0, math.prod(dims))
        def _(n):
            at = (n,) if len(dims) == 1 else (n // dims[1], lax.rem(n, dims[1]))
            total = self.mine[at].astype(F32)
            for k in range(3):
                total = total + self.got1[k][at].astype(F32)
            self.sum1[at] = total.astype(BF)

        for k in (2, 1, 3):
            self.copy(1, k).start()

    def three(self):
        for k in (1, 2, 3):
            self.copy(1, k).wait_recv()
        total = self.inner(self.sum1, self.at(self.order[1], 0))[...].astype(F32)
        for k in range(3):
            total = total + self.got2[k].astype(F32)
        return total

    def finish(self, stages=(0, 1)):
        for stage in stages:
            for k in (1, 2, 3):
                self.copy(stage, k).wait_send()


def reduce_specs(d_in, d_gu, d_d, d_o):
    def split(ref, lo, hi, r, order):
        def quarter(axis, i):
            return ref.at[:, i, :, :, lo:hi] if axis == "x" else ref.at[:, :, i, :, lo:hi]

        return quarter, lambda q, i: q.at[:, i], order, (2, 4, r, hi - lo), (2, r, hi - lo)

    return {
        "g": split(d_gu, 0, 512, 48, "yx"),
        "u": split(d_gu, 512, 1024, 48, "xy"),
        "da": split(d_d, 0, 768, 16, "yx"),
        "db": split(d_d, 768, 1536, 16, "xy"),
        "ia": split(d_in, 0, 256, 48, "yx"),
        "ib": split(d_in, 256, 384, 48, "xy"),
        "o": (lambda axis, i: d_o.at[:, i], lambda q, i: q.at[i], "xy", (4, 16, WIDE), (16, WIDE)),
    }


REDUCE = reduce_specs(None, None, None, None)
def reduce_scratch(names, staged):
    out = []
    for name in names:
        big, small = REDUCE[name][3:]
        out += [vm(big), vm((3,) + big)] if name in staged else []
        out += [vm(big), vm((3,) + small)]
    n = len(names)
    return out + [dma(n, 6), dma(n, 6), dma(n, 4)]


def make_reduces(me, names, parts, refs, land=None, landed=(), stage=None):
    specs, out = reduce_specs(*parts), {}
    for name in names:
        if stage and name in stage:
            own, got = stage[name]
        else:
            own, got = refs.pop(0), refs.pop(0)
            got = [got.at[k] for k in range(3)]
        out[name] = (own, got, refs.pop(0), refs.pop(0))
    ssem, rsem, loc = refs.pop(0), refs.pop(0), refs.pop(0)
    for n, (name, bufs) in enumerate(out.items()):
        there = land.get(name) if land else None
        out[name] = Reduce(me, specs[name], *bufs, ssem.at[n], rsem.at[n], loc.at[n], there, name in landed)
    return out


COLUMNS = {"ia": (0, 256), "ib": (256, 384), "g": (384, 896), "u": (896, 1408)}
MLP = ("g", "u", "da", "db")
REST = ("ia", "ib", "o")


def finish_columns(reds, names, fin):
    for name in names:
        lo, hi = COLUMNS[name]
        total = reds[name].three()
        for dp in range(2):
            for z in range(4):
                fin[dp, z, :, lo:hi] = padded(total[dp, 12 * z : 12 * z + 12])


def finish_down(reds, down):
    down[:, :, 0:768] = reds["da"].three().astype(BF)
    down[:, :, 768:1536] = reds["db"].three().astype(BF)


def lane_masks(rows):
    lane = lax.broadcasted_iota(jnp.int32, (rows, 128), 1)
    v0 = ((lane >= 48) & (lane < 64)) | (lane >= 112)
    v1 = ((lane >= 64) & (lane < 80)) | (lane < 16)
    v2 = ((lane >= 80) & (lane < 96)) | ((lane >= 16) & (lane < 32))
    return v0, v1, v2


def split_packed(packed, key_ref, value_ref):
    v0, v1, v2 = lane_masks(128)

    @pl.loop(0, 8)
    def _(p):
        rows = span_of(p * 128, 128)
        t0, t1, t2 = (packed[rows, 128 * t : 128 * t + 128].astype(F32) for t in range(3))
        key_ref[rows] = jnp.where(v0, 0.0, t2).astype(BF)
        value = jnp.where(v0, t0, 0.0)
        value = value + jnp.where(v1, pltpu.roll(t1, 16, 1), 0.0)
        value = value + jnp.where(v2, pltpu.roll(t2, 32, 1), 0.0)
        value_ref[rows] = value.astype(BF)


def flip(ref):
    return jnp.transpose(ref[...].astype(F32)).astype(BF)


def stacked(ref, rows):
    return jnp.concatenate([ref[rows, 0:128], ref[rows, 128:256]], axis=0)


def rms_of(values):
    return lax.rsqrt(jnp.mean(values * values, axis=-1, keepdims=True) + EPS)


def fwd_kernel(l, *refs):
    first = l == 0
    g_attn, g_mlp = (slice(2 * l + i, 2 * l + i + 1) for i in (0, 1))
    refs = list(refs)
    take = lambda n: [refs.pop(0) for _ in range(n)]
    (stream,) = take(1)
    (gains_in,) = (None,) if first else take(1)
    cos, sin, pcol, prow = take(4)
    (h_in,) = take(1)
    w_out, w_down, s_g, s_u = take(4)
    s_gain, s_next = take(2) if first else (None, None)
    (cot,) = (None,) if first else take(1)
    (o_stream,) = take(1) if first else (None,)
    o_middle, o_lse = take(2)
    (o_gains,) = take(1) if first else (gains_in,)
    o_normed, o_qkv, o_mixed, o_nmlp, o_gate, o_up, o_hidden, o_wo, o_wg, o_wu, o_wd = take(11)
    o_win, o_next = take(2) if first else (None, None)
    (o_down,) = (None,) if first else take(1)
    w_in, w_o, w_g, w_u, w_d = take(5)
    buf1, buf2, qs, qr, ms, mr, gate_v, up_v, hid, keys, vals, vals_t, middle = take(13)
    whole, keep, give, got, ring_out, ring_in = take(6)
    ag_s, ag_r, ag2_s, ag2_r, rs_s, rs_r, rs2_s, rs2_r, ax_s, ax_r, bx_s, bx_r, loc, loc2, ga_s, ga_r = take(16)
    w_gain, w_next = take(2) if first else (None, None)
    cot_all, cot_s, cot_r = (None,) * 3 if first else take(3)
    me = Place()
    stores = []

    def store(src, dst):
        stores.append(pltpu.make_async_copy(src, dst, loc2.at[len(stores)]))
        stores[-1].start()

    n_item = [0]

    def down_rows(core, cols):
        row = pl.multiple_of((core * 4 + me.z) * 32 + me.yl * 16, 16)
        return w_down.at[l, pl.ds(row, 16), cols]

    def item(src, dst, order, *cols):
        i = n_item[0]
        n_item[0] += 1
        if not callable(src):
            src = lambda core, cols, ref=src: ref.at[core, :, cols]
        return Gather(me, src, dst, ga_s.at[i], ga_r.at[i], loc.at[i], order, cols)

    g_g, g_u = item(s_g.at[l], w_g, "xy", 0, 512), item(s_u.at[l], w_u, "yx", 0, 512)
    g_d = [item(down_rows, w_d, "xy", 0, 768), item(down_rows, w_d, "yx", 768, WIDE)]
    g_o = OutGather(me, w_out.at[l], w_o, ga_s.at[4], ga_r.at[4], loc.at[pl.ds(10, 3)])
    n_item[0] = 5
    g_in, g_next, g_gain = [], [], []
    if first:
        g_gain = [item(s_gain, w_gain, "yx", 0, 256)]
        g_in = [item(h_in.at[0], w_in, "yx", 0, 256), item(h_in.at[0], w_in, "xy", 256, 384)]
        g_next = [item(s_next.at[1], w_next, "yx", 0, 256), item(s_next.at[1], w_next, "xy", 256, 384)]
    everything = g_gain + g_in + [g_o, g_g, g_u] + g_d + g_next

    def each(items, step):
        for one in items:
            getattr(one, step)()

    own_rows = slot_rows(me.z, me.core)
    raw = buf2 if first else buf1
    if first:
        raw[own_rows] = stream[...]
    else:
        load_in = pltpu.make_async_copy(h_in, w_in, loc.at[5])
        load_in.start()
        load_cot = pltpu.make_async_copy(cot, cot_all.at[own_rows], loc.at[6])
        load_cot.start()
        s = stream[...]
        raw[own_rows] = (s * rms_of(s) * gains_in[g_attn, :]).astype(BF)
    me.greet(me.layer_partners())
    each(everything, "zero")
    ax = Exchange(me, qs, qr, ax_s, ax_r, True)

    def project(zz):
        rows = span_of(zz * 256, 256)
        y = mm(buf1[rows], w_in[...].reshape(WIDE, 384))
        for t in range(3):
            tile = y[:, 128 * t : 128 * t + 128]
            tile = tile * cos[...] + pltpu.roll(tile, 64, 1) * sin[...]
            qs[rows, 128 * t : 128 * t + 128] = tile.astype(BF)
        ax.send(zz * 2)
        ax.send(zz * 2 + 1)

    def normalise(zz):
        rows = span_of(zz * 256, 256)
        s = raw[rows].astype(F32)
        buf1[rows] = (s * rms_of(s) * o_gains[g_attn, :]).astype(BF)

    if first:

        def own_pair():
            each(g_gain + g_in, "two")

        def gains_here():
            each(g_gain, "three")
            o_gains[...] = jnp.zeros_like(o_gains)
            for owner in range(16):
                base = 96 * owner // 128 * 128
                width = min(256, WIDE - base)
                row = w_gain[owner // 8, owner % 8 // 2, owner % 2 * 2]
                o_gains[:, base : base + width] += row[:, :width]
            normalise(me.z)
            g_o.one()

        hooks = (lambda: each(g_gain + g_in, "one"), own_pair, gains_here)

        def others(zz):
            if zz is not me.z:
                normalise(zz)

        done_ag = all_gather(me, raw, ag_s, ag_r, others, hooks)
        done_ag()
        each(g_in, "three")

        @pl.loop(0, 4)
        def _(k):
            project(lax.rem(me.z + k, 4))

    else:
        load_in.wait()
        done_ag = all_gather(me, raw, ag_s, ag_r, project, (g_o.one,))
        load_cot.wait()
        ring = gather_steps(me, cot_all, cot_s, cot_r, lambda zz: None)
        next(ring)
    g_o.two()
    each((g_g, g_u), "one")
    ax.arrive()
    if not first:
        next(ring)
    store(buf1, o_normed)
    store(qr, o_qkv)
    split_packed(qr, keys, vals)
    vals_t[...] = flip(vals)
    bx = Exchange(me, ms, mr, bx_s, bx_r, False)

    @pl.loop(0, 8)
    def _(k):
        p = lax.rem(me.c + 1 + k, 8)
        rows = span_of(p * 128, 128)
        q = stacked(qr, rows)
        scores = mm_nt(keys[...], q)
        scores = jnp.where(pcol[...] <= prow[pl.ds(p, 1), :], scores, -1e30)
        top = jnp.max(scores, axis=0, keepdims=True)
        weights = jnp.exp2((scores - top) * SCALE2)
        total = jnp.sum(weights, axis=0, keepdims=True)
        o_lse[pl.ds(p, 1), :] = top * SCALE2 + jnp.log2(total)
        probs = (weights * (1.0 / total)).astype(BF)
        out = jnp.transpose(mm(vals_t[...], probs)).astype(BF)
        ms[rows, 0:128] = out[0:128]
        ms[rows, 128:256] = out[128:256]
        bx.send(p)

    each((g_g, g_u), "two")
    if not first:
        next(ring)
    each(g_d, "one")
    g_o.three()
    bx.arrive()
    store(mr, o_mixed)

    def out_part(zz):
        return mm(mr[span_of(zz * 256, 256)], w_o[...].reshape(256, WIDE))

    rs = (whole, keep, give, got, ring_out, ring_in)
    total, done_rs = reduce_scatter(me, out_part, *rs, rs_s, rs_r)
    mid = total + (stream[...].astype(F32) if first else stream[...])
    middle[...] = mid
    o_middle[...] = mid
    buf2[own_rows] = (mid * rms_of(mid) * o_gains[g_mlp, :]).astype(BF)
    waited = []
    if not first:
        done_cot = run(ring)
        store(cot_all, o_down)

    def gated(zz):
        if not waited:
            waited.append(1)
            each((g_g, g_u), "three")
        rows = span_of(zz * 256, 256)
        gate = mm(buf2[rows], w_g[...].reshape(WIDE, 512))
        gate_v[rows] = gate.astype(BF)
        up = mm(buf2[rows], w_u[...].reshape(WIDE, 512))
        up_v[rows] = up.astype(BF)
        hid[rows] = (gate / (1.0 + jnp.exp(-gate)) * up).astype(BF)
        for src, dst in ((buf2, o_nmlp), (gate_v, o_gate), (up_v, o_up), (hid, o_hidden)):
            store(src.at[rows], dst.at[rows])

    def weights_out():
        each(g_next, "one")
        for w, o in [(w_o, o_wo), (w_g, o_wg), (w_u, o_wu)] + ([(w_in, o_win)] if first else []):
            store(w, o)

    def down_here():
        each(g_d, "three")
        store(w_d, o_wd)

    hooks = (lambda: each(g_d, "two"), lambda: None, weights_out, down_here)
    done_ag2 = all_gather(me, buf2, ag2_s, ag2_r, gated, hooks)
    each(g_next, "two")
    done_rs()

    if not first:
        for done in (done_ag, ax.finish, bx.finish, done_ag2, done_cot):
            done()
        each(everything, "finish")
        for copy in stores:
            copy.wait()
        return

    def down_part(zz):
        return mm(hid[span_of(zz * 256, 256)], w_d[...].reshape(512, WIDE))

    def fill(n):
        if n == 2:
            each(g_next, "three")
            store(w_next, o_next)

    total, done_rs2 = reduce_scatter(me, down_part, *rs, rs2_s, rs2_r, fill)
    o_stream[...] = middle[...] + total
    for done in (ax.finish, bx.finish, done_ag2, done_rs2):
        done()
    each(everything, "finish")
    for copy in stores:
        copy.wait()


def norm_back_of(e, values, gain):
    q = rms_of(values)
    n = values * q
    dn = e * gain
    part = q * (dn - n * jnp.mean(dn * n, axis=-1, keepdims=True))
    return part, jnp.sum(e * n, axis=0, keepdims=True)


def bwd_kernel(l, *refs):
    last = l == 0
    g_attn, g_mlp = (slice(2 * l + i, 2 * l + i + 1) for i in (0, 1))
    refs = list(refs)
    take = lambda n: [refs.pop(0) for _ in range(n)]
    grad, stream, middle, gains, cos, sin, pcol, prow, lse = take(9)
    h_in, h_o, h_g, h_u, h_d, h_qkv, h_gate, h_up, h_normed, h_mixed, h_nmlp, h_hidden = take(12)
    above, landed = (take(4), dict(zip(MLP, take(4)))) if last else (None, None)
    (h_down,) = (None,) if last else take(1)
    o_grad, o_gains = take(2)
    (o_block,) = (None,) if last else take(1)
    o_fin, o_down, o_out = take(3) if last else (None,) * 3
    parts = take(4)
    o_din, o_dgu, o_dd, o_do = parts
    landing = dict(zip(MLP, take(4)))
    if last:
        landing["o"] = take(1)[0]
    w_in, w_o, w_g, w_u, w_d, buf1, buf2, qr, gate_v, up_v, gu, mgs, mgr = take(13)
    keys, vals, keys_t, dk, dv, dqs, ps, pr, mid_grad, mixed, nmlp, hid = take(12)
    d_in, d_gu, d_d, d_o = take(4)
    whole, keep, give, got, ring_out, ring_in = take(6)
    ag_s, ag_r, ag2_s, ag2_r, rs_s, rs_r, rs2_s, rs2_r, ax_s, ax_r, bx_s, bx_r, loc, loc2 = take(14)
    me = Place()
    pairs = (
        (h_d, w_d), (h_gate, gate_v), (h_up, up_v), (h_g, w_g), (h_u, w_u), (h_o, w_o), (h_qkv, qr), (h_in, w_in),
        (h_hidden, hid), (h_nmlp, nmlp), (h_mixed, mixed),
    )
    loads = [pltpu.make_async_copy(h, v, loc.at[i]) for i, (h, v) in enumerate(pairs)]
    for load in loads if last else loads[:5]:
        load.start()
    stores = []

    def store(src, dst):
        stores.append(pltpu.make_async_copy(src, dst, loc2.at[len(stores)]))
        stores[-1].start()

    rs3 = refs
    local = (d_in, d_gu, d_d, d_o)
    upper = {}
    if last:
        stage = {
            "g": [d_gu.at[:, :, k, :, 0:512] for k in range(4)], "u": [d_gu.at[:, :, k, :, 512:1024] for k in range(4)],
            "da": [d_d.at[:, :, k, :, 0:768] for k in range(4)], "db": [d_d.at[:, :, k, :, 768:WIDE] for k in range(4)],
        }
        stage["ia"] = [d_in.at[:, :, k, :, 0:256] for k in range(4)]
        stage["ib"] = [d_in.at[:, :, k, :, 256:384] for k in range(4)]
        stage["o"] = [d_o.at[:, k] for k in range(4)]
        stage = {name: (views[3], views[:3]) for name, views in stage.items()}
        upper = make_reduces(me, MLP + REST, above, refs, landed, MLP, stage)
        stage = {
            "g": [w_g.at[k] for k in range(4)], "u": [w_u.at[k] for k in range(4)],
            "da": [w_d.at[k, :, :, :, 0:768] for k in range(4)], "db": [w_d.at[k, :, :, :, 768:WIDE] for k in range(4)],
        }
        stage = {name: (views[3], views[:3]) for name, views in stage.items()}
        own = make_reduces(me, MLP, local, refs, landing, (), stage)
        es, er = refs
        own["o"] = Reduce(me, reduce_specs(*local)["o"], None, None, None, None, es, er, None, landing["o"])
    else:
        es, er = rs3[6:]
        specs = reduce_specs(*local)
        own = {
            name: Reduce(me, specs[name], None, None, None, None, es.at[n], er.at[n], None, landing[name])
            for n, name in enumerate(MLP)
        }

    def each(reds, names, step):
        for name in names:
            if name in reds:
                getattr(reds[name], step)()

    own_rows = slot_rows(me.z, me.core)
    if last:
        buf1[own_rows] = grad[...].astype(BF)
    else:
        load_down = pltpu.make_async_copy(h_down, buf1, loc.at[11])
        load_down.start()
    me.greet(me.layer_partners())
    each(upper, MLP, "load")
    each(upper, REST, "one")
    for load in loads[:3]:
        load.wait()

    def unit(zz):
        rows = span_of(zz * 256, 256)
        hg = mm_nt(buf1[rows], w_d[...].reshape(512, WIDE))
        gate, up = gate_v[rows].astype(F32), up_v[rows].astype(F32)
        sig = 1.0 / (1.0 + jnp.exp(-gate))
        gu[rows, 0:512] = (hg * up * (sig * (1.0 + gate * (1.0 - sig)))).astype(BF)
        gu[rows, 512:1024] = (hg * (gate * sig)).astype(BF)

    if last:
        hooks = (lambda: each(upper, REST, "load"), lambda: None, lambda: each(upper, MLP, "two"))
        done_ag = all_gather(me, buf1, ag_s, ag_r, unit, hooks)
    else:
        load_down.wait()
        for zz in range(4):
            unit(zz)
    for load in loads[3:5]:
        load.wait()
    for load in () if last else loads[5:]:
        load.start()

    def mlp_part(zz):
        rows = span_of(zz * 256, 256)
        return mm_nt(gu[rows, 0:512], w_g[...].reshape(WIDE, 512)) + mm_nt(gu[rows, 512:1024], w_u[...].reshape(WIDE, 512))

    def grad_down(b):
        cols = slice(256 * b, 256 * b + 256)
        d_d[b] = mm_tn(hid[:, cols], buf1[...]).astype(BF).reshape(4, 4, 16, WIDE)

    def grad_gu(b):
        cols = slice(384 * b, 384 * b + 384)
        pair = slice(b % 2 * 2, b % 2 * 2 + 2)
        d_gu[b // 2, pair] = mm_tn(nmlp[:, cols], gu[...]).astype(BF).reshape(2, 4, 48, 1024)

    def fill1(n):
        if n == 0:
            for load in loads[5:]:
                load.wait()
            grad_down(0)
            grad_down(1)
        elif n == 1:
            grad_gu(0)
            grad_gu(1)
        else:
            grad_gu(2)
            grad_gu(3)
            each(own, ("g", "u"), "one")

    rs = (whole, keep, give, got, ring_out, ring_in)
    e, done_rs = reduce_scatter(me, mlp_part, *rs, rs_s, rs_r, fill1)
    part, gain_part = norm_back_of(e, middle[...], gains[g_mlp, :])
    o_gains[1:2, :] = gain_part
    gm = grad[...].astype(F32) + part
    mid_grad[...] = gm
    buf2[own_rows] = gm.astype(BF)
    ax = Exchange(me, mgs, mgr, ax_s, ax_r, True)

    def mixed_back(zz):
        rows = span_of(zz * 256, 256)
        mgs[rows] = mm_nt(buf2[rows], w_o[...]).astype(BF)
        ax.send(zz * 2)
        ax.send(zz * 2 + 1)

    def hook0():
        split_packed(qr, keys, vals)
        keys_t[...] = flip(keys)
        dk[...] = jnp.zeros_like(dk)
        dv[...] = jnp.zeros_like(dv)

    def hook2():
        each(upper, REST, "arrive")
        each(upper, REST, "two")

    done_ag2 = all_gather(me, buf2, ag2_s, ag2_r, mixed_back, (hook0, lambda: None, hook2))
    if last:
        done_ag()
    normed = buf1
    load_normed = pltpu.make_async_copy(h_normed, normed, loc.at[11])
    load_normed.start()
    store(d_d, o_dd)
    store(d_gu, o_dgu)
    lanes = mm_tn(mixed[...], buf2[...])
    for head in range(2):
        chunk = [lanes[128 * head + 16 * c : 128 * head + 16 * c + 16] for c in (3, 7, 4, 0, 5, 1)]
        for b in range(8):
            first, shift = 12 * b // 16, 12 * b % 16
            piece = chunk[first][shift:]
            if shift > 4:
                piece = jnp.concatenate([piece, chunk[first + 1][: shift - 4]], axis=0)
            d_o[head * 2 + b // 4, b % 4] = padded(piece[0:12])
    store(d_o, o_do)
    if not last:

        def down_part(zz):
            return mm(hid[span_of(zz * 256, 256)], w_d[...].reshape(512, WIDE))

        done_rs()
        final = reduce_steps(me, down_part, whole, keep, *rs3[:6])
        next(final)
    ax.arrive()
    each(own, ("da", "db"), "one")

    @pl.loop(0, 8)
    def _(p):
        rows = span_of(p * 128, 128)
        q = stacked(qr, rows)
        mg = stacked(mgr, rows)
        scores = mm_nt(keys[...], q)
        allowed = pcol[...] <= prow[pl.ds(p, 1), :]
        probs = jnp.where(allowed, jnp.exp2(scores * SCALE2 - lse[pl.ds(p, 1), :]), 0.0)
        pg = mm_nt(vals[...], mg)
        inner = jnp.sum(probs * pg, axis=0, keepdims=True)
        sg = (probs * (pg - inner)).astype(BF)
        dk[...] += mm(sg, q)
        dv[...] += mm(probs.astype(BF), mg)
        dq = jnp.transpose(mm(keys_t[...], sg)) * SCALE
        dqs[rows, 0:128] = dq[0:128].astype(BF)
        dqs[rows, 128:256] = dq[128:256].astype(BF)

    if not last:
        next(final)
    bx = Exchange(me, ps, pr, bx_s, bx_r, False)
    v0, _, _ = lane_masks(128)

    @pl.loop(0, 8)
    def _(k):
        p = lax.rem(me.c + 1 + k, 8)
        rows = span_of(p * 128, 128)
        value = dv[rows]
        ps[rows, 0:128] = jnp.where(v0, value, dqs[rows, 0:128].astype(F32)).astype(BF)
        ps[rows, 128:256] = jnp.where(v0, pltpu.roll(value, 112, 1), dqs[rows, 128:256].astype(F32)).astype(BF)
        ps[rows, 256:384] = jnp.where(v0, pltpu.roll(value, 96, 1), dk[rows] * SCALE).astype(BF)
        bx.send(p)

    if last:
        each(own, MLP, "arrive")
        each(own, MLP, "load")
        done_rs()
    else:
        total, done_rs3 = run(final)
        o_block[...] = (middle[...] + total).astype(BF)
    load_normed.wait()
    bx.arrive()
    pre = qr

    def in_part(zz):
        rows = span_of(zz * 256, 256)
        for t in range(3):
            cols = slice(128 * t, 128 * t + 128)
            tile = pr[rows, cols].astype(F32)
            pre[rows, cols] = (tile * cos[...] - pltpu.roll(tile, 64, 1) * sin[...]).astype(BF)
        return mm_nt(pre[rows], w_in[...])

    def fill2(n):
        for b in ((0, 1), (2,), (3,))[n]:
            cols = slice(384 * b, 384 * b + 384)
            pair = slice(b % 2 * 2, b % 2 * 2 + 2)
            d_in[b // 2, pair] = mm_tn(normed[:, cols], pre[...]).astype(BF).reshape(2, 4, 48, 384)
        if n == 2:
            store(d_in, o_din)
        if n == 0 and last:
            each(own, MLP, "two")
            each(own, ("o",), "one")
        if n == 1 and last:
            finish_columns(upper, COLUMNS, o_fin.at[:, :, 1])
            finish_down(upper, o_down.at[:, 1])
            o_out[...] = upper["o"].three().astype(BF)

    e, done_rs2 = reduce_scatter(me, in_part, *rs, rs2_s, rs2_r, fill2)
    part, gain_part = norm_back_of(e, stream[...].astype(F32), gains[g_attn, :])
    o_gains[0:1, :] = gain_part
    o_grad[...] = mid_grad[...] + part
    for done in (done_ag2, ax.finish, bx.finish, done_rs2):
        done()
    for name, red in upper.items():
        red.finish((1,) if name in MLP else (0, 1))
    if last:
        finish_columns(own, ("g", "u"), o_fin.at[:, :, 0])
        finish_down(own, o_down.at[:, 0])
        own["o"].arrive()
    else:
        done_rs3()
        each(own, MLP, "arrive")
    for name, red in own.items():
        red.finish((0, 1) if last and name in MLP else (0,))
    for copy in stores:
        copy.wait()


def padded(rows):
    return jnp.concatenate([rows, jnp.zeros((4, rows.shape[1]), F32)], axis=0).astype(BF)


def grads_kernel(*refs):
    refs = list(refs)
    take = lambda n: [refs.pop(0) for _ in range(n)]
    gp0, gp1, fin_in, down_s, out1 = take(5)
    d_in, d_o, land_o = take(3)
    o_rows, o_down, o_out, o_gains = take(4)
    me = Place()
    reds = make_reduces(me, REST, (d_in, None, None, d_o), refs, {"o": land_o}, ("o",))
    gains, fin_s, fin_r, down_r, out_s, out_r, sum_a, sum_b, got_a, got_b, got_c = take(11)
    fin_ss, fin_rs, gain_s, gain_r, down_ss, down_rs, out_ss = take(7)
    rest = [reds["ia"], reds["ib"]]
    group = [(k, c) for k in range(4) for c in range(2) if k or c]

    def mate(k, c):
        return {"z": lax.rem(me.z + k, 4), "core": lax.rem(me.core + c, 2)}

    mirror = {"x": me.z, "z": me.x}
    apart = me.x != me.z
    for red in reds.values():
        red.load()
    gains[...] = jnp.zeros_like(gains)
    gains[0:2] = gp0[0:2]
    gains[2:4] = gp1[0:2]
    me.greet(
        [me.near("x", k) for k in (1, 2, 3)] + [me.near("y", k) for k in (1, 2, 3)]
        + [mate(*m) for m in group] + [{"yl": 1 - me.yl, "core": me.oc}],
        mirror=True,
    )

    def gain_copy(stage, axis, src, got, k):
        i = 3 * stage + k - 1
        return push(src, got.at[k - 1], gain_s.at[i], gain_r.at[i], me.near(axis, k))

    def gain_sum(stage, axis, src, got, dst):
        total = src[...]
        for k in (1, 2, 3):
            gain_copy(stage, axis, src, got, k).wait_recv()
            total = total + got[k - 1]
        dst[...] = total

    slot = me.z * 2 + me.core

    def fin(l, i, come):
        k, c = group[i]
        to_z, to_core = lax.rem(me.z + k, 4), lax.rem(me.core + c, 2)
        from_z = lax.rem(me.z + 4 - k, 4)
        dst = fin_r.at[from_z * 2 + to_core, l] if come else fin_r.at[slot, l]
        src = fin_in.at[to_core, to_z, l] if l else fin_s.at[to_core, to_z]
        return push(src, dst, fin_ss.at[l, i], fin_rs.at[l, i], mate(k, c))

    def down(dp, half):
        dev = {"core": jnp.int32(dp), "yl": me.core}
        return push(down_s.at[dp], down_r.at[half], down_ss.at[dp], down_rs.at[half], dev)

    mine = me.yl == me.core

    for k in (1, 2, 3):
        gain_copy(0, "y", gains, got_a, k).start()
    for red in rest:
        red.one()
    for i in range(7):
        fin(1, i, False).start()
    for dp in range(2):
        keep = mine & (me.core == dp)

        @pl.when(jnp.logical_not(keep))
        def _(dp=dp):
            down(dp, me.yl).start()

        @pl.when(keep)
        def _(dp=dp):
            down_r[me.yl] = down_s[dp]

    reds["o"].two()
    fin_s[...] = fin_in[:, :, 0]
    for red in rest:
        red.arrive()
    gain_sum(0, "y", gains, got_a, sum_a)
    for k in (1, 2, 3):
        gain_copy(1, "x", sum_a, got_b, k).start()
    for red in rest:
        red.two()
    gain_sum(1, "x", sum_a, got_b, sum_b)

    def gain_mate(i):
        return push(sum_b, got_c.at[i], gain_s.at[6 + i], gain_r.at[6 + i], mate(*group[i]))

    for i in range(7):
        gain_mate(i).start()
    out_s[1] = out1[...]
    finish_columns(reds, ("ia", "ib"), fin_s)
    out_s[0] = reds["o"].three().astype(BF)

    def out_copy():
        return push(out_s, out_r, out_ss.at[0], out_ss.at[1], mirror)

    for i in range(7):
        fin(0, i, False).start()
    @pl.when(apart)
    def _():
        out_copy().start()

    @pl.when(jnp.logical_not(apart))
    def _():
        out_r[...] = out_s[...]

    fin_r[slot, 0] = fin_s[me.core, me.z]
    fin_r[slot, 1] = fin_in[me.core, me.z, 1]
    total = sum_b[...]
    for i in range(7):
        gain_mate(i).wait_recv()
        total = total + got_c[i]
    o_gains[...] = total
    for i in range(7):
        fin(0, i, True).wait_recv()
        fin(1, i, True).wait_recv()
    o_rows[...] = fin_r[...]
    for half in range(2):

        @pl.when(jnp.logical_not(mine & (me.yl == half)))
        def _(half=half):
            down(0, half).wait_recv()

    o_down[...] = down_r[...]

    @pl.when(apart)
    def _():
        out_copy().wait_recv()

    o_out[...] = out_r[...]
    reds["o"].finish((1,))
    for red in rest:
        red.finish()
    for k in (1, 2, 3):
        gain_copy(0, "y", gains, got_a, k).wait_send()
        gain_copy(1, "x", sum_a, got_b, k).wait_send()
    for i in range(7):
        gain_mate(i).wait_send()
        fin(0, i, False).wait_send()
        fin(1, i, False).wait_send()
    for dp in range(2):

        @pl.when(jnp.logical_not(mine & (me.core == dp)))
        def _(dp=dp):
            down(dp, me.yl).wait_send()

    @pl.when(apart)
    def _():
        out_copy().wait_send()


def vm(shape, dtype=BF):
    return pltpu.VMEM(shape, dtype)


def rs_scratch():
    return [vm((4, 128, WIDE)), vm((4, 128, WIDE)), vm((6, 64, WIDE)), vm((6, 64, WIDE))]


def dma(*shape):
    return pltpu.SemaphoreType.DMA(shape)


def sems():
    return [dma(n) for n in (13, 13, 13, 13, 10, 10, 10, 10, 8, 8, 8, 8, 16, 32)]


WEIGHTS = [(WIDE, 384), (256, WIDE), (WIDE, 512), (WIDE, 512), (512, WIDE)]
SPLIT = [(2, 4, 4, 48, 384), (4, 64, WIDE), (2, 4, 4, 48, 512), (2, 4, 4, 48, 512), (2, 4, 4, 16, WIDE)]
PARTS = [(2, 4, 4, 48, 384), (2, 4, 4, 48, 1024), (2, 4, 4, 16, WIDE), (4, 4, 16, WIDE)]
RING = [((256, WIDE), F32), ((4, 128, WIDE), BF)]


def run_kernel(kernel, name, cid, ins, in_vmem, outs, out_vmem, scratch):
    place = {True: pltpu.VMEM, False: pl.ANY}
    return pl.pallas_call(
        kernel,
        name=name,
        out_shape=[jax.ShapeDtypeStruct(s, d) for s, d in outs],
        in_specs=[pl.BlockSpec(memory_space=place[i < in_vmem]) for i in range(len(ins))],
        out_specs=[pl.BlockSpec(memory_space=place[i < out_vmem]) for i in range(len(outs))],
        scratch_shapes=scratch,
        compiler_params=pltpu.CompilerParams(
            collective_id=cid, has_side_effects=True, vmem_limit_bytes=58 * 2**20
        ),
    )(*ins)


def layer_fwd(l, stream, gains, tables, h_in, sources, extra):
    first = l == 0
    outs = [((128, WIDE), F32)] * (2 if first else 1) + [((8, 256), F32)] + ([((8, WIDE), F32)] if first else [])
    n_vmem = len(outs)
    outs += [
        ((1024, WIDE), BF), ((1024, 384), BF), ((1024, 256), BF), ((1024, WIDE), BF),
        ((1024, 512), BF), ((1024, 512), BF), ((1024, 512), BF),
    ] + [(s, BF) for s in SPLIT[1:]] + ([(SPLIT[0], BF)] * 2 if first else [((1024, WIDE), BF)])
    scratch = [vm(s) for s in SPLIT] + [
        vm((1024, WIDE)), vm((1024, WIDE)), vm((1024, 384)), vm((1024, 384)), vm((1024, 256)), vm((1024, 256)),
        vm((1024, 512)), vm((1024, 512)), vm((1024, 512)),
        vm((1024, 128)), vm((1024, 128)), vm((128, 1024)), vm((128, WIDE), F32),
    ] + [vm(*s) for s in RING] + rs_scratch() + sems() + [dma(10, 7), dma(10, 7)]
    if first:
        scratch += [vm((2, 4, 4, 8, 256), F32), vm(SPLIT[0])]
    else:
        scratch += [vm((1024, WIDE)), dma(13), dma(13)]
    ins = [stream] + ([] if first else [gains]) + [*tables, h_in, *sources, *extra]
    kernel = functools.partial(fwd_kernel, l)
    return run_kernel(kernel, f"layer_forward_{l}", 1 + l, ins, 5 if first else 6, outs, n_vmem, scratch)


def layer_bwd(l, grad, stream, middle, gains, tables, lse, weights, saved, above):
    last = l == 0
    outs = [((128, WIDE), F32), ((8, WIDE), F32)]
    outs += [((2, 4, 2, 16, 1408), BF), ((2, 2, 16, WIDE), BF), ((16, WIDE), BF)] if last else [((128, WIDE), BF)]
    n_vmem = len(outs)
    outs += [(s, BF) for s in PARTS]
    outs += [((3,) + REDUCE[n][3], BF) for n in (MLP + ("o",) if last else MLP)]
    shapes = WEIGHTS[:2] + [(4, 2, 4, 48, 512), (4, 2, 4, 48, 512), (4, 2, 4, 16, WIDE)]
    scratch = [vm(s) for s in shapes] + [
        vm((1024, WIDE)), vm((1024, WIDE)), vm((1024, 384)), vm((1024, 512)), vm((1024, 512)),
        vm((1024, 1024)), vm((1024, 256)), vm((1024, 256)),
        vm((1024, 128)), vm((1024, 128)), vm((128, 1024)), vm((1024, 128), F32), vm((1024, 128), F32),
        vm((1024, 256)), vm((1024, 384)), vm((1024, 384)), vm((128, WIDE), F32),
        vm((1024, 256)), vm((1024, WIDE)), vm((1024, 512)),
    ] + [vm(s) for s in PARTS] + [vm(*s) for s in RING] + rs_scratch() + sems()
    if last:
        scratch += reduce_scratch(MLP + REST, ()) + reduce_scratch(MLP, ()) + [dma(6), dma(6)]
    else:
        scratch += rs_scratch() + [dma(10), dma(10), dma(4, 6), dma(4, 6)]
    weights = [w.reshape(s) for w, s in zip(weights, shapes)]
    ins = [grad, stream, middle, gains, *tables, lse, *weights, *saved, *(above or ())]
    kernel = functools.partial(bwd_kernel, l)
    return run_kernel(kernel, f"layer_backward_{l}", 3 + l, ins, 9, outs, n_vmem, scratch)


def picks(rows, cols, test):
    r = lax.broadcasted_iota(jnp.int32, (rows, cols), 0)
    c = lax.broadcasted_iota(jnp.int32, (rows, cols), 1)
    return jnp.where(test(r, c), 1.0, 0.0).astype(BF)


def packed_place(n):
    t, i = n // 128, n % 128
    value = ((i >= 48) & (i < 64)) | (i >= 112)
    feature = jnp.where(value, 32 * t + jnp.where(i < 64, i - 48, i - 96), jnp.where(i < 48, i, i - 16))
    return t, feature, value


def prepare_kernel(
    order, wq, wk, wv, wg, wu, ga, gm, o_in, o_g, o_u, o_gain, o_cos, o_sin, o_pcol, o_prow, vq, vk, vv, vg, vu, loc
):
    core, z, yl = lax.axis_index("core"), lax.axis_index("z"), lax.axis_index("yl")
    own = pl.ds(pl.multiple_of(yl * 48, 16), 48)
    loads = [
        pltpu.make_async_copy(h.at[:, own], v, loc.at[i])
        for i, (h, v) in enumerate(((wq, vq), (wk, vk), (wv, vv), (wg, vg), (wu, vu)))
    ]
    for load in loads:
        load.start()
    ctx = lax.axis_index("x") * 2 + lax.axis_index("yh")
    for span in range(16):
        o_pcol[64 * span : 64 * span + 64] = order[span] * 64 + lax.broadcasted_iota(jnp.int32, (64, 1), 0)
    lane = lax.broadcasted_iota(jnp.int32, (1, 256), 1)
    for p in range(8):
        start = jnp.where(lane % 128 < 64, order[2 * p], order[2 * p + 1]) * 64
        o_prow[p : p + 1, :] = start + lane % 64
    row = lax.broadcasted_iota(jnp.int32, (128, 128), 0)
    col = lax.broadcasted_iota(jnp.int32, (128, 128), 1)
    place = jnp.where(row < 64, order[2 * ctx], order[2 * ctx + 1]) * 64 + row % 64
    turning = (col % 64) < 48
    freq = jnp.exp((col % 64).astype(F32) * (-2.0 * math.log(ROPE_BASE) / HEAD))
    angles = place.astype(F32) * freq
    cos = jnp.where(turning, jnp.cos(angles), 1.0)
    sin = jnp.where(turning, jnp.sin(angles), 0.0)
    sin = jnp.where(col < 64, -sin, sin)
    for half in range(2):
        o_cos[128 * half : 128 * half + 128] = cos
        o_sin[128 * half : 128 * half + 128] = sin
    owner = core * 8 + ctx
    shift = lax.rem(96 * owner, 128)
    move = picks(96, 256, lambda r, c: c == r + shift)
    zero = jnp.zeros((4, 96), F32)
    both = jnp.concatenate([ga[0:1], gm[0:1], ga[1:2], gm[1:2]], axis=0).astype(F32)
    placed = mm(jnp.concatenate([both, zero], axis=0).astype(BF), move)
    o_gain[0] = placed
    o_gain[1] = placed
    spread = [
        picks(1024, 128, lambda r, c, j=cc * 4 + z: (r // 256 == c // 32) & (r % 256 == 32 * j + c % 32)) for cc in range(2)
    ]
    spread = jnp.concatenate(spread, axis=1)

    def query(r, n, j):
        t, f, value = packed_place(n)
        return jnp.logical_not(value) & (t < 2) & (r == j * 192 + t * 96 + f)

    def key(r, n, j):
        t, f, value = packed_place(n)
        return jnp.logical_not(value) & (t == 2) & (r == j * 96 + f)

    def val(r, n, j):
        t, f, value = packed_place(n)
        return value & (r == j * 96 + f)

    for load in loads[:3]:
        load.wait()
    for cc in range(2):
        j = cc * 4 + z
        out = mm(vq[...].reshape(96, WIDE), picks(WIDE, 384, lambda r, n: query(r, n, j)))
        out = out + mm(vk[...].reshape(96, 768), picks(768, 384, lambda r, n: key(r, n, j)))
        out = out + mm(vv[...].reshape(96, 768), picks(768, 384, lambda r, n: val(r, n, j)))
        o_in[:, cc] = out.astype(BF).reshape(LAYERS, 48, 384)
    for load in loads[3:]:
        load.wait()
    for v, o in ((vg, o_g), (vu, o_u)):
        for b in range(4):
            out = mm(v[:, :, 1024 * b : 1024 * b + 1024].reshape(96, 1024), spread).astype(BF)
            for cc in range(2):
                o[:, cc, :, 128 * b : 128 * b + 128] = out[:, 128 * cc : 128 * cc + 128].reshape(LAYERS, 48, 128)


def prepare(order, wq, wk, wv, wg, wu, ga, gm):
    shapes = [((LAYERS, 2, 48, 384), BF), ((LAYERS, 2, 48, 512), BF), ((LAYERS, 2, 48, 512), BF), ((2, 8, 256), F32)]
    shapes += [((256, 128), F32), ((256, 128), F32), ((1024, 1), jnp.int32), ((8, 256), jnp.int32)]
    in_vmem = pl.BlockSpec(memory_space=pltpu.VMEM)
    return pl.pallas_call(
        prepare_kernel,
        name="prepare_sources",
        out_shape=[jax.ShapeDtypeStruct(s, d) for s, d in shapes],
        in_specs=[pl.BlockSpec(memory_space=pltpu.SMEM)] + [pl.BlockSpec(memory_space=pl.ANY)] * 5 + [in_vmem] * 2,
        out_specs=[in_vmem] * 8,
        scratch_shapes=[vm((LAYERS, 48, n)) for n in (WIDE, 768, 768, 4096, 4096)] + [dma(5)],
        compiler_params=pltpu.CompilerParams(vmem_limit_bytes=60 * 2**20),
    )(order, wq, wk, wv, wg, wu, ga, gm)


def assemble_kernel(cols, downs, outs, o_q, o_k, o_v, o_o, o_g, o_u, o_d):
    def member(j, lo, hi):
        return cols[j % 4 * 2 + j // 4, :, :, lo:hi].reshape(32, hi - lo)

    def put(dst, lo, hi, value):
        for l in range(LAYERS):
            dst[:, l, lo:hi] = value[16 * l : 16 * l + 12]

    def query(n, c, i):
        t, f, value = packed_place(n)
        return jnp.logical_not(value) & (t < 2) & (c == i * 192 + t * 96 + f)

    def key(n, c, i):
        t, f, value = packed_place(n)
        return jnp.logical_not(value) & (t == 2) & (c == i * 96 + f)

    def val(n, c, i):
        t, f, value = packed_place(n)
        return value & (c == i * 96 + f)

    for dst, test, per in ((o_q, query, 2), (o_k, key, 4), (o_v, val, 4)):
        moves = [picks(384, 384, lambda n, c, i=i: test(n, c, i)) for i in range(per)]
        for m in range(8 // per):
            total = sum(mm(member(per * m + i, 0, 384), moves[i]) for i in range(per))
            put(dst, 384 * m, 384 * m + 384, total)
    back = [picks(128, 1024, lambda r, c, j=j: (c // 256 == r // 32) & (c % 256 == 32 * j + r % 32)) for j in range(8)]
    for dst, start in ((o_g, 384), (o_u, 896)):
        for b in range(4):
            total = sum(mm(member(j, start + 128 * b, start + 128 * b + 128), back[j]) for j in range(8))
            put(dst, 1024 * b, 1024 * b + 1024, total)
    for l in range(LAYERS):
        o_o[:, l, :] = outs[l, 0:12].astype(F32)
        for h in range(2):
            o_d[l, 16 * h : 16 * h + 16] = downs[h, l].astype(F32)


def assemble(cols, downs, outs):
    shapes = [(12, LAYERS, n) for n in (WIDE, 768, 768, WIDE, 4096, 4096)] + [(LAYERS, 32, WIDE)]
    in_vmem = pl.BlockSpec(memory_space=pltpu.VMEM)
    *grads, d_d = pl.pallas_call(
        assemble_kernel,
        name="assemble_gradients",
        out_shape=[jax.ShapeDtypeStruct(s, F32) for s in shapes],
        in_specs=[in_vmem] * 3,
        out_specs=[in_vmem] * 7,
        compiler_params=pltpu.CompilerParams(vmem_limit_bytes=60 * 2**20),
    )(cols, downs, outs)
    return [grad.transpose(1, 0, 2) for grad in grads] + [d_d]


def reduce_grads(gain_parts, done, parts):
    outs = [((8, 2, 16, 1408), BF), ((2, 2, 16, WIDE), BF), ((2, 16, WIDE), BF), ((8, WIDE), F32)]
    scratch = reduce_scratch(REST, REST) + [
        vm((8, WIDE), F32), vm((2, 4, 16, 1408)), vm((8, 2, 16, 1408)), vm((2, 2, 16, WIDE)),
        vm((2, 16, WIDE)), vm((2, 16, WIDE)), vm((8, WIDE), F32), vm((8, WIDE), F32),
        vm((3, 8, WIDE), F32), vm((3, 8, WIDE), F32), vm((7, 8, WIDE), F32),
        dma(2, 7), dma(2, 7), dma(13), dma(13), dma(2), dma(2), dma(2),
    ]
    return run_kernel(grads_kernel, "reduce_gradients", 5, [*gain_parts, *done, *parts], 5, outs, 4, scratch)


def body(
    tokens, span_order, attn_gain, w_query, key_matrix, value_matrix, w_out, mlp_gain, w_gate, w_up,
    w_down, cotangent,
):
    core, z, yl = lax.axis_index("core"), lax.axis_index("z"), lax.axis_index("yl")
    ctx = lax.axis_index("x") * 2 + lax.axis_index("yh")
    s_in, s_g, s_u, s_gain, *tables = prepare(
        span_order, w_query, key_matrix, value_matrix, w_gate, w_up, attn_gain, mlp_gain
    )
    stream, gains = tokens[0], None
    kept = []
    sources = (w_out, w_down, s_g, s_u)
    outs = layer_fwd(0, stream, gains, tables, s_in, sources, (s_gain, s_in))
    gains, w_next = outs[3], outs[-1]
    kept.append((stream, outs[1:3], outs[-2], outs[4:-2]))
    stream = outs[0]
    outs = layer_fwd(1, stream, gains, tables, w_next, sources, (cotangent[0],))
    kept.append((stream, outs[:2], w_next, outs[2:-1]))
    down_grad = outs[-1]

    g, gain_parts, above = cotangent[0], [None] * LAYERS, (down_grad,)
    for l in reversed(range(LAYERS)):
        stream, (middle, lse), w_in, outs = kept[l]
        normed, qkv, mixed, nmlp, gate, up, hid = outs[:7]
        saved = (qkv, gate, up, normed, mixed, nmlp, hid)
        res = layer_bwd(l, g, stream, middle, gains, tables, lse, (w_in, *outs[7:]), saved, above)
        g, gain_parts[l] = res[:2]
        if l:
            block_out, above = res[2][None], tuple(res[3:])
    cols, d_d, d_o, gp = reduce_grads(gain_parts, res[2:5], (res[5], res[8], res[13]))
    d_q, d_k, d_v, d_o, d_g, d_u, d_d = assemble(cols, d_d, d_o)
    owner = (core * 8 + ctx) * 8 + yl * 4 + z
    gp = lax.dynamic_slice(gp, (0, owner * 12), (4, 12)).reshape(2, 2, 12)
    return (block_out, g[None], gp[:, 0], d_q, d_k, d_v, d_o, gp[:, 1], d_g, d_u, d_d)


def solution(mesh):
    fine = Mesh(mesh.devices.reshape(2, 4, 2, 2, 4), ALL)
    seq, ctx, own, every = ("core", "yl", "z"), CTX, OWN, ALL
    act = P(seq, ctx, None)
    in_specs = (act, P(), P(None, own)) + (P(None, own, None),) * 4 + (P(None, own),) + (P(None, own, None),) * 3 + (act,)
    grad = P(None, every, None)
    out_specs = (act, act, P(None, every)) + (grad,) * 4 + (P(None, every),) + (grad,) * 3
    return jax.shard_map(body, mesh=fine, in_specs=in_specs, out_specs=out_specs, check_vma=False)
```

```python
import functools
import math

import jax
import jax.numpy as jnp
import numpy as np
from jax import lax
from jax.experimental import pallas as pl
from jax.experimental.pallas import tpu as pltpu
from jax.sharding import Mesh, PartitionSpec as P

HEAD = 96
LAYERS = 2
ROPE_BASE = 100000.0
EPS = 1e-05
CTX = ("x", "yh")
TP = ("z", "core")
OWN = ("core", "x", "yh")
ALL = ("core", "x", "yh", "yl", "z")
BF = jnp.bfloat16
F32 = jnp.float32
MESH = pl.DeviceIdType.MESH
SCALE = 1.0 / math.sqrt(HEAD)
SCALE2 = SCALE * math.log2(math.e)
WIDE = 1536


def mm(a, b):
    return jnp.dot(a, b, preferred_element_type=F32)


def mm_tn(a, b):
    return lax.dot_general(a, b, (((0,), (0,)), ((), ())), preferred_element_type=F32)


def mm_nt(a, b):
    return lax.dot_general(a, b, (((1,), (1,)), ((), ())), preferred_element_type=F32)


class Place:
    def __init__(self):
        self.z, self.core = lax.axis_index("z"), lax.axis_index("core")
        self.x, self.yh, self.yl = lax.axis_index("x"), lax.axis_index("yh"), lax.axis_index("yl")
        self.y = self.yh * 2 + self.yl
        self.c = self.x * 2 + self.yh
        self.zp, self.zm, self.zo = (lax.rem(self.z + k, 4) for k in (1, 3, 2))
        self.oc = 1 - self.core

    def near(self, axis, k):
        if axis == "x":
            return {"x": lax.rem(self.x + k, 4)}
        return at_y(lax.rem(self.y + k, 4))

    def greet(self, others, mirror=False):
        barrier = pltpu.get_barrier_semaphore()
        for dev in others:
            pl.semaphore_signal(barrier, inc=1, device_id=dev, device_id_type=MESH)
        if not mirror:
            pl.semaphore_wait(barrier, len(others))
            return

        @pl.when(self.x != self.z)
        def _():
            there = {"x": self.z, "z": self.x}
            pl.semaphore_signal(barrier, inc=1, device_id=there, device_id_type=MESH)
            pl.semaphore_wait(barrier, len(others) + 1)

        @pl.when(self.x == self.z)
        def _():
            pl.semaphore_wait(barrier, len(others))

    def layer_partners(self):
        return (
            [{"z": self.zp}, {"z": self.zm}, {"core": self.oc}]
            + [at_ctx(lax.rem(self.c + k, 8)) for k in range(1, 8)]
            + [{"yl": 1 - self.yl}, {"yh": 1 - self.yh, "yl": 1 - self.yl}]
        )


def at_y(y):
    return {"yh": y // 2, "yl": lax.rem(y, 2)}


def at_ctx(c):
    return {"x": c // 2, "yh": lax.rem(c, 2)}


def span_of(start, size):
    return pl.ds(pl.multiple_of(start, 64), size)


def slot_rows(zz, cc, half=None):
    base = (zz * 2 + cc) * 128
    return span_of(base, 128) if half is None else span_of(base + 64 * half, 64)


def all_gather(*args):
    return run(gather_steps(*args))


def run(steps):
    while True:
        try:
            next(steps)
        except StopIteration as stop:
            return stop.value


def gather_steps(me, buf, ssem, rsem, on_pair, hooks=()):
    z, zp, zm, zo, core, oc = me.z, me.zp, me.zm, me.zo, me.core, me.oc
    up, down, across = {"z": zp}, {"z": zm}, {"core": oc}
    sent = [
        (z, core, 0, up), (z, core, 1, up), (z, core, 1, down), (z, core, 0, down),
        (zm, core, 0, up), (zp, core, 1, down), (z, core, None, across),
        (zm, core, 0, across), (zm, core, 1, across), (zp, core, 1, across), (zp, core, 0, across),
        (zo, core, 0, across), (zo, core, 1, across),
    ]
    come = [
        (zm, core, 0), (zm, core, 1), (zp, core, 1), (zp, core, 0), (zo, core, 0), (zo, core, 1),
        (z, oc, None), (zm, oc, 0), (zm, oc, 1), (zp, oc, 1), (zp, oc, 0), (zo, oc, 0), (zo, oc, 1),
    ]

    def copy(i, rows, dev):
        return pltpu.make_async_remote_copy(
            src_ref=buf.at[rows], dst_ref=buf.at[rows], send_sem=ssem.at[i], recv_sem=rsem.at[i],
            device_id=dev, device_id_type=MESH,
        )

    def send(*which):
        for i in which:
            copy(i, slot_rows(*sent[i][:3]), sent[i][3]).start()

    def arrive(*which):
        for i in which:
            copy(i, slot_rows(*come[i]), sent[i][3]).wait_recv()

    def hook(i):
        if i < len(hooks):
            hooks[i]()

    send(0, 2, 1, 3, 6)
    hook(0)
    yield
    arrive(6)
    on_pair(z)
    arrive(0)
    send(4, 7)
    arrive(2)
    send(5, 9)
    hook(1)
    arrive(1)
    send(8)
    arrive(3)
    send(10)
    hook(2)
    yield
    arrive(7, 8)
    on_pair(zm)
    arrive(9, 10)
    on_pair(zp)
    hook(3)
    arrive(4)
    send(11)
    arrive(5)
    send(12)
    yield
    arrive(11, 12)
    on_pair(zo)

    def finish():
        for i in range(13):
            copy(i, slot_rows(*sent[i][:3]), sent[i][3]).wait_send()

    return finish


def reduce_scatter(*args):
    return run(reduce_steps(*args))


def reduce_steps(me, part, whole, keep, give, take, ring_out, ring_in, ssem, rsem, fill=lambda n: None):
    z, zp, zm, zo, core, oc = me.z, me.zp, me.zm, me.zo, me.core, me.oc
    up, down, across = {"z": zp}, {"z": zm}, {"core": oc}
    mine = span_of(core * 128, 128)
    theirs = span_of(oc * 128, 128)

    def swap(k):
        return pltpu.make_async_remote_copy(
            src_ref=give.at[k], dst_ref=take.at[k], send_sem=ssem.at[k], recv_sem=rsem.at[k],
            device_id=across, device_id_type=MESH,
        )

    def ring(i):
        return pltpu.make_async_remote_copy(
            src_ref=ring_out.at[i], dst_ref=ring_in.at[i], send_sem=ssem.at[4 + i], recv_sem=rsem.at[4 + i],
            device_id=up if i < 3 else down, device_id_type=MESH,
        )

    def make(k, zz):
        whole[...] = part(zz)
        give[k] = whole[theirs].astype(BF)
        keep[k] = whole[mine].astype(BF)
        swap(k).start()

    def merged(k, half):
        rows = slice(64 * half, 64 * half + 64)
        return keep[k, rows].astype(F32) + take[k, rows].astype(F32)

    def push(i, value):
        ring_out[i] = value.astype(BF)
        ring(i).start()

    make(0, zo)
    make(1, zp)
    swap(0).wait_recv()
    push(0, merged(0, 0))
    push(3, merged(0, 1))
    make(2, zm)
    swap(1).wait_recv()
    push(1, merged(1, 1))
    swap(2).wait_recv()
    push(4, merged(2, 0))
    make(3, z)
    fill(0)
    yield
    ring(0).wait_recv()
    push(2, merged(1, 0) + ring_in[0].astype(F32))
    ring(3).wait_recv()
    push(5, merged(2, 1) + ring_in[3].astype(F32))
    swap(3).wait_recv()
    fill(1)
    own = [merged(3, 0), merged(3, 1)]
    ring(1).wait_recv()
    own[1] = own[1] + ring_in[1].astype(F32)
    ring(4).wait_recv()
    own[0] = own[0] + ring_in[4].astype(F32)
    fill(2)
    yield
    ring(2).wait_recv()
    own[0] = own[0] + ring_in[2].astype(F32)
    ring(5).wait_recv()
    own[1] = own[1] + ring_in[5].astype(F32)

    def finish():
        for k in range(4):
            swap(k).wait_send()
        for i in range(6):
            ring(i).wait_send()

    return jnp.concatenate(own, axis=0), finish


def ctx_of(slot, core):
    zz, cc = slot // 2, lax.rem(slot, 2)
    return lax.rem(zz + 2 * cc + core, 4) * 2 + cc


def slot_of(ctx, core):
    x, yh = ctx // 2, lax.rem(ctx, 2)
    return lax.rem(x + 2 * yh + 3 * core, 4) * 2 + yh


class Exchange:
    def __init__(self, me, src, dst, ssem, rsem, out):
        self.me, self.src, self.dst, self.ssem, self.rsem = me, src, dst, ssem, rsem
        same = lambda v: v
        ctx, slot = (lambda v, f=f: f(v, me.core) for f in (ctx_of, slot_of))
        self.to, self.block, self.lands = (ctx, slot, same) if out else (same, same, slot)

    def copy(self, b, come):
        return pltpu.make_async_remote_copy(
            src_ref=self.src.at[span_of(b * 128, 128)], dst_ref=self.dst.at[span_of(come * 128, 128)],
            send_sem=self.ssem.at[b], recv_sem=self.rsem.at[come],
            device_id=at_ctx(self.to(b)), device_id_type=MESH,
        )

    def send(self, b):
        there, come = self.to(b), self.lands(self.me.c)

        @pl.when(there != self.me.c)
        def _():
            self.copy(b, come).start()

        @pl.when(there == self.me.c)
        def _():
            self.dst[span_of(come * 128, 128)] = self.src[span_of(b * 128, 128)]

    def arrive(self):
        @pl.loop(1, 8)
        def _(k):
            there = lax.rem(self.me.c + k, 8)
            self.copy(self.block(there), self.lands(there)).wait_recv()

    def finish(self):
        @pl.loop(1, 8)
        def _(k):
            there = lax.rem(self.me.c + k, 8)
            self.copy(self.block(there), self.lands(self.me.c)).wait_send()


def push(src, dst, ssem, rsem, dev):
    return pltpu.make_async_remote_copy(
        src_ref=src, dst_ref=dst, send_sem=ssem, recv_sem=rsem, device_id=dev, device_id_type=MESH
    )


class Gather:
    def __init__(self, me, src, dst, ssem, rsem, loc, order, cols):
        self.me, self.src, self.dst, self.ssem, self.rsem, self.order = me, src, dst, ssem, rsem, order
        self.loc, self.cols = loc, slice(*cols)

    def own(self):
        me = self.me
        return pltpu.make_async_copy(
            self.src(me.core, self.cols), self.dst.at[me.core, me.x, me.y, :, self.cols], self.loc
        )

    def cross(self, come=False):
        me = self.me
        row = me.oc if come else me.core
        return push(
            self.src(me.oc, self.cols), self.dst.at[row, me.x, me.y, :, self.cols],
            self.ssem.at[0], self.rsem.at[0], {"core": me.oc},
        )

    def region(self, stage, k):
        me = self.me
        x, y = (lax.rem(v + 4 - k, 4) for v in (me.x, me.y))
        if stage == 0:
            return self.dst.at[:, x if self.order[0] == "x" else me.x, y if self.order[0] == "y" else me.y, :, self.cols]
        if self.order[1] == "y":
            return self.dst.at[:, :, y, :, self.cols]
        return self.dst.at[:, x, :, :, self.cols]

    def copy(self, stage, k, come):
        ref = self.region(stage, k if come else 0)
        i = 1 + 3 * stage + k - 1
        return push(ref, ref, self.ssem.at[i], self.rsem.at[i], self.me.near(self.order[stage], k))

    def zero(self):
        self.own().start()
        self.cross().start()

    def one(self):
        self.own().wait()
        self.cross(True).wait_recv()
        for k in (2, 1, 3):
            self.copy(0, k, False).start()

    def two(self):
        for k in (1, 3, 2):
            self.copy(0, k, True).wait_recv()
        for k in (2, 1, 3):
            self.copy(1, k, False).start()

    def three(self):
        for k in (1, 3, 2):
            self.copy(1, k, True).wait_recv()

    def finish(self):
        self.cross().wait_send()
        for stage in (0, 1):
            for k in (1, 2, 3):
                self.copy(stage, k, False).wait_send()


class OutGather:
    def __init__(self, me, src, dst, ssem, rsem, loc):
        self.me, self.dst, self.ssem, self.rsem = me, dst, ssem, rsem
        self.src, self.loc = src, loc
        self.far = lax.rem(me.x + 4 - me.z, 4)

    def copy(self, stage, k, come):
        me = self.me
        y = lax.rem(me.y + 4 - k, 4) if stage and come else me.y
        ref, i = self.dst.at[y], 3 * stage + k - 1
        return push(ref, ref, self.ssem.at[i], self.rsem.at[i], me.near("xy"[stage], k))

    def own(self):
        y, yl = self.me.y, self.me.yl
        return [
            pltpu.make_async_copy(
                self.src.at[pl.ds(pl.multiple_of(row, 16), 16)], self.dst.at[y, to : to + 16], self.loc.at[i]
            )
            for i, (row, to) in enumerate(((48 - 16 * yl, 0), (80 - 16 * yl, 16), (16 * yl, 48)))
        ]

    def zero(self):
        @pl.when(self.far == 0)
        def _():
            for copy in self.own():
                copy.start()
            self.dst[self.me.y, 32:48] = jnp.zeros((16, WIDE), BF)

    def one(self):
        @pl.when(self.far == 0)
        def _():
            for copy in self.own():
                copy.wait()
            for k in (2, 1, 3):
                self.copy(0, k, False).start()

    def two(self):
        for k in (1, 2, 3):

            @pl.when(self.far == k)
            def _(k=k):
                self.copy(0, k, True).wait_recv()

        for k in (2, 1, 3):
            self.copy(1, k, False).start()

    def three(self):
        for k in (1, 3, 2):
            self.copy(1, k, True).wait_recv()

    def finish(self):
        @pl.when(self.far == 0)
        def _():
            for k in (1, 2, 3):
                self.copy(0, k, False).wait_send()

        for k in (1, 2, 3):
            self.copy(1, k, False).wait_send()


class Reduce:
    def __init__(self, me, spec, mine, got1, sum1, got2, ssem, rsem, loc, land=None, landed=False):
        self.me = me
        self.quarter, self.inner, self.order = spec[:3]
        self.mine, self.got1, self.sum1, self.got2, self.ssem, self.rsem, self.loc = mine, got1, sum1, got2, ssem, rsem, loc
        self.land, self.landed = land, landed

    def at(self, axis, k):
        return lax.rem((self.me.x if axis == "x" else self.me.y) + k, 4)

    def copy(self, stage, k):
        axis = self.order[stage]
        to = self.at(axis, k)
        src = self.inner(self.sum1, to) if stage else self.quarter(axis, to)
        dst = self.got2.at[k - 1] if stage else self.got1[k - 1] if self.land is None else self.land.at[k - 1]
        i = 3 * stage + k - 1
        return push(src, dst, self.ssem.at[i], self.rsem.at[i], self.me.near(axis, k))

    def loads(self):
        axis = self.order[0]
        out = [pltpu.make_async_copy(self.quarter(axis, self.at(axis, 0)), self.mine, self.loc.at[0])]
        if self.land is not None:
            for k in range(3):
                out.append(pltpu.make_async_copy(self.land.at[k], self.got1[k], self.loc.at[1 + k]))
        return out

    def load(self):
        for load in self.loads():
            load.start()

    def one(self):
        for k in (2, 1, 3):
            self.copy(0, k).start()

    def arrive(self):
        if not self.landed:
            for k in (1, 2, 3):
                self.copy(0, k).wait_recv()

    def two(self):
        for load in self.loads():
            load.wait()
        dims = self.sum1.shape[:-2]

        @pl.loop(0, math.prod(dims))
        def _(n):
            at = (n,) if len(dims) == 1 else (n // dims[1], lax.rem(n, dims[1]))
            total = self.mine[at].astype(F32)
            for k in range(3):
                total = total + self.got1[k][at].astype(F32)
            self.sum1[at] = total.astype(BF)

        for k in (2, 1, 3):
            self.copy(1, k).start()

    def three(self):
        for k in (1, 2, 3):
            self.copy(1, k).wait_recv()
        total = self.inner(self.sum1, self.at(self.order[1], 0))[...].astype(F32)
        for k in range(3):
            total = total + self.got2[k].astype(F32)
        return total

    def finish(self, stages=(0, 1)):
        for stage in stages:
            for k in (1, 2, 3):
                self.copy(stage, k).wait_send()


def reduce_specs(d_in, d_gu, d_d, d_o):
    def split(ref, lo, hi, r, order):
        def quarter(axis, i):
            return ref.at[:, i, :, :, lo:hi] if axis == "x" else ref.at[:, :, i, :, lo:hi]

        return quarter, lambda q, i: q.at[:, i], order, (2, 4, r, hi - lo), (2, r, hi - lo)

    return {
        "g": split(d_gu, 0, 512, 48, "yx"),
        "u": split(d_gu, 512, 1024, 48, "xy"),
        "da": split(d_d, 0, 768, 16, "yx"),
        "db": split(d_d, 768, 1536, 16, "xy"),
        "ia": split(d_in, 0, 256, 48, "yx"),
        "ib": split(d_in, 256, 384, 48, "xy"),
        "o": (lambda axis, i: d_o.at[:, i], lambda q, i: q.at[i], "xy", (4, 16, WIDE), (16, WIDE)),
    }


REDUCE = reduce_specs(None, None, None, None)
def reduce_scratch(names, staged):
    out = []
    for name in names:
        big, small = REDUCE[name][3:]
        out += [vm(big), vm((3,) + big)] if name in staged else []
        out += [vm(big), vm((3,) + small)]
    n = len(names)
    return out + [dma(n, 6), dma(n, 6), dma(n, 4)]


def make_reduces(me, names, parts, refs, land=None, landed=(), stage=None):
    specs, out = reduce_specs(*parts), {}
    for name in names:
        if stage and name in stage:
            own, got = stage[name]
        else:
            own, got = refs.pop(0), refs.pop(0)
            got = [got.at[k] for k in range(3)]
        out[name] = (own, got, refs.pop(0), refs.pop(0))
    ssem, rsem, loc = refs.pop(0), refs.pop(0), refs.pop(0)
    for n, (name, bufs) in enumerate(out.items()):
        there = land.get(name) if land else None
        out[name] = Reduce(me, specs[name], *bufs, ssem.at[n], rsem.at[n], loc.at[n], there, name in landed)
    return out


COLUMNS = {"ia": (0, 256), "ib": (256, 384), "g": (384, 896), "u": (896, 1408)}
MLP = ("g", "u", "da", "db")
REST = ("ia", "ib", "o")


def finish_columns(reds, names, fin):
    for name in names:
        lo, hi = COLUMNS[name]
        total = reds[name].three()
        for dp in range(2):
            for z in range(4):
                fin[dp, z, :, lo:hi] = padded(total[dp, 12 * z : 12 * z + 12])


def finish_down(reds, down):
    down[:, :, 0:768] = reds["da"].three().astype(BF)
    down[:, :, 768:1536] = reds["db"].three().astype(BF)


def lane_masks(rows):
    lane = lax.broadcasted_iota(jnp.int32, (rows, 128), 1)
    v0 = ((lane >= 48) & (lane < 64)) | (lane >= 112)
    v1 = ((lane >= 64) & (lane < 80)) | (lane < 16)
    v2 = ((lane >= 80) & (lane < 96)) | ((lane >= 16) & (lane < 32))
    return v0, v1, v2


def split_packed(packed, key_ref, value_ref):
    v0, v1, v2 = lane_masks(128)

    @pl.loop(0, 8)
    def _(p):
        rows = span_of(p * 128, 128)
        t0, t1, t2 = (packed[rows, 128 * t : 128 * t + 128].astype(F32) for t in range(3))
        key_ref[rows] = jnp.where(v0, 0.0, t2).astype(BF)
        value = jnp.where(v0, t0, 0.0)
        value = value + jnp.where(v1, pltpu.roll(t1, 16, 1), 0.0)
        value = value + jnp.where(v2, pltpu.roll(t2, 32, 1), 0.0)
        value_ref[rows] = value.astype(BF)


def flip(ref):
    return jnp.transpose(ref[...].astype(F32)).astype(BF)


def stacked(ref, rows):
    return jnp.concatenate([ref[rows, 0:128], ref[rows, 128:256]], axis=0)


def rms_of(values):
    return lax.rsqrt(jnp.mean(values * values, axis=-1, keepdims=True) + EPS)


def fwd_kernel(l, *refs):
    first = l == 0
    g_attn, g_mlp = (slice(2 * l + i, 2 * l + i + 1) for i in (0, 1))
    refs = list(refs)
    take = lambda n: [refs.pop(0) for _ in range(n)]
    (stream,) = take(1)
    (gains_in,) = (None,) if first else take(1)
    cos, sin, pcol, prow = take(4)
    (h_in,) = take(1)
    w_out, w_down, s_g, s_u = take(4)
    s_gain, s_next = take(2) if first else (None, None)
    (cot,) = (None,) if first else take(1)
    (o_stream,) = take(1) if first else (None,)
    o_middle, o_lse = take(2)
    (o_gains,) = take(1) if first else (gains_in,)
    o_normed, o_qkv, o_mixed, o_nmlp, o_gate, o_up, o_hidden, o_wo, o_wg, o_wu, o_wd = take(11)
    o_win, o_next = take(2) if first else (None, None)
    (o_down,) = (None,) if first else take(1)
    w_in, w_o, w_g, w_u, w_d = take(5)
    buf1, buf2, qs, qr, ms, mr, gate_v, up_v, hid, keys, vals, vals_t, middle = take(13)
    whole, keep, give, got, ring_out, ring_in = take(6)
    ag_s, ag_r, ag2_s, ag2_r, rs_s, rs_r, rs2_s, rs2_r, ax_s, ax_r, bx_s, bx_r, loc, loc2, ga_s, ga_r = take(16)
    w_gain, w_next = take(2) if first else (None, None)
    cot_all, cot_s, cot_r = (None,) * 3 if first else take(3)
    me = Place()
    stores = []

    def store(src, dst):
        stores.append(pltpu.make_async_copy(src, dst, loc2.at[len(stores)]))
        stores[-1].start()

    n_item = [0]

    def down_rows(core, cols):
        row = pl.multiple_of((core * 4 + me.z) * 32 + me.yl * 16, 16)
        return w_down.at[l, pl.ds(row, 16), cols]

    def item(src, dst, order, *cols):
        i = n_item[0]
        n_item[0] += 1
        if not callable(src):
            src = lambda core, cols, ref=src: ref.at[core, :, cols]
        return Gather(me, src, dst, ga_s.at[i], ga_r.at[i], loc.at[i], order, cols)

    g_g, g_u = item(s_g.at[l], w_g, "xy", 0, 512), item(s_u.at[l], w_u, "yx", 0, 512)
    g_d = [item(down_rows, w_d, "xy", 0, 768), item(down_rows, w_d, "yx", 768, WIDE)]
    g_o = OutGather(me, w_out.at[l], w_o, ga_s.at[4], ga_r.at[4], loc.at[pl.ds(10, 3)])
    n_item[0] = 5
    g_in, g_next, g_gain = [], [], []
    if first:
        g_gain = [item(s_gain, w_gain, "yx", 0, 256)]
        g_in = [item(h_in.at[0], w_in, "yx", 0, 256), item(h_in.at[0], w_in, "xy", 256, 384)]
        g_next = [item(s_next.at[1], w_next, "yx", 0, 256), item(s_next.at[1], w_next, "xy", 256, 384)]
    everything = g_gain + g_in + [g_o, g_g, g_u] + g_d + g_next

    def each(items, step):
        for one in items:
            getattr(one, step)()

    own_rows = slot_rows(me.z, me.core)
    raw = buf2 if first else buf1
    if first:
        raw[own_rows] = stream[...]
    else:
        load_in = pltpu.make_async_copy(h_in, w_in, loc.at[5])
        load_in.start()
        load_cot = pltpu.make_async_copy(cot, cot_all.at[own_rows], loc.at[6])
        load_cot.start()
        s = stream[...]
        raw[own_rows] = (s * rms_of(s) * gains_in[g_attn, :]).astype(BF)
    me.greet(me.layer_partners())
    each(everything, "zero")
    ax = Exchange(me, qs, qr, ax_s, ax_r, True)

    def project(zz):
        rows = span_of(zz * 256, 256)
        y = mm(buf1[rows], w_in[...].reshape(WIDE, 384))
        for t in range(3):
            tile = y[:, 128 * t : 128 * t + 128]
            tile = tile * cos[...] + pltpu.roll(tile, 64, 1) * sin[...]
            qs[rows, 128 * t : 128 * t + 128] = tile.astype(BF)
        ax.send(zz * 2)
        ax.send(zz * 2 + 1)

    def normalise(zz):
        rows = span_of(zz * 256, 256)
        s = raw[rows].astype(F32)
        buf1[rows] = (s * rms_of(s) * o_gains[g_attn, :]).astype(BF)

    if first:

        def own_pair():
            each(g_gain + g_in, "two")

        def gains_here():
            each(g_gain, "three")
            o_gains[...] = jnp.zeros_like(o_gains)
            for owner in range(16):
                base = 96 * owner // 128 * 128
                width = min(256, WIDE - base)
                row = w_gain[owner // 8, owner % 8 // 2, owner % 2 * 2]
                o_gains[:, base : base + width] += row[:, :width]
            normalise(me.z)
            g_o.one()

        hooks = (lambda: each(g_gain + g_in, "one"), own_pair, gains_here)

        def others(zz):
            if zz is not me.z:
                normalise(zz)

        done_ag = all_gather(me, raw, ag_s, ag_r, others, hooks)
        done_ag()
        each(g_in, "three")

        @pl.loop(0, 4)
        def _(k):
            project(lax.rem(me.z + k, 4))

    else:
        load_in.wait()
        done_ag = all_gather(me, raw, ag_s, ag_r, project, (g_o.one,))
        load_cot.wait()
        ring = gather_steps(me, cot_all, cot_s, cot_r, lambda zz: None)
        next(ring)
    g_o.two()
    each((g_g, g_u), "one")
    ax.arrive()
    if not first:
        next(ring)
    store(buf1, o_normed)
    store(qr, o_qkv)
    split_packed(qr, keys, vals)
    vals_t[...] = flip(vals)
    bx = Exchange(me, ms, mr, bx_s, bx_r, False)

    @pl.loop(0, 8)
    def _(k):
        p = lax.rem(me.c + 1 + k, 8)
        rows = span_of(p * 128, 128)
        q = stacked(qr, rows)
        scores = mm_nt(keys[...], q)
        scores = jnp.where(pcol[...] <= prow[pl.ds(p, 1), :], scores, -1e30)
        top = jnp.max(scores, axis=0, keepdims=True)
        weights = jnp.exp2((scores - top) * SCALE2)
        total = jnp.sum(weights, axis=0, keepdims=True)
        o_lse[pl.ds(p, 1), :] = top * SCALE2 + jnp.log2(total)
        probs = (weights * (1.0 / total)).astype(BF)
        out = jnp.transpose(mm(vals_t[...], probs)).astype(BF)
        ms[rows, 0:128] = out[0:128]
        ms[rows, 128:256] = out[128:256]
        bx.send(p)

    each((g_g, g_u), "two")
    if not first:
        next(ring)
    each(g_d, "one")
    g_o.three()
    bx.arrive()
    store(mr, o_mixed)

    def out_part(zz):
        return mm(mr[span_of(zz * 256, 256)], w_o[...].reshape(256, WIDE))

    rs = (whole, keep, give, got, ring_out, ring_in)
    total, done_rs = reduce_scatter(me, out_part, *rs, rs_s, rs_r)
    mid = total + (stream[...].astype(F32) if first else stream[...])
    middle[...] = mid
    o_middle[...] = mid
    buf2[own_rows] = (mid * rms_of(mid) * o_gains[g_mlp, :]).astype(BF)
    waited = []
    if not first:
        done_cot = run(ring)
        store(cot_all, o_down)

    def gated(zz):
        if not waited:
            waited.append(1)
            each((g_g, g_u), "three")
        rows = span_of(zz * 256, 256)
        gate = mm(buf2[rows], w_g[...].reshape(WIDE, 512))
        gate_v[rows] = gate.astype(BF)
        up = mm(buf2[rows], w_u[...].reshape(WIDE, 512))
        up_v[rows] = up.astype(BF)
        hid[rows] = (gate / (1.0 + jnp.exp(-gate)) * up).astype(BF)
        for src, dst in ((buf2, o_nmlp), (gate_v, o_gate), (up_v, o_up), (hid, o_hidden)):
            store(src.at[rows], dst.at[rows])

    def weights_out():
        each(g_next, "one")
        for w, o in [(w_o, o_wo), (w_g, o_wg), (w_u, o_wu)] + ([(w_in, o_win)] if first else []):
            store(w, o)

    def down_here():
        each(g_d, "three")
        store(w_d, o_wd)

    hooks = (lambda: each(g_d, "two"), lambda: None, weights_out, down_here)
    done_ag2 = all_gather(me, buf2, ag2_s, ag2_r, gated, hooks)
    each(g_next, "two")
    done_rs()

    if not first:
        for done in (done_ag, ax.finish, bx.finish, done_ag2, done_cot):
            done()
        each(everything, "finish")
        for copy in stores:
            copy.wait()
        return

    def down_part(zz):
        return mm(hid[span_of(zz * 256, 256)], w_d[...].reshape(512, WIDE))

    def fill(n):
        if n == 2:
            each(g_next, "three")
            store(w_next, o_next)

    total, done_rs2 = reduce_scatter(me, down_part, *rs, rs2_s, rs2_r, fill)
    o_stream[...] = middle[...] + total
    for done in (ax.finish, bx.finish, done_ag2, done_rs2):
        done()
    each(everything, "finish")
    for copy in stores:
        copy.wait()


def norm_back_of(e, values, gain):
    q = rms_of(values)
    n = values * q
    dn = e * gain
    part = q * (dn - n * jnp.mean(dn * n, axis=-1, keepdims=True))
    return part, jnp.sum(e * n, axis=0, keepdims=True)


def bwd_kernel(l, *refs):
    last = l == 0
    g_attn, g_mlp = (slice(2 * l + i, 2 * l + i + 1) for i in (0, 1))
    refs = list(refs)
    take = lambda n: [refs.pop(0) for _ in range(n)]
    grad, stream, middle, gains, cos, sin, pcol, prow, lse = take(9)
    h_in, h_o, h_g, h_u, h_d, h_qkv, h_gate, h_up, h_normed, h_mixed, h_nmlp, h_hidden = take(12)
    above, landed = (take(4), dict(zip(MLP, take(4)))) if last else (None, None)
    (h_down,) = (None,) if last else take(1)
    o_grad, o_gains = take(2)
    (o_block,) = (None,) if last else take(1)
    o_fin, o_down, o_out = take(3) if last else (None,) * 3
    parts = take(4)
    o_din, o_dgu, o_dd, o_do = parts
    landing = dict(zip(MLP, take(4)))
    if last:
        landing["o"] = take(1)[0]
    w_in, w_o, w_g, w_u, w_d, buf1, buf2, qr, gate_v, up_v, gu, mgs, mgr = take(13)
    keys, vals, keys_t, dk, dv, dqs, ps, pr, mid_grad, mixed, nmlp, hid = take(12)
    d_in, d_gu, d_d, d_o = take(4)
    whole, keep, give, got, ring_out, ring_in = take(6)
    ag_s, ag_r, ag2_s, ag2_r, rs_s, rs_r, rs2_s, rs2_r, ax_s, ax_r, bx_s, bx_r, loc, loc2 = take(14)
    me = Place()
    pairs = (
        (h_d, w_d), (h_gate, gate_v), (h_up, up_v), (h_g, w_g), (h_u, w_u), (h_o, w_o), (h_qkv, qr), (h_in, w_in),
        (h_hidden, hid), (h_nmlp, nmlp), (h_mixed, mixed),
    )
    loads = [pltpu.make_async_copy(h, v, loc.at[i]) for i, (h, v) in enumerate(pairs)]
    for load in loads if last else loads[:5]:
        load.start()
    stores = []

    def store(src, dst):
        stores.append(pltpu.make_async_copy(src, dst, loc2.at[len(stores)]))
        stores[-1].start()

    rs3 = refs
    local = (d_in, d_gu, d_d, d_o)
    upper = {}
    if last:
        stage = {
            "g": [d_gu.at[:, :, k, :, 0:512] for k in range(4)], "u": [d_gu.at[:, :, k, :, 512:1024] for k in range(4)],
            "da": [d_d.at[:, :, k, :, 0:768] for k in range(4)], "db": [d_d.at[:, :, k, :, 768:WIDE] for k in range(4)],
        }
        stage["ia"] = [d_in.at[:, :, k, :, 0:256] for k in range(4)]
        stage["ib"] = [d_in.at[:, :, k, :, 256:384] for k in range(4)]
        stage["o"] = [d_o.at[:, k] for k in range(4)]
        stage = {name: (views[3], views[:3]) for name, views in stage.items()}
        upper = make_reduces(me, MLP + REST, above, refs, landed, MLP, stage)
        stage = {
            "g": [w_g.at[k] for k in range(4)], "u": [w_u.at[k] for k in range(4)],
            "da": [w_d.at[k, :, :, :, 0:768] for k in range(4)], "db": [w_d.at[k, :, :, :, 768:WIDE] for k in range(4)],
        }
        stage = {name: (views[3], views[:3]) for name, views in stage.items()}
        own = make_reduces(me, MLP, local, refs, landing, (), stage)
        es, er = refs
        own["o"] = Reduce(me, reduce_specs(*local)["o"], None, None, None, None, es, er, None, landing["o"])
    else:
        es, er = rs3[6:]
        specs = reduce_specs(*local)
        own = {
            name: Reduce(me, specs[name], None, None, None, None, es.at[n], er.at[n], None, landing[name])
            for n, name in enumerate(MLP)
        }

    def each(reds, names, step):
        for name in names:
            if name in reds:
                getattr(reds[name], step)()

    own_rows = slot_rows(me.z, me.core)
    if last:
        buf1[own_rows] = grad[...].astype(BF)
    else:
        load_down = pltpu.make_async_copy(h_down, buf1, loc.at[11])
        load_down.start()
    me.greet(me.layer_partners())
    each(upper, MLP, "load")
    each(upper, REST, "one")
    for load in loads[:3]:
        load.wait()

    def unit(zz):
        rows = span_of(zz * 256, 256)
        hg = mm_nt(buf1[rows], w_d[...].reshape(512, WIDE))
        gate, up = gate_v[rows].astype(F32), up_v[rows].astype(F32)
        sig = 1.0 / (1.0 + jnp.exp(-gate))
        gu[rows, 0:512] = (hg * up * (sig * (1.0 + gate * (1.0 - sig)))).astype(BF)
        gu[rows, 512:1024] = (hg * (gate * sig)).astype(BF)

    if last:
        hooks = (lambda: each(upper, REST, "load"), lambda: None, lambda: each(upper, MLP, "two"))
        done_ag = all_gather(me, buf1, ag_s, ag_r, unit, hooks)
    else:
        load_down.wait()
        for zz in range(4):
            unit(zz)
    for load in loads[3:5]:
        load.wait()
    for load in () if last else loads[5:]:
        load.start()

    def mlp_part(zz):
        rows = span_of(zz * 256, 256)
        return mm_nt(gu[rows, 0:512], w_g[...].reshape(WIDE, 512)) + mm_nt(gu[rows, 512:1024], w_u[...].reshape(WIDE, 512))

    def grad_down(b):
        cols = slice(256 * b, 256 * b + 256)
        d_d[b] = mm_tn(hid[:, cols], buf1[...]).astype(BF).reshape(4, 4, 16, WIDE)

    def grad_gu(b):
        cols = slice(384 * b, 384 * b + 384)
        pair = slice(b % 2 * 2, b % 2 * 2 + 2)
        d_gu[b // 2, pair] = mm_tn(nmlp[:, cols], gu[...]).astype(BF).reshape(2, 4, 48, 1024)

    def fill1(n):
        if n == 0:
            for load in loads[5:]:
                load.wait()
            grad_down(0)
            grad_down(1)
        elif n == 1:
            grad_gu(0)
            grad_gu(1)
        else:
            grad_gu(2)
            grad_gu(3)
            each(own, ("g", "u"), "one")

    rs = (whole, keep, give, got, ring_out, ring_in)
    e, done_rs = reduce_scatter(me, mlp_part, *rs, rs_s, rs_r, fill1)
    part, gain_part = norm_back_of(e, middle[...], gains[g_mlp, :])
    o_gains[1:2, :] = gain_part
    gm = grad[...].astype(F32) + part
    mid_grad[...] = gm
    buf2[own_rows] = gm.astype(BF)
    ax = Exchange(me, mgs, mgr, ax_s, ax_r, True)

    def mixed_back(zz):
        rows = span_of(zz * 256, 256)
        mgs[rows] = mm_nt(buf2[rows], w_o[...]).astype(BF)
        ax.send(zz * 2)
        ax.send(zz * 2 + 1)

    def hook0():
        split_packed(qr, keys, vals)
        keys_t[...] = flip(keys)
        dk[...] = jnp.zeros_like(dk)
        dv[...] = jnp.zeros_like(dv)

    def hook2():
        each(upper, REST, "arrive")
        each(upper, REST, "two")

    done_ag2 = all_gather(me, buf2, ag2_s, ag2_r, mixed_back, (hook0, lambda: None, hook2))
    if last:
        done_ag()
    normed = buf1
    load_normed = pltpu.make_async_copy(h_normed, normed, loc.at[11])
    load_normed.start()
    store(d_d, o_dd)
    store(d_gu, o_dgu)
    lanes = mm_tn(mixed[...], buf2[...])
    for head in range(2):
        chunk = [lanes[128 * head + 16 * c : 128 * head + 16 * c + 16] for c in (3, 7, 4, 0, 5, 1)]
        for b in range(8):
            first, shift = 12 * b // 16, 12 * b % 16
            piece = chunk[first][shift:]
            if shift > 4:
                piece = jnp.concatenate([piece, chunk[first + 1][: shift - 4]], axis=0)
            d_o[head * 2 + b // 4, b % 4] = padded(piece[0:12])
    store(d_o, o_do)
    if not last:

        def down_part(zz):
            return mm(hid[span_of(zz * 256, 256)], w_d[...].reshape(512, WIDE))

        done_rs()
        final = reduce_steps(me, down_part, whole, keep, *rs3[:6])
        next(final)
    ax.arrive()
    each(own, ("da", "db"), "one")

    @pl.loop(0, 8)
    def _(p):
        rows = span_of(p * 128, 128)
        q = stacked(qr, rows)
        mg = stacked(mgr, rows)
        scores = mm_nt(keys[...], q)
        allowed = pcol[...] <= prow[pl.ds(p, 1), :]
        probs = jnp.where(allowed, jnp.exp2(scores * SCALE2 - lse[pl.ds(p, 1), :]), 0.0)
        pg = mm_nt(vals[...], mg)
        inner = jnp.sum(probs * pg, axis=0, keepdims=True)
        sg = (probs * (pg - inner)).astype(BF)
        dk[...] += mm(sg, q)
        dv[...] += mm(probs.astype(BF), mg)
        dq = jnp.transpose(mm(keys_t[...], sg)) * SCALE
        dqs[rows, 0:128] = dq[0:128].astype(BF)
        dqs[rows, 128:256] = dq[128:256].astype(BF)

    if not last:
        next(final)
    bx = Exchange(me, ps, pr, bx_s, bx_r, False)
    v0, _, _ = lane_masks(128)

    @pl.loop(0, 8)
    def _(k):
        p = lax.rem(me.c + 1 + k, 8)
        rows = span_of(p * 128, 128)
        value = dv[rows]
        ps[rows, 0:128] = jnp.where(v0, value, dqs[rows, 0:128].astype(F32)).astype(BF)
        ps[rows, 128:256] = jnp.where(v0, pltpu.roll(value, 112, 1), dqs[rows, 128:256].astype(F32)).astype(BF)
        ps[rows, 256:384] = jnp.where(v0, pltpu.roll(value, 96, 1), dk[rows] * SCALE).astype(BF)
        bx.send(p)

    if last:
        each(own, MLP, "arrive")
        each(own, MLP, "load")
        done_rs()
    else:
        total, done_rs3 = run(final)
        o_block[...] = (middle[...] + total).astype(BF)
    load_normed.wait()
    bx.arrive()
    pre = qr

    def in_part(zz):
        rows = span_of(zz * 256, 256)
        for t in range(3):
            cols = slice(128 * t, 128 * t + 128)
            tile = pr[rows, cols].astype(F32)
            pre[rows, cols] = (tile * cos[...] - pltpu.roll(tile, 64, 1) * sin[...]).astype(BF)
        return mm_nt(pre[rows], w_in[...])

    def fill2(n):
        for b in ((0, 1), (2,), (3,))[n]:
            cols = slice(384 * b, 384 * b + 384)
            pair = slice(b % 2 * 2, b % 2 * 2 + 2)
            d_in[b // 2, pair] = mm_tn(normed[:, cols], pre[...]).astype(BF).reshape(2, 4, 48, 384)
        if n == 2:
            store(d_in, o_din)
        if n == 0 and last:
            each(own, MLP, "two")
            each(own, ("o",), "one")
        if n == 1 and last:
            finish_columns(upper, COLUMNS, o_fin.at[:, :, 1])
            finish_down(upper, o_down.at[:, 1])
            o_out[...] = upper["o"].three().astype(BF)

    e, done_rs2 = reduce_scatter(me, in_part, *rs, rs2_s, rs2_r, fill2)
    part, gain_part = norm_back_of(e, stream[...].astype(F32), gains[g_attn, :])
    o_gains[0:1, :] = gain_part
    o_grad[...] = mid_grad[...] + part
    for done in (done_ag2, ax.finish, bx.finish, done_rs2):
        done()
    for name, red in upper.items():
        red.finish((1,) if name in MLP else (0, 1))
    if last:
        finish_columns(own, ("g", "u"), o_fin.at[:, :, 0])
        finish_down(own, o_down.at[:, 0])
        own["o"].arrive()
    else:
        done_rs3()
        each(own, MLP, "arrive")
    for name, red in own.items():
        red.finish((0, 1) if last and name in MLP else (0,))
    for copy in stores:
        copy.wait()


def padded(rows):
    return jnp.concatenate([rows, jnp.zeros((4, rows.shape[1]), F32)], axis=0).astype(BF)


def grads_kernel(*refs):
    refs = list(refs)
    take = lambda n: [refs.pop(0) for _ in range(n)]
    gp0, gp1, fin_in, down_s, out1 = take(5)
    d_in, d_o, land_o = take(3)
    o_rows, o_down, o_out, o_gains = take(4)
    me = Place()
    reds = make_reduces(me, REST, (d_in, None, None, d_o), refs, {"o": land_o}, ("o",))
    gains, fin_s, fin_r, down_r, out_s, out_r, sum_a, sum_b, got_a, got_b, got_c = take(11)
    fin_ss, fin_rs, gain_s, gain_r, down_ss, down_rs, out_ss = take(7)
    rest = [reds["ia"], reds["ib"]]
    group = [(k, c) for k in range(4) for c in range(2) if k or c]

    def mate(k, c):
        return {"z": lax.rem(me.z + k, 4), "core": lax.rem(me.core + c, 2)}

    mirror = {"x": me.z, "z": me.x}
    apart = me.x != me.z
    for red in reds.values():
        red.load()
    gains[...] = jnp.zeros_like(gains)
    gains[0:2] = gp0[0:2]
    gains[2:4] = gp1[0:2]
    me.greet(
        [me.near("x", k) for k in (1, 2, 3)] + [me.near("y", k) for k in (1, 2, 3)]
        + [mate(*m) for m in group] + [{"yl": 1 - me.yl, "core": me.oc}],
        mirror=True,
    )

    def gain_copy(stage, axis, src, got, k):
        i = 3 * stage + k - 1
        return push(src, got.at[k - 1], gain_s.at[i], gain_r.at[i], me.near(axis, k))

    def gain_sum(stage, axis, src, got, dst):
        total = src[...]
        for k in (1, 2, 3):
            gain_copy(stage, axis, src, got, k).wait_recv()
            total = total + got[k - 1]
        dst[...] = total

    slot = me.z * 2 + me.core

    def fin(l, i, come):
        k, c = group[i]
        to_z, to_core = lax.rem(me.z + k, 4), lax.rem(me.core + c, 2)
        from_z = lax.rem(me.z + 4 - k, 4)
        dst = fin_r.at[from_z * 2 + to_core, l] if come else fin_r.at[slot, l]
        src = fin_in.at[to_core, to_z, l] if l else fin_s.at[to_core, to_z]
        return push(src, dst, fin_ss.at[l, i], fin_rs.at[l, i], mate(k, c))

    def down(dp, half):
        dev = {"core": jnp.int32(dp), "yl": me.core}
        return push(down_s.at[dp], down_r.at[half], down_ss.at[dp], down_rs.at[half], dev)

    mine = me.yl == me.core

    for k in (1, 2, 3):
        gain_copy(0, "y", gains, got_a, k).start()
    for red in rest:
        red.one()
    for i in range(7):
        fin(1, i, False).start()
    for dp in range(2):
        keep = mine & (me.core == dp)

        @pl.when(jnp.logical_not(keep))
        def _(dp=dp):
            down(dp, me.yl).start()

        @pl.when(keep)
        def _(dp=dp):
            down_r[me.yl] = down_s[dp]

    reds["o"].two()
    fin_s[...] = fin_in[:, :, 0]
    for red in rest:
        red.arrive()
    gain_sum(0, "y", gains, got_a, sum_a)
    for k in (1, 2, 3):
        gain_copy(1, "x", sum_a, got_b, k).start()
    for red in rest:
        red.two()
    gain_sum(1, "x", sum_a, got_b, sum_b)

    def gain_mate(i):
        return push(sum_b, got_c.at[i], gain_s.at[6 + i], gain_r.at[6 + i], mate(*group[i]))

    for i in range(7):
        gain_mate(i).start()
    out_s[1] = out1[...]
    finish_columns(reds, ("ia", "ib"), fin_s)
    out_s[0] = reds["o"].three().astype(BF)

    def out_copy():
        return push(out_s, out_r, out_ss.at[0], out_ss.at[1], mirror)

    for i in range(7):
        fin(0, i, False).start()
    @pl.when(apart)
    def _():
        out_copy().start()

    @pl.when(jnp.logical_not(apart))
    def _():
        out_r[...] = out_s[...]

    fin_r[slot, 0] = fin_s[me.core, me.z]
    fin_r[slot, 1] = fin_in[me.core, me.z, 1]
    total = sum_b[...]
    for i in range(7):
        gain_mate(i).wait_recv()
        total = total + got_c[i]
    o_gains[...] = total
    for i in range(7):
        fin(0, i, True).wait_recv()
        fin(1, i, True).wait_recv()
    o_rows[...] = fin_r[...]
    for half in range(2):

        @pl.when(jnp.logical_not(mine & (me.yl == half)))
        def _(half=half):
            down(0, half).wait_recv()

    o_down[...] = down_r[...]

    @pl.when(apart)
    def _():
        out_copy().wait_recv()

    o_out[...] = out_r[...]
    reds["o"].finish((1,))
    for red in rest:
        red.finish()
    for k in (1, 2, 3):
        gain_copy(0, "y", gains, got_a, k).wait_send()
        gain_copy(1, "x", sum_a, got_b, k).wait_send()
    for i in range(7):
        gain_mate(i).wait_send()
        fin(0, i, False).wait_send()
        fin(1, i, False).wait_send()
    for dp in range(2):

        @pl.when(jnp.logical_not(mine & (me.core == dp)))
        def _(dp=dp):
            down(dp, me.yl).wait_send()

    @pl.when(apart)
    def _():
        out_copy().wait_send()


def vm(shape, dtype=BF):
    return pltpu.VMEM(shape, dtype)


def rs_scratch():
    return [vm((4, 128, WIDE)), vm((4, 128, WIDE)), vm((6, 64, WIDE)), vm((6, 64, WIDE))]


def dma(*shape):
    return pltpu.SemaphoreType.DMA(shape)


def sems():
    return [dma(n) for n in (13, 13, 13, 13, 10, 10, 10, 10, 8, 8, 8, 8, 16, 32)]


WEIGHTS = [(WIDE, 384), (256, WIDE), (WIDE, 512), (WIDE, 512), (512, WIDE)]
SPLIT = [(2, 4, 4, 48, 384), (4, 64, WIDE), (2, 4, 4, 48, 512), (2, 4, 4, 48, 512), (2, 4, 4, 16, WIDE)]
PARTS = [(2, 4, 4, 48, 384), (2, 4, 4, 48, 1024), (2, 4, 4, 16, WIDE), (4, 4, 16, WIDE)]
RING = [((256, WIDE), F32), ((4, 128, WIDE), BF)]


def run_kernel(kernel, name, cid, ins, in_vmem, outs, out_vmem, scratch):
    place = {True: pltpu.VMEM, False: pl.ANY}
    return pl.pallas_call(
        kernel,
        name=name,
        out_shape=[jax.ShapeDtypeStruct(s, d) for s, d in outs],
        in_specs=[pl.BlockSpec(memory_space=place[i < in_vmem]) for i in range(len(ins))],
        out_specs=[pl.BlockSpec(memory_space=place[i < out_vmem]) for i in range(len(outs))],
        scratch_shapes=scratch,
        compiler_params=pltpu.CompilerParams(
            collective_id=cid, has_side_effects=True, vmem_limit_bytes=58 * 2**20
        ),
    )(*ins)


def layer_fwd(l, stream, gains, tables, h_in, sources, extra):
    first = l == 0
    outs = [((128, WIDE), F32)] * (2 if first else 1) + [((8, 256), F32)] + ([((8, WIDE), F32)] if first else [])
    n_vmem = len(outs)
    outs += [
        ((1024, WIDE), BF), ((1024, 384), BF), ((1024, 256), BF), ((1024, WIDE), BF),
        ((1024, 512), BF), ((1024, 512), BF), ((1024, 512), BF),
    ] + [(s, BF) for s in SPLIT[1:]] + ([(SPLIT[0], BF)] * 2 if first else [((1024, WIDE), BF)])
    scratch = [vm(s) for s in SPLIT] + [
        vm((1024, WIDE)), vm((1024, WIDE)), vm((1024, 384)), vm((1024, 384)), vm((1024, 256)), vm((1024, 256)),
        vm((1024, 512)), vm((1024, 512)), vm((1024, 512)),
        vm((1024, 128)), vm((1024, 128)), vm((128, 1024)), vm((128, WIDE), F32),
    ] + [vm(*s) for s in RING] + rs_scratch() + sems() + [dma(10, 7), dma(10, 7)]
    if first:
        scratch += [vm((2, 4, 4, 8, 256), F32), vm(SPLIT[0])]
    else:
        scratch += [vm((1024, WIDE)), dma(13), dma(13)]
    ins = [stream] + ([] if first else [gains]) + [*tables, h_in, *sources, *extra]
    kernel = functools.partial(fwd_kernel, l)
    return run_kernel(kernel, f"layer_forward_{l}", 1 + l, ins, 5 if first else 6, outs, n_vmem, scratch)


def layer_bwd(l, grad, stream, middle, gains, tables, lse, weights, saved, above):
    last = l == 0
    outs = [((128, WIDE), F32), ((8, WIDE), F32)]
    outs += [((2, 4, 2, 16, 1408), BF), ((2, 2, 16, WIDE), BF), ((16, WIDE), BF)] if last else [((128, WIDE), BF)]
    n_vmem = len(outs)
    outs += [(s, BF) for s in PARTS]
    outs += [((3,) + REDUCE[n][3], BF) for n in (MLP + ("o",) if last else MLP)]
    shapes = WEIGHTS[:2] + [(4, 2, 4, 48, 512), (4, 2, 4, 48, 512), (4, 2, 4, 16, WIDE)]
    scratch = [vm(s) for s in shapes] + [
        vm((1024, WIDE)), vm((1024, WIDE)), vm((1024, 384)), vm((1024, 512)), vm((1024, 512)),
        vm((1024, 1024)), vm((1024, 256)), vm((1024, 256)),
        vm((1024, 128)), vm((1024, 128)), vm((128, 1024)), vm((1024, 128), F32), vm((1024, 128), F32),
        vm((1024, 256)), vm((1024, 384)), vm((1024, 384)), vm((128, WIDE), F32),
        vm((1024, 256)), vm((1024, WIDE)), vm((1024, 512)),
    ] + [vm(s) for s in PARTS] + [vm(*s) for s in RING] + rs_scratch() + sems()
    if last:
        scratch += reduce_scratch(MLP + REST, ()) + reduce_scratch(MLP, ()) + [dma(6), dma(6)]
    else:
        scratch += rs_scratch() + [dma(10), dma(10), dma(4, 6), dma(4, 6)]
    weights = [w.reshape(s) for w, s in zip(weights, shapes)]
    ins = [grad, stream, middle, gains, *tables, lse, *weights, *saved, *(above or ())]
    kernel = functools.partial(bwd_kernel, l)
    return run_kernel(kernel, f"layer_backward_{l}", 3 + l, ins, 9, outs, n_vmem, scratch)


def picks(rows, cols, test):
    r = lax.broadcasted_iota(jnp.int32, (rows, cols), 0)
    c = lax.broadcasted_iota(jnp.int32, (rows, cols), 1)
    return jnp.where(test(r, c), 1.0, 0.0).astype(BF)


def packed_place(n):
    t, i = n // 128, n % 128
    value = ((i >= 48) & (i < 64)) | (i >= 112)
    feature = jnp.where(value, 32 * t + jnp.where(i < 64, i - 48, i - 96), jnp.where(i < 48, i, i - 16))
    return t, feature, value


def prepare_kernel(
    order, wq, wk, wv, wg, wu, ga, gm, o_in, o_g, o_u, o_gain, o_cos, o_sin, o_pcol, o_prow, vq, vk, vv, vg, vu, loc
):
    core, z, yl = lax.axis_index("core"), lax.axis_index("z"), lax.axis_index("yl")
    own = pl.ds(pl.multiple_of(yl * 48, 16), 48)
    loads = [
        pltpu.make_async_copy(h.at[:, own], v, loc.at[i])
        for i, (h, v) in enumerate(((wq, vq), (wk, vk), (wv, vv), (wg, vg), (wu, vu)))
    ]
    for load in loads:
        load.start()
    ctx = lax.axis_index("x") * 2 + lax.axis_index("yh")
    for span in range(16):
        o_pcol[64 * span : 64 * span + 64] = order[span] * 64 + lax.broadcasted_iota(jnp.int32, (64, 1), 0)
    lane = lax.broadcasted_iota(jnp.int32, (1, 256), 1)
    for p in range(8):
        start = jnp.where(lane % 128 < 64, order[2 * p], order[2 * p + 1]) * 64
        o_prow[p : p + 1, :] = start + lane % 64
    row = lax.broadcasted_iota(jnp.int32, (128, 128), 0)
    col = lax.broadcasted_iota(jnp.int32, (128, 128), 1)
    place = jnp.where(row < 64, order[2 * ctx], order[2 * ctx + 1]) * 64 + row % 64
    turning = (col % 64) < 48
    freq = jnp.exp((col % 64).astype(F32) * (-2.0 * math.log(ROPE_BASE) / HEAD))
    angles = place.astype(F32) * freq
    cos = jnp.where(turning, jnp.cos(angles), 1.0)
    sin = jnp.where(turning, jnp.sin(angles), 0.0)
    sin = jnp.where(col < 64, -sin, sin)
    for half in range(2):
        o_cos[128 * half : 128 * half + 128] = cos
        o_sin[128 * half : 128 * half + 128] = sin
    owner = core * 8 + ctx
    shift = lax.rem(96 * owner, 128)
    move = picks(96, 256, lambda r, c: c == r + shift)
    zero = jnp.zeros((4, 96), F32)
    attn, mlp = ga[...].astype(F32), gm[...].astype(F32)
    both = jnp.concatenate([attn[0:1], mlp[0:1], attn[1:2], mlp[1:2]], axis=0)
    placed = mm(jnp.concatenate([both, zero], axis=0).astype(BF), move)
    o_gain[0] = placed
    o_gain[1] = placed
    spread = [
        picks(1024, 128, lambda r, c, j=cc * 4 + z: (r // 256 == c // 32) & (r % 256 == 32 * j + c % 32)) for cc in range(2)
    ]
    spread = jnp.concatenate(spread, axis=1)

    def query(r, n, j):
        t, f, value = packed_place(n)
        return jnp.logical_not(value) & (t < 2) & (r == j * 192 + t * 96 + f)

    def key(r, n, j):
        t, f, value = packed_place(n)
        return jnp.logical_not(value) & (t == 2) & (r == j * 96 + f)

    def val(r, n, j):
        t, f, value = packed_place(n)
        return value & (r == j * 96 + f)

    for load in loads[:3]:
        load.wait()
    for cc in range(2):
        j = cc * 4 + z
        out = mm(vq[...].reshape(96, WIDE), picks(WIDE, 384, lambda r, n: query(r, n, j)))
        out = out + mm(vk[...].reshape(96, 768), picks(768, 384, lambda r, n: key(r, n, j)))
        out = out + mm(vv[...].reshape(96, 768), picks(768, 384, lambda r, n: val(r, n, j)))
        o_in[:, cc] = out.astype(BF).reshape(LAYERS, 48, 384)
    for load in loads[3:]:
        load.wait()
    for v, o in ((vg, o_g), (vu, o_u)):
        for b in range(4):
            out = mm(v[:, :, 1024 * b : 1024 * b + 1024].reshape(96, 1024), spread).astype(BF)
            for cc in range(2):
                o[:, cc, :, 128 * b : 128 * b + 128] = out[:, 128 * cc : 128 * cc + 128].reshape(LAYERS, 48, 128)


def prepare(order, wq, wk, wv, wg, wu, ga, gm):
    shapes = [((LAYERS, 2, 48, 384), BF), ((LAYERS, 2, 48, 512), BF), ((LAYERS, 2, 48, 512), BF), ((2, 8, 256), F32)]
    shapes += [((256, 128), F32), ((256, 128), F32), ((1024, 1), jnp.int32), ((8, 256), jnp.int32)]
    in_vmem = pl.BlockSpec(memory_space=pltpu.VMEM)
    return pl.pallas_call(
        prepare_kernel,
        name="prepare_sources",
        out_shape=[jax.ShapeDtypeStruct(s, d) for s, d in shapes],
        in_specs=[pl.BlockSpec(memory_space=pltpu.SMEM)] + [pl.BlockSpec(memory_space=pl.ANY)] * 5 + [in_vmem] * 2,
        out_specs=[in_vmem] * 8,
        scratch_shapes=[vm((LAYERS, 48, n)) for n in (WIDE, 768, 768, 4096, 4096)] + [dma(5)],
        compiler_params=pltpu.CompilerParams(vmem_limit_bytes=60 * 2**20),
    )(order, wq, wk, wv, wg, wu, ga, gm)


def assemble_kernel(cols, downs, outs, o_q, o_k, o_v, o_o, o_g, o_u, o_d):
    def member(j, lo, hi):
        return cols[j % 4 * 2 + j // 4, :, :, lo:hi].reshape(32, hi - lo)

    def put(dst, lo, hi, value):
        for l in range(LAYERS):
            dst[:, l, lo:hi] = value[16 * l : 16 * l + 12]

    def query(n, c, i):
        t, f, value = packed_place(n)
        return jnp.logical_not(value) & (t < 2) & (c == i * 192 + t * 96 + f)

    def key(n, c, i):
        t, f, value = packed_place(n)
        return jnp.logical_not(value) & (t == 2) & (c == i * 96 + f)

    def val(n, c, i):
        t, f, value = packed_place(n)
        return value & (c == i * 96 + f)

    for dst, test, per in ((o_q, query, 2), (o_k, key, 4), (o_v, val, 4)):
        moves = [picks(384, 384, lambda n, c, i=i: test(n, c, i)) for i in range(per)]
        for m in range(8 // per):
            total = sum(mm(member(per * m + i, 0, 384), moves[i]) for i in range(per))
            put(dst, 384 * m, 384 * m + 384, total)
    back = [picks(128, 1024, lambda r, c, j=j: (c // 256 == r // 32) & (c % 256 == 32 * j + r % 32)) for j in range(8)]
    for dst, start in ((o_g, 384), (o_u, 896)):
        for b in range(4):
            total = sum(mm(member(j, start + 128 * b, start + 128 * b + 128), back[j]) for j in range(8))
            put(dst, 1024 * b, 1024 * b + 1024, total)
    for l in range(LAYERS):
        o_o[:, l, :] = outs[l].astype(F32)[0:12]
        for h in range(2):
            o_d[l, 16 * h : 16 * h + 16] = downs[h, l].astype(F32)


def assemble(cols, downs, outs):
    shapes = [(12, LAYERS, n) for n in (WIDE, 768, 768, WIDE, 4096, 4096)] + [(LAYERS, 32, WIDE)]
    in_vmem = pl.BlockSpec(memory_space=pltpu.VMEM)
    *grads, d_d = pl.pallas_call(
        assemble_kernel,
        name="assemble_gradients",
        out_shape=[jax.ShapeDtypeStruct(s, F32) for s in shapes],
        in_specs=[in_vmem] * 3,
        out_specs=[in_vmem] * 7,
        compiler_params=pltpu.CompilerParams(vmem_limit_bytes=60 * 2**20),
    )(cols, downs, outs)
    return [grad.transpose(1, 0, 2) for grad in grads] + [d_d]


def reduce_grads(gain_parts, done, parts):
    outs = [((8, 2, 16, 1408), BF), ((2, 2, 16, WIDE), BF), ((2, 16, WIDE), BF), ((8, WIDE), F32)]
    scratch = reduce_scratch(REST, REST) + [
        vm((8, WIDE), F32), vm((2, 4, 16, 1408)), vm((8, 2, 16, 1408)), vm((2, 2, 16, WIDE)),
        vm((2, 16, WIDE)), vm((2, 16, WIDE)), vm((8, WIDE), F32), vm((8, WIDE), F32),
        vm((3, 8, WIDE), F32), vm((3, 8, WIDE), F32), vm((7, 8, WIDE), F32),
        dma(2, 7), dma(2, 7), dma(13), dma(13), dma(2), dma(2), dma(2),
    ]
    return run_kernel(grads_kernel, "reduce_gradients", 5, [*gain_parts, *done, *parts], 5, outs, 4, scratch)


def body(
    tokens, span_order, attn_gain, w_query, key_matrix, value_matrix, w_out, mlp_gain, w_gate, w_up,
    w_down, cotangent,
):
    core, z, yl = lax.axis_index("core"), lax.axis_index("z"), lax.axis_index("yl")
    ctx = lax.axis_index("x") * 2 + lax.axis_index("yh")
    s_in, s_g, s_u, s_gain, *tables = prepare(
        span_order, w_query, key_matrix, value_matrix, w_gate, w_up, attn_gain, mlp_gain
    )
    stream, gains = tokens[0], None
    kept = []
    sources = (w_out, w_down, s_g, s_u)
    outs = layer_fwd(0, stream, gains, tables, s_in, sources, (s_gain, s_in))
    gains, w_next = outs[3], outs[-1]
    kept.append((stream, outs[1:3], outs[-2], outs[4:-2]))
    stream = outs[0]
    outs = layer_fwd(1, stream, gains, tables, w_next, sources, (cotangent[0],))
    kept.append((stream, outs[:2], w_next, outs[2:-1]))
    down_grad = outs[-1]

    g, gain_parts, above = cotangent[0], [None] * LAYERS, (down_grad,)
    for l in reversed(range(LAYERS)):
        stream, (middle, lse), w_in, outs = kept[l]
        normed, qkv, mixed, nmlp, gate, up, hid = outs[:7]
        saved = (qkv, gate, up, normed, mixed, nmlp, hid)
        res = layer_bwd(l, g, stream, middle, gains, tables, lse, (w_in, *outs[7:]), saved, above)
        g, gain_parts[l] = res[:2]
        if l:
            block_out, above = res[2][None], tuple(res[3:])
    cols, d_d, d_o, gp = reduce_grads(gain_parts, res[2:5], (res[5], res[8], res[13]))
    d_q, d_k, d_v, d_o, d_g, d_u, d_d = assemble(cols, d_d, d_o)
    owner = (core * 8 + ctx) * 8 + yl * 4 + z
    gp = lax.dynamic_slice(gp, (0, owner * 12), (4, 12)).reshape(2, 2, 12)
    return (block_out, g[None], gp[:, 0], d_q, d_k, d_v, d_o, gp[:, 1], d_g, d_u, d_d)


def solution(mesh):
    fine = Mesh(mesh.devices.reshape(2, 4, 2, 2, 4), ALL)
    seq, ctx, own, every = ("core", "yl", "z"), CTX, OWN, ALL
    act = P(seq, ctx, None)
    in_specs = (act, P(), P(None, own)) + (P(None, own, None),) * 4 + (P(None, own),) + (P(None, own, None),) * 3 + (act,)
    grad = P(None, every, None)
    out_specs = (act, act, P(None, every)) + (grad,) * 4 + (P(None, every),) + (grad,) * 3
    return jax.shard_map(body, mesh=fine, in_specs=in_specs, out_specs=out_specs, check_vma=False)
```
